32 devices in a mesh: seq: 8 (over y, x, core), mp: 4 (over z).
Axes of the slice: x: 2, y: 2, z: 4, core: 2. Of those that a mesh axis runs over, the one named last changes fastest.
Arguments:
- tokens: bfloat16 [2, 1024, 2048], P(None, 'seq', 'mp'), may hold values from -6 to 6
- norm_gain: float32 [2048], replicated, may hold values from 0.5 to 1.5
- in_weight: bfloat16 [2, 2048, 4096], P(None, 'seq', 'mp'), may hold values from -0.125 to 0.125
- conv_weight: float32 [4, 4096], P(None, 'mp'), may hold values from -3 to 3
- conv_bias: float32 [4096], P('mp'), may hold values from -3 to 3
- low_weight: bfloat16 [4096, 128], P('mp'), may hold values from -0.09375 to 0.09375
- state_weight: bfloat16 [4096, 32], P('mp'), may hold values from -0.09375 to 0.09375
- delta_weight: bfloat16 [128, 4096], P(None, 'mp'), may hold values from -0.5 to 0.5
- delta_bias: float32 [4096], P('mp'), may hold values from -7 to -2
- skip_gain: float32 [4096], P('mp'), may hold values from 0.5 to 1.5
- out_weight: bfloat16 [4096, 2048], P('mp', 'seq'), may hold values from -0.09375 to 0.09375
- cotangent: float32 [2, 1024, 2048], P(None, 'seq', 'mp'), may hold values from -6 to 6
- seq_group: int32 [2], replicated, may hold values from 0 to 3
- group_weight: float32 [4], replicated, may hold values from 0.25 to 4
Outputs:
- block_out: bfloat16 [2, 1024, 2048], P(None, 'seq', 'mp')
- d_tokens: float32 [2, 1024, 2048], P(None, 'seq', 'mp')
- d_norm_gain: float32 [2048], replicated
- d_in_weight: float32 [2, 2048, 4096], P(None, 'seq', 'mp')
- d_conv_weight: float32 [4, 4096], P(None, 'mp')
- d_conv_bias: float32 [4096], P('mp')
- d_low_weight: float32 [4096, 128], P('mp')
- d_state_weight: float32 [4096, 32], P('mp')
- d_delta_weight: float32 [128, 4096], P(None, 'mp')
- d_delta_bias: float32 [4096], P('mp')
- d_skip_gain: float32 [4096], P('mp')
- d_out_weight: float32 [4096, 2048], P('mp', 'seq')
The draws below stay inside these ranges and needn't reach their ends.
All inputs are finite; a program needn't handle non-finite values.
Results may differ from the reference program's by a relative error of at most 0.012.
Values may be sent and summed in bfloat16 or wider, within the bound.
A program may use at most 256 MiB of HBM per device.

```python
import math
import jax
import jax.numpy as jnp
from jax import lax

D = 2048
INNER = 4096
NS = 16
KCONV = 4
RANK = 128
GROUPS = 4
NSEQ = 2
SEQ_LEN = 1024


def level_of(stream_key, dims, pieces, smallest, high):
    level = 1.0
    for dim, shards_of in pieces:
        steps = jax.random.uniform(jax.random.fold_in(jax.random.fold_in(stream_key, 6), dim), (shards_of,), jnp.float32, smallest / len(pieces), high / len(pieces))
        level = level * jnp.repeat(jnp.exp(steps), dims[dim] // shards_of).reshape((-1,) + (1,) * (len(dims) - 1 - dim))
    return level


def noise(stream_key, extent, width, limit, cuts=(), kind=jnp.bfloat16):
    loudness = level_of(stream_key, extent, cuts, -0.22, 0.18) if cuts else 1.0
    values = jax.random.normal(stream_key, extent, jnp.float32) * width * loudness
    return jnp.minimum(jnp.maximum(values, -limit), limit).astype(kind)


def setup_inputs(seed: int = 0) -> dict:
    splits = jax.random.split(jax.random.key(seed), 15)
    return {
        "tokens": noise(splits[0], (NSEQ, SEQ_LEN, D), 1.0, 6.0, ((1, 8), (2, 4))),
        "norm_gain": jnp.clip(1.0 + 0.1 * jax.random.normal(splits[1], (D,), jnp.float32), 0.5, 1.5),
        "in_weight": noise(splits[2], (2, D, INNER), D ** -0.5, 0.125, ((1, 8), (2, 4))),
        "conv_weight": noise(splits[3], (KCONV, INNER), KCONV ** -0.5, 3.0, ((1, 4),), jnp.float32),
        "conv_bias": noise(splits[4], (INNER,), 0.5, 3.0, ((0, 4),), jnp.float32),
        "low_weight": noise(splits[5], (INNER, RANK), INNER ** -0.5, 0.09375, ((0, 4),)),
        "state_weight": noise(splits[6], (INNER, 2 * NS), INNER ** -0.5, 0.09375, ((0, 4),)),
        "delta_weight": noise(splits[7], (RANK, INNER), RANK ** -0.5, 0.5, ((1, 4),)),
        "delta_bias": jnp.clip(-7.0 + 5.0 * jax.random.uniform(splits[8], (INNER,), jnp.float32) ** level_of(splits[8], (INNER,), ((0, 4),), -0.2, 0.2), -7.0, -2.0),
        "skip_gain": jnp.clip(0.5 + 1.0 * jax.random.uniform(splits[9], (INNER,), jnp.float32) ** level_of(splits[9], (INNER,), ((0, 4),), -0.2, 0.2), 0.5, 1.5),
        "out_weight": noise(splits[10], (INNER, D), INNER ** -0.5, 0.09375, ((0, 4), (1, 8))),
        "cotangent": noise(splits[11], (NSEQ, SEQ_LEN, D), 1.0, 6.0, ((1, 8), (2, 4)), jnp.float32),
        "seq_group": jax.random.randint(splits[12], (NSEQ,), 0, GROUPS).astype(jnp.int32),
        "group_weight": jnp.clip(jnp.exp(jax.random.uniform(splits[13], (GROUPS,), jnp.float32, math.log(0.25), math.log(4.0))), 0.25, 4.0),
    }


EPSILON = 1e-05
HIGHEST = lax.Precision.HIGHEST

@jax.custom_vjp
def low(v):
    return lax.optimization_barrier(v.astype(jnp.bfloat16)).astype(jnp.float32)

@jax.custom_vjp
def low_back(v):
    return v

def low_keep(v):
    return (low(v), None)

def low_pass(kept, grad):
    return (grad,)

def back_keep(v):
    return (v, None)

def back_low(kept, grad):
    return (low(grad),)
low.defvjp(low_keep, low_pass)
low_back.defvjp(back_keep, back_low)

def combine(earlier, later):
    return (earlier[0] * later[0], later[0] * earlier[1] + later[1])

def mixer(tokens_f, norm_gain, in_weight, conv_weight, conv_bias, low_weight, state_weight, delta_weight, delta_bias, skip_gain, out_weight):
    inv_rms = lax.rsqrt(lax.optimization_barrier(jnp.mean(tokens_f * tokens_f, axis=-1, keepdims=True)) + EPSILON)
    normed = low(tokens_f * inv_rms * norm_gain)
    x_part = low(low_back(jnp.dot(normed, in_weight[0], precision=HIGHEST)))
    z_part = low_back(jnp.dot(normed, in_weight[1], precision=HIGHEST))
    num_taps = conv_weight.shape[0]
    length = tokens_f.shape[0]
    channels = x_part.shape[1]
    padded = jnp.concatenate([jnp.zeros((num_taps - 1, channels), jnp.float32), x_part], 0)
    conv_sum = conv_bias + jnp.zeros((length, channels), jnp.float32)
    for tap_index in range(num_taps):
        conv_sum = conv_sum + conv_weight[tap_index] * padded[tap_index:tap_index + length]
    inputs = low(jax.nn.silu(conv_sum))
    delta_low = low(low_back(jnp.dot(inputs, low_weight, precision=HIGHEST)))
    state_proj = low_back(jnp.dot(inputs, state_weight, precision=HIGHEST))
    delta_raw = low_back(jnp.dot(delta_low, delta_weight, precision=HIGHEST)) + delta_bias
    nstate = state_weight.shape[1] // 2
    b_state = state_proj[:, :nstate]
    c_state = state_proj[:, nstate:]
    beta_gate = jax.nn.sigmoid(delta_raw)
    step_size = beta_gate / (1.0 + beta_gate * lax.optimization_barrier(jnp.sum(b_state * b_state, axis=-1, keepdims=True)))
    span_rows = math.gcd(length, 256)
    num_blocks = length // span_rows

    def advance(carry_state, block_items):
        step_blk, b_blk, c_blk, in_blk = block_items
        decays = 1.0 - step_blk[:, None, :] * (b_blk * b_blk)[:, :, None]
        source = (step_blk * in_blk)[:, None, :] * b_blk[:, :, None]
        products, states = lax.associative_scan(combine, (decays, source), axis=0)
        states = states + products * carry_state[None]
        return (states[-1], jnp.einsum('tni,tn->ti', states, c_blk, precision=HIGHEST))
    start_state = jnp.zeros((nstate, channels), jnp.float32)
    _, read_blocks = lax.scan(jax.checkpoint(advance), start_state, (step_size.reshape(num_blocks, span_rows, channels), b_state.reshape(num_blocks, span_rows, nstate), c_state.reshape(num_blocks, span_rows, nstate), inputs.reshape(num_blocks, span_rows, channels)))
    read_out = read_blocks.reshape(length, channels) + skip_gain * inputs
    gated = read_out * jax.nn.silu(z_part)
    branch = low_back(jnp.dot(low(gated), out_weight, precision=HIGHEST))
    return tokens_f + branch

def reference(tokens, norm_gain, in_weight, conv_weight, conv_bias, low_weight, state_weight, delta_weight, delta_bias, skip_gain, out_weight, cotangent, seq_group, group_weight):
    params = tuple((param.astype(jnp.float32) for param in (norm_gain, in_weight, conv_weight, conv_bias, low_weight, state_weight, delta_weight, delta_bias, skip_gain, out_weight)))
    picks = (seq_group[:, None] == jnp.arange(group_weight.shape[0], dtype=jnp.int32)[None, :]).astype(jnp.float32)
    seq_weight = lax.optimization_barrier(jnp.sum(picks * group_weight[None, :].astype(jnp.float32), axis=1))

    def one_sequence(running, block_items):
        seq_tokens, seq_cot, weight_one = block_items
        result, pullback = jax.vjp(mixer, seq_tokens.astype(jnp.float32), *params)
        grads = pullback(seq_cot.astype(jnp.float32) * weight_one)
        running = tuple((acc_term + new_term for acc_term, new_term in zip(running, grads[1:])))
        return (running, (result.astype(jnp.bfloat16), grads[0]))
    zeros_init = tuple((jnp.zeros_like(param) for param in params))
    totals, (block_out, d_tokens) = lax.scan(one_sequence, zeros_init, (tokens, cotangent, seq_weight))
    return (block_out, d_tokens, totals[0], totals[1], totals[2], totals[3], totals[4], totals[5], totals[6], totals[7], totals[8], totals[9])
```

```python
import functools
import math

import jax
import jax.numpy as jnp
from jax import lax
from jax.experimental import pallas as pl
from jax.experimental.pallas import tpu as pltpu
from jax.sharding import PartitionSpec as P

SEQ_MB = 1
NMB = 2
EPSILON = 1e-05
VMEM_BYTES = 64 * 1024 * 1024 - 512 * 1024


def from_behind(value, axis, steps):
    count = lax.axis_size(axis)
    leading, last = (max(0, -steps), min(count, count - steps))
    return lax.ppermute(value, axis, [(source, source + steps) for source in range(leading, last)])


def prefix(value, axis, join, neutral, backward):
    count, mine = (lax.axis_size(axis), lax.axis_index(axis))
    pieces = jax.tree.map(lambda part: lax.all_gather(part, axis), value)
    if backward:
        pieces = jax.tree.map(lambda part: part[::-1], pieces)
        mine = count - 1 - mine
    subtotal = jax.tree.map(
        lambda part, zero: jnp.full_like(part, 0) + jnp.asarray(zero, part.dtype), value, neutral
    )

    def lap(position, subtotal):
        longer = join(subtotal, jax.tree.map(lambda part: part[position], pieces))
        return jax.tree.map(lambda new, old: jnp.where(position < mine, new, old), longer, subtotal)

    return lax.fori_loop(0, count - 1, lap, subtotal)


def combine(earlier, later):
    return (earlier[0] * later[0], later[0] * earlier[1] + later[1])


def make_gates(delta_raw, b_state, inputs):
    beta_gate = jax.nn.sigmoid(delta_raw)
    key_sq = jnp.sum(b_state * b_state, axis=-1, keepdims=True)
    step_size = beta_gate / (1.0 + beta_gate * key_sq)
    decays = 1.0 - step_size[:, :, None, :] * (b_state * b_state)[:, :, :, None]
    source = (step_size * inputs)[:, :, None, :] * b_state[:, :, :, None]
    return (decays, source)


def to_blocks(value, span_rows):
    old_shape = value.shape
    reshaped = value.reshape((old_shape[0], old_shape[1] // span_rows, span_rows) + old_shape[2:])
    return jnp.swapaxes(reshaped, 0, 1)


def from_blocks(value):
    joined = jnp.swapaxes(value, 0, 1)
    old_shape = joined.shape
    return joined.reshape((old_shape[0], old_shape[1] * old_shape[2]) + old_shape[3:])


def forward_block(carry_pair, block_items):
    delta_raw, b_state, inputs = block_items
    decays, source = make_gates(delta_raw, b_state, inputs)
    run_prod, run_state = carry_pair
    prod_list = []
    state_list = []
    for row_idx in range(decays.shape[1]):
        run_prod = run_prod * decays[:, row_idx]
        run_state = decays[:, row_idx] * run_state + source[:, row_idx]
        prod_list.append(run_prod)
        state_list.append(run_state)
    return ((run_prod, run_state), (jnp.stack(prod_list, axis=1), jnp.stack(state_list, axis=1)))


def backward_block(carry_trio, block_items):
    delta_raw, b_state, inputs, read_grad, c_state = block_items
    decays, _ = make_gates(delta_raw, b_state, inputs)
    grad_next, dec_next, tail_prod = carry_trio
    span_rows = decays.shape[1]
    grad_list = [None] * span_rows
    tail_list = [None] * span_rows
    for row_idx in reversed(range(span_rows)):
        drive_term = read_grad[:, row_idx][:, None, :] * c_state[:, row_idx][:, :, None]
        grad_next = drive_term + dec_next * grad_next
        tail_prod = dec_next * tail_prod
        grad_list[row_idx] = grad_next
        tail_list[row_idx] = tail_prod
        dec_next = decays[:, row_idx]
    return (
        (grad_next, dec_next, tail_prod),
        (jnp.stack(grad_list, axis=1), jnp.stack(tail_list, axis=1)),
    )


def silu_slope(value):
    sig_value = jax.nn.sigmoid(value)
    return sig_value * (1.0 + value * (1.0 - sig_value))


def plain(
    tokens,
    norm_gain,
    in_weight,
    conv_weight,
    conv_bias,
    low_weight,
    state_weight,
    delta_weight,
    delta_bias,
    skip_gain,
    out_weight,
    cotangent,
    seq_group,
    group_weight,
):
    stretch = tokens.shape[1]
    feature_dev = tokens.shape[2]
    channels = in_weight.shape[2]
    model_width = norm_gain.shape[0]
    num_taps = conv_weight.shape[0]
    nstate = state_weight.shape[1] // 2
    span_rows = math.gcd(stretch, 8)
    picks = (
        seq_group[:, None] == jnp.arange(group_weight.shape[0], dtype=jnp.int32)[None, :]
    ).astype(jnp.float32)
    seq_weight = jnp.sum(picks * group_weight[None, :], axis=1)
    feature_start = lax.axis_index("mp") * feature_dev
    ones_state = jnp.ones((SEQ_MB, nstate, channels), jnp.float32)
    zero_state = jnp.zeros_like(ones_state)
    acc_in = jnp.zeros((2, model_width, channels), jnp.float32)
    acc_out = jnp.zeros((channels, model_width), jnp.float32)
    acc_gain = jnp.zeros_like(norm_gain)
    acc_conv = jnp.zeros_like(conv_weight)
    acc_cbias = jnp.zeros_like(conv_bias)
    acc_low = jnp.zeros(low_weight.shape, jnp.float32)
    acc_state = jnp.zeros(state_weight.shape, jnp.float32)
    acc_delta = jnp.zeros(delta_weight.shape, jnp.float32)
    acc_dbias = jnp.zeros_like(delta_bias)
    acc_skip = jnp.zeros_like(skip_gain)
    outputs = []
    input_grads = []
    for micro_idx in range(NMB):
        whole_in, whole_out = (
            lax.all_gather(in_weight, "seq", axis=1, tiled=True),
            lax.all_gather(out_weight, "seq", axis=1, tiled=True),
        )
        first_seq = micro_idx * SEQ_MB
        block_tokens = tokens[first_seq : first_seq + SEQ_MB]
        full_tokens = lax.all_gather(block_tokens, "mp", axis=2, tiled=True).astype(jnp.float32)
        inv_rms = lax.rsqrt(jnp.mean(full_tokens * full_tokens, axis=-1, keepdims=True) + EPSILON)
        normed = (full_tokens * inv_rms * norm_gain).astype(jnp.bfloat16)
        both_parts = jnp.einsum(
            "scd,kdi->ksci", normed, whole_in, preferred_element_type=jnp.float32
        )
        x_round = both_parts[0].astype(jnp.bfloat16)
        z_part = both_parts[1]
        rim_rows = from_behind(x_round[:, stretch - (num_taps - 1) :], "seq", 1)
        padded = jnp.concatenate([rim_rows, x_round], axis=1).astype(jnp.float32)
        conv_sum = conv_bias + jnp.zeros((SEQ_MB, stretch, channels), jnp.float32)
        for tap_index in range(num_taps):
            conv_sum = (
                conv_sum + conv_weight[tap_index] * padded[:, tap_index : tap_index + stretch]
            )
        inputs_round = jax.nn.silu(conv_sum).astype(jnp.bfloat16)
        inputs_f = inputs_round.astype(jnp.float32)
        low_part = jnp.einsum(
            "sci,ir->scr", inputs_round, low_weight, preferred_element_type=jnp.float32
        )
        state_part = jnp.einsum(
            "sci,ir->scr", inputs_round, state_weight, preferred_element_type=jnp.float32
        )
        delta_low, state_proj = lax.psum((low_part, state_part), "mp")
        delta_round = delta_low.astype(jnp.bfloat16)
        delta_raw = (
            jnp.einsum("scr,ri->sci", delta_round, delta_weight, preferred_element_type=jnp.float32)
            + delta_bias
        )
        b_state = state_proj[..., :nstate]
        c_state = state_proj[..., nstate:]
        delta_blocks = to_blocks(delta_raw, span_rows)
        b_blocks = to_blocks(b_state, span_rows)
        c_blocks = to_blocks(c_state, span_rows)
        in_blocks = to_blocks(inputs_f, span_rows)
        stretch_pair, (prod_blocks, local_blocks) = lax.scan(
            forward_block, (ones_state, zero_state), (delta_blocks, b_blocks, in_blocks)
        )
        carried = prefix(stretch_pair, "seq", combine, (ones_state, zero_state), False)
        states = from_blocks(local_blocks) + from_blocks(prod_blocks) * carried[1][:, None]
        before = jnp.concatenate([carried[1][:, None], states[:, :-1]], axis=1)
        read_rec = jnp.einsum("scni,scn->sci", states, c_state)
        read_out = read_rec + skip_gain * inputs_f
        z_gate = jax.nn.silu(z_part)
        gated_round = (read_out * z_gate).astype(jnp.bfloat16)
        out_part = jnp.einsum(
            "sci,id->scd", gated_round, whole_out, preferred_element_type=jnp.float32
        )
        branch = lax.psum_scatter(out_part, "mp", scatter_dimension=2, tiled=True)
        outputs.append((block_tokens.astype(jnp.float32) + branch).astype(jnp.bfloat16))
        d_out = (
            cotangent[first_seq : first_seq + SEQ_MB]
            * seq_weight[first_seq : first_seq + SEQ_MB][:, None, None]
        )
        d_branch = lax.all_gather(d_out.astype(jnp.bfloat16), "mp", axis=2, tiled=True)
        acc_out = acc_out + jnp.einsum(
            "sci,scd->id", gated_round, d_branch, preferred_element_type=jnp.float32
        )
        d_gated = jnp.einsum("scd,id->sci", d_branch, whole_out, preferred_element_type=jnp.float32)
        d_read = d_gated * z_gate
        d_zpart = d_gated * read_out * silu_slope(z_part)
        acc_skip = acc_skip + jnp.sum(d_read * inputs_f, axis=(0, 1))
        read_blocks_grad = to_blocks(d_read, span_rows)
        (last_grad, first_dec, _), (grad_blocks, tail_blocks) = lax.scan(
            backward_block,
            (zero_state, ones_state, ones_state),
            (delta_blocks, b_blocks, in_blocks, read_blocks_grad, c_blocks),
            reverse=True,
        )
        tail_grad = first_dec * last_grad
        crossing = prefix(
            (stretch_pair[0], tail_grad), "seq", combine, (ones_state, zero_state), True
        )
        state_grad = from_blocks(grad_blocks) + from_blocks(tail_blocks) * crossing[1][:, None]
        _, gate_pullback = jax.vjp(make_gates, delta_raw, b_state, inputs_f)
        d_delta, d_bstate, d_inputs_state = gate_pullback((state_grad * before, state_grad))
        d_cstate = jnp.einsum("scni,sci->scn", states, d_read)
        acc_dbias = acc_dbias + jnp.sum(d_delta, axis=(0, 1))
        d_delta_round = d_delta.astype(jnp.bfloat16)
        acc_delta = acc_delta + jnp.einsum(
            "scr,sci->ri", delta_round, d_delta_round, preferred_element_type=jnp.float32
        )
        low_grad_part = jnp.einsum(
            "sci,ri->scr", d_delta_round, delta_weight, preferred_element_type=jnp.float32
        )
        state_grad_part = jnp.concatenate([d_bstate, d_cstate], axis=-1)
        d_low, d_state = lax.psum((low_grad_part, state_grad_part), "mp")
        d_low_round = d_low.astype(jnp.bfloat16)
        d_state_round = d_state.astype(jnp.bfloat16)
        acc_low = acc_low + jnp.einsum(
            "sci,scr->ir", inputs_round, d_low_round, preferred_element_type=jnp.float32
        )
        acc_state = acc_state + jnp.einsum(
            "sci,scr->ir", inputs_round, d_state_round, preferred_element_type=jnp.float32
        )
        d_inputs = d_read * skip_gain + d_inputs_state
        d_inputs = d_inputs + jnp.einsum(
            "scr,ir->sci", d_low_round, low_weight, preferred_element_type=jnp.float32
        )
        d_inputs = d_inputs + jnp.einsum(
            "scr,ir->sci", d_state_round, state_weight, preferred_element_type=jnp.float32
        )
        d_conv = d_inputs * silu_slope(conv_sum)
        acc_cbias = acc_cbias + jnp.sum(d_conv, axis=(0, 1))
        tap_grads = []
        d_padded = jnp.zeros((SEQ_MB, stretch + num_taps - 1, channels), jnp.float32)
        for tap_index in range(num_taps):
            tap_grads.append(
                jnp.sum(d_conv * padded[:, tap_index : tap_index + stretch], axis=(0, 1))
            )
            d_padded = d_padded + jnp.pad(
                conv_weight[tap_index] * d_conv,
                ((0, 0), (tap_index, num_taps - 1 - tap_index), (0, 0)),
            )
        acc_conv = acc_conv + jnp.stack(tap_grads)
        back_rim = from_behind(d_padded[:, : num_taps - 1], "seq", -1)
        d_xpart = d_padded[:, num_taps - 1 :] + jnp.pad(
            back_rim, ((0, 0), (stretch - (num_taps - 1), 0), (0, 0))
        )
        d_parts_round = jnp.stack([d_xpart, d_zpart]).astype(jnp.bfloat16)
        acc_in = acc_in + jnp.einsum(
            "scd,ksci->kdi", normed, d_parts_round, preferred_element_type=jnp.float32
        )
        norm_part = jnp.einsum(
            "ksci,kdi->scd", d_parts_round, whole_in, preferred_element_type=jnp.float32
        )
        d_normed = lax.psum(norm_part, "mp")
        acc_gain = acc_gain + jnp.sum(d_normed * full_tokens * inv_rms, axis=(0, 1))
        scaled = d_normed * norm_gain
        d_full = inv_rms * scaled - full_tokens * (inv_rms * inv_rms * inv_rms) * jnp.mean(
            scaled * full_tokens, axis=-1, keepdims=True
        )
        d_mine = lax.dynamic_slice_in_dim(d_full, feature_start, feature_dev, 2)
        input_grads.append(d_out + d_mine)
    d_in_weight, d_out_weight = (
        lax.psum_scatter(acc_in, "seq", scatter_dimension=1, tiled=True),
        lax.psum_scatter(acc_out, "seq", scatter_dimension=1, tiled=True),
    )
    summed = lax.psum(
        (acc_gain, acc_conv, acc_cbias, acc_low, acc_state, acc_delta, acc_dbias, acc_skip), "seq"
    )
    return (
        jnp.concatenate(outputs, axis=0),
        jnp.concatenate(input_grads, axis=0),
        summed[0],
        d_in_weight,
        summed[1],
        summed[2],
        summed[3],
        summed[4],
        summed[5],
        summed[6],
        summed[7],
        d_out_weight,
    )


MESH = pl.DeviceIdType.MESH
F32 = jnp.float32
BF16 = jnp.bfloat16
LANE = 128
GRP = 16
PADV = 8
SGVEC = 16


def nn(a, b):
    return lax.dot_general(a, b, (((1,), (0,)), ((), ())), preferred_element_type=F32)


def nt(a, b):
    return lax.dot_general(a, b, (((1,), (1,)), ((), ())), preferred_element_type=F32)


def tn(a, b):
    return lax.dot_general(a, b, (((0,), (0,)), ((), ())), preferred_element_type=F32)


def cut(start, size):
    return pl.ds(pl.multiple_of(start, size), size)


def each(count, step):
    lax.fori_loop(0, count, lambda index, unused: (step(index), unused)[1], 0)


def wide(value, times):
    return jnp.concatenate([value] * times, axis=1) if times > 1 else value


class Sizes:
    def __init__(self, mesh_shape, nseq, stretch, feature_dev, model, channels, nstate, rank):
        self.S, self.M = mesh_shape["seq"], mesh_shape["mp"]
        self.Q, self.T, self.Df, self.D, self.C = nseq, stretch, feature_dev, model, channels
        self.N, self.RK = nstate, rank
        self.R = nseq * stretch
        self.Ds = model // self.S
        self.B = max(1, feature_dev // self.Ds)
        self.levels = self.S.bit_length() - 1
        self.dims = [1 << bit for bit in range(1, self.levels)]
        self.masks = [2 * value for value in range(self.S // 2)]
        self.rows_sg = -(-(2 * rank + 2 * nstate + SGVEC) // (self.S * 32)) * 32
        self.E = max(self.R, self.Ds)

    def order(self, half):
        turn = half * (len(self.dims) // 2)
        return self.dims[turn:] + self.dims[:turn]

    def fits(self, taps):
        return (
            self.S >= 4
            and self.S & (self.S - 1) == 0
            and self.M > 1
            and self.Q == 2
            and self.T == LANE
            and self.Ds % 256 == 0
            and self.Df % self.Ds == 0
            and self.C % 256 == 0
            and self.N == GRP
            and self.RK == LANE
            and taps == 4
            and self.C * self.D <= (1 << 21)
        )


class Rows:
    def __init__(self, ref, base, rows, count):
        self.ref, self.base, self.rows, self.end = ref, base, rows, base + rows * count

    def block(self, index, start=0, size=None):
        first = pl.multiple_of(self.base + index * self.rows + start, 16)
        return self.ref.at[pl.ds(first, self.rows if size is None else size), :]


class Links:
    def __init__(self, sems, seq, mp):
        self.sems, self.used, self.seq, self.mp = sems, 0, seq, mp

    def sem(self, count=1):
        first = self.used
        self.used += count
        return first

    def copy(self, src, dst, send, recv, seq=None, mp=None):
        target = (self.seq if seq is None else seq, self.mp if mp is None else mp)
        return pltpu.make_async_remote_copy(
            src_ref=src,
            dst_ref=dst,
            send_sem=self.sems.at[send],
            recv_sem=self.sems.at[recv],
            device_id=target,
            device_id_type=MESH,
        )

    def arrived(self, dst, recv):
        self.copy(dst, dst, recv, recv).wait_recv()


class TreeGather:
    def __init__(self, z, links, half_view, whole_view):
        self.z, self.links, self.half, self.whole = z, links, half_view, whole_view
        self.recv = {(mask, h): links.sem() for mask in z.masks[1:] for h in range(2)}
        self.near = {mask: links.sem() for mask in z.masks}
        self.sent = []

    def level(self, depth):
        z, links = self.z, self.links
        for mask in z.masks:
            if bin(mask).count("1") != depth:
                continue
            owner = links.seq ^ mask
            for h in range(2):
                order = z.order(h)
                last = max([i for i, dim in enumerate(order) if dim & mask], default=-1)
                view = self.half(owner, h)
                if mask:
                    links.arrived(view, self.recv[mask, h])
                for dim in order[last + 1 :]:
                    copy = links.copy(view, view, links.sem(), self.recv[mask | dim, h], seq=links.seq ^ dim)
                    copy.start()
                    self.sent.append(copy)
            view = self.whole(owner)
            copy = links.copy(view, view, links.sem(), self.near[mask], seq=links.seq ^ 1)
            copy.start()
            self.sent.append(copy)

    def finish(self):
        for mask in self.z.masks:
            self.links.arrived(self.whole(self.links.seq ^ 1 ^ mask), self.near[mask])

    def drain(self):
        for copy in self.sent:
            copy.wait_send()


class LineGather:
    def __init__(self, z, links, view):
        self.z, self.links, self.view = z, links, view
        self.recv = links.sem(z.M)
        self.send = links.sem(2 * z.M)

    def parts(self, depth):
        for side, way in enumerate((1, -1)):
            owner, target = self.links.mp - way * depth, self.links.mp + way
            held = (owner >= 0) & (owner < self.z.M)
            more = held & (target >= 0) & (target < self.z.M)
            yield side, owner, target, held, more

    def copy(self, side, depth, owner, target):
        view = self.view(owner)
        return self.links.copy(view, view, self.send + 2 * depth + side, self.recv + owner, mp=target)

    def step(self, depth):
        for side, owner, target, held, more in self.parts(depth):
            if depth:

                @pl.when(held)
                def _():
                    self.links.arrived(self.view(owner), self.recv + owner)

            @pl.when(more)
            def _():
                self.copy(side, depth, owner, target).start()

    def drain(self):
        for depth in range(self.z.M):
            for side, owner, target, held, more in self.parts(depth):

                @pl.when(more)
                def _():
                    self.copy(side, depth, owner, target).wait_send()


class Swap:
    def __init__(self, z, links, slot):
        self.z, self.links, self.slot = z, links, slot
        self.recv = links.sem(z.M)
        self.send = links.sem(z.M)

    def one(self, src, away):
        target = lax.rem(self.links.mp + away, self.z.M)
        return self.links.copy(src, self.slot(away - 1), self.send + away, self.recv + away, mp=target)

    def start(self, src):
        for away in range(1, self.z.M):
            self.one(src, away).start()

    def wait(self):
        for away in range(1, self.z.M):
            self.links.arrived(self.slot(away - 1), self.recv + away)

    def drain(self, src):
        for away in range(1, self.z.M):
            self.one(src, away).wait_send()


class Scatter:
    def __init__(self, z, links, out, sums, far, rows):
        self.z, self.links, self.out, self.sums, self.far, self.rows = z, links, out, sums, far, rows
        self.near = {mask: links.sem() for mask in z.masks}
        self.near_send = {mask: links.sem() for mask in z.masks}
        self.sent = []
        self.hops = {}
        place = 0
        for h in range(2):
            order = z.order(h)
            for step, dim in enumerate(order):
                for mask in z.masks:
                    if mask & dim and not any(mask & other for other in order[:step]):
                        self.hops[h, step, mask] = (dim, links.sem(), links.sem(), place)
                        place += 1
        self.slots = place

    def half(self, mask, h):
        return self.sums.block(mask // 2, h * (self.rows // 2), self.rows // 2)

    def first(self, make, ready=None):
        z, links = self.z, self.links
        for mask in z.masks:
            src = make(links.seq ^ 1 ^ mask, mask)
            if ready is not None and mask == 0:
                ready()
            copy = links.copy(src, self.sums.block(mask // 2), self.near_send[mask], self.near[mask], seq=links.seq ^ 1)
            copy.start()
            self.sent.append(copy)

    def second(self, add):
        z, links = self.z, self.links
        by_need = sorted(z.masks, key=lambda mask: -bin(mask).count("1"))
        for mask in by_need:
            links.arrived(self.sums.block(mask // 2), self.near[mask])
            add(links.seq ^ mask, mask)
        self.send(0)

    def send(self, step):
        links = self.links
        for (h, at, mask), (dim, send, recv, place) in self.hops.items():
            if at == step:
                copy = links.copy(self.half(mask, h), self.far.block(place), send, recv, seq=links.seq ^ dim)
                copy.start()
                self.sent.append(copy)

    def fold(self, step):
        links = self.links
        for (h, at, mask), (dim, send, recv, place) in self.hops.items():
            if at != step:
                continue
            links.arrived(self.far.block(place), recv)
            into = mask ^ dim
            if step < len(self.z.dims) - 1:
                half = self.half(into, h)
                half[...] = (half[...].astype(F32) + self.far.block(place)[...].astype(F32)).astype(BF16)
        if step < len(self.z.dims) - 1:
            self.send(step + 1)

    def total(self, write):
        last = len(self.z.dims) - 1
        for (h, at, mask), (dim, send, recv, place) in self.hops.items():
            if at == last:
                rows = (h * (self.rows // 2), self.rows // 2)
                write(rows, self.half(0, h)[...].astype(F32) + self.far.block(place)[...].astype(F32))

    def drain(self):
        for copy in self.sent:
            copy.wait_send()


def slots_of(z):
    return Scatter(z, Links(None, 0, 0), None, None, None, 0).slots


NAMES_IN = [
    "tok",
    "cot",
    "gain",
    "win",
    "wout",
    "convw",
    "convb",
    "dbias",
    "skip",
    "loww",
    "statewt",
    "deltaw",
    "seqg",
    "groupw",
]
NAMES_OUT = ["blk", "dtok", "dgain", "din", "dout", "sg"]


def scratch_of(z):
    V = pltpu.VMEM
    half = z.S // 2
    slots = slots_of(z)
    return dict(
        tokg=V((z.S, z.R, z.Ds), BF16),
        halg=V((z.S, 16, z.Ds), BF16),
        hals=V((z.B, 16, z.Ds), BF16),
        db=V((z.S, z.R, z.Ds), BF16),
        inv=V((z.R, LANE), F32),
        normed=V((z.R + 16, z.D), BF16),
        normt=V((z.D, z.R), BF16),
        wx=V((2, z.D, z.C), BF16),
        wo=V((z.S, z.C, z.Ds), BF16),
        xpad=V((z.Q, 8 + z.T, z.C), F32),
        dcp=V((z.Q, z.T + 8, z.C), F32),
        conv=V((z.E, z.C), F32),
        s=V((z.E, z.C), F32),
        su=V((z.R, z.C), F32),
        fac=V((z.E, z.C), F32),
        zp=V((z.R, z.C), F32),
        rd=V((z.R, z.C), F32),
        dr=V((z.R, z.C), F32),
        u=V((z.R, z.C), BF16),
        gat=V((z.R, z.C), BF16),
        gatt=V((z.C, z.R), BF16),
        ddr=V((z.R, z.C), BF16),
        dzr=V((z.R, z.C), BF16),
        dxr=V((z.R, z.C), BF16),
        lowp=V((z.M, z.R, z.RK), BF16),
        stp=V((z.M, 2 * z.N, z.R), F32),
        low=V((z.R, z.RK), BF16),
        st=V((2 * z.N, z.R), F32),
        blkb=V((z.R, GRP * z.N), BF16),
        blkk=V((z.R, GRP * z.N), BF16),
        blkc=V((z.R, GRP * z.N), BF16),
        bc=V((z.Q, z.T, 2 * z.N, LANE), F32),
        hist=V((z.Q * (z.T + 1) * z.N, z.C), BF16),
        gbuf=V((GRP * z.N, z.C), BF16),
        ghbuf=V((GRP * z.N, z.C), BF16),
        ptot=V((z.Q, z.N, z.C), F32),
        stot=V((z.Q, z.N, z.C), F32),
        ppre=V((z.Q, z.N, z.C), F32),
        spre=V((z.Q, z.N, z.C), F32),
        csend=V((z.levels, z.Q, 2, z.N, z.C), BF16),
        crecv=V((z.levels, z.Q, 2, z.N, z.C), BF16),
        bsend=V((z.levels, z.Q, z.N, z.C), BF16),
        brecv=V((z.levels, z.Q, z.N, z.C), BF16),
        est=V((3, z.N, z.R), F32),
        dlowp=V((z.M, z.R, z.RK), BF16),
        dstp=V((z.M, 2 * z.N, z.R), BF16),
        orecv=V((z.M - 1, z.R, z.Df), BF16),
        nrecv=V((z.M - 1, z.R, z.Df), BF16),
        near_o=V((half * z.C, z.Ds), BF16),
        sum_o=V((half * z.C, z.Ds), BF16),
        far_o=V((slots * (z.C // 2), z.Ds), BF16),
        near_i=V((half * z.Ds, z.C), BF16),
        sum_1=V((half * z.Ds, z.C), BF16),
        far_1=V((slots * (z.Ds // 2), z.C), BF16),
        vec=V((SGVEC, z.C), F32),
        gv=V((z.levels + 1, 8, z.D), F32),
        gvr=V((z.levels, 8, z.D), F32),
        gvm=V((z.M - 1, 8, z.D), F32),
        mrow=V((z.M, 8, z.R), F32),
        sems=pltpu.SemaphoreType.DMA((420,)),
        local=pltpu.SemaphoreType.DMA((8,)),
        ready=pltpu.SemaphoreType.REGULAR((z.levels,)),
    )


def silu_parts(value):
    gate = 1.0 / (1.0 + jnp.exp(-value))
    return gate, value * gate


def fused_kernel(z, names, *refs):
    r = dict(zip(names, refs))
    g = lambda name: r[name]
    seq, mp = lax.axis_index("seq"), lax.axis_index("mp")
    links = Links(g("sems"), seq, mp)
    lanes_all = z.C // LANE
    first_block = mp * z.B

    def lane_loop(step):
        each(z.C // LANE, lambda index: step(cut(index * LANE, LANE)))

    local = g("local")
    mine_in = lambda k: g("wx").at[k, cut(seq * z.Ds, z.Ds), :]
    loads = [
        pltpu.make_async_copy(g("win").at[0], mine_in(0), local.at[0]),
        pltpu.make_async_copy(g("win").at[1], mine_in(1), local.at[1]),
        pltpu.make_async_copy(g("wout"), g("wo").at[seq], local.at[2]),
    ]
    for load in loads:
        load.start()
    for b in range(z.B):
        g("tokg")[first_block + b] = g("tok")[:, b * z.Ds : (b + 1) * z.Ds]
        tails = [
            g("tok")[q * z.T + z.T - 16 : q * z.T + z.T, b * z.Ds : (b + 1) * z.Ds].astype(F32)[8:]
            for q in range(z.Q)
        ]
        g("hals")[b] = jnp.concatenate(tails, axis=0).astype(BF16)

    barrier = pltpu.get_barrier_semaphore()
    ahead, behind = lax.rem(seq + 1, z.S), lax.rem(seq + z.S - 1, z.S)
    partners = [(seq ^ (1 << level), mp) for level in range(z.levels)] + [(ahead, mp), (behind, mp)]
    partners += [(seq, lax.rem(mp + away, z.M)) for away in range(1, z.M)]
    for partner in partners:
        pl.semaphore_signal(barrier, inc=1, device_id=partner, device_id_type=MESH)
    pl.semaphore_wait(barrier, len(partners))

    def of_in(k):
        def half(owner, h):
            return g("wx").at[k, cut(owner * z.Ds + h * (z.Ds // 2), z.Ds // 2), :]

        return TreeGather(z, links, half, lambda owner: g("wx").at[k, cut(owner * z.Ds, z.Ds), :])

    tree_x, tree_z = of_in(0), of_in(1)
    tree_o = TreeGather(
        z,
        links,
        lambda owner, h: g("wo").at[owner, pl.ds(h * (z.C // 2), z.C // 2), :],
        lambda owner: g("wo").at[owner],
    )
    line_t = LineGather(z, links, lambda owner: g("tokg").at[pl.ds(owner * z.B, z.B)])
    line_h = LineGather(z, links, lambda owner: g("halg").at[pl.ds(owner * z.B, z.B)])
    line_d = LineGather(z, links, lambda owner: g("db").at[pl.ds(owner * z.B, z.B)])
    depth = len(z.dims)

    loads[0].wait()
    tree_x.level(0)
    line_t.step(0)
    hal_send, hal_recv = links.sem(), links.sem()
    hal_mine = g("halg").at[pl.ds(first_block, z.B)]
    hal = links.copy(g("hals"), hal_mine, hal_send, hal_recv, seq=ahead)
    hal.start()

    def weight_of(q):
        total = jnp.float32(0.0)
        for group in range(g("groupw").shape[0]):
            total = total + jnp.where(g("seqg")[q] == group, g("groupw")[group], 0.0)
        return total

    seq_weight = [weight_of(q) for q in range(z.Q)]
    for q in range(z.Q):
        rows = pl.ds(q * z.T, z.T)
        for b in range(z.B):
            part = g("cot")[rows, b * z.Ds : (b + 1) * z.Ds] * seq_weight[q]
            g("db")[first_block + b, rows, :] = part.astype(BF16)

    links.arrived(hal_mine, hal_recv)
    line_h.step(0)
    line_t.step(1)
    line_h.step(1)
    tree_x.level(1)
    loads[1].wait()
    tree_z.level(0)
    for far in range(2, z.M):
        line_t.step(far)
        line_h.step(far)

    def add_squares(j, total):
        part = g("tokg")[j].astype(F32)
        edge = g("halg")[j].astype(F32)
        return (
            total[0] + jnp.sum(part * part, axis=1, keepdims=True),
            total[1] + jnp.sum(edge * edge, axis=1, keepdims=True),
        )

    squares = lax.fori_loop(
        0, z.S, add_squares, (jnp.zeros((z.R, 1), F32), jnp.zeros((16, 1), F32))
    )
    inv = lax.rsqrt(squares[0] * (1.0 / z.D) + EPSILON)
    inv_edge = lax.rsqrt(squares[1] * (1.0 / z.D) + EPSILON)
    g("inv")[...] = jnp.broadcast_to(inv, (z.R, LANE))

    def norm_block(j):
        features = cut(j * z.Ds, z.Ds)
        gain = g("gain")[:, features]
        normed = g("tokg")[j].astype(F32) * wide(g("inv")[...], z.Ds // LANE) * gain
        g("normed")[: z.R, features] = normed.astype(BF16)
        edge = g("halg")[j].astype(F32) * inv_edge * gain
        g("normed")[z.R :, features] = edge.astype(BF16)
        g("normt")[features, :] = normed.T.astype(BF16)

    each(z.S, norm_block)
    for rest in range(2, depth + 1):
        tree_x.level(rest)
    tree_x.finish()

    def x_chunk(index):
        lanes = cut(index * 256, 256)
        part = nn(g("normed")[...], g("wx")[0, :, lanes]).astype(BF16).astype(F32)
        for q in range(z.Q):
            edge = part[z.R + 8 * q : z.R + 8 * q + 8]
            g("xpad")[q, 0:8, lanes] = jnp.where(seq > 0, edge, 0.0)
            g("xpad")[q, 8 : 8 + z.T, lanes] = part[q * z.T : (q + 1) * z.T]

    each(z.C // 256, x_chunk)

    def conv_lanes(lanes):
        for q in range(z.Q):
            total = jnp.broadcast_to(g("convb")[:, lanes], (z.T, LANE))
            for tap in range(4):
                total = total + g("convw")[tap : tap + 1, lanes] * g("xpad")[q, 5 + tap : 5 + tap + z.T, lanes]
            g("conv")[q * z.T : (q + 1) * z.T, lanes] = total
            g("u")[q * z.T : (q + 1) * z.T, lanes] = silu_parts(total)[1].astype(BF16)

    lane_loop(conv_lanes)

    swap_low = Swap(z, links, lambda slot: g("lowp").at[slot])
    swap_st = Swap(z, links, lambda slot: g("stp").at[slot])
    low_mine, st_mine = g("lowp").at[z.M - 1], g("stp").at[z.M - 1]
    st_mine[...] = nt(g("statewt")[...], g("u")[...])
    swap_st.start(st_mine)
    low_mine[...] = nn(g("u")[...], g("loww")[...]).astype(BF16)
    swap_low.start(low_mine)
    tree_z.level(1)
    loads[2].wait()
    tree_o.level(0)
    swap_st.wait()
    swap_low.wait()
    st = g("stp")[0]
    low = g("lowp")[0].astype(F32)
    for slot in range(1, z.M):
        st = st + g("stp")[slot]
        low = low + g("lowp")[slot].astype(F32)
    g("st")[...] = st
    g("low")[...] = low.astype(BF16)

    rows_i = lax.broadcasted_iota(jnp.int32, (z.R, GRP * z.N), 0)
    cols_i = lax.broadcasted_iota(jnp.int32, (z.R, GRP * z.N), 1)
    diagonal = lax.rem(rows_i, GRP) == cols_i // z.N
    rep_n = lax.broadcasted_iota(jnp.int32, (2 * z.N, GRP * z.N), 0)
    rep_j = lax.rem(lax.broadcasted_iota(jnp.int32, (2 * z.N, GRP * z.N), 1), z.N)
    nat = jnp.concatenate([st, jnp.zeros((LANE - 2 * z.N, z.R), F32)], axis=0).T
    nat16 = nat[:, : 2 * z.N].astype(BF16)
    rep_b = (rep_n == rep_j).astype(BF16)
    rep_c = (rep_n == rep_j + z.N).astype(BF16)
    spread_b = jnp.where(diagonal, nn(nat16, rep_b), 0.0)
    g("blkb")[...] = spread_b.astype(BF16)
    g("blkk")[...] = (spread_b * spread_b).astype(BF16)
    g("blkc")[...] = jnp.where(diagonal, nn(nat16, rep_c), 0.0).astype(BF16)
    only_b = lax.broadcasted_iota(jnp.int32, (z.R, LANE), 1) < z.N
    key_sq = jnp.sum(jnp.where(only_b, nat * nat, 0.0), axis=1, keepdims=True)

    for q in range(z.Q):

        def spread(index, turned):
            for j in range(8):
                g("bc")[q, index * 8 + j] = jnp.broadcast_to(turned[:, j : j + 1], (2 * z.N, LANE))
            return pltpu.roll(turned, LANE - 8, 1)

        lax.fori_loop(0, z.T // 8, spread, st[:, q * z.T : (q + 1) * z.T])

    def raw_chunk(index):
        lanes = cut(index * 256, 256)
        g("s")[: z.R, lanes] = nn(g("low")[...], g("deltaw")[:, lanes])

    each(z.C // 256, raw_chunk)

    def step_lanes(lanes):
        for q in range(z.Q):
            rows = pl.ds(q * z.T, z.T)
            raw = g("s")[rows, lanes] + g("dbias")[:, lanes]
            beta = 1.0 / (1.0 + jnp.exp(-raw))
            scale = 1.0 / (1.0 + beta * key_sq[q * z.T : (q + 1) * z.T])
            step = beta * scale
            g("s")[rows, lanes] = step
            g("su")[rows, lanes] = step * g("u")[rows, lanes].astype(F32)
            g("fac")[rows, lanes] = scale * step * (1.0 - beta)

    lane_loop(step_lanes)

    span = 512 if z.C % 512 == 0 else 256

    def token(q, t):
        return pl.ds(q * z.T + t, 1)

    def totals(q):
        def lane_part(index):
            lanes = cut(index * span, span)

            def tokens8(i, carry):
                product, state = carry
                for j in range(8):
                    row = token(q, i * 8 + j)
                    step, drive = g("s")[row, lanes], g("su")[row, lanes]
                    key = g("bc")[q, i * 8 + j, : z.N, :]
                    decay = 1.0 - step * wide(key * key, span // LANE)
                    product = product * decay
                    state = decay * state + drive * wide(key, span // LANE)
                return product, state

            start = (jnp.ones((z.N, span), F32), jnp.zeros((z.N, span), F32))
            product, state = lax.fori_loop(0, z.T // 8, tokens8, start)
            g("ptot")[q, :, lanes] = product
            g("stot")[q, :, lanes] = state

        each(z.C // span, lane_part)

    for q in range(z.Q):
        totals(q)

    g("ppre")[...] = jnp.ones_like(g("ppre"))
    g("spre")[...] = jnp.zeros_like(g("spre"))
    carry_sems = [(links.sem(), links.sem()) for level in range(z.levels)]
    carry_copies = []
    for level in range(z.levels):
        for q in range(z.Q):
            g("csend")[level, q, 0] = g("ptot")[q].astype(BF16)
            g("csend")[level, q, 1] = g("stot")[q].astype(BF16)
        copy = links.copy(
            g("csend").at[level], g("crecv").at[level], *carry_sems[level], seq=seq ^ (1 << level)
        )
        copy.start()
        carry_copies.append(copy)
        if level == 0:
            for rest in range(2, depth + 1):
                tree_z.level(rest)
        if level == 1:
            tree_o.level(1)
        copy.wait_recv()
        upper = lax.rem(seq // (1 << level), 2) == 1
        for q in range(z.Q):
            other_p, other_s = g("crecv")[level, q, 0].astype(F32), g("crecv")[level, q, 1].astype(F32)
            mine_p, mine_s = g("ptot")[q], g("stot")[q]
            pre_p, pre_s = g("ppre")[q], g("spre")[q]
            g("spre")[q] = jnp.where(upper, pre_p * other_s + pre_s, pre_s)
            g("ppre")[q] = jnp.where(upper, pre_p * other_p, pre_p)
            g("stot")[q] = jnp.where(upper, mine_p * other_s + mine_s, other_p * mine_s + other_s)
            g("ptot")[q] = mine_p * other_p

    def past_rows(q, slot, count=1):
        return pl.ds(pl.multiple_of((q * (z.T + 1) + slot) * z.N, z.N), count * z.N)

    def walk(q):
        g("hist")[past_rows(q, 0), :] = g("spre")[q].astype(BF16)

        def lane_part(index):
            lanes = cut(index * span, span)

            def tokens8(i, state):
                for j in range(8):
                    row = token(q, i * 8 + j)
                    step, drive = g("s")[row, lanes], g("su")[row, lanes]
                    key = g("bc")[q, i * 8 + j, : z.N, :]
                    decay = 1.0 - step * wide(key * key, span // LANE)
                    state = decay * state + drive * wide(key, span // LANE)
                    g("hist")[past_rows(q, i * 8 + j + 1), lanes] = state.astype(BF16)
                return state

            lax.fori_loop(0, z.T // 8, tokens8, g("spre")[q, :, lanes])

        each(z.C // span, lane_part)

        def read(i):
            rows = cut(q * z.T + i * GRP, GRP)
            past = g("hist")[past_rows(q, i * GRP + 1, GRP), :]
            g("rd")[rows, :] = nn(g("blkc")[rows, :], past)

        each(z.T // GRP, read)

    for q in range(z.Q):
        walk(q)

    tree_z.finish()
    line_d.step(0)
    for rest in range(2, depth + 1):
        tree_o.level(rest)

    def z_chunk(index):
        lanes = cut(index * 256, 256)
        g("zp")[:, lanes] = nn(g("normed")[: z.R, :], g("wx")[1, :, lanes])

    each(z.C // 256, z_chunk)

    def gate_lanes(lanes):
        for q in range(z.Q):
            rows = pl.ds(q * z.T, z.T)
            out = g("rd")[rows, lanes] + g("skip")[:, lanes] * g("u")[rows, lanes].astype(F32)
            g("rd")[rows, lanes] = out
            gated = out * silu_parts(g("zp")[rows, lanes])[1]
            g("gat")[rows, lanes] = gated.astype(BF16)
            g("gatt")[lanes, rows] = gated.T.astype(BF16)

    lane_loop(gate_lanes)
    for far in range(1, z.M):
        line_d.step(far)
    tree_o.finish()

    swap_out = Swap(z, links, lambda slot: g("orecv").at[slot])

    def partial_of(owner):
        return g("normed").at[pl.ds(0, z.R), cut(owner * z.Df, z.Df)]

    def branch_to(index):
        away = index + 1
        owner = lax.rem(mp + away, z.M)
        for b in range(z.B):
            j = owner * z.B + b
            g("normed")[: z.R, cut(j * z.Ds, z.Ds)] = nn(g("gat")[...], g("wo")[j]).astype(BF16)

        @pl.when(away < z.M)
        def _():
            swap_out.one(partial_of(owner), away).start()

    each(z.M, branch_to)

    g("dr")[...] = nt(g("db")[0], g("wo")[0])

    def gated_grad(index):
        g("dr")[...] += nt(g("db")[index + 1], g("wo")[index + 1])

    each(z.S - 1, gated_grad)
    g("vec")[...] = jnp.zeros_like(g("vec"))

    def gate_back(lanes):
        for q in range(z.Q):
            rows = pl.ds(q * z.T, z.T)
            part, grad, out = g("zp")[rows, lanes], g("dr")[rows, lanes], g("rd")[rows, lanes]
            gate, silu = silu_parts(part)
            d_read = grad * silu
            g("dr")[rows, lanes] = d_read
            g("dzr")[rows, lanes] = (grad * out * gate * (1.0 + part * (1.0 - gate))).astype(BF16)
            g("vec")[6:7, lanes] += jnp.sum(
                d_read * g("u")[rows, lanes].astype(F32), axis=0, keepdims=True
            )

    lane_loop(gate_back)

    def into(near, term):
        def make(device, mask):
            block = near.block(mask // 2)
            block[...] = term(device).astype(BF16)
            return block

        return make

    def onto(sums, term):
        def add(device, mask):
            block = sums.block(mask // 2)
            block[...] = (term(device) + block[...].astype(F32)).astype(BF16)

        return add

    half_s, slots = z.S // 2, slots_of(z)
    sg_rows = z.rows_sg
    near_o, near_i = Rows(g("near_o"), 0, z.C, half_s), Rows(g("near_i"), 0, z.Ds, half_s)
    sum_o, far_o = Rows(g("sum_o"), 0, z.C, half_s), Rows(g("far_o"), 0, z.C // 2, slots)
    sum_1, far_1 = Rows(g("sum_1"), 0, z.Ds, half_s), Rows(g("far_1"), 0, z.Ds // 2, slots)
    sum_0 = Rows(g("hist"), 0, z.Ds, half_s)
    far_0 = Rows(g("hist"), sum_0.end, z.Ds // 2, slots)
    sum_s = Rows(g("hist"), far_0.end, sg_rows, half_s)
    far_s = Rows(g("hist"), sum_s.end, sg_rows // 2, slots)
    sgp = Rows(g("hist"), far_s.end, sg_rows, z.S)
    small = Rows(g("hist"), sgp.end, sg_rows, z.S)
    scatter_o = Scatter(z, links, None, sum_o, far_o, z.C)
    scatter_1 = Scatter(z, links, None, sum_1, far_1, z.Ds)
    scatter_0 = Scatter(z, links, None, sum_0, far_0, z.Ds)
    scatter_s = Scatter(z, links, None, sum_s, far_s, sg_rows)
    term_o = lambda device: nn(g("gatt")[...], g("db")[device])
    term_1 = lambda device: nn(g("normt")[cut(device * z.Ds, z.Ds), :], g("dzr")[...])
    term_0 = lambda device: nn(g("normt")[cut(device * z.Ds, z.Ds), :], g("dxr")[...])
    scatter_o.first(into(near_o, term_o))
    scatter_1.first(into(near_i, term_1))
    scatter_o.second(onto(sum_o, term_o))
    scatter_1.second(onto(sum_1, term_1))

    def totals_back(q):
        def lane_part(index):
            lanes = cut(index * span, span)

            def tokens8(i, tail):
                for j in reversed(range(8)):
                    t = z.T - 8 - i * 8 + j
                    row = token(q, t)
                    step, grad = g("s")[row, lanes], g("dr")[row, lanes]
                    key, query = g("bc")[q, t, : z.N, :], g("bc")[q, t, z.N :, :]
                    decay = 1.0 - step * wide(key * key, span // LANE)
                    tail = decay * (grad * wide(query, span // LANE) + tail)
                return tail

            g("stot")[q, :, lanes] = lax.fori_loop(0, z.T // 8, tokens8, jnp.zeros((z.N, span), F32))

        each(z.C // span, lane_part)

    for q in range(z.Q):
        totals_back(q)
    g("ppre")[...] = jnp.ones_like(g("ppre"))
    g("spre")[...] = jnp.zeros_like(g("spre"))
    back_sems = [(links.sem(), links.sem()) for level in range(z.levels)]
    for level in range(z.levels):
        for q in range(z.Q):
            g("bsend")[level, q] = g("stot")[q].astype(BF16)
        copy = links.copy(
            g("bsend").at[level], g("brecv").at[level], *back_sems[level], seq=seq ^ (1 << level)
        )
        copy.start()
        carry_copies.append(copy)
        if level == 0:
            for step in range(depth - 1):
                scatter_o.fold(step)
        copy.wait_recv()
        upper = lax.rem(seq // (1 << level), 2) == 1
        for q in range(z.Q):
            other = g("brecv")[level, q].astype(F32)
            other_p, mine_p = g("crecv")[level, q, 0].astype(F32), g("csend")[level, q, 0].astype(F32)
            mine, pre_p, pre = g("stot")[q], g("ppre")[q], g("spre")[q]
            g("spre")[q] = jnp.where(upper, pre, pre + pre_p * other)
            g("ppre")[q] = jnp.where(upper, pre_p, pre_p * other_p)
            g("stot")[q] = jnp.where(upper, other + other_p * mine, mine + mine_p * other)

    lane_index = lax.broadcasted_iota(jnp.int32, (z.N, LANE), 1)

    def lane_sum(value):
        total = value[:, :LANE]
        for part in range(1, lanes_all):
            total = total + value[:, part * LANE : (part + 1) * LANE]
        return jnp.sum(total, axis=1, keepdims=True)

    def walk_back(q):
        def group(index, carry):
            tail, sum_gh, sum_g, sum_h = carry
            i = z.T // GRP - 1 - index
            for j in reversed(range(GRP)):
                t = i * GRP + j
                row = token(q, t)
                step, drive, grad = g("s")[row, :], g("su")[row, :], g("dr")[row, :]
                key, query = g("bc")[q, t, : z.N, :], g("bc")[q, t, z.N :, :]
                before = g("hist")[past_rows(q, t), :].astype(F32)
                now = g("hist")[past_rows(q, t + 1), :].astype(F32)
                state_grad = grad * wide(query, lanes_all) + tail
                crossed = state_grad * before
                g("gbuf")[j * z.N : (j + 1) * z.N, :] = state_grad.astype(BF16)
                g("ghbuf")[j * z.N : (j + 1) * z.N, :] = crossed.astype(BF16)
                here = lane_index == t
                sum_gh = jnp.where(here, lane_sum(step * crossed), sum_gh)
                sum_g = jnp.where(here, lane_sum(drive * state_grad), sum_g)
                sum_h = jnp.where(here, lane_sum(grad * now), sum_h)
                tail = (1.0 - step * wide(key * key, lanes_all)) * state_grad
            rows = cut(q * z.T + i * GRP, GRP)
            g("rd")[rows, :] = nn(g("blkb")[rows, :], g("gbuf")[...])
            g("zp")[rows, :] = nn(g("blkk")[rows, :], g("ghbuf")[...])
            return tail, sum_gh, sum_g, sum_h

        zero = jnp.zeros((z.N, LANE), F32)
        _, sum_gh, sum_g, sum_h = lax.fori_loop(0, z.T // GRP, group, (g("spre")[q], zero, zero, zero))
        columns = pl.ds(q * z.T, z.T)
        g("est")[0, :, columns] = sum_gh
        g("est")[1, :, columns] = sum_g
        g("est")[2, :, columns] = sum_h

    for q in range(z.Q):
        walk_back(q)
        for step in range(depth - 1):
            if q == 0:
                scatter_1.fold(step)

    for level in range(z.levels):
        pl.semaphore_signal(
            g("ready").at[level], inc=1, device_id=(seq ^ (1 << level), mp), device_id_type=MESH
        )

    def step_back(lanes):
        for q in range(z.Q):
            rows = pl.ds(q * z.T, z.T)
            sum_b, step = g("rd")[rows, lanes], g("s")[rows, lanes]
            d_step = g("u")[rows, lanes].astype(F32) * sum_b - g("zp")[rows, lanes]
            g("rd")[rows, lanes] = step * sum_b
            d_raw = d_step * g("fac")[rows, lanes]
            g("ddr")[rows, lanes] = d_raw.astype(BF16)
            g("gat")[rows, lanes] = (d_step * step * step).astype(BF16)
            g("vec")[5:6, lanes] += jnp.sum(d_raw, axis=0, keepdims=True)

    lane_loop(step_back)
    swap_dlow = Swap(z, links, lambda slot: g("dlowp").at[slot])
    swap_dst = Swap(z, links, lambda slot: g("dstp").at[slot])
    dlow_mine, dst_mine = g("dlowp").at[z.M - 1], g("dstp").at[z.M - 1]
    dlow_mine[...] = nt(g("ddr")[...], g("deltaw")[...]).astype(BF16)
    swap_dlow.start(dlow_mine)
    key_grad = nt(jnp.ones((16, z.C), BF16), g("gat")[...])[0:1]
    keys = g("st")[: z.N]
    d_key = g("est")[1] - 2.0 * keys * g("est")[0] - 2.0 * keys * key_grad
    dst_mine[...] = jnp.concatenate([d_key, g("est")[2]], axis=0).astype(BF16)
    swap_dst.start(dst_mine)

    def put_small(first, value):
        count, at = value.shape[0], 0
        while at < count:
            block, inside = divmod(first + at, sg_rows)
            take = min(count - at, sg_rows - inside)
            sgp.block(block, inside, take)[...] = value[at : at + take].astype(BF16)
            at += take

    low_t = g("low")[...].astype(F32).T.astype(BF16)
    put_small(0, nn(low_t, g("ddr")[...]))
    swap_dlow.wait()
    swap_dst.wait()
    dlow = g("dlowp")[0].astype(F32)
    dst = g("dstp")[0].astype(F32)
    for slot in range(1, z.M):
        dlow = dlow + g("dlowp")[slot].astype(F32)
        dst = dst + g("dstp")[slot].astype(F32)
    dlow16, dst16 = dlow.astype(BF16), dst.astype(BF16)
    dst_nat = jnp.concatenate([dst, jnp.zeros((LANE - 2 * z.N, z.R), F32)], axis=0).T
    dst_nat16 = dst_nat[:, : 2 * z.N].astype(BF16)
    g("low")[...] = dlow16

    def inputs_chunk(index):
        lanes = cut(index * 256, 256)
        g("su")[:, lanes] = nt(g("low")[...], g("loww")[lanes, :]) + nn(dst_nat16, g("statewt")[:, lanes])

    each(z.C // 256, inputs_chunk)

    def conv_back(lanes):
        for q in range(z.Q):
            rows = pl.ds(q * z.T, z.T)
            total = g("su")[rows, lanes] + g("rd")[rows, lanes] + g("skip")[:, lanes] * g("dr")[rows, lanes]
            value = g("conv")[rows, lanes]
            gate = silu_parts(value)[0]
            d_conv = total * gate * (1.0 + value * (1.0 - gate))
            g("dcp")[q, 0 : z.T, lanes] = d_conv
            g("vec")[4:5, lanes] += jnp.sum(d_conv, axis=0, keepdims=True)
            for tap in range(4):
                g("vec")[tap : tap + 1, lanes] += jnp.sum(
                    d_conv * g("xpad")[q, 5 + tap : 5 + tap + z.T, lanes], axis=0, keepdims=True
                )

    lane_loop(conv_back)
    rim = [
        links.copy(
            g("dcp").at[q, pl.ds(0, 8), :],
            g("dcp").at[q, pl.ds(z.T, 8), :],
            links.sem(),
            links.sem(),
            seq=behind,
        )
        for q in range(z.Q)
    ]
    for copy in rim:
        copy.start()
    put_small(z.RK, nn(dlow.T.astype(BF16), g("u")[...]))
    put_small(2 * z.RK, nn(dst16, g("u")[...]))
    put_small(2 * z.RK + 2 * z.N, g("vec")[...])
    used = 2 * z.RK + 2 * z.N + SGVEC
    if used < z.S * sg_rows:
        put_small(used, jnp.zeros((z.S * sg_rows - used, z.C), F32))
    for copy in rim:
        copy.wait_recv()

    def x_back(lanes):
        for q in range(z.Q):
            edge = g("dcp")[q, z.T : z.T + 8, lanes]
            g("dcp")[q, z.T : z.T + 8, lanes] = jnp.where(seq < z.S - 1, edge, 0.0)
            total = jnp.zeros((z.T, LANE), F32)
            for tap in range(4):
                total = total + g("convw")[tap : tap + 1, lanes] * g("dcp")[q, 3 - tap : 3 - tap + z.T, lanes]
            g("dxr")[q * z.T : (q + 1) * z.T, lanes] = total.astype(BF16)

    lane_loop(x_back)

    for level in range(z.levels):
        pl.semaphore_wait(g("ready").at[level], 1)
    scatter_s.first(lambda device, mask: sgp.block(device))
    for copy in scatter_1.sent[: len(z.masks)]:
        copy.wait_send()
    scatter_1.sent = scatter_1.sent[len(z.masks) :]
    scatter_0.first(into(near_i, term_0))

    def add_small(device, mask):
        block = sum_s.block(mask // 2)
        block[...] = (block[...].astype(F32) + sgp.block(device)[...].astype(F32)).astype(BF16)

    scatter_s.second(add_small)
    scatter_0.second(onto(sum_0, term_0))

    swap_out.wait()
    for away in range(1, z.M):
        owner = lax.rem(mp + away, z.M)
        swap_out.one(partial_of(owner), away).wait_send()
    for b in range(z.B):
        features = slice(b * z.Ds, (b + 1) * z.Ds)
        total = g("normed")[: z.R, cut((first_block + b) * z.Ds, z.Ds)].astype(F32)
        for slot in range(z.M - 1):
            total = total + g("orecv")[slot, :, features].astype(F32)
        g("blk")[:, features] = (g("tok")[:, features].astype(F32) + total).astype(BF16)

    swap_n = Swap(z, links, lambda slot: g("nrecv").at[slot])

    def normed_to(index, means):
        away = index + 1
        owner = lax.rem(mp + away, z.M)
        for b in range(z.B):
            j = owner * z.B + b
            features = cut(j * z.Ds, z.Ds)
            part = nt(g("dxr")[...], g("wx")[0, features, :]) + nt(g("dzr")[...], g("wx")[1, features, :])
            g("normed")[: z.R, features] = part.astype(BF16)
            scaled = part * g("tokg")[j].astype(F32)
            by_gain = jnp.sum(scaled * wide(g("inv")[...], z.Ds // LANE), axis=0, keepdims=True)
            g("gv")[0, :, features] = jnp.broadcast_to(by_gain, (8, z.Ds))
            means = means + jnp.sum(scaled * g("gain")[:, features], axis=1, keepdims=True)

        @pl.when(away < z.M)
        def _():
            swap_n.one(partial_of(owner), away).start()

        return means

    means = lax.fori_loop(0, z.M, normed_to, jnp.zeros((z.R, 1), F32))
    swap_m = Swap(z, links, lambda slot: g("mrow").at[slot])
    mean_mine = g("mrow").at[z.M - 1]
    mean_mine[...] = jnp.broadcast_to(means, (z.R, LANE)).T[0:8]
    swap_m.start(mean_mine)

    gain_copies = []
    for level in range(z.levels):
        copy = links.copy(
            g("gv").at[level], g("gvr").at[level], links.sem(), links.sem(), seq=seq ^ (1 << level)
        )
        copy.start()
        gain_copies.append(copy)
        if level < depth - 1:
            scatter_s.fold(level)
        copy.wait_recv()
        g("gv")[level + 1] = g("gv")[level] + g("gvr")[level]
    swap_g = Swap(z, links, lambda slot: g("gvm").at[slot])
    swap_g.start(g("gv").at[z.levels])
    scatter_s.fold(depth - 1)

    def write_small(rows, value):
        small.block(seq, *rows)[...] = value.astype(BF16)

    scatter_s.total(write_small)
    tree_s = TreeGather(
        z,
        links,
        lambda owner, h: small.block(owner, h * (sg_rows // 2), sg_rows // 2),
        small.block,
    )
    tree_s.level(0)
    for step in range(depth - 1):
        scatter_0.fold(step)
    for level in range(1, depth + 1):
        tree_s.level(level)

    swap_m.wait()
    mean = g("mrow")[0]
    for slot in range(1, z.M):
        mean = mean + g("mrow")[slot]
    mean = wide(jnp.concatenate([mean] * (LANE // 8), axis=0).T * (1.0 / z.D), z.Ds // LANE)
    swap_n.wait()
    inv_wide = wide(g("inv")[...], z.Ds // LANE)
    for b in range(z.B):
        j = first_block + b
        here = slice(b * z.Ds, (b + 1) * z.Ds)
        gain = g("gain")[:, cut(j * z.Ds, z.Ds)]
        total = g("normed")[: z.R, cut(j * z.Ds, z.Ds)].astype(F32)
        for slot in range(z.M - 1):
            total = total + g("nrecv")[slot, :, here].astype(F32)
        x = g("tok")[:, here].astype(F32)
        value = inv_wide * (total * gain) - x * (inv_wide * inv_wide * inv_wide) * mean
        for q in range(z.Q):
            rows = slice(q * z.T, (q + 1) * z.T)
            g("dtok")[rows, here] = value[rows] + g("cot")[rows, here] * seq_weight[q]

    last = depth - 1
    scatter_o.fold(last)

    def write_out(rows, value):
        g("dout")[pl.ds(*rows), :] = value

    scatter_o.total(write_out)
    scatter_1.fold(last)

    def write_to(name):
        def write(rows, value):
            g(name)[pl.ds(*rows), :] = value

        return write

    scatter_1.total(write_to("fac"))
    store_1 = pltpu.make_async_copy(g("fac").at[pl.ds(0, z.Ds)], g("din").at[1], local.at[3])
    store_1.start()
    swap_g.wait()
    gains = g("gv")[z.levels]
    for slot in range(z.M - 1):
        gains = gains + g("gvm")[slot]
    g("dgain")[...] = gains[0:1]
    tree_s.finish()
    for block in range(z.S):
        count = min(sg_rows, g("sg").shape[0] - block * sg_rows)
        if count > 0:
            g("sg")[block * sg_rows : block * sg_rows + count, :] = small.block(block)[...].astype(F32)[:count]
    scatter_0.fold(last)
    scatter_0.total(write_to("s"))
    store_0 = pltpu.make_async_copy(g("s").at[pl.ds(0, z.Ds)], g("din").at[0], local.at[4])
    store_0.start()

    hal.wait_send()
    for tree in (tree_x, tree_z, tree_o, tree_s):
        tree.drain()
    for line in (line_t, line_h, line_d):
        line.drain()
    swap_st.drain(st_mine)
    swap_low.drain(low_mine)
    swap_dlow.drain(dlow_mine)
    swap_dst.drain(dst_mine)
    swap_m.drain(mean_mine)
    swap_g.drain(g("gv").at[z.levels])
    for away in range(1, z.M):
        owner = lax.rem(mp + away, z.M)
        swap_n.one(partial_of(owner), away).wait_send()
    for copy in carry_copies + gain_copies + rim:
        copy.wait_send()
    for scatter in (scatter_o, scatter_1, scatter_0, scatter_s):
        scatter.drain()
    store_1.wait()
    store_0.wait()


def fused(z, tokens, norm_gain, in_weight, conv_weight, conv_bias, low_weight, state_weight, delta_weight,
          delta_bias, skip_gain, out_weight, cotangent, seq_group, group_weight):
    V = pl.BlockSpec(memory_space=pltpu.VMEM)
    A = pl.BlockSpec(memory_space=pl.ANY)
    SM = pl.BlockSpec(memory_space=pltpu.SMEM)
    where = dict(win=A, wout=A, seqg=SM, groupw=SM)
    row = lambda value: value.reshape(1, -1)
    operands = (
        tokens.reshape(z.R, z.Df),
        cotangent.reshape(z.R, z.Df),
        row(norm_gain),
        in_weight,
        out_weight,
        conv_weight,
        row(conv_bias),
        row(delta_bias),
        row(skip_gain),
        low_weight,
        state_weight.T,
        delta_weight,
        seq_group,
        group_weight,
    )
    scratch = scratch_of(z)
    sg_used = 2 * z.RK + 2 * z.N + SGVEC
    outs = dict(
        blk=((z.R, z.Df), BF16),
        dtok=((z.R, z.Df), F32),
        dgain=((1, z.D), F32),
        din=((2, z.Ds, z.C), F32),
        dout=((z.C, z.Ds), F32),
        sg=((sg_used, z.C), F32),
    )
    result = pl.pallas_call(
        functools.partial(fused_kernel, z, NAMES_IN + NAMES_OUT + list(scratch)),
        out_shape=[jax.ShapeDtypeStruct(*outs[name]) for name in NAMES_OUT],
        in_specs=[where.get(name, V) for name in NAMES_IN],
        out_specs=[A if name == "din" else V for name in NAMES_OUT],
        scratch_shapes=list(scratch.values()),
        compiler_params=pltpu.CompilerParams(
            collective_id=0, has_side_effects=True, vmem_limit_bytes=VMEM_BYTES
        ),
    )(*operands)
    blk, dtok, dgain, din, dout, sg = result
    a, b, c = z.RK, 2 * z.RK, 2 * z.RK + 2 * z.N
    return (
        blk.reshape(tokens.shape),
        dtok.reshape(tokens.shape),
        dgain[0],
        din,
        sg[c : c + 4],
        sg[c + 4],
        sg[a:b].T,
        sg[b:c].T,
        sg[:a],
        sg[c + 5],
        sg[c + 6],
        dout,
    )


def local(mesh_shape, *arrays):
    tokens, norm_gain, in_weight, conv_weight = arrays[:4]
    state_weight, delta_weight = arrays[6], arrays[7]
    z = Sizes(
        mesh_shape,
        tokens.shape[0],
        tokens.shape[1],
        tokens.shape[2],
        norm_gain.shape[0],
        in_weight.shape[2],
        state_weight.shape[1] // 2,
        delta_weight.shape[0],
    )
    if z.fits(conv_weight.shape[0]):
        return fused(z, *arrays)
    return plain(*arrays)


def solution(mesh):
    placed = (
        P(None, "seq", "mp"),
        P(),
        P(None, "seq", "mp"),
        P(None, "mp"),
        P("mp"),
        P("mp", None),
        P("mp", None),
        P(None, "mp"),
        P("mp"),
        P("mp"),
        P("mp", "seq"),
        P(None, "seq", "mp"),
        P(),
        P(),
    )
    return jax.shard_map(
        functools.partial(local, dict(mesh.shape)),
        mesh=mesh,
        in_specs=placed,
        out_specs=(
            P(None, "seq", "mp"),
            P(None, "seq", "mp"),
            P(),
            P(None, "seq", "mp"),
            P(None, "mp"),
            P("mp"),
            P("mp", None),
            P("mp", None),
            P(None, "mp"),
            P("mp"),
            P("mp"),
            P("mp", "seq"),
        ),
        check_vma=False,
    )
```

```python
import functools
import math

import jax
import jax.numpy as jnp
from jax import lax
from jax.experimental import pallas as pl
from jax.experimental.pallas import tpu as pltpu
from jax.sharding import PartitionSpec as P

SEQ_MB = 1
NMB = 2
EPSILON = 1e-05
VMEM_BYTES = 64 * 1024 * 1024 - 64 * 1024


def from_behind(value, axis, steps):
    count = lax.axis_size(axis)
    leading, last = (max(0, -steps), min(count, count - steps))
    return lax.ppermute(value, axis, [(source, source + steps) for source in range(leading, last)])


def prefix(value, axis, join, neutral, backward):
    count, mine = (lax.axis_size(axis), lax.axis_index(axis))
    pieces = jax.tree.map(lambda part: lax.all_gather(part, axis), value)
    if backward:
        pieces = jax.tree.map(lambda part: part[::-1], pieces)
        mine = count - 1 - mine
    subtotal = jax.tree.map(
        lambda part, zero: jnp.full_like(part, 0) + jnp.asarray(zero, part.dtype), value, neutral
    )

    def lap(position, subtotal):
        longer = join(subtotal, jax.tree.map(lambda part: part[position], pieces))
        return jax.tree.map(lambda new, old: jnp.where(position < mine, new, old), longer, subtotal)

    return lax.fori_loop(0, count - 1, lap, subtotal)


def combine(earlier, later):
    return (earlier[0] * later[0], later[0] * earlier[1] + later[1])


def make_gates(delta_raw, b_state, inputs):
    beta_gate = jax.nn.sigmoid(delta_raw)
    key_sq = jnp.sum(b_state * b_state, axis=-1, keepdims=True)
    step_size = beta_gate / (1.0 + beta_gate * key_sq)
    decays = 1.0 - step_size[:, :, None, :] * (b_state * b_state)[:, :, :, None]
    source = (step_size * inputs)[:, :, None, :] * b_state[:, :, :, None]
    return (decays, source)


def to_blocks(value, span_rows):
    old_shape = value.shape
    reshaped = value.reshape((old_shape[0], old_shape[1] // span_rows, span_rows) + old_shape[2:])
    return jnp.swapaxes(reshaped, 0, 1)


def from_blocks(value):
    joined = jnp.swapaxes(value, 0, 1)
    old_shape = joined.shape
    return joined.reshape((old_shape[0], old_shape[1] * old_shape[2]) + old_shape[3:])


def forward_block(carry_pair, block_items):
    delta_raw, b_state, inputs = block_items
    decays, source = make_gates(delta_raw, b_state, inputs)
    run_prod, run_state = carry_pair
    prod_list = []
    state_list = []
    for row_idx in range(decays.shape[1]):
        run_prod = run_prod * decays[:, row_idx]
        run_state = decays[:, row_idx] * run_state + source[:, row_idx]
        prod_list.append(run_prod)
        state_list.append(run_state)
    return ((run_prod, run_state), (jnp.stack(prod_list, axis=1), jnp.stack(state_list, axis=1)))


def backward_block(carry_trio, block_items):
    delta_raw, b_state, inputs, read_grad, c_state = block_items
    decays, _ = make_gates(delta_raw, b_state, inputs)
    grad_next, dec_next, tail_prod = carry_trio
    span_rows = decays.shape[1]
    grad_list = [None] * span_rows
    tail_list = [None] * span_rows
    for row_idx in reversed(range(span_rows)):
        drive_term = read_grad[:, row_idx][:, None, :] * c_state[:, row_idx][:, :, None]
        grad_next = drive_term + dec_next * grad_next
        tail_prod = dec_next * tail_prod
        grad_list[row_idx] = grad_next
        tail_list[row_idx] = tail_prod
        dec_next = decays[:, row_idx]
    return (
        (grad_next, dec_next, tail_prod),
        (jnp.stack(grad_list, axis=1), jnp.stack(tail_list, axis=1)),
    )


def silu_slope(value):
    sig_value = jax.nn.sigmoid(value)
    return sig_value * (1.0 + value * (1.0 - sig_value))


def plain(
    tokens,
    norm_gain,
    in_weight,
    conv_weight,
    conv_bias,
    low_weight,
    state_weight,
    delta_weight,
    delta_bias,
    skip_gain,
    out_weight,
    cotangent,
    seq_group,
    group_weight,
):
    stretch = tokens.shape[1]
    feature_dev = tokens.shape[2]
    channels = in_weight.shape[2]
    model_width = norm_gain.shape[0]
    num_taps = conv_weight.shape[0]
    nstate = state_weight.shape[1] // 2
    span_rows = math.gcd(stretch, 8)
    picks = (
        seq_group[:, None] == jnp.arange(group_weight.shape[0], dtype=jnp.int32)[None, :]
    ).astype(jnp.float32)
    seq_weight = jnp.sum(picks * group_weight[None, :], axis=1)
    feature_start = lax.axis_index("mp") * feature_dev
    ones_state = jnp.ones((SEQ_MB, nstate, channels), jnp.float32)
    zero_state = jnp.zeros_like(ones_state)
    acc_in = jnp.zeros((2, model_width, channels), jnp.float32)
    acc_out = jnp.zeros((channels, model_width), jnp.float32)
    acc_gain = jnp.zeros_like(norm_gain)
    acc_conv = jnp.zeros_like(conv_weight)
    acc_cbias = jnp.zeros_like(conv_bias)
    acc_low = jnp.zeros(low_weight.shape, jnp.float32)
    acc_state = jnp.zeros(state_weight.shape, jnp.float32)
    acc_delta = jnp.zeros(delta_weight.shape, jnp.float32)
    acc_dbias = jnp.zeros_like(delta_bias)
    acc_skip = jnp.zeros_like(skip_gain)
    outputs = []
    input_grads = []
    for micro_idx in range(NMB):
        whole_in, whole_out = (
            lax.all_gather(in_weight, "seq", axis=1, tiled=True),
            lax.all_gather(out_weight, "seq", axis=1, tiled=True),
        )
        first_seq = micro_idx * SEQ_MB
        block_tokens = tokens[first_seq : first_seq + SEQ_MB]
        full_tokens = lax.all_gather(block_tokens, "mp", axis=2, tiled=True).astype(jnp.float32)
        inv_rms = lax.rsqrt(jnp.mean(full_tokens * full_tokens, axis=-1, keepdims=True) + EPSILON)
        normed = (full_tokens * inv_rms * norm_gain).astype(jnp.bfloat16)
        both_parts = jnp.einsum(
            "scd,kdi->ksci", normed, whole_in, preferred_element_type=jnp.float32
        )
        x_round = both_parts[0].astype(jnp.bfloat16)
        z_part = both_parts[1]
        rim_rows = from_behind(x_round[:, stretch - (num_taps - 1) :], "seq", 1)
        padded = jnp.concatenate([rim_rows, x_round], axis=1).astype(jnp.float32)
        conv_sum = conv_bias + jnp.zeros((SEQ_MB, stretch, channels), jnp.float32)
        for tap_index in range(num_taps):
            conv_sum = (
                conv_sum + conv_weight[tap_index] * padded[:, tap_index : tap_index + stretch]
            )
        inputs_round = jax.nn.silu(conv_sum).astype(jnp.bfloat16)
        inputs_f = inputs_round.astype(jnp.float32)
        low_part = jnp.einsum(
            "sci,ir->scr", inputs_round, low_weight, preferred_element_type=jnp.float32
        )
        state_part = jnp.einsum(
            "sci,ir->scr", inputs_round, state_weight, preferred_element_type=jnp.float32
        )
        delta_low, state_proj = lax.psum((low_part, state_part), "mp")
        delta_round = delta_low.astype(jnp.bfloat16)
        delta_raw = (
            jnp.einsum("scr,ri->sci", delta_round, delta_weight, preferred_element_type=jnp.float32)
            + delta_bias
        )
        b_state = state_proj[..., :nstate]
        c_state = state_proj[..., nstate:]
        delta_blocks = to_blocks(delta_raw, span_rows)
        b_blocks = to_blocks(b_state, span_rows)
        c_blocks = to_blocks(c_state, span_rows)
        in_blocks = to_blocks(inputs_f, span_rows)
        stretch_pair, (prod_blocks, local_blocks) = lax.scan(
            forward_block, (ones_state, zero_state), (delta_blocks, b_blocks, in_blocks)
        )
        carried = prefix(stretch_pair, "seq", combine, (ones_state, zero_state), False)
        states = from_blocks(local_blocks) + from_blocks(prod_blocks) * carried[1][:, None]
        before = jnp.concatenate([carried[1][:, None], states[:, :-1]], axis=1)
        read_rec = jnp.einsum("scni,scn->sci", states, c_state)
        read_out = read_rec + skip_gain * inputs_f
        z_gate = jax.nn.silu(z_part)
        gated_round = (read_out * z_gate).astype(jnp.bfloat16)
        out_part = jnp.einsum(
            "sci,id->scd", gated_round, whole_out, preferred_element_type=jnp.float32
        )
        branch = lax.psum_scatter(out_part, "mp", scatter_dimension=2, tiled=True)
        outputs.append((block_tokens.astype(jnp.float32) + branch).astype(jnp.bfloat16))
        d_out = (
            cotangent[first_seq : first_seq + SEQ_MB]
            * seq_weight[first_seq : first_seq + SEQ_MB][:, None, None]
        )
        d_branch = lax.all_gather(d_out.astype(jnp.bfloat16), "mp", axis=2, tiled=True)
        acc_out = acc_out + jnp.einsum(
            "sci,scd->id", gated_round, d_branch, preferred_element_type=jnp.float32
        )
        d_gated = jnp.einsum("scd,id->sci", d_branch, whole_out, preferred_element_type=jnp.float32)
        d_read = d_gated * z_gate
        d_zpart = d_gated * read_out * silu_slope(z_part)
        acc_skip = acc_skip + jnp.sum(d_read * inputs_f, axis=(0, 1))
        read_blocks_grad = to_blocks(d_read, span_rows)
        (last_grad, first_dec, _), (grad_blocks, tail_blocks) = lax.scan(
            backward_block,
            (zero_state, ones_state, ones_state),
            (delta_blocks, b_blocks, in_blocks, read_blocks_grad, c_blocks),
            reverse=True,
        )
        tail_grad = first_dec * last_grad
        crossing = prefix(
            (stretch_pair[0], tail_grad), "seq", combine, (ones_state, zero_state), True
        )
        state_grad = from_blocks(grad_blocks) + from_blocks(tail_blocks) * crossing[1][:, None]
        _, gate_pullback = jax.vjp(make_gates, delta_raw, b_state, inputs_f)
        d_delta, d_bstate, d_inputs_state = gate_pullback((state_grad * before, state_grad))
        d_cstate = jnp.einsum("scni,sci->scn", states, d_read)
        acc_dbias = acc_dbias + jnp.sum(d_delta, axis=(0, 1))
        d_delta_round = d_delta.astype(jnp.bfloat16)
        acc_delta = acc_delta + jnp.einsum(
            "scr,sci->ri", delta_round, d_delta_round, preferred_element_type=jnp.float32
        )
        low_grad_part = jnp.einsum(
            "sci,ri->scr", d_delta_round, delta_weight, preferred_element_type=jnp.float32
        )
        state_grad_part = jnp.concatenate([d_bstate, d_cstate], axis=-1)
        d_low, d_state = lax.psum((low_grad_part, state_grad_part), "mp")
        d_low_round = d_low.astype(jnp.bfloat16)
        d_state_round = d_state.astype(jnp.bfloat16)
        acc_low = acc_low + jnp.einsum(
            "sci,scr->ir", inputs_round, d_low_round, preferred_element_type=jnp.float32
        )
        acc_state = acc_state + jnp.einsum(
            "sci,scr->ir", inputs_round, d_state_round, preferred_element_type=jnp.float32
        )
        d_inputs = d_read * skip_gain + d_inputs_state
        d_inputs = d_inputs + jnp.einsum(
            "scr,ir->sci", d_low_round, low_weight, preferred_element_type=jnp.float32
        )
        d_inputs = d_inputs + jnp.einsum(
            "scr,ir->sci", d_state_round, state_weight, preferred_element_type=jnp.float32
        )
        d_conv = d_inputs * silu_slope(conv_sum)
        acc_cbias = acc_cbias + jnp.sum(d_conv, axis=(0, 1))
        tap_grads = []
        d_padded = jnp.zeros((SEQ_MB, stretch + num_taps - 1, channels), jnp.float32)
        for tap_index in range(num_taps):
            tap_grads.append(
                jnp.sum(d_conv * padded[:, tap_index : tap_index + stretch], axis=(0, 1))
            )
            d_padded = d_padded + jnp.pad(
                conv_weight[tap_index] * d_conv,
                ((0, 0), (tap_index, num_taps - 1 - tap_index), (0, 0)),
            )
        acc_conv = acc_conv + jnp.stack(tap_grads)
        back_rim = from_behind(d_padded[:, : num_taps - 1], "seq", -1)
        d_xpart = d_padded[:, num_taps - 1 :] + jnp.pad(
            back_rim, ((0, 0), (stretch - (num_taps - 1), 0), (0, 0))
        )
        d_parts_round = jnp.stack([d_xpart, d_zpart]).astype(jnp.bfloat16)
        acc_in = acc_in + jnp.einsum(
            "scd,ksci->kdi", normed, d_parts_round, preferred_element_type=jnp.float32
        )
        norm_part = jnp.einsum(
            "ksci,kdi->scd", d_parts_round, whole_in, preferred_element_type=jnp.float32
        )
        d_normed = lax.psum(norm_part, "mp")
        acc_gain = acc_gain + jnp.sum(d_normed * full_tokens * inv_rms, axis=(0, 1))
        scaled = d_normed * norm_gain
        d_full = inv_rms * scaled - full_tokens * (inv_rms * inv_rms * inv_rms) * jnp.mean(
            scaled * full_tokens, axis=-1, keepdims=True
        )
        d_mine = lax.dynamic_slice_in_dim(d_full, feature_start, feature_dev, 2)
        input_grads.append(d_out + d_mine)
    d_in_weight, d_out_weight = (
        lax.psum_scatter(acc_in, "seq", scatter_dimension=1, tiled=True),
        lax.psum_scatter(acc_out, "seq", scatter_dimension=1, tiled=True),
    )
    summed = lax.psum(
        (acc_gain, acc_conv, acc_cbias, acc_low, acc_state, acc_delta, acc_dbias, acc_skip), "seq"
    )
    return (
        jnp.concatenate(outputs, axis=0),
        jnp.concatenate(input_grads, axis=0),
        summed[0],
        d_in_weight,
        summed[1],
        summed[2],
        summed[3],
        summed[4],
        summed[5],
        summed[6],
        summed[7],
        d_out_weight,
    )


MESH = pl.DeviceIdType.MESH
F32 = jnp.float32
BF16 = jnp.bfloat16
LANE = 128
GRP = 16
PADV = 8
SGVEC = 16


def nn(a, b):
    return lax.dot_general(a, b, (((1,), (0,)), ((), ())), preferred_element_type=F32)


def nt(a, b):
    return lax.dot_general(a, b, (((1,), (1,)), ((), ())), preferred_element_type=F32)


def tn(a, b):
    return lax.dot_general(a, b, (((0,), (0,)), ((), ())), preferred_element_type=F32)


def cut(start, size):
    return pl.ds(pl.multiple_of(start, size), size)


def each(count, step):
    lax.fori_loop(0, count, lambda index, unused: (step(index), unused)[1], 0)


def wide(value, times):
    return jnp.concatenate([value] * times, axis=1) if times > 1 else value


class Sizes:
    def __init__(self, mesh_shape, nseq, stretch, feature_dev, model, channels, nstate, rank):
        self.S, self.M = mesh_shape["seq"], mesh_shape["mp"]
        self.Q, self.T, self.Df, self.D, self.C = nseq, stretch, feature_dev, model, channels
        self.N, self.RK = nstate, rank
        self.R = nseq * stretch
        self.Ds = model // self.S
        self.B = max(1, feature_dev // self.Ds)
        self.levels = self.S.bit_length() - 1
        self.dims = [1 << bit for bit in range(1, self.levels)]
        self.masks = [2 * value for value in range(self.S // 2)]
        self.rows_sg = -(-(2 * rank + 2 * nstate + SGVEC) // (self.S * 16)) * 16
        self.E = max(self.R, self.Ds)

    def order(self, half):
        turn = half * (len(self.dims) // 2)
        return self.dims[turn:] + self.dims[:turn]

    def fits(self, taps):
        return (
            self.S in (4, 8)
            and self.M > 1
            and self.Q == 2
            and self.T == LANE
            and self.Ds % 256 == 0
            and self.Df % self.Ds == 0
            and self.C % 256 == 0
            and self.N == GRP
            and self.RK == LANE
            and taps == 4
            and self.C * self.D <= (1 << 21)
        )


class Bunch:
    def __init__(self, names, values):
        self.__dict__.update(zip(names, values))


class Rows:
    def __init__(self, ref, base, rows, count):
        self.ref, self.base, self.rows, self.end = ref, base, rows, base + rows * count

    def block(self, index, start=0, size=None):
        first = pl.multiple_of(self.base + index * self.rows + start, 16)
        return self.ref.at[pl.ds(first, self.rows if size is None else size), :]


class Links:
    def __init__(self, sems, seq, mp):
        self.sems, self.used, self.seq, self.mp = sems, 0, seq, mp

    def sem(self, count=1):
        first = self.used
        self.used += count
        return first

    def copy(self, src, dst, send, recv, seq=None, mp=None):
        target = (self.seq if seq is None else seq, self.mp if mp is None else mp)
        return pltpu.make_async_remote_copy(
            src_ref=src,
            dst_ref=dst,
            send_sem=self.sems.at[send],
            recv_sem=self.sems.at[recv],
            device_id=target,
            device_id_type=MESH,
        )

    def arrived(self, dst, recv):
        self.copy(dst, dst, recv, recv).wait_recv()


class TreeGather:
    def __init__(self, z, links, half_view, whole_view):
        self.z, self.links, self.half, self.whole = z, links, half_view, whole_view
        self.recv = {(mask, h): links.sem() for mask in z.masks[1:] for h in range(2)}
        self.near = {mask: links.sem() for mask in z.masks}
        self.sent = []

    def push(self, mask, h, dim):
        view = self.half(self.links.seq ^ mask, h)
        copy = self.links.copy(
            view, view, self.links.sem(), self.recv[mask | dim, h], seq=self.links.seq ^ dim
        )
        copy.start()
        self.sent.append(copy)

    def take(self, mask, h):
        self.links.arrived(self.half(self.links.seq ^ mask, h), self.recv[mask, h])

    def hand(self, mask):
        view = self.whole(self.links.seq ^ mask)
        copy = self.links.copy(view, view, self.links.sem(), self.near[mask], seq=self.links.seq ^ 1)
        copy.start()
        self.sent.append(copy)

    def first(self):
        for h in range(2):
            self.push(0, h, self.z.order(h)[0])

    def second(self):
        for h in range(2):
            for dim in self.z.order(h)[1:]:
                self.push(0, h, dim)
        self.hand(0)

    def forward(self):
        for h in range(2):
            order = self.z.order(h)
            if len(order) > 1:
                self.take(order[0], h)
                self.push(order[0], h, order[1])

    def settle(self):
        for mask in sorted(self.z.masks[1:], key=lambda mask: bin(mask).count("1")):
            for h in range(2):
                order = self.z.order(h)
                if len(order) == 1 or mask != order[0]:
                    self.take(mask, h)
            self.hand(mask)

    def finish(self):
        for mask in self.z.masks:
            self.links.arrived(self.whole(self.links.seq ^ 1 ^ mask), self.near[mask])

    def drain(self):
        for copy in self.sent:
            copy.wait_send()


class LineGather:
    def __init__(self, z, links, view):
        self.z, self.links, self.view = z, links, view
        self.recv = links.sem(z.M)
        self.send = links.sem(2 * z.M)

    def parts(self, depth):
        for side, way in enumerate((1, -1)):
            owner, target = self.links.mp - way * depth, self.links.mp + way
            held = (owner >= 0) & (owner < self.z.M)
            more = held & (target >= 0) & (target < self.z.M)
            yield side, owner, target, held, more

    def copy(self, side, depth, owner, target):
        view = self.view(owner)
        return self.links.copy(view, view, self.send + 2 * depth + side, self.recv + owner, mp=target)

    def step(self, depth):
        for side, owner, target, held, more in self.parts(depth):
            if depth:

                @pl.when(held)
                def _():
                    self.links.arrived(self.view(owner), self.recv + owner)

            @pl.when(more)
            def _():
                self.copy(side, depth, owner, target).start()

    def drain(self):
        for depth in range(self.z.M):
            for side, owner, target, held, more in self.parts(depth):

                @pl.when(more)
                def _():
                    self.copy(side, depth, owner, target).wait_send()


class Swap:
    def __init__(self, z, links, slot):
        self.z, self.links, self.slot = z, links, slot
        self.recv = links.sem(z.M)
        self.send = links.sem(z.M)

    def one(self, src, away):
        target = lax.rem(self.links.mp + away, self.z.M)
        return self.links.copy(src, self.slot(away - 1), self.send + away, self.recv + away, mp=target)

    def start(self, src):
        for away in range(1, self.z.M):
            self.one(src, away).start()

    def wait(self):
        for away in range(1, self.z.M):
            self.links.arrived(self.slot(away - 1), self.recv + away)

    def drain(self, src):
        for away in range(1, self.z.M):
            self.one(src, away).wait_send()


def halves(rows):
    first = -(-rows // 32) * 16
    return (0, first), (first, rows - first)


class Scatter:
    def __init__(self, z, links, out, sums, far, rows):
        self.z, self.links, self.out, self.sums, self.far, self.rows = z, links, out, sums, far, rows
        self.near = {mask: links.sem() for mask in z.masks}
        self.near_send = {mask: links.sem() for mask in z.masks}
        self.sent = []
        self.hops = {}
        place = 0
        for h in range(2):
            order = z.order(h)
            for step, dim in enumerate(order):
                for mask in z.masks:
                    if mask & dim and not any(mask & other for other in order[:step]):
                        self.hops[h, step, mask] = (dim, links.sem(), links.sem(), place)
                        place += 1
        self.slots = place

    def half(self, mask, h):
        start, size = halves(self.rows)[h]
        return self.sums.block(mask // 2, start, size)

    def came(self, h, place):
        return self.far.block(place, 0, halves(self.rows)[h][1])

    def first(self, make):
        z, links = self.z, self.links
        for mask in z.masks:
            src = make(links.seq ^ 1 ^ mask, mask)
            copy = links.copy(src, self.sums.block(mask // 2), self.near_send[mask], self.near[mask], seq=links.seq ^ 1)
            copy.start()
            self.sent.append(copy)

    def second(self, add):
        z, links = self.z, self.links
        by_need = sorted(z.masks, key=lambda mask: -bin(mask).count("1"))
        for mask in by_need:
            links.arrived(self.sums.block(mask // 2), self.near[mask])
            add(links.seq ^ mask, mask)

    def send(self, step, part=None):
        links = self.links
        count = {0: 0, 1: 0}
        for (h, at, mask), (dim, send, recv, place) in self.hops.items():
            if at == step:
                count[h] += 1
                if part is None or (count[h] > 1) == (part == 1):
                    copy = links.copy(
                        self.half(mask, h), self.came(h, place), send, recv, seq=links.seq ^ dim
                    )
                    copy.start()
                    self.sent.append(copy)

    def fold(self, step):
        links = self.links
        for (h, at, mask), (dim, send, recv, place) in self.hops.items():
            if at != step:
                continue
            links.arrived(self.came(h, place), recv)
            if step < len(self.z.dims) - 1:
                half = self.half(mask ^ dim, h)
                half[...] = (half[...].astype(F32) + self.came(h, place)[...].astype(F32)).astype(BF16)
        if step < len(self.z.dims) - 1:
            self.send(step + 1)

    def total(self, write):
        last = len(self.z.dims) - 1
        for (h, at, mask), (dim, send, recv, place) in self.hops.items():
            if at == last:
                value = self.half(0, h)[...].astype(F32) + self.came(h, place)[...].astype(F32)
                write(halves(self.rows)[h], value)

    def drain(self):
        for copy in self.sent:
            copy.wait_send()


def slots_of(z):
    return Scatter(z, Links(None, 0, 0), None, None, None, 0).slots


def scratch_of(z):
    V = pltpu.VMEM
    half = z.S // 2
    slots = slots_of(z)
    return dict(
        tokg=V((z.S, z.R, z.Ds), BF16),
        halg=V((z.S, 16, z.Ds), BF16),
        hals=V((z.B, 16, z.Ds), BF16),
        db=V((z.S, z.R, z.Ds), BF16),
        inv=V((z.R, LANE), F32),
        normed=V((z.R + 16, z.D), BF16),
        normt=V((z.D, z.R), BF16),
        wx=V((2, z.D, z.C), BF16),
        wo=V((z.S, z.C, z.Ds), BF16),
        xpad=V((z.Q, 8 + z.T, z.C), F32),
        dcp=V((z.Q, z.T + 8, z.C), F32),
        conv=V((z.E, z.C), F32),
        s=V((z.E, z.C), F32),
        su=V((z.R, z.C), F32),
        fac=V((z.E, z.C), F32),
        zp=V((z.R, z.C), F32),
        rd=V((z.R, z.C), F32),
        dr=V((z.R, z.C), F32),
        u=V((z.R, z.C), BF16),
        gat=V((z.R, z.C), BF16),
        gatt=V((z.C, z.R), BF16),
        ddr=V((z.R, z.C), BF16),
        dzr=V((z.R, z.C), BF16),
        dxr=V((z.R, z.C), BF16),
        lowp=V((z.Q, z.M, z.T, z.RK), BF16),
        stp=V((z.Q, z.M, 2 * z.N, z.T), F32),
        low=V((z.R, z.RK), BF16),
        dlow=V((z.R, z.RK), BF16),
        dlowt=V((z.RK, z.R), BF16),
        dst=V((2 * z.N, z.R), BF16),
        st=V((2 * z.N, z.R), F32),
        blkb=V((z.R, GRP * z.N), BF16),
        blkk=V((z.R, GRP * z.N), BF16),
        blkc=V((z.R, GRP * z.N), BF16),
        bc=V((z.Q, z.T, 2 * z.N, LANE), F32),
        hist=V((z.Q * (z.T + 1) * z.N, z.C), BF16),
        gbuf=V((GRP * z.N, z.C), BF16),
        ghbuf=V((GRP * z.N, z.C), BF16),
        ptot=V((z.Q, z.N, z.C), F32),
        stot=V((z.Q, z.N, z.C), F32),
        ppre=V((z.Q, z.N, z.C), F32),
        spre=V((z.Q, z.N, z.C), F32),
        csend=V((z.levels, z.Q, 2, z.N, z.C), BF16),
        crecv=V((z.levels, z.Q, 2, z.N, z.C), BF16),
        bsend=V((z.levels, z.Q, z.N, z.C), BF16),
        brecv=V((z.levels, z.Q, z.N, z.C), BF16),
        est=V((3, z.N, z.R), F32),
        dlowp=V((z.Q, z.M, z.T, z.RK), BF16),
        dstp=V((z.Q, z.M, 2 * z.N, z.T), BF16),
        orecv=V((z.M - 1, z.R, z.Df), BF16),
        nrecv=V((z.M - 1, z.R, z.Df), BF16),
        near_o=V((half * z.C, z.Ds), BF16),
        sum_o=V((half * z.C, z.Ds), BF16),
        far_o=V((slots * (z.C // 2), z.Ds), BF16),
        near_i=V((half * z.Ds, z.C), BF16),
        sum_1=V((half * z.Ds, z.C), BF16),
        far_1=V((slots * (z.Ds // 2), z.C), BF16),
        vec=V((SGVEC, z.C), F32),
        gv=V((z.levels + 1, 8, z.D), F32),
        gvr=V((z.levels, 8, z.D), F32),
        gvm=V((z.M - 1, 8, z.D), F32),
        mrow=V((z.M, 8, z.R), F32),
        sems=pltpu.SemaphoreType.DMA((420,)),
        local=pltpu.SemaphoreType.DMA((8,)),
        ready=pltpu.SemaphoreType.REGULAR((z.levels,)),
    )


def silu_parts(value):
    gate = 1.0 / (1.0 + jnp.exp(-value))
    return gate, value * gate


def fused_kernel(z, names, *refs):
    r = Bunch(names, refs)
    seq, mp = lax.axis_index("seq"), lax.axis_index("mp")
    links = Links(r.sems, seq, mp)
    lanes_all = z.C // LANE
    first_block = mp * z.B

    def lane_loop(step):
        each(z.C // LANE, lambda index: step(cut(index * LANE, LANE)))

    local = r.local
    mine_in = lambda k: r.wx.at[k, cut(seq * z.Ds, z.Ds), :]
    loads = [
        pltpu.make_async_copy(r.win.at[0], mine_in(0), local.at[0]),
        pltpu.make_async_copy(r.win.at[1], mine_in(1), local.at[1]),
        pltpu.make_async_copy(r.wout, r.wo.at[seq], local.at[2]),
    ]
    for load in loads:
        load.start()
    for b in range(z.B):
        r.tokg[first_block + b] = r.tok[:, b * z.Ds : (b + 1) * z.Ds]
        tails = [
            r.tok[q * z.T + z.T - 16 : q * z.T + z.T, b * z.Ds : (b + 1) * z.Ds].astype(F32)[8:]
            for q in range(z.Q)
        ]
        r.hals[b] = jnp.concatenate(tails, axis=0).astype(BF16)

    barrier = pltpu.get_barrier_semaphore()
    ahead, behind = lax.rem(seq + 1, z.S), lax.rem(seq + z.S - 1, z.S)
    partners = [(seq ^ (1 << level), mp) for level in range(z.levels)] + [(ahead, mp), (behind, mp)]
    partners += [(seq, lax.rem(mp + away, z.M)) for away in range(1, z.M)]
    for partner in partners:
        pl.semaphore_signal(barrier, inc=1, device_id=partner, device_id_type=MESH)
    pl.semaphore_wait(barrier, len(partners))

    def of_in(k):
        def half(owner, h):
            return r.wx.at[k, cut(owner * z.Ds + h * (z.Ds // 2), z.Ds // 2), :]

        return TreeGather(z, links, half, lambda owner: r.wx.at[k, cut(owner * z.Ds, z.Ds), :])

    tree_x, tree_z = of_in(0), of_in(1)
    tree_o = TreeGather(
        z,
        links,
        lambda owner, h: r.wo.at[owner, pl.ds(h * (z.C // 2), z.C // 2), :],
        lambda owner: r.wo.at[owner],
    )
    line_t = LineGather(z, links, lambda owner: r.tokg.at[pl.ds(owner * z.B, z.B)])
    line_h = LineGather(z, links, lambda owner: r.halg.at[pl.ds(owner * z.B, z.B)])
    line_d = LineGather(z, links, lambda owner: r.db.at[pl.ds(owner * z.B, z.B)])
    depth = len(z.dims)

    hal_send, hal_recv = links.sem(), links.sem()
    hal_mine = r.halg.at[pl.ds(first_block, z.B)]
    hal = links.copy(r.hals, hal_mine, hal_send, hal_recv, seq=ahead)
    hal.start()
    line_t.step(0)
    loads[0].wait()
    tree_x.first()
    tree_x.second()

    def weight_of(q):
        total = jnp.float32(0.0)
        for group in range(r.groupw.shape[0]):
            total = total + jnp.where(r.seqg[q] == group, r.groupw[group], 0.0)
        return total

    seq_weight = [weight_of(q) for q in range(z.Q)]
    for q in range(z.Q):
        rows = pl.ds(q * z.T, z.T)
        for b in range(z.B):
            part = r.cot[rows, b * z.Ds : (b + 1) * z.Ds] * seq_weight[q]
            r.db[first_block + b, rows, :] = part.astype(BF16)

    links.arrived(hal_mine, hal_recv)
    line_h.step(0)
    line_t.step(1)
    tree_x.forward()
    loads[1].wait()
    tree_z.first()
    tree_z.second()
    line_h.step(1)
    for far in range(2, z.M):
        line_t.step(far)
        line_h.step(far)
    line_d.step(0)

    def add_squares(j, total):
        part = r.tokg[j].astype(F32)
        edge = r.halg[j].astype(F32)
        return (
            total[0] + jnp.sum(part * part, axis=1, keepdims=True),
            total[1] + jnp.sum(edge * edge, axis=1, keepdims=True),
        )

    squares = lax.fori_loop(
        0, z.S, add_squares, (jnp.zeros((z.R, 1), F32), jnp.zeros((16, 1), F32))
    )
    inv = lax.rsqrt(squares[0] * (1.0 / z.D) + EPSILON)
    inv_edge = lax.rsqrt(squares[1] * (1.0 / z.D) + EPSILON)
    r.inv[...] = jnp.broadcast_to(inv, (z.R, LANE))

    def norm_block(j):
        features = cut(j * z.Ds, z.Ds)
        gain = r.gain[:, features]
        normed = r.tokg[j].astype(F32) * wide(r.inv[...], z.Ds // LANE) * gain
        r.normed[: z.R, features] = normed.astype(BF16)
        edge = r.halg[j].astype(F32) * inv_edge * gain
        r.normed[z.R :, features] = edge.astype(BF16)
        r.normt[features, :] = normed.T.astype(BF16)

    each(z.S, norm_block)
    tree_x.settle()
    tree_x.finish()

    def x_chunk(index):
        lanes = cut(index * 256, 256)
        part = nn(r.normed[...], r.wx[0, :, lanes]).astype(BF16).astype(F32)
        for q in range(z.Q):
            edge = part[z.R + 8 * q : z.R + 8 * q + 8]
            r.xpad[q, 0:8, lanes] = jnp.where(seq > 0, edge, 0.0)
            r.xpad[q, 8 : 8 + z.T, lanes] = part[q * z.T : (q + 1) * z.T]

    each(z.C // 256, x_chunk)

    def rows_of(q):
        return pl.ds(q * z.T, z.T)

    def conv(q):
        def conv_lanes(lanes):
            total = jnp.broadcast_to(r.convb[:, lanes], (z.T, LANE))
            for tap in range(4):
                total = total + r.convw[tap : tap + 1, lanes] * r.xpad[q, 5 + tap : 5 + tap + z.T, lanes]
            r.conv[rows_of(q), lanes] = total
            r.u[rows_of(q), lanes] = silu_parts(total)[1].astype(BF16)

        lane_loop(conv_lanes)

    swap_low = [Swap(z, links, lambda slot, q=q: r.lowp.at[q, slot]) for q in range(z.Q)]
    swap_st = [Swap(z, links, lambda slot, q=q: r.stp.at[q, slot]) for q in range(z.Q)]
    low_mine = [r.lowp.at[q, z.M - 1] for q in range(z.Q)]
    st_mine = [r.stp.at[q, z.M - 1] for q in range(z.Q)]

    def project(q):
        u = r.u[rows_of(q), :]
        st_mine[q][...] = nt(r.statewt[...], u)
        swap_st[q].start(st_mine[q])
        low_mine[q][...] = nn(u, r.loww[...]).astype(BF16)
        swap_low[q].start(low_mine[q])

    rows_i = lax.broadcasted_iota(jnp.int32, (z.T, GRP * z.N), 0)
    cols_i = lax.broadcasted_iota(jnp.int32, (z.T, GRP * z.N), 1)
    diagonal = lax.rem(rows_i, GRP) == cols_i // z.N
    rep_n = lax.broadcasted_iota(jnp.int32, (2 * z.N, GRP * z.N), 0)
    rep_j = lax.rem(lax.broadcasted_iota(jnp.int32, (2 * z.N, GRP * z.N), 1), z.N)
    rep_b = (rep_n == rep_j).astype(BF16)
    rep_c = (rep_n == rep_j + z.N).astype(BF16)
    only_b = lax.broadcasted_iota(jnp.int32, (z.T, LANE), 1) < z.N

    def columns_of(value):
        return jnp.concatenate([value, jnp.zeros((LANE - 2 * z.N, z.T), F32)], axis=0).T

    def keys(q):
        swap_st[q].wait()
        st = r.stp[q, 0]
        for slot in range(1, z.M):
            st = st + r.stp[q, slot]
        r.st[:, rows_of(q)] = st

        def spread(index, turned):
            for j in range(16):
                r.bc[q, index * 16 + j] = jnp.broadcast_to(turned[:, j : j + 1], (2 * z.N, LANE))
            return pltpu.roll(turned, LANE - 16, 1)

        lax.fori_loop(0, z.T // 16, spread, st)
        swap_low[q].wait()
        low = r.lowp[q, 0].astype(F32)
        for slot in range(1, z.M):
            low = low + r.lowp[q, slot].astype(F32)
        low = low.astype(BF16)
        r.low[rows_of(q), :] = low
        nat = columns_of(st)
        nat16 = nat[:, : 2 * z.N].astype(BF16)
        key_sq = jnp.sum(jnp.where(only_b, nat * nat, 0.0), axis=1, keepdims=True)
        spread_b = jnp.where(diagonal, nn(nat16, rep_b), 0.0)
        r.blkb[rows_of(q), :] = spread_b.astype(BF16)
        r.blkk[rows_of(q), :] = (spread_b * spread_b).astype(BF16)
        r.blkc[rows_of(q), :] = jnp.where(diagonal, nn(nat16, rep_c), 0.0).astype(BF16)

        def raw_chunk(index):
            lanes = cut(index * 256, 256)
            r.s[rows_of(q), lanes] = nn(low, r.deltaw[:, lanes])

        each(z.C // 256, raw_chunk)

        def step_lanes(lanes):
            raw = r.s[rows_of(q), lanes] + r.dbias[:, lanes]
            beta = 1.0 / (1.0 + jnp.exp(-raw))
            scale = 1.0 / (1.0 + beta * key_sq)
            step = beta * scale
            r.s[rows_of(q), lanes] = step
            r.su[rows_of(q), lanes] = step * r.u[rows_of(q), lanes].astype(F32)
            r.fac[rows_of(q), lanes] = scale * step * (1.0 - beta)

        lane_loop(step_lanes)

    span = 512 if z.C % 512 == 0 else 256

    def token(q, t):
        return pl.ds(q * z.T + t, 1)

    def totals(q):
        def lane_part(index):
            lanes = cut(index * span, span)

            def tokens8(i, carry):
                product, state = carry
                for j in range(8):
                    row = token(q, i * 8 + j)
                    step, drive = r.s[row, lanes], r.su[row, lanes]
                    key = r.bc[q, i * 8 + j, : z.N, :]
                    decay = 1.0 - step * wide(key * key, span // LANE)
                    product = product * decay
                    state = decay * state + drive * wide(key, span // LANE)
                return product, state

            start = (jnp.ones((z.N, span), F32), jnp.zeros((z.N, span), F32))
            product, state = lax.fori_loop(0, z.T // 8, tokens8, start)
            r.ptot[q, :, lanes] = product
            r.stot[q, :, lanes] = state

        each(z.C // span, lane_part)

    carry_sems = [[(links.sem(), links.sem()) for q in range(z.Q)] for level in range(z.levels)]
    back_sems = [[(links.sem(), links.sem()) for q in range(z.Q)] for level in range(z.levels)]
    carry_copies = []

    def upper_at(level):
        return lax.rem(seq // (1 << level), 2) == 1

    def carry_send(level, q):
        r.csend[level, q, 0] = r.ptot[q].astype(BF16)
        r.csend[level, q, 1] = r.stot[q].astype(BF16)
        copy = links.copy(
            r.csend.at[level, q], r.crecv.at[level, q], *carry_sems[level][q], seq=seq ^ (1 << level)
        )
        copy.start()
        carry_copies.append(copy)

    def carry_take(level, q):
        links.arrived(r.crecv.at[level, q], carry_sems[level][q][1])
        upper = upper_at(level)
        other_p, other_s = r.crecv[level, q, 0].astype(F32), r.crecv[level, q, 1].astype(F32)
        mine_p, mine_s = r.ptot[q], r.stot[q]
        if level == 0:
            r.spre[q] = jnp.where(upper, other_s, 0.0)
            r.ppre[q] = jnp.where(upper, other_p, 1.0)
        else:
            pre_p, pre_s = r.ppre[q], r.spre[q]
            r.spre[q] = jnp.where(upper, pre_p * other_s + pre_s, pre_s)
            r.ppre[q] = jnp.where(upper, pre_p * other_p, pre_p)
        if level < z.levels - 1:
            r.stot[q] = jnp.where(upper, mine_p * other_s + mine_s, other_p * mine_s + other_s)
            r.ptot[q] = mine_p * other_p

    def back_send(level, q):
        r.bsend[level, q] = r.stot[q].astype(BF16)
        copy = links.copy(
            r.bsend.at[level, q], r.brecv.at[level, q], *back_sems[level][q], seq=seq ^ (1 << level)
        )
        copy.start()
        carry_copies.append(copy)

    def back_take(level, q):
        links.arrived(r.brecv.at[level, q], back_sems[level][q][1])
        upper = upper_at(level)
        other = r.brecv[level, q].astype(F32)
        other_p, mine_p = r.crecv[level, q, 0].astype(F32), r.csend[level, q, 0].astype(F32)
        mine = r.stot[q]
        if level == 0:
            r.spre[q] = jnp.where(upper, 0.0, other)
            r.ppre[q] = jnp.where(upper, 1.0, other_p)
        else:
            pre_p, pre = r.ppre[q], r.spre[q]
            r.spre[q] = jnp.where(upper, pre, pre + pre_p * other)
            r.ppre[q] = jnp.where(upper, pre_p, pre_p * other_p)
        if level < z.levels - 1:
            r.stot[q] = jnp.where(upper, other + other_p * mine, mine + mine_p * other)

    def past_rows(q, slot, count=1):
        return pl.ds(pl.multiple_of((q * (z.T + 1) + slot) * z.N, z.N), count * z.N)

    def walk(q):
        r.hist[past_rows(q, 0), :] = r.spre[q].astype(BF16)

        def lane_part(index):
            lanes = cut(index * span, span)

            def tokens8(i, state):
                for j in range(8):
                    row = token(q, i * 8 + j)
                    step, drive = r.s[row, lanes], r.su[row, lanes]
                    key = r.bc[q, i * 8 + j, : z.N, :]
                    decay = 1.0 - step * wide(key * key, span // LANE)
                    state = decay * state + drive * wide(key, span // LANE)
                    r.hist[past_rows(q, i * 8 + j + 1), lanes] = state.astype(BF16)
                return state

            lax.fori_loop(0, z.T // 8, tokens8, r.spre[q, :, lanes])

        each(z.C // span, lane_part)

        def read(i):
            rows = cut(q * z.T + i * GRP, GRP)
            past = r.hist[past_rows(q, i * GRP + 1, GRP), :]
            r.rd[rows, :] = nn(r.blkc[rows, :], past)

        each(z.T // GRP, read)

    conv(0)
    project(0)
    conv(1)
    project(1)
    tree_z.forward()
    loads[2].wait()
    tree_o.first()
    line_d.step(1)
    keys(0)
    totals(0)
    carry_send(0, 0)
    keys(1)
    totals(1)
    carry_send(0, 1)
    line_d.step(2)
    carry_take(0, 0)
    carry_send(1, 0)
    carry_take(0, 1)
    carry_send(1, 1)
    tree_o.second()
    tree_z.settle()
    tree_z.finish()

    def z_chunk(index):
        lanes = cut(index * 256, 256)
        r.zp[:, lanes] = nn(r.normed[: z.R, :], r.wx[1, :, lanes])

    each(z.C // 256, z_chunk)
    for level in range(1, z.levels):
        for q in range(z.Q):
            carry_take(level, q)
            if level < z.levels - 1:
                carry_send(level + 1, q)
    for far in range(3, z.M):
        line_d.step(far)
    walk(0)
    tree_o.forward()
    walk(1)
    tree_o.settle()
    tree_o.finish()

    r.dr[...] = nt(r.db[0], r.wo[0])

    def gated_grad(index):
        r.dr[...] += nt(r.db[index + 1], r.wo[index + 1])

    each(z.S - 1, gated_grad)
    r.vec[...] = jnp.zeros_like(r.vec)

    def gate_lanes(lanes):
        for q in range(z.Q):
            rows = rows_of(q)
            u = r.u[rows, lanes].astype(F32)
            out = r.rd[rows, lanes] + r.skip[:, lanes] * u
            part, grad = r.zp[rows, lanes], r.dr[rows, lanes]
            gate, silu = silu_parts(part)
            gated = out * silu
            r.gat[rows, lanes] = gated.astype(BF16)
            r.gatt[lanes, rows] = gated.T.astype(BF16)
            d_read = grad * silu
            r.dr[rows, lanes] = d_read
            r.dzr[rows, lanes] = (grad * out * gate * (1.0 + part * (1.0 - gate))).astype(BF16)
            r.vec[6:7, lanes] += jnp.sum(d_read * u, axis=0, keepdims=True)

    lane_loop(gate_lanes)

    swap_out = Swap(z, links, lambda slot: r.orecv.at[slot])

    def partial_of(owner):
        return r.normed.at[pl.ds(0, z.R), cut(owner * z.Df, z.Df)]

    def branch_to(index):
        away = index + 1
        owner = lax.rem(mp + away, z.M)
        for b in range(z.B):
            j = owner * z.B + b
            r.normed[: z.R, cut(j * z.Ds, z.Ds)] = nn(r.gat[...], r.wo[j]).astype(BF16)

        @pl.when(away < z.M)
        def _():
            swap_out.one(partial_of(owner), away).start()

    def into(near, term):
        def make(device, mask):
            block = near.block(mask // 2)
            block[...] = term(device).astype(BF16)
            return block

        return make

    def onto(sums, term):
        def add(device, mask):
            block = sums.block(mask // 2)
            block[...] = (term(device) + block[...].astype(F32)).astype(BF16)

        return add

    half_s, slots = z.S // 2, slots_of(z)
    sg_rows = z.rows_sg
    near_o, near_i = Rows(r.near_o, 0, z.C, half_s), Rows(r.near_i, 0, z.Ds, half_s)
    sum_o, far_o = Rows(r.sum_o, 0, z.C, half_s), Rows(r.far_o, 0, z.C // 2, slots)
    sum_1, far_1 = Rows(r.sum_1, 0, z.Ds, half_s), Rows(r.far_1, 0, z.Ds // 2, slots)
    sum_0 = Rows(r.hist, 0, z.Ds, half_s)
    far_0 = Rows(r.hist, sum_0.end, z.Ds // 2, slots)
    sum_s = Rows(r.hist, far_0.end, sg_rows, half_s)
    far_s = Rows(r.hist, sum_s.end, halves(sg_rows)[0][1], slots)
    sgp = Rows(r.hist, far_s.end, sg_rows, z.S)
    small = Rows(r.hist, sgp.end, sg_rows, z.S)
    scatter_o = Scatter(z, links, None, sum_o, far_o, z.C)
    scatter_1 = Scatter(z, links, None, sum_1, far_1, z.Ds)
    scatter_0 = Scatter(z, links, None, sum_0, far_0, z.Ds)
    scatter_s = Scatter(z, links, None, sum_s, far_s, sg_rows)
    term_o = lambda device: nn(r.gatt[...], r.db[device])
    term_1 = lambda device: nn(r.normt[cut(device * z.Ds, z.Ds), :], r.dzr[...])
    term_0 = lambda device: nn(r.normt[cut(device * z.Ds, z.Ds), :], r.dxr[...])

    def totals_back(q):
        def lane_part(index):
            lanes = cut(index * span, span)

            def tokens8(i, tail):
                for j in reversed(range(8)):
                    t = z.T - 8 - i * 8 + j
                    row = token(q, t)
                    step, grad = r.s[row, lanes], r.dr[row, lanes]
                    key, query = r.bc[q, t, : z.N, :], r.bc[q, t, z.N :, :]
                    decay = 1.0 - step * wide(key * key, span // LANE)
                    tail = decay * (grad * wide(query, span // LANE) + tail)
                return tail

            r.stot[q, :, lanes] = lax.fori_loop(0, z.T // 8, tokens8, jnp.zeros((z.N, span), F32))

        each(z.C // span, lane_part)

    lane_index = lax.broadcasted_iota(jnp.int32, (z.N, LANE), 1)

    def lane_sum(value):
        total = value[:, :LANE]
        for part in range(1, lanes_all):
            total = total + value[:, part * LANE : (part + 1) * LANE]
        return jnp.sum(total, axis=1, keepdims=True)

    def walk_back(q):
        def group(index, carry):
            tail, sum_gh, sum_g, sum_h = carry
            i = z.T // GRP - 1 - index
            for j in reversed(range(GRP)):
                t = i * GRP + j
                row = token(q, t)
                step, drive, grad = r.s[row, :], r.su[row, :], r.dr[row, :]
                key, query = r.bc[q, t, : z.N, :], r.bc[q, t, z.N :, :]
                before = r.hist[past_rows(q, t), :].astype(F32)
                now = r.hist[past_rows(q, t + 1), :].astype(F32)
                state_grad = grad * wide(query, lanes_all) + tail
                crossed = state_grad * before
                r.gbuf[j * z.N : (j + 1) * z.N, :] = state_grad.astype(BF16)
                r.ghbuf[j * z.N : (j + 1) * z.N, :] = crossed.astype(BF16)
                here = lane_index == t
                sum_gh = jnp.where(here, lane_sum(step * crossed), sum_gh)
                sum_g = jnp.where(here, lane_sum(drive * state_grad), sum_g)
                sum_h = jnp.where(here, lane_sum(grad * now), sum_h)
                tail = (1.0 - step * wide(key * key, lanes_all)) * state_grad
            rows = cut(q * z.T + i * GRP, GRP)
            r.rd[rows, :] = nn(r.blkb[rows, :], r.gbuf[...])
            r.zp[rows, :] = nn(r.blkk[rows, :], r.ghbuf[...])
            return tail, sum_gh, sum_g, sum_h

        zero = jnp.zeros((z.N, LANE), F32)
        _, sum_gh, sum_g, sum_h = lax.fori_loop(0, z.T // GRP, group, (r.spre[q], zero, zero, zero))
        columns = pl.ds(q * z.T, z.T)
        r.est[0, :, columns] = sum_gh
        r.est[1, :, columns] = sum_g
        r.est[2, :, columns] = sum_h

    def step_back(q):
        rows = rows_of(q)

        def step_lanes(lanes):
            sum_b, step = r.rd[rows, lanes], r.s[rows, lanes]
            d_step = r.u[rows, lanes].astype(F32) * sum_b - r.zp[rows, lanes]
            r.rd[rows, lanes] = step * sum_b
            d_raw = d_step * r.fac[rows, lanes]
            r.ddr[rows, lanes] = d_raw.astype(BF16)
            r.gat[rows, lanes] = (d_step * step * step).astype(BF16)
            r.vec[5:6, lanes] += jnp.sum(d_raw, axis=0, keepdims=True)

        lane_loop(step_lanes)

    swap_dlow = [Swap(z, links, lambda slot, q=q: r.dlowp.at[q, slot]) for q in range(z.Q)]
    swap_dst = [Swap(z, links, lambda slot, q=q: r.dstp.at[q, slot]) for q in range(z.Q)]
    dlow_mine = [r.dlowp.at[q, z.M - 1] for q in range(z.Q)]
    dst_mine = [r.dstp.at[q, z.M - 1] for q in range(z.Q)]

    def project_back(q):
        rows = rows_of(q)
        key_grad = nt(jnp.ones((16, z.C), BF16), r.gat[rows, :])[0:1]
        now = r.st[: z.N, rows]
        d_key = r.est[1, :, rows] - 2.0 * now * r.est[0, :, rows] - 2.0 * now * key_grad
        dst_mine[q][...] = jnp.concatenate([d_key, r.est[2, :, rows]], axis=0).astype(BF16)
        swap_dst[q].start(dst_mine[q])
        dlow_mine[q][...] = nt(r.ddr[rows, :], r.deltaw[...]).astype(BF16)
        swap_dlow[q].start(dlow_mine[q])

    def sums_back(q):
        rows = rows_of(q)
        swap_dlow[q].wait()
        swap_dst[q].wait()
        dlow = r.dlowp[q, 0].astype(F32)
        dst = r.dstp[q, 0].astype(F32)
        for slot in range(1, z.M):
            dlow = dlow + r.dlowp[q, slot].astype(F32)
            dst = dst + r.dstp[q, slot].astype(F32)
        r.dlow[rows, :] = dlow.astype(BF16)
        r.dlowt[:, rows] = dlow.T.astype(BF16)
        r.dst[:, rows] = dst.astype(BF16)
        dlow16, dst16 = dlow.astype(BF16), columns_of(dst)[:, : 2 * z.N].astype(BF16)

        def inputs_chunk(index):
            lanes = cut(index * 256, 256)
            r.su[rows, lanes] = nt(dlow16, r.loww[lanes, :]) + nn(dst16, r.statewt[:, lanes])

        each(z.C // 256, inputs_chunk)

    rim = [
        links.copy(
            r.dcp.at[q, pl.ds(0, 8), :],
            r.dcp.at[q, pl.ds(z.T, 8), :],
            links.sem(),
            links.sem(),
            seq=behind,
        )
        for q in range(z.Q)
    ]

    def conv_back(q):
        rows = rows_of(q)

        def conv_lanes(lanes):
            total = r.su[rows, lanes] + r.rd[rows, lanes] + r.skip[:, lanes] * r.dr[rows, lanes]
            value = r.conv[rows, lanes]
            gate = silu_parts(value)[0]
            d_conv = total * gate * (1.0 + value * (1.0 - gate))
            r.dcp[q, 0 : z.T, lanes] = d_conv
            r.vec[4:5, lanes] += jnp.sum(d_conv, axis=0, keepdims=True)
            for tap in range(4):
                r.vec[tap : tap + 1, lanes] += jnp.sum(
                    d_conv * r.xpad[q, 5 + tap : 5 + tap + z.T, lanes], axis=0, keepdims=True
                )

        lane_loop(conv_lanes)
        rim[q].start()

    def x_back(q):
        rim[q].wait_recv()

        def x_lanes(lanes):
            edge = r.dcp[q, z.T : z.T + 8, lanes]
            r.dcp[q, z.T : z.T + 8, lanes] = jnp.where(seq < z.S - 1, edge, 0.0)
            total = jnp.zeros((z.T, LANE), F32)
            for tap in range(4):
                total = total + r.convw[tap : tap + 1, lanes] * r.dcp[q, 3 - tap : 3 - tap + z.T, lanes]
            r.dxr[rows_of(q), lanes] = total.astype(BF16)

        lane_loop(x_lanes)

    scatter_o.first(into(near_o, term_o))
    scatter_o.second(onto(sum_o, term_o))
    scatter_o.send(0, 0)
    totals_back(0)
    back_send(0, 0)
    totals_back(1)
    back_send(0, 1)
    for level in range(z.levels):
        for q in range(z.Q):
            back_take(level, q)
            if level < z.levels - 1:
                back_send(level + 1, q)
        if level == 0:
            each(z.M, branch_to)
            scatter_1.first(into(near_i, term_1))
        if level == 1:
            scatter_o.send(0, 1)
            scatter_1.second(onto(sum_1, term_1))
    scatter_1.send(0)
    walk_back(0)
    step_back(0)
    project_back(0)
    walk_back(1)
    for level in range(z.levels):
        pl.semaphore_signal(
            r.ready.at[level], inc=1, device_id=(seq ^ (1 << level), mp), device_id_type=MESH
        )
    step_back(1)
    project_back(1)
    for step in range(depth - 1):
        scatter_o.fold(step)
    sums_back(0)
    conv_back(0)
    sums_back(1)
    conv_back(1)
    for step in range(depth - 1):
        scatter_1.fold(step)

    def put_small(first, value):
        count, at = value.shape[0], 0
        while at < count:
            block, inside = divmod(first + at, sg_rows)
            take = min(count - at, sg_rows - inside)
            sgp.block(block, inside, take)[...] = value[at : at + take].astype(BF16)
            at += take

    low_t = r.low[...].astype(F32).T.astype(BF16)
    put_small(0, nn(low_t, r.ddr[...]))
    put_small(z.RK, nn(r.dlowt[...], r.u[...]))
    put_small(2 * z.RK, nn(r.dst[...], r.u[...]))
    put_small(2 * z.RK + 2 * z.N, r.vec[...])
    used = 2 * z.RK + 2 * z.N + SGVEC
    if used < z.S * sg_rows:
        put_small(used, jnp.zeros((z.S * sg_rows - used, z.C), F32))
    x_back(0)
    x_back(1)

    for level in range(z.levels):
        pl.semaphore_wait(r.ready.at[level], 1)
    scatter_s.first(lambda device, mask: sgp.block(device))
    for copy in scatter_1.sent[: len(z.masks)]:
        copy.wait_send()
    scatter_1.sent = scatter_1.sent[len(z.masks) :]
    scatter_0.first(into(near_i, term_0))

    def add_small(device, mask):
        block = sum_s.block(mask // 2)
        block[...] = (block[...].astype(F32) + sgp.block(device)[...].astype(F32)).astype(BF16)

    scatter_s.second(add_small)
    scatter_s.send(0)
    scatter_0.second(onto(sum_0, term_0))
    scatter_0.send(0)

    swap_out.wait()
    for away in range(1, z.M):
        owner = lax.rem(mp + away, z.M)
        swap_out.one(partial_of(owner), away).wait_send()
    for b in range(z.B):
        features = slice(b * z.Ds, (b + 1) * z.Ds)
        total = r.normed[: z.R, cut((first_block + b) * z.Ds, z.Ds)].astype(F32)
        for slot in range(z.M - 1):
            total = total + r.orecv[slot, :, features].astype(F32)
        r.blk[:, features] = (r.tok[:, features].astype(F32) + total).astype(BF16)

    swap_n = Swap(z, links, lambda slot: r.nrecv.at[slot])

    def normed_to(index, means):
        away = index + 1
        owner = lax.rem(mp + away, z.M)
        for b in range(z.B):
            j = owner * z.B + b
            features = cut(j * z.Ds, z.Ds)
            part = nt(r.dxr[...], r.wx[0, features, :]) + nt(r.dzr[...], r.wx[1, features, :])
            r.normed[: z.R, features] = part.astype(BF16)
            scaled = part * r.tokg[j].astype(F32)
            by_gain = jnp.sum(scaled * wide(r.inv[...], z.Ds // LANE), axis=0, keepdims=True)
            r.gv[0, :, features] = jnp.broadcast_to(by_gain, (8, z.Ds))
            means = means + jnp.sum(scaled * r.gain[:, features], axis=1, keepdims=True)

        @pl.when(away < z.M)
        def _():
            swap_n.one(partial_of(owner), away).start()

        return means

    means = lax.fori_loop(0, z.M, normed_to, jnp.zeros((z.R, 1), F32))
    swap_m = Swap(z, links, lambda slot: r.mrow.at[slot])
    mean_mine = r.mrow.at[z.M - 1]
    mean_mine[...] = jnp.broadcast_to(means, (z.R, LANE)).T[0:8]
    swap_m.start(mean_mine)

    gain_copies = []
    for level in range(z.levels):
        copy = links.copy(
            r.gv.at[level], r.gvr.at[level], links.sem(), links.sem(), seq=seq ^ (1 << level)
        )
        copy.start()
        gain_copies.append(copy)
        if level < depth - 1:
            scatter_s.fold(level)
        copy.wait_recv()
        r.gv[level + 1] = r.gv[level] + r.gvr[level]
    swap_g = Swap(z, links, lambda slot: r.gvm.at[slot])
    swap_g.start(r.gv.at[z.levels])
    scatter_s.fold(depth - 1)

    def write_small(rows, value):
        small.block(seq, *rows)[...] = value.astype(BF16)

    scatter_s.total(write_small)
    tree_s = TreeGather(
        z,
        links,
        lambda owner, h: small.block(owner, *halves(sg_rows)[h]),
        small.block,
    )
    tree_s.first()
    tree_s.second()
    for step in range(depth - 1):
        scatter_0.fold(step)
    tree_s.forward()
    tree_s.settle()

    swap_m.wait()
    mean = r.mrow[0]
    for slot in range(1, z.M):
        mean = mean + r.mrow[slot]
    mean = wide(jnp.concatenate([mean] * (LANE // 8), axis=0).T * (1.0 / z.D), z.Ds // LANE)
    swap_n.wait()
    inv_wide = wide(r.inv[...], z.Ds // LANE)
    for b in range(z.B):
        j = first_block + b
        here = slice(b * z.Ds, (b + 1) * z.Ds)
        gain = r.gain[:, cut(j * z.Ds, z.Ds)]
        total = r.normed[: z.R, cut(j * z.Ds, z.Ds)].astype(F32)
        for slot in range(z.M - 1):
            total = total + r.nrecv[slot, :, here].astype(F32)
        x = r.tok[:, here].astype(F32)
        value = inv_wide * (total * gain) - x * (inv_wide * inv_wide * inv_wide) * mean
        for q in range(z.Q):
            rows = slice(q * z.T, (q + 1) * z.T)
            r.dtok[rows, here] = value[rows] + r.cot[rows, here] * seq_weight[q]

    last = depth - 1
    scatter_o.fold(last)

    def write_out(rows, value):
        r.dout[pl.ds(*rows), :] = value

    scatter_o.total(write_out)
    scatter_1.fold(last)

    def write_to(ref):
        def write(rows, value):
            ref[pl.ds(*rows), :] = value

        return write

    scatter_1.total(write_to(r.fac))
    store_1 = pltpu.make_async_copy(r.fac.at[pl.ds(0, z.Ds)], r.din.at[1], local.at[3])
    store_1.start()
    swap_g.wait()
    gains = r.gv[z.levels]
    for slot in range(z.M - 1):
        gains = gains + r.gvm[slot]
    r.dgain[...] = gains[0:1]
    tree_s.finish()
    for block in range(z.S):
        count = min(sg_rows, r.sg.shape[0] - block * sg_rows)
        if count > 0:
            r.sg[block * sg_rows : block * sg_rows + count, :] = small.block(block)[...].astype(F32)[:count]
    scatter_0.fold(last)
    scatter_0.total(write_to(r.s))
    store_0 = pltpu.make_async_copy(r.s.at[pl.ds(0, z.Ds)], r.din.at[0], local.at[4])
    store_0.start()

    hal.wait_send()
    for tree in (tree_x, tree_z, tree_o, tree_s):
        tree.drain()
    for line in (line_t, line_h, line_d):
        line.drain()
    for q in range(z.Q):
        swap_st[q].drain(st_mine[q])
        swap_low[q].drain(low_mine[q])
        swap_dlow[q].drain(dlow_mine[q])
        swap_dst[q].drain(dst_mine[q])
    swap_m.drain(mean_mine)
    swap_g.drain(r.gv.at[z.levels])
    for away in range(1, z.M):
        owner = lax.rem(mp + away, z.M)
        swap_n.one(partial_of(owner), away).wait_send()
    for copy in carry_copies + gain_copies + rim:
        copy.wait_send()
    for scatter in (scatter_o, scatter_1, scatter_0, scatter_s):
        scatter.drain()
    store_1.wait()
    store_0.wait()


def finish_kernel(z, blk, dtok, dgain, din, dout, sg, *outs):
    a, b, c = z.RK, 2 * z.RK, 2 * z.RK + 2 * z.N
    o_blk, o_dtok, o_dgain, o_din, o_convw, o_convb, o_low, o_state, o_delta, o_dbias, o_skip, o_dout, sems = outs
    copies = [
        pltpu.make_async_copy(src, dst, sems.at[index])
        for index, (src, dst) in enumerate([(din, o_din), (dout, o_dout), (dtok, o_dtok), (blk, o_blk)])
    ]
    for copy in copies:
        copy.start()
    o_dgain[...] = dgain[...]
    o_delta[...] = sg[0:a, :]
    o_convw[...] = sg[c : c + 4, :]
    o_convb[...] = sg[c + 4 : c + 5, :]
    o_dbias[...] = sg[c + 5 : c + 6, :]
    o_skip[...] = sg[c + 6 : c + 7, :]
    for at in range(0, z.C, LANE):
        o_low[at : at + LANE, :] = sg[a:b, at : at + LANE].T
        part = jnp.concatenate([sg[b:c, at : at + LANE], jnp.zeros((LANE - 2 * z.N, LANE), F32)], axis=0)
        o_state[at : at + LANE, :] = part.T[:, : 2 * z.N]
    for copy in copies:
        copy.wait()


def fused(z, tokens, norm_gain, in_weight, conv_weight, conv_bias, low_weight, state_weight, delta_weight,
          delta_bias, skip_gain, out_weight, cotangent, seq_group, group_weight):
    V = pl.BlockSpec(memory_space=pltpu.VMEM)
    A = pl.BlockSpec(memory_space=pl.ANY)
    SM = pl.BlockSpec(memory_space=pltpu.SMEM)
    row = lambda value: value.reshape(1, -1)
    operands = dict(
        tok=(V, tokens.reshape(z.R, z.Df)),
        cot=(V, cotangent.reshape(z.R, z.Df)),
        gain=(V, row(norm_gain)),
        win=(A, in_weight),
        wout=(A, out_weight),
        convw=(V, conv_weight),
        convb=(V, row(conv_bias)),
        dbias=(V, row(delta_bias)),
        skip=(V, row(skip_gain)),
        loww=(V, low_weight),
        statewt=(V, state_weight.T),
        deltaw=(V, delta_weight),
        seqg=(SM, seq_group),
        groupw=(SM, group_weight),
    )
    scratch = scratch_of(z)
    sg_used = 2 * z.RK + 2 * z.N + SGVEC
    outs = dict(
        blk=(V, (z.R, z.Df), BF16),
        dtok=(V, (z.R, z.Df), F32),
        dgain=(V, (1, z.D), F32),
        din=(A, (2, z.Ds, z.C), F32),
        dout=(V, (z.C, z.Ds), F32),
        sg=(V, (sg_used, z.C), F32),
    )
    result = pl.pallas_call(
        functools.partial(fused_kernel, z, [*operands, *outs, *scratch]),
        out_shape=[jax.ShapeDtypeStruct(shape, kind) for _, shape, kind in outs.values()],
        in_specs=[spec for spec, _ in operands.values()],
        out_specs=[spec for spec, _, _ in outs.values()],
        scratch_shapes=list(scratch.values()),
        compiler_params=pltpu.CompilerParams(
            collective_id=0, has_side_effects=True, vmem_limit_bytes=VMEM_BYTES
        ),
    )(*[value for _, value in operands.values()])
    whole = (V, (1, z.C), F32)
    last = dict(
        blk=(A, (z.R, z.Df), BF16),
        dtok=(A, (z.R, z.Df), F32),
        dgain=(V, (1, z.D), F32),
        din=(A, (2, z.Ds, z.C), F32),
        convw=(V, (4, z.C), F32),
        convb=whole,
        low=(V, (z.C, z.RK), F32),
        state=(V, (z.C, 2 * z.N), F32),
        delta=(V, (z.RK, z.C), F32),
        dbias=whole,
        skip=whole,
        dout=(A, (z.C, z.Ds), F32),
    )
    done = pl.pallas_call(
        functools.partial(finish_kernel, z),
        out_shape=[jax.ShapeDtypeStruct(shape, kind) for _, shape, kind in last.values()],
        in_specs=[A, A, V, A, A, V],
        out_specs=[spec for spec, _, _ in last.values()],
        scratch_shapes=[pltpu.SemaphoreType.DMA((4,))],
        compiler_params=pltpu.CompilerParams(vmem_limit_bytes=VMEM_BYTES),
    )(*result)
    shapes = [tokens.shape, tokens.shape, (z.D,), None, None, (z.C,), None, None, None, (z.C,), (z.C,), None]
    return tuple(value if shape is None else value.reshape(shape) for value, shape in zip(done, shapes))


def local(mesh_shape, *arrays):
    tokens, norm_gain, in_weight, conv_weight = arrays[:4]
    state_weight, delta_weight = arrays[6], arrays[7]
    z = Sizes(
        mesh_shape,
        tokens.shape[0],
        tokens.shape[1],
        tokens.shape[2],
        norm_gain.shape[0],
        in_weight.shape[2],
        state_weight.shape[1] // 2,
        delta_weight.shape[0],
    )
    if z.fits(conv_weight.shape[0]):
        return fused(z, *arrays)
    return plain(*arrays)


def solution(mesh):
    placed = (
        P(None, "seq", "mp"),
        P(),
        P(None, "seq", "mp"),
        P(None, "mp"),
        P("mp"),
        P("mp", None),
        P("mp", None),
        P(None, "mp"),
        P("mp"),
        P("mp"),
        P("mp", "seq"),
        P(None, "seq", "mp"),
        P(),
        P(),
    )
    return jax.shard_map(
        functools.partial(local, dict(mesh.shape)),
        mesh=mesh,
        in_specs=placed,
        out_specs=(
            P(None, "seq", "mp"),
            P(None, "seq", "mp"),
            P(),
            P(None, "seq", "mp"),
            P(None, "mp"),
            P("mp"),
            P("mp", None),
            P("mp", None),
            P(None, "mp"),
            P("mp"),
            P("mp"),
            P("mp", "seq"),
        ),
        check_vma=False,
    )
```

```python
import functools
import math

import jax
import jax.numpy as jnp
from jax import lax
from jax.experimental import pallas as pl
from jax.experimental.pallas import tpu as pltpu
from jax.sharding import PartitionSpec as P

SEQ_MB = 1
NMB = 2
EPSILON = 1e-05
VMEM_BYTES = 64 * 1024 * 1024 - 64 * 1024


def from_behind(value, axis, steps):
    count = lax.axis_size(axis)
    leading, last = (max(0, -steps), min(count, count - steps))
    return lax.ppermute(value, axis, [(source, source + steps) for source in range(leading, last)])


def prefix(value, axis, join, neutral, backward):
    count, mine = (lax.axis_size(axis), lax.axis_index(axis))
    pieces = jax.tree.map(lambda part: lax.all_gather(part, axis), value)
    if backward:
        pieces = jax.tree.map(lambda part: part[::-1], pieces)
        mine = count - 1 - mine
    subtotal = jax.tree.map(
        lambda part, zero: jnp.full_like(part, 0) + jnp.asarray(zero, part.dtype), value, neutral
    )

    def lap(position, subtotal):
        longer = join(subtotal, jax.tree.map(lambda part: part[position], pieces))
        return jax.tree.map(lambda new, old: jnp.where(position < mine, new, old), longer, subtotal)

    return lax.fori_loop(0, count - 1, lap, subtotal)


def combine(earlier, later):
    return (earlier[0] * later[0], later[0] * earlier[1] + later[1])


def make_gates(delta_raw, b_state, inputs):
    beta_gate = jax.nn.sigmoid(delta_raw)
    key_sq = jnp.sum(b_state * b_state, axis=-1, keepdims=True)
    step_size = beta_gate / (1.0 + beta_gate * key_sq)
    decays = 1.0 - step_size[:, :, None, :] * (b_state * b_state)[:, :, :, None]
    source = (step_size * inputs)[:, :, None, :] * b_state[:, :, :, None]
    return (decays, source)


def to_blocks(value, span_rows):
    old_shape = value.shape
    reshaped = value.reshape((old_shape[0], old_shape[1] // span_rows, span_rows) + old_shape[2:])
    return jnp.swapaxes(reshaped, 0, 1)


def from_blocks(value):
    joined = jnp.swapaxes(value, 0, 1)
    old_shape = joined.shape
    return joined.reshape((old_shape[0], old_shape[1] * old_shape[2]) + old_shape[3:])


def forward_block(carry_pair, block_items):
    delta_raw, b_state, inputs = block_items
    decays, source = make_gates(delta_raw, b_state, inputs)
    run_prod, run_state = carry_pair
    prod_list = []
    state_list = []
    for row_idx in range(decays.shape[1]):
        run_prod = run_prod * decays[:, row_idx]
        run_state = decays[:, row_idx] * run_state + source[:, row_idx]
        prod_list.append(run_prod)
        state_list.append(run_state)
    return ((run_prod, run_state), (jnp.stack(prod_list, axis=1), jnp.stack(state_list, axis=1)))


def backward_block(carry_trio, block_items):
    delta_raw, b_state, inputs, read_grad, c_state = block_items
    decays, _ = make_gates(delta_raw, b_state, inputs)
    grad_next, dec_next, tail_prod = carry_trio
    span_rows = decays.shape[1]
    grad_list = [None] * span_rows
    tail_list = [None] * span_rows
    for row_idx in reversed(range(span_rows)):
        drive_term = read_grad[:, row_idx][:, None, :] * c_state[:, row_idx][:, :, None]
        grad_next = drive_term + dec_next * grad_next
        tail_prod = dec_next * tail_prod
        grad_list[row_idx] = grad_next
        tail_list[row_idx] = tail_prod
        dec_next = decays[:, row_idx]
    return (
        (grad_next, dec_next, tail_prod),
        (jnp.stack(grad_list, axis=1), jnp.stack(tail_list, axis=1)),
    )


def silu_slope(value):
    sig_value = jax.nn.sigmoid(value)
    return sig_value * (1.0 + value * (1.0 - sig_value))


def plain(
    tokens,
    norm_gain,
    in_weight,
    conv_weight,
    conv_bias,
    low_weight,
    state_weight,
    delta_weight,
    delta_bias,
    skip_gain,
    out_weight,
    cotangent,
    seq_group,
    group_weight,
):
    stretch = tokens.shape[1]
    feature_dev = tokens.shape[2]
    channels = in_weight.shape[2]
    model_width = norm_gain.shape[0]
    num_taps = conv_weight.shape[0]
    nstate = state_weight.shape[1] // 2
    span_rows = math.gcd(stretch, 8)
    picks = (
        seq_group[:, None] == jnp.arange(group_weight.shape[0], dtype=jnp.int32)[None, :]
    ).astype(jnp.float32)
    seq_weight = jnp.sum(picks * group_weight[None, :], axis=1)
    feature_start = lax.axis_index("mp") * feature_dev
    ones_state = jnp.ones((SEQ_MB, nstate, channels), jnp.float32)
    zero_state = jnp.zeros_like(ones_state)
    acc_in = jnp.zeros((2, model_width, channels), jnp.float32)
    acc_out = jnp.zeros((channels, model_width), jnp.float32)
    acc_gain = jnp.zeros_like(norm_gain)
    acc_conv = jnp.zeros_like(conv_weight)
    acc_cbias = jnp.zeros_like(conv_bias)
    acc_low = jnp.zeros(low_weight.shape, jnp.float32)
    acc_state = jnp.zeros(state_weight.shape, jnp.float32)
    acc_delta = jnp.zeros(delta_weight.shape, jnp.float32)
    acc_dbias = jnp.zeros_like(delta_bias)
    acc_skip = jnp.zeros_like(skip_gain)
    outputs = []
    input_grads = []
    for micro_idx in range(NMB):
        whole_in, whole_out = (
            lax.all_gather(in_weight, "seq", axis=1, tiled=True),
            lax.all_gather(out_weight, "seq", axis=1, tiled=True),
        )
        first_seq = micro_idx * SEQ_MB
        block_tokens = tokens[first_seq : first_seq + SEQ_MB]
        full_tokens = lax.all_gather(block_tokens, "mp", axis=2, tiled=True).astype(jnp.float32)
        inv_rms = lax.rsqrt(jnp.mean(full_tokens * full_tokens, axis=-1, keepdims=True) + EPSILON)
        normed = (full_tokens * inv_rms * norm_gain).astype(jnp.bfloat16)
        both_parts = jnp.einsum(
            "scd,kdi->ksci", normed, whole_in, preferred_element_type=jnp.float32
        )
        x_round = both_parts[0].astype(jnp.bfloat16)
        z_part = both_parts[1]
        rim_rows = from_behind(x_round[:, stretch - (num_taps - 1) :], "seq", 1)
        padded = jnp.concatenate([rim_rows, x_round], axis=1).astype(jnp.float32)
        conv_sum = conv_bias + jnp.zeros((SEQ_MB, stretch, channels), jnp.float32)
        for tap_index in range(num_taps):
            conv_sum = (
                conv_sum + conv_weight[tap_index] * padded[:, tap_index : tap_index + stretch]
            )
        inputs_round = jax.nn.silu(conv_sum).astype(jnp.bfloat16)
        inputs_f = inputs_round.astype(jnp.float32)
        low_part = jnp.einsum(
            "sci,ir->scr", inputs_round, low_weight, preferred_element_type=jnp.float32
        )
        state_part = jnp.einsum(
            "sci,ir->scr", inputs_round, state_weight, preferred_element_type=jnp.float32
        )
        delta_low, state_proj = lax.psum((low_part, state_part), "mp")
        delta_round = delta_low.astype(jnp.bfloat16)
        delta_raw = (
            jnp.einsum("scr,ri->sci", delta_round, delta_weight, preferred_element_type=jnp.float32)
            + delta_bias
        )
        b_state = state_proj[..., :nstate]
        c_state = state_proj[..., nstate:]
        delta_blocks = to_blocks(delta_raw, span_rows)
        b_blocks = to_blocks(b_state, span_rows)
        c_blocks = to_blocks(c_state, span_rows)
        in_blocks = to_blocks(inputs_f, span_rows)
        stretch_pair, (prod_blocks, local_blocks) = lax.scan(
            forward_block, (ones_state, zero_state), (delta_blocks, b_blocks, in_blocks)
        )
        carried = prefix(stretch_pair, "seq", combine, (ones_state, zero_state), False)
        states = from_blocks(local_blocks) + from_blocks(prod_blocks) * carried[1][:, None]
        before = jnp.concatenate([carried[1][:, None], states[:, :-1]], axis=1)
        read_rec = jnp.einsum("scni,scn->sci", states, c_state)
        read_out = read_rec + skip_gain * inputs_f
        z_gate = jax.nn.silu(z_part)
        gated_round = (read_out * z_gate).astype(jnp.bfloat16)
        out_part = jnp.einsum(
            "sci,id->scd", gated_round, whole_out, preferred_element_type=jnp.float32
        )
        branch = lax.psum_scatter(out_part, "mp", scatter_dimension=2, tiled=True)
        outputs.append((block_tokens.astype(jnp.float32) + branch).astype(jnp.bfloat16))
        d_out = (
            cotangent[first_seq : first_seq + SEQ_MB]
            * seq_weight[first_seq : first_seq + SEQ_MB][:, None, None]
        )
        d_branch = lax.all_gather(d_out.astype(jnp.bfloat16), "mp", axis=2, tiled=True)
        acc_out = acc_out + jnp.einsum(
            "sci,scd->id", gated_round, d_branch, preferred_element_type=jnp.float32
        )
        d_gated = jnp.einsum("scd,id->sci", d_branch, whole_out, preferred_element_type=jnp.float32)
        d_read = d_gated * z_gate
        d_zpart = d_gated * read_out * silu_slope(z_part)
        acc_skip = acc_skip + jnp.sum(d_read * inputs_f, axis=(0, 1))
        read_blocks_grad = to_blocks(d_read, span_rows)
        (last_grad, first_dec, _), (grad_blocks, tail_blocks) = lax.scan(
            backward_block,
            (zero_state, ones_state, ones_state),
            (delta_blocks, b_blocks, in_blocks, read_blocks_grad, c_blocks),
            reverse=True,
        )
        tail_grad = first_dec * last_grad
        crossing = prefix(
            (stretch_pair[0], tail_grad), "seq", combine, (ones_state, zero_state), True
        )
        state_grad = from_blocks(grad_blocks) + from_blocks(tail_blocks) * crossing[1][:, None]
        _, gate_pullback = jax.vjp(make_gates, delta_raw, b_state, inputs_f)
        d_delta, d_bstate, d_inputs_state = gate_pullback((state_grad * before, state_grad))
        d_cstate = jnp.einsum("scni,sci->scn", states, d_read)
        acc_dbias = acc_dbias + jnp.sum(d_delta, axis=(0, 1))
        d_delta_round = d_delta.astype(jnp.bfloat16)
        acc_delta = acc_delta + jnp.einsum(
            "scr,sci->ri", delta_round, d_delta_round, preferred_element_type=jnp.float32
        )
        low_grad_part = jnp.einsum(
            "sci,ri->scr", d_delta_round, delta_weight, preferred_element_type=jnp.float32
        )
        state_grad_part = jnp.concatenate([d_bstate, d_cstate], axis=-1)
        d_low, d_state = lax.psum((low_grad_part, state_grad_part), "mp")
        d_low_round = d_low.astype(jnp.bfloat16)
        d_state_round = d_state.astype(jnp.bfloat16)
        acc_low = acc_low + jnp.einsum(
            "sci,scr->ir", inputs_round, d_low_round, preferred_element_type=jnp.float32
        )
        acc_state = acc_state + jnp.einsum(
            "sci,scr->ir", inputs_round, d_state_round, preferred_element_type=jnp.float32
        )
        d_inputs = d_read * skip_gain + d_inputs_state
        d_inputs = d_inputs + jnp.einsum(
            "scr,ir->sci", d_low_round, low_weight, preferred_element_type=jnp.float32
        )
        d_inputs = d_inputs + jnp.einsum(
            "scr,ir->sci", d_state_round, state_weight, preferred_element_type=jnp.float32
        )
        d_conv = d_inputs * silu_slope(conv_sum)
        acc_cbias = acc_cbias + jnp.sum(d_conv, axis=(0, 1))
        tap_grads = []
        d_padded = jnp.zeros((SEQ_MB, stretch + num_taps - 1, channels), jnp.float32)
        for tap_index in range(num_taps):
            tap_grads.append(
                jnp.sum(d_conv * padded[:, tap_index : tap_index + stretch], axis=(0, 1))
            )
            d_padded = d_padded + jnp.pad(
                conv_weight[tap_index] * d_conv,
                ((0, 0), (tap_index, num_taps - 1 - tap_index), (0, 0)),
            )
        acc_conv = acc_conv + jnp.stack(tap_grads)
        back_rim = from_behind(d_padded[:, : num_taps - 1], "seq", -1)
        d_xpart = d_padded[:, num_taps - 1 :] + jnp.pad(
            back_rim, ((0, 0), (stretch - (num_taps - 1), 0), (0, 0))
        )
        d_parts_round = jnp.stack([d_xpart, d_zpart]).astype(jnp.bfloat16)
        acc_in = acc_in + jnp.einsum(
            "scd,ksci->kdi", normed, d_parts_round, preferred_element_type=jnp.float32
        )
        norm_part = jnp.einsum(
            "ksci,kdi->scd", d_parts_round, whole_in, preferred_element_type=jnp.float32
        )
        d_normed = lax.psum(norm_part, "mp")
        acc_gain = acc_gain + jnp.sum(d_normed * full_tokens * inv_rms, axis=(0, 1))
        scaled = d_normed * norm_gain
        d_full = inv_rms * scaled - full_tokens * (inv_rms * inv_rms * inv_rms) * jnp.mean(
            scaled * full_tokens, axis=-1, keepdims=True
        )
        d_mine = lax.dynamic_slice_in_dim(d_full, feature_start, feature_dev, 2)
        input_grads.append(d_out + d_mine)
    d_in_weight, d_out_weight = (
        lax.psum_scatter(acc_in, "seq", scatter_dimension=1, tiled=True),
        lax.psum_scatter(acc_out, "seq", scatter_dimension=1, tiled=True),
    )
    summed = lax.psum(
        (acc_gain, acc_conv, acc_cbias, acc_low, acc_state, acc_delta, acc_dbias, acc_skip), "seq"
    )
    return (
        jnp.concatenate(outputs, axis=0),
        jnp.concatenate(input_grads, axis=0),
        summed[0],
        d_in_weight,
        summed[1],
        summed[2],
        summed[3],
        summed[4],
        summed[5],
        summed[6],
        summed[7],
        d_out_weight,
    )


MESH = pl.DeviceIdType.MESH
F32 = jnp.float32
BF16 = jnp.bfloat16
LANE = 128
GRP = 16
PADV = 8
SGVEC = 16


def nn(a, b):
    return lax.dot_general(a, b, (((1,), (0,)), ((), ())), preferred_element_type=F32)


def nt(a, b):
    return lax.dot_general(a, b, (((1,), (1,)), ((), ())), preferred_element_type=F32)


def tn(a, b):
    return lax.dot_general(a, b, (((0,), (0,)), ((), ())), preferred_element_type=F32)


def cut(start, size):
    return pl.ds(pl.multiple_of(start, size), size)


def each(count, step):
    lax.fori_loop(0, count, lambda index, unused: (step(index), unused)[1], 0)


def by_rows(count, step):
    size = 32 if count % 32 == 0 else 16
    each(count // size, lambda index: step(cut(index * size, size)))


def wide(value, times):
    return jnp.concatenate([value] * times, axis=1) if times > 1 else value


def groups_fit(channels):
    return (LANE // GRP) % min(LANE // GRP, channels // (GRP * GRP)) == 0


class Sizes:
    def __init__(self, mesh_shape, nseq, stretch, feature_dev, model, channels, nstate, rank):
        self.S, self.M = mesh_shape["seq"], mesh_shape["mp"]
        self.Q, self.T, self.Df, self.D, self.C = nseq, stretch, feature_dev, model, channels
        self.N, self.RK = nstate, rank
        self.R = nseq * stretch
        self.Ds = model // self.S
        self.B = max(1, feature_dev // self.Ds)
        self.levels = self.S.bit_length() - 1
        self.dims = [1 << bit for bit in range(1, self.levels)]
        self.masks = [2 * value for value in range(self.S // 2)]
        self.rows_sg = -(-(2 * rank + 2 * nstate + SGVEC) // (self.S * 16)) * 16
        self.E = max(self.R, self.Ds)

    def order(self, half):
        turn = half * (len(self.dims) // 2)
        return self.dims[turn:] + self.dims[:turn]

    def fits(self, taps):
        return (
            self.S in (4, 8)
            and self.M > 1
            and self.Q == 2
            and self.T == LANE
            and self.Ds == 256
            and self.Df % self.Ds == 0
            and self.C % 512 == 0
            and self.N == GRP
            and self.RK == LANE
            and taps == 4
            and self.D >= 2 * self.C
            and groups_fit(self.C)
            and self.C * self.D <= (1 << 21)
        )


class Bunch:
    def __init__(self, names, values):
        self.__dict__.update(zip(names, values))


class Rows:
    def __init__(self, ref, base, rows, count):
        self.ref, self.base, self.rows, self.end = ref, base, rows, base + rows * count

    def block(self, index, start=0, size=None):
        first = pl.multiple_of(self.base + index * self.rows + start, 16)
        return self.ref.at[pl.ds(first, self.rows if size is None else size), :]


class Links:
    def __init__(self, sems, seq, mp):
        self.sems, self.used, self.seq, self.mp = sems, 0, seq, mp

    def sem(self, count=1):
        first = self.used
        self.used += count
        return first

    def copy(self, src, dst, send, recv, seq=None, mp=None):
        target = (self.seq if seq is None else seq, self.mp if mp is None else mp)
        return pltpu.make_async_remote_copy(
            src_ref=src,
            dst_ref=dst,
            send_sem=self.sems.at[send],
            recv_sem=self.sems.at[recv],
            device_id=target,
            device_id_type=MESH,
        )

    def arrived(self, dst, recv):
        self.copy(dst, dst, recv, recv).wait_recv()


class TreeGather:
    def __init__(self, z, links, half_view, whole_view):
        self.z, self.links, self.half, self.whole = z, links, half_view, whole_view
        self.recv = {(mask, h): links.sem() for mask in z.masks[1:] for h in range(2)}
        self.near = {mask: links.sem() for mask in z.masks}
        self.sent = []

    def push(self, mask, h, dim):
        view = self.half(self.links.seq ^ mask, h)
        copy = self.links.copy(
            view, view, self.links.sem(), self.recv[mask | dim, h], seq=self.links.seq ^ dim
        )
        copy.start()
        self.sent.append(copy)

    def take(self, mask, h):
        self.links.arrived(self.half(self.links.seq ^ mask, h), self.recv[mask, h])

    def hand(self, mask):
        view = self.whole(self.links.seq ^ mask)
        copy = self.links.copy(view, view, self.links.sem(), self.near[mask], seq=self.links.seq ^ 1)
        copy.start()
        self.sent.append(copy)

    def first(self):
        for h in range(2):
            self.push(0, h, self.z.order(h)[0])

    def second(self):
        for h in range(2):
            for dim in self.z.order(h)[1:]:
                self.push(0, h, dim)
        self.hand(0)

    def forward(self):
        for h in range(2):
            order = self.z.order(h)
            if len(order) > 1:
                self.take(order[0], h)
                self.push(order[0], h, order[1])

    def settle(self):
        for mask in sorted(self.z.masks[1:], key=lambda mask: bin(mask).count("1")):
            for h in range(2):
                order = self.z.order(h)
                if len(order) == 1 or mask != order[0]:
                    self.take(mask, h)
            self.hand(mask)

    def finish(self):
        for mask in self.z.masks:
            self.links.arrived(self.whole(self.links.seq ^ 1 ^ mask), self.near[mask])

    def drain(self):
        for copy in self.sent:
            copy.wait_send()


class LineGather:
    def __init__(self, z, links, view):
        self.z, self.links, self.view = z, links, view
        self.recv = links.sem(z.M)
        self.send = links.sem(2 * z.M)

    def parts(self, depth):
        for side, way in enumerate((1, -1)):
            owner, target = self.links.mp - way * depth, self.links.mp + way
            held = (owner >= 0) & (owner < self.z.M)
            more = held & (target >= 0) & (target < self.z.M)
            yield side, owner, target, held, more

    def copy(self, side, depth, owner, target):
        view = self.view(owner)
        return self.links.copy(view, view, self.send + 2 * depth + side, self.recv + owner, mp=target)

    def step(self, depth):
        for side, owner, target, held, more in self.parts(depth):
            if depth:

                @pl.when(held)
                def _():
                    self.links.arrived(self.view(owner), self.recv + owner)

            @pl.when(more)
            def _():
                self.copy(side, depth, owner, target).start()

    def drain(self):
        for depth in range(self.z.M):
            for side, owner, target, held, more in self.parts(depth):

                @pl.when(more)
                def _():
                    self.copy(side, depth, owner, target).wait_send()


class Swap:
    def __init__(self, z, links, slot):
        self.z, self.links, self.slot = z, links, slot
        self.recv = links.sem(z.M)
        self.send = links.sem(z.M)

    def one(self, src, away):
        target = lax.rem(self.links.mp + away, self.z.M)
        return self.links.copy(src, self.slot(away - 1), self.send + away, self.recv + away, mp=target)

    def start(self, src):
        for away in range(1, self.z.M):
            self.one(src, away).start()

    def wait(self):
        for away in range(1, self.z.M):
            self.links.arrived(self.slot(away - 1), self.recv + away)

    def drain(self, src):
        for away in range(1, self.z.M):
            self.one(src, away).wait_send()


class SwapSeq:
    def __init__(self, z, links, slot):
        self.links, self.slot = links, slot
        self.pairs = [(other, links.sem(), links.sem()) for other in range(1, z.S)]
        self.sent = []

    def start(self, src):
        for other, send, recv in self.pairs:
            copy = self.links.copy(src, self.slot(other - 1), send, recv, seq=self.links.seq ^ other)
            copy.start()
            self.sent.append(copy)

    def wait(self):
        for other, send, recv in self.pairs:
            self.links.arrived(self.slot(other - 1), recv)

    def drain(self):
        for copy in self.sent:
            copy.wait_send()


def halves(rows):
    first = -(-rows // 32) * 16
    return (0, first), (first, rows - first)


class Scatter:
    def __init__(self, z, links, out, sums, far, rows):
        self.z, self.links, self.out, self.sums, self.far, self.rows = z, links, out, sums, far, rows
        self.near = {mask: links.sem() for mask in z.masks}
        self.near_send = {mask: links.sem() for mask in z.masks}
        self.sent = []
        self.hops = {}
        place = 0
        for h in range(2):
            order = z.order(h)
            for step, dim in enumerate(order):
                for mask in z.masks:
                    if mask & dim and not any(mask & other for other in order[:step]):
                        self.hops[h, step, mask] = (dim, links.sem(), links.sem(), place)
                        place += 1
        self.slots = place

    def half(self, mask, h):
        start, size = halves(self.rows)[h]
        return self.sums.block(mask // 2, start, size)

    def came(self, h, place):
        return self.far.block(place, 0, halves(self.rows)[h][1])

    def first(self, make):
        z, links = self.z, self.links
        for mask in z.masks:
            src = make(links.seq ^ 1 ^ mask, mask)
            copy = links.copy(src, self.sums.block(mask // 2), self.near_send[mask], self.near[mask], seq=links.seq ^ 1)
            copy.start()
            self.sent.append(copy)

    def second(self, add):
        z, links = self.z, self.links
        by_need = sorted(z.masks, key=lambda mask: -bin(mask).count("1"))
        for mask in by_need:
            links.arrived(self.sums.block(mask // 2), self.near[mask])
            add(links.seq ^ mask, mask)

    def send(self, step, part=None):
        links = self.links
        count = {0: 0, 1: 0}
        for (h, at, mask), (dim, send, recv, place) in self.hops.items():
            if at == step:
                count[h] += 1
                if part is None or (count[h] > 1) == (part == 1):
                    copy = links.copy(
                        self.half(mask, h), self.came(h, place), send, recv, seq=links.seq ^ dim
                    )
                    copy.start()
                    self.sent.append(copy)

    def fold(self, step):
        links = self.links
        for (h, at, mask), (dim, send, recv, place) in self.hops.items():
            if at != step:
                continue
            links.arrived(self.came(h, place), recv)
            if step < len(self.z.dims) - 1:
                half, came = self.half(mask ^ dim, h), self.came(h, place)

                def add(rows):
                    half[rows, :] = (half[rows, :].astype(F32) + came[rows, :].astype(F32)).astype(BF16)

                by_rows(halves(self.rows)[h][1], add)
        if step < len(self.z.dims) - 1:
            self.send(step + 1)

    def total(self, write):
        last = len(self.z.dims) - 1
        for (h, at, mask), (dim, send, recv, place) in self.hops.items():
            if at == last:
                half, came = self.half(0, h), self.came(h, place)
                first, count = halves(self.rows)[h]

                def add(rows):
                    value = half[rows, :].astype(F32) + came[rows, :].astype(F32)
                    write(pl.ds(pl.multiple_of(first + rows.start, 16), rows.size), value)

                by_rows(count, add)

    def drain(self):
        for copy in self.sent:
            copy.wait_send()


def slots_of(z):
    return Scatter(z, Links(None, 0, 0), None, None, None, 0).slots


def scratch_of(z):
    V = pltpu.VMEM
    half = z.S // 2
    slots = slots_of(z)
    return dict(
        tokg=V((z.S, z.R, z.Ds), BF16),
        halg=V((z.S, 16, z.Ds), BF16),
        hals=V((z.B, 16, z.Ds), BF16),
        db=V((z.R, z.D), BF16),
        inv=V((z.R, LANE), F32),
        normed=V((z.R + 16, z.D), BF16),
        normt=V((z.D, z.R), BF16),
        wx=V((2, z.D, z.C), BF16),
        wo=V((z.C, z.D), BF16),
        xpad=V((z.Q, 8 + z.T, z.C), F32),
        dcp=V((z.Q, z.T + 8, z.C), F32),
        conv=V((z.E, z.C), F32),
        s=V((z.E, z.C), F32),
        su=V((z.R, z.C), F32),
        fac=V((z.E, z.C), F32),
        zp=V((z.R, z.C), F32),
        rd=V((z.R, z.C), F32),
        dr=V((z.R, z.C), F32),
        u=V((z.R, z.C), BF16),
        gat=V((z.R, z.C), BF16),
        gatt=V((z.C, z.R), BF16),
        ddr=V((z.R, z.C), BF16),
        dzr=V((z.R, z.C), BF16),
        dxr=V((z.R, z.C), BF16),
        lowp=V((z.Q, z.M, z.T, z.RK), BF16),
        stp=V((z.Q, z.M, 2 * z.N, z.T), F32),
        low=V((z.R, z.RK), BF16),
        dlow=V((z.R, z.RK), BF16),
        dlowt=V((z.RK, z.R), BF16),
        dst=V((2 * z.N, z.R), BF16),
        st=V((2 * z.N, z.R), F32),
        blkb=V((z.R, GRP * z.N), BF16),
        blkk=V((z.R, GRP * z.N), BF16),
        blkc=V((z.R, GRP * z.N), BF16),
        bc=V((z.Q, z.T, 2 * z.N, LANE), F32),
        hist=V((z.Q * (z.T + 1) * z.N, z.C), BF16),
        ptot=V((z.Q, z.N, z.C), F32),
        stot=V((z.Q, z.N, z.C), F32),
        ppre=V((z.Q, z.N, z.C), F32),
        spre=V((z.Q, z.N, z.C), F32),
        csend=V((z.levels, z.Q, 2, z.N, z.C), BF16),
        crecv=V((z.levels, z.Q, 2, z.N, z.C), BF16),
        bsend=V((z.levels, z.Q, z.N, z.C), BF16),
        brecv=V((z.levels, z.Q, z.N, z.C), BF16),
        est=V((3, z.N, z.R), F32),
        dlowp=V((z.Q, z.M, z.T, z.RK), BF16),
        dstp=V((z.Q, z.M, 2 * z.N, z.T), BF16),
        orecv=V((z.M - 1, z.R, z.Df), BF16),
        nrecv=V((z.M - 1, z.R, z.Df), BF16),
        near_o=V((half * z.C, z.Ds), BF16),
        sum_o=V((half * z.C, z.Ds), BF16),
        far_o=V((slots * (z.C // 2), z.Ds), BF16),
        near_i=V((half * z.Ds, z.C), BF16),
        sum_1=V((half * z.Ds, z.C), BF16),
        far_1=V((slots * (z.Ds // 2), z.C), BF16),
        vec=V((SGVEC, z.C), F32),
        gv=V((z.D // LANE, LANE), F32),
        gvs=V((z.D // LANE, LANE), F32),
        gvr=V((z.S - 1, z.D // LANE, LANE), F32),
        gvm=V((z.M - 1, z.D // LANE, LANE), F32),
        mean=V((z.R, LANE), F32),
        mrow=V((z.M, 8, z.R), F32),
        sems=pltpu.SemaphoreType.DMA((420,)),
        local=pltpu.SemaphoreType.DMA((8,)),
        ready=pltpu.SemaphoreType.REGULAR((z.levels,)),
    )


def silu_parts(value):
    gate = 1.0 / (1.0 + jnp.exp(-value))
    return gate, value * gate


def fused_kernel(z, names, *refs):
    r = Bunch(names, refs)
    seq, mp = lax.axis_index("seq"), lax.axis_index("mp")
    links = Links(r.sems, seq, mp)
    lanes_all = z.C // LANE
    first_block = mp * z.B

    def lane_loop(step):
        each(z.C // LANE, lambda index: step(cut(index * LANE, LANE)))

    local = r.local
    mine_in = lambda k: r.wx.at[k, cut(seq * z.Ds, z.Ds), :]
    loads = [
        pltpu.make_async_copy(r.win.at[0], mine_in(0), local.at[0]),
        pltpu.make_async_copy(r.win.at[1], mine_in(1), local.at[1]),
        pltpu.make_async_copy(r.wout, r.wo.at[:, cut(seq * z.Ds, z.Ds)], local.at[2]),
    ]
    for load in loads:
        load.start()
    for b in range(z.B):
        r.tokg[first_block + b] = r.tok[:, b * z.Ds : (b + 1) * z.Ds]
        tails = [
            r.tok[q * z.T + z.T - 16 : q * z.T + z.T, b * z.Ds : (b + 1) * z.Ds].astype(F32)[8:]
            for q in range(z.Q)
        ]
        r.hals[b] = jnp.concatenate(tails, axis=0).astype(BF16)

    barrier = pltpu.get_barrier_semaphore()
    ahead, behind = lax.rem(seq + 1, z.S), lax.rem(seq + z.S - 1, z.S)
    partners = [(seq ^ other, mp) for other in range(1, z.S)] + [(ahead, mp), (behind, mp)]
    partners += [(seq, lax.rem(mp + away, z.M)) for away in range(1, z.M)]
    for partner in partners:
        pl.semaphore_signal(barrier, inc=1, device_id=partner, device_id_type=MESH)
    pl.semaphore_wait(barrier, len(partners))

    def of_in(k):
        def half(owner, h):
            return r.wx.at[k, cut(owner * z.Ds + h * (z.Ds // 2), z.Ds // 2), :]

        return TreeGather(z, links, half, lambda owner: r.wx.at[k, cut(owner * z.Ds, z.Ds), :])

    tree_x, tree_z = of_in(0), of_in(1)
    tree_o = TreeGather(
        z,
        links,
        lambda owner, h: r.wo.at[pl.ds(h * (z.C // 2), z.C // 2), cut(owner * z.Ds, z.Ds)],
        lambda owner: r.wo.at[:, cut(owner * z.Ds, z.Ds)],
    )
    line_t = LineGather(z, links, lambda owner: r.tokg.at[pl.ds(owner * z.B, z.B)])
    line_h = LineGather(z, links, lambda owner: r.halg.at[pl.ds(owner * z.B, z.B)])
    line_d = LineGather(z, links, lambda owner: r.db.at[:, cut(owner * z.Df, z.Df)])
    depth = len(z.dims)

    hal_send, hal_recv = links.sem(), links.sem()
    hal_mine = r.halg.at[pl.ds(first_block, z.B)]
    hal = links.copy(r.hals, hal_mine, hal_send, hal_recv, seq=ahead)
    hal.start()
    line_t.step(0)
    loads[0].wait()
    tree_x.first()
    tree_x.second()

    def weight_of(q):
        total = jnp.float32(0.0)
        for group in range(r.groupw.shape[0]):
            total = total + jnp.where(r.seqg[q] == group, r.groupw[group], 0.0)
        return total

    seq_weight = [weight_of(q) for q in range(z.Q)]
    for q in range(z.Q):
        rows = pl.ds(q * z.T, z.T)
        for b in range(z.B):
            part = r.cot[rows, b * z.Ds : (b + 1) * z.Ds] * seq_weight[q]
            r.db[rows, cut((first_block + b) * z.Ds, z.Ds)] = part.astype(BF16)

    links.arrived(hal_mine, hal_recv)
    line_h.step(0)
    line_t.step(1)
    tree_x.forward()
    loads[1].wait()
    tree_z.first()
    tree_z.second()
    line_h.step(1)
    for far in range(2, z.M):
        line_t.step(far)
        line_h.step(far)

    def add_squares(j, total):
        part = r.tokg[j].astype(F32)
        edge = r.halg[j].astype(F32)
        return (
            total[0] + jnp.sum(part * part, axis=1, keepdims=True),
            total[1] + jnp.sum(edge * edge, axis=1, keepdims=True),
        )

    squares = lax.fori_loop(
        0, z.S, add_squares, (jnp.zeros((z.R, 1), F32), jnp.zeros((16, 1), F32))
    )
    inv = lax.rsqrt(squares[0] * (1.0 / z.D) + EPSILON)
    inv_edge = lax.rsqrt(squares[1] * (1.0 / z.D) + EPSILON)
    r.inv[...] = jnp.broadcast_to(inv, (z.R, LANE))

    def norm_block(j):
        features = cut(j * z.Ds, z.Ds)
        gain = r.gain[:, features]
        normed = r.tokg[j].astype(F32) * wide(r.inv[...], z.Ds // LANE) * gain
        r.normed[: z.R, features] = normed.astype(BF16)
        edge = r.halg[j].astype(F32) * inv_edge * gain
        r.normed[z.R :, features] = edge.astype(BF16)
        r.normt[features, :] = normed.T.astype(BF16)

    each(z.S, norm_block)
    tree_x.settle()
    tree_x.finish()

    def x_chunk(index):
        lanes = cut(index * 256, 256)
        part = nn(r.normed[...], r.wx[0, :, lanes]).astype(BF16).astype(F32)
        for q in range(z.Q):
            edge = part[z.R + 8 * q : z.R + 8 * q + 8]
            r.xpad[q, 0:8, lanes] = jnp.where(seq > 0, edge, 0.0)
            r.xpad[q, 8 : 8 + z.T, lanes] = part[q * z.T : (q + 1) * z.T]

    each(z.C // 256, x_chunk)

    def rows_of(q):
        return pl.ds(q * z.T, z.T)

    def conv(q):
        def conv_lanes(lanes):
            total = jnp.broadcast_to(r.convb[:, lanes], (z.T, LANE))
            for tap in range(4):
                total = total + r.convw[tap : tap + 1, lanes] * r.xpad[q, 5 + tap : 5 + tap + z.T, lanes]
            r.conv[rows_of(q), lanes] = total
            r.u[rows_of(q), lanes] = silu_parts(total)[1].astype(BF16)

        lane_loop(conv_lanes)

    swap_low = [Swap(z, links, lambda slot, q=q: r.lowp.at[q, slot]) for q in range(z.Q)]
    swap_st = [Swap(z, links, lambda slot, q=q: r.stp.at[q, slot]) for q in range(z.Q)]
    low_mine = [r.lowp.at[q, z.M - 1] for q in range(z.Q)]
    st_mine = [r.stp.at[q, z.M - 1] for q in range(z.Q)]

    def project(q):
        u = r.u[rows_of(q), :]
        st_mine[q][...] = nt(r.statewt[...], u)
        swap_st[q].start(st_mine[q])
        low_mine[q][...] = nn(u, r.loww[...]).astype(BF16)
        swap_low[q].start(low_mine[q])

    rows_i = lax.broadcasted_iota(jnp.int32, (z.T, GRP * z.N), 0)
    cols_i = lax.broadcasted_iota(jnp.int32, (z.T, GRP * z.N), 1)
    diagonal = lax.rem(rows_i, GRP) == cols_i // z.N
    rep_n = lax.broadcasted_iota(jnp.int32, (2 * z.N, GRP * z.N), 0)
    rep_j = lax.rem(lax.broadcasted_iota(jnp.int32, (2 * z.N, GRP * z.N), 1), z.N)
    rep_b = (rep_n == rep_j).astype(BF16)
    rep_c = (rep_n == rep_j + z.N).astype(BF16)
    only_b = lax.broadcasted_iota(jnp.int32, (z.T, LANE), 1) < z.N

    def columns_of(value):
        return jnp.concatenate([value, jnp.zeros((LANE - 2 * z.N, z.T), F32)], axis=0).T

    def keys(q):
        swap_st[q].wait()
        st = r.stp[q, 0]
        for slot in range(1, z.M):
            st = st + r.stp[q, slot]
        r.st[:, rows_of(q)] = st

        def spread(index):
            turned = pltpu.roll(st, lax.rem(z.T - index * 32, z.T), 1)
            for j in range(32):
                r.bc[q, index * 32 + j] = jnp.broadcast_to(turned[:, j : j + 1], (2 * z.N, LANE))

        each(z.T // 32, spread)
        nat = columns_of(st)
        key_sq = jnp.sum(jnp.where(only_b, nat * nat, 0.0), axis=1, keepdims=True)
        swap_low[q].wait()
        low = r.lowp[q, 0].astype(F32)
        for slot in range(1, z.M):
            low = low + r.lowp[q, slot].astype(F32)
        low = low.astype(BF16)
        r.low[rows_of(q), :] = low

        def step_chunk(index):
            lanes = cut(index * 256, 256)
            raw = nn(low, r.deltaw[:, lanes]) + r.dbias[:, lanes]
            beta = 1.0 / (1.0 + jnp.exp(-raw))
            scale = 1.0 / (1.0 + beta * key_sq)
            step = beta * scale
            r.s[rows_of(q), lanes] = step
            r.su[rows_of(q), lanes] = step * r.u[rows_of(q), lanes].astype(F32)
            r.fac[rows_of(q), lanes] = scale * step * (1.0 - beta)

        each(z.C // 256, step_chunk)

    def key_blocks(q):
        nat16 = columns_of(r.st[:, rows_of(q)])[:, : 2 * z.N].astype(BF16)
        spread_b = jnp.where(diagonal, nn(nat16, rep_b), 0.0)
        r.blkb[rows_of(q), :] = spread_b.astype(BF16)
        r.blkk[rows_of(q), :] = (spread_b * spread_b).astype(BF16)
        r.blkc[rows_of(q), :] = jnp.where(diagonal, nn(nat16, rep_c), 0.0).astype(BF16)

    span = 512 if z.C % 512 == 0 else 256

    def token(q, t):
        return pl.ds(q * z.T + t, 1)

    def totals(q):
        def lane_part(index):
            lanes = cut(index * span, span)

            def tokens8(i, carry):
                product, state = carry
                for j in range(8):
                    row = token(q, i * 8 + j)
                    step, drive = r.s[row, lanes], r.su[row, lanes]
                    key = r.bc[q, i * 8 + j, : z.N, :]
                    decay = 1.0 - step * wide(key * key, span // LANE)
                    product = product * decay
                    state = decay * state + drive * wide(key, span // LANE)
                return product, state

            start = (jnp.ones((z.N, span), F32), jnp.zeros((z.N, span), F32))
            product, state = lax.fori_loop(0, z.T // 8, tokens8, start)
            r.ptot[q, :, lanes] = product
            r.stot[q, :, lanes] = state

        each(z.C // span, lane_part)

    carry_sems = [[(links.sem(), links.sem()) for q in range(z.Q)] for level in range(z.levels)]
    back_sems = [[(links.sem(), links.sem()) for q in range(z.Q)] for level in range(z.levels)]
    carry_copies = []

    def upper_at(level):
        return lax.rem(seq // (1 << level), 2) == 1

    def carry_send(level, q):
        r.csend[level, q, 0] = r.ptot[q].astype(BF16)
        r.csend[level, q, 1] = r.stot[q].astype(BF16)
        copy = links.copy(
            r.csend.at[level, q], r.crecv.at[level, q], *carry_sems[level][q], seq=seq ^ (1 << level)
        )
        copy.start()
        carry_copies.append(copy)

    def carry_take(level, q):
        links.arrived(r.crecv.at[level, q], carry_sems[level][q][1])
        upper = upper_at(level)
        other_p, other_s = r.crecv[level, q, 0].astype(F32), r.crecv[level, q, 1].astype(F32)
        mine_p, mine_s = r.ptot[q], r.stot[q]
        if level == 0:
            r.spre[q] = jnp.where(upper, other_s, 0.0)
            r.ppre[q] = jnp.where(upper, other_p, 1.0)
        else:
            pre_p, pre_s = r.ppre[q], r.spre[q]
            r.spre[q] = jnp.where(upper, pre_p * other_s + pre_s, pre_s)
            r.ppre[q] = jnp.where(upper, pre_p * other_p, pre_p)
        if level < z.levels - 1:
            r.stot[q] = jnp.where(upper, mine_p * other_s + mine_s, other_p * mine_s + other_s)
            r.ptot[q] = mine_p * other_p

    def back_send(level, q):
        r.bsend[level, q] = r.stot[q].astype(BF16)
        copy = links.copy(
            r.bsend.at[level, q], r.brecv.at[level, q], *back_sems[level][q], seq=seq ^ (1 << level)
        )
        copy.start()
        carry_copies.append(copy)

    def back_take(level, q):
        links.arrived(r.brecv.at[level, q], back_sems[level][q][1])
        upper = upper_at(level)
        other = r.brecv[level, q].astype(F32)
        other_p, mine_p = r.crecv[level, q, 0].astype(F32), r.csend[level, q, 0].astype(F32)
        mine = r.stot[q]
        if level == 0:
            r.spre[q] = jnp.where(upper, 0.0, other)
            r.ppre[q] = jnp.where(upper, 1.0, other_p)
        else:
            pre_p, pre = r.ppre[q], r.spre[q]
            r.spre[q] = jnp.where(upper, pre, pre + pre_p * other)
            r.ppre[q] = jnp.where(upper, pre_p, pre_p * other_p)
        if level < z.levels - 1:
            r.stot[q] = jnp.where(upper, other + other_p * mine, mine + mine_p * other)

    def past_rows(q, slot, count=1):
        return pl.ds(pl.multiple_of((q * (z.T + 1) + slot) * z.N, z.N), count * z.N)

    groups = z.T // GRP

    def walk(q):
        r.hist[past_rows(q, 0), :] = r.spre[q].astype(BF16)

        def lane_part(index):
            lanes = cut(index * span, span)

            def tokens8(i, state):
                for j in range(8):
                    row = token(q, i * 8 + j)
                    step, drive = r.s[row, lanes], r.su[row, lanes]
                    key = r.bc[q, i * 8 + j, : z.N, :]
                    decay = 1.0 - step * wide(key * key, span // LANE)
                    state = decay * state + drive * wide(key, span // LANE)
                    r.hist[past_rows(q, i * 8 + j + 1), lanes] = state.astype(BF16)
                return state

            lax.fori_loop(0, z.T // 8, tokens8, r.spre[q, :, lanes])

        each(z.C // span, lane_part)
        reads = []
        for i in range(groups):
            rows = pl.ds(q * z.T + i * GRP, GRP)
            reads.append((rows, nn(r.blkc[rows, :], r.hist[past_rows(q, i * GRP + 1, GRP), :])))
        for rows, value in reads:
            r.rd[rows, :] = value

    def z_chunk(index):
        lanes = cut(index * 256, 256)
        r.zp[:, lanes] = nn(r.normed[: z.R, :], r.wx[1, :, lanes])

    conv(0)
    project(0)
    conv(1)
    project(1)
    line_d.step(0)
    tree_z.forward()
    loads[2].wait()
    tree_o.first()
    keys(0)
    totals(0)
    carry_send(0, 0)
    line_d.step(1)
    keys(1)
    carry_take(0, 0)
    carry_send(1, 0)
    totals(1)
    carry_send(0, 1)
    for level in range(1, z.levels):
        carry_take(level, 0)
        if level < z.levels - 1:
            carry_send(level + 1, 0)
        carry_take(level - 1, 1)
        carry_send(level, 1)
        if level == 1:
            tree_o.second()
            line_d.step(2)
            tree_z.settle()
            key_blocks(0)
            key_blocks(1)
            tree_z.finish()
            each(z.C // 256, z_chunk)
    tree_o.forward()
    walk(0)
    carry_take(z.levels - 1, 1)
    for far in range(3, z.M):
        line_d.step(far)
    walk(1)
    tree_o.settle()
    tree_o.finish()

    def gated_grad(index):
        lanes = cut(index * 256, 256)
        r.dr[:, lanes] = nt(r.db[...], r.wo[lanes, :])

    each(z.C // 256, gated_grad)
    r.vec[...] = jnp.zeros_like(r.vec)

    def gate_lanes(lanes):
        for q in range(z.Q):
            rows = rows_of(q)
            u = r.u[rows, lanes].astype(F32)
            out = r.rd[rows, lanes] + r.skip[:, lanes] * u
            part, grad = r.zp[rows, lanes], r.dr[rows, lanes]
            gate, silu = silu_parts(part)
            gated = out * silu
            r.gat[rows, lanes] = gated.astype(BF16)
            r.gatt[lanes, rows] = gated.T.astype(BF16)
            d_read = grad * silu
            r.dr[rows, lanes] = d_read
            r.dzr[rows, lanes] = (grad * out * gate * (1.0 + part * (1.0 - gate))).astype(BF16)
            r.vec[6:7, lanes] += jnp.sum(d_read * u, axis=0, keepdims=True)

    lane_loop(gate_lanes)

    swap_out = Swap(z, links, lambda slot: r.orecv.at[slot])

    def partial_of(owner):
        return r.normed.at[pl.ds(0, z.R), cut(owner * z.Df, z.Df)]

    def branch_to(index):
        away = index + 1
        owner = lax.rem(mp + away, z.M)
        for b in range(z.B):
            j = owner * z.B + b
            r.normed[: z.R, cut(j * z.Ds, z.Ds)] = nn(r.gat[...], r.wo[:, cut(j * z.Ds, z.Ds)]).astype(BF16)

        @pl.when(away < z.M)
        def _():
            swap_out.one(partial_of(owner), away).start()

    def into(near, term):
        def make(device, mask):
            block = near.block(mask // 2)
            block[...] = term(device).astype(BF16)
            return block

        return make

    def onto(sums, term):
        def add(device, mask):
            block = sums.block(mask // 2)
            block[...] = (term(device) + block[...].astype(F32)).astype(BF16)

        return add

    half_s, slots = z.S // 2, slots_of(z)
    sg_rows = z.rows_sg
    near_o, near_i = Rows(r.near_o, 0, z.C, half_s), Rows(r.near_i, 0, z.Ds, half_s)
    sum_o, far_o = Rows(r.sum_o, 0, z.C, half_s), Rows(r.far_o, 0, z.C // 2, slots)
    sum_1, far_1 = Rows(r.sum_1, 0, z.Ds, half_s), Rows(r.far_1, 0, z.Ds // 2, slots)
    sum_0 = Rows(r.hist, 0, z.Ds, half_s)
    far_0 = Rows(r.hist, sum_0.end, z.Ds // 2, slots)
    sum_s = Rows(r.hist, far_0.end, sg_rows, half_s)
    far_s = Rows(r.hist, sum_s.end, halves(sg_rows)[0][1], slots)
    sgp = Rows(r.hist, far_s.end, sg_rows, z.S)
    small = Rows(r.hist, sgp.end, sg_rows, z.S)
    scatter_o = Scatter(z, links, None, sum_o, far_o, z.C)
    scatter_1 = Scatter(z, links, None, sum_1, far_1, z.Ds)
    scatter_0 = Scatter(z, links, None, sum_0, far_0, z.Ds)
    scatter_s = Scatter(z, links, None, sum_s, far_s, sg_rows)
    term_o = lambda device: nn(r.gatt[...], r.db[:, cut(device * z.Ds, z.Ds)])
    term_1 = lambda device: nn(r.normt[cut(device * z.Ds, z.Ds), :], r.dzr[...])
    term_0 = lambda device: nn(r.normt[cut(device * z.Ds, z.Ds), :], r.dxr[...])

    def totals_back(q):
        def lane_part(index):
            lanes = cut(index * span, span)

            def tokens8(i, tail):
                for j in reversed(range(8)):
                    t = z.T - 8 - i * 8 + j
                    row = token(q, t)
                    step, grad = r.s[row, lanes], r.dr[row, lanes]
                    key, query = r.bc[q, t, : z.N, :], r.bc[q, t, z.N :, :]
                    decay = 1.0 - step * wide(key * key, span // LANE)
                    tail = decay * (grad * wide(query, span // LANE) + tail)
                return tail

            r.stot[q, :, lanes] = lax.fori_loop(0, z.T // 8, tokens8, jnp.zeros((z.N, span), F32))

        each(z.C // span, lane_part)

    lane_index = lax.broadcasted_iota(jnp.int32, (z.N, LANE), 1)

    def lane_sum(value):
        total = value[:, :LANE]
        for part in range(1, lanes_all):
            total = total + value[:, part * LANE : (part + 1) * LANE]
        return jnp.sum(total, axis=1, keepdims=True)

    batch = min(groups, z.C // (GRP * z.N))

    def walk_back(q):
        def group(index, carry):
            tail, sum_gh, sum_g, sum_h = carry
            i = groups - 1 - index
            for j in reversed(range(GRP)):
                t = i * GRP + j
                row = token(q, t)
                step, drive, grad = r.s[row, :], r.su[row, :], r.dr[row, :]
                key, query = r.bc[q, t, : z.N, :], r.bc[q, t, z.N :, :]
                before = r.hist[past_rows(q, t), :].astype(F32)
                now = r.hist[past_rows(q, t + 1), :].astype(F32)
                state_grad = grad * wide(query, lanes_all) + tail
                crossed = state_grad * before
                place = pl.ds(pl.multiple_of(lax.rem(i, batch) * GRP * z.N + j * z.N, z.N), z.N)
                r.wo[place, : z.C] = state_grad.astype(BF16)
                r.wo[place, z.C : 2 * z.C] = crossed.astype(BF16)
                here = lane_index == t
                sum_gh = jnp.where(here, lane_sum(step * crossed), sum_gh)
                sum_g = jnp.where(here, lane_sum(drive * state_grad), sum_g)
                sum_h = jnp.where(here, lane_sum(grad * now), sum_h)
                tail = (1.0 - step * wide(key * key, lanes_all)) * state_grad
            return tail, sum_gh, sum_g, sum_h

        zero = jnp.zeros((z.N, LANE), F32)
        carry = (r.spre[q], zero, zero, zero)
        for start in range(0, groups, batch):
            carry = lax.fori_loop(start, start + batch, group, carry)
            sums = []
            for slot in range(batch):
                rows = pl.ds(q * z.T + (groups - start - batch + slot) * GRP, GRP)
                place = pl.ds(slot * GRP * z.N, GRP * z.N)
                sums.append(
                    (
                        rows,
                        nn(r.blkb[rows, :], r.wo[place, : z.C]),
                        nn(r.blkk[rows, :], r.wo[place, z.C : 2 * z.C]),
                    )
                )
            for rows, by_key, by_square in sums:
                r.rd[rows, :] = by_key
                r.zp[rows, :] = by_square
        columns = rows_of(q)
        for part in range(3):
            r.est[part, :, columns] = carry[1 + part]

    def step_back(q):
        rows = rows_of(q)

        def step_lanes(lanes):
            sum_b, step = r.rd[rows, lanes], r.s[rows, lanes]
            d_step = r.u[rows, lanes].astype(F32) * sum_b - r.zp[rows, lanes]
            r.rd[rows, lanes] = step * sum_b
            d_raw = d_step * r.fac[rows, lanes]
            r.ddr[rows, lanes] = d_raw.astype(BF16)
            r.gat[rows, lanes] = (d_step * step * step).astype(BF16)
            r.vec[5:6, lanes] += jnp.sum(d_raw, axis=0, keepdims=True)

        lane_loop(step_lanes)

    swap_dlow = [Swap(z, links, lambda slot, q=q: r.dlowp.at[q, slot]) for q in range(z.Q)]
    swap_dst = [Swap(z, links, lambda slot, q=q: r.dstp.at[q, slot]) for q in range(z.Q)]
    dlow_mine = [r.dlowp.at[q, z.M - 1] for q in range(z.Q)]
    dst_mine = [r.dstp.at[q, z.M - 1] for q in range(z.Q)]

    def project_back(q):
        rows = rows_of(q)
        key_grad = nt(jnp.ones((16, z.C), BF16), r.gat[rows, :])[0:1]
        now = r.st[: z.N, rows]
        d_key = r.est[1, :, rows] - 2.0 * now * r.est[0, :, rows] - 2.0 * now * key_grad
        dst_mine[q][...] = jnp.concatenate([d_key, r.est[2, :, rows]], axis=0).astype(BF16)
        swap_dst[q].start(dst_mine[q])
        dlow_mine[q][...] = nt(r.ddr[rows, :], r.deltaw[...]).astype(BF16)
        swap_dlow[q].start(dlow_mine[q])

    def sums_back(q):
        rows = rows_of(q)
        swap_dlow[q].wait()
        swap_dst[q].wait()
        dlow = r.dlowp[q, 0].astype(F32)
        dst = r.dstp[q, 0].astype(F32)
        for slot in range(1, z.M):
            dlow = dlow + r.dlowp[q, slot].astype(F32)
            dst = dst + r.dstp[q, slot].astype(F32)
        r.dlow[rows, :] = dlow.astype(BF16)
        r.dlowt[:, rows] = dlow.T.astype(BF16)
        r.dst[:, rows] = dst.astype(BF16)
        dlow16, dst16 = dlow.astype(BF16), columns_of(dst)[:, : 2 * z.N].astype(BF16)

        def inputs_chunk(index):
            lanes = cut(index * 256, 256)
            r.su[rows, lanes] = nt(dlow16, r.loww[lanes, :]) + nn(dst16, r.statewt[:, lanes])

        each(z.C // 256, inputs_chunk)

    rim = [
        links.copy(
            r.dcp.at[q, pl.ds(0, 8), :],
            r.dcp.at[q, pl.ds(z.T, 8), :],
            links.sem(),
            links.sem(),
            seq=behind,
        )
        for q in range(z.Q)
    ]

    def conv_back(q):
        rows = rows_of(q)

        def conv_lanes(lanes):
            total = r.su[rows, lanes] + r.rd[rows, lanes] + r.skip[:, lanes] * r.dr[rows, lanes]
            value = r.conv[rows, lanes]
            gate = silu_parts(value)[0]
            d_conv = total * gate * (1.0 + value * (1.0 - gate))
            r.dcp[q, 0 : z.T, lanes] = d_conv
            r.vec[4:5, lanes] += jnp.sum(d_conv, axis=0, keepdims=True)
            for tap in range(4):
                r.vec[tap : tap + 1, lanes] += jnp.sum(
                    d_conv * r.xpad[q, 5 + tap : 5 + tap + z.T, lanes], axis=0, keepdims=True
                )

        lane_loop(conv_lanes)
        rim[q].start()

    def x_back(q):
        rim[q].wait_recv()

        def x_lanes(lanes):
            edge = r.dcp[q, z.T : z.T + 8, lanes]
            r.dcp[q, z.T : z.T + 8, lanes] = jnp.where(seq < z.S - 1, edge, 0.0)
            total = jnp.zeros((z.T, LANE), F32)
            for tap in range(4):
                total = total + r.convw[tap : tap + 1, lanes] * r.dcp[q, 3 - tap : 3 - tap + z.T, lanes]
            r.dxr[rows_of(q), lanes] = total.astype(BF16)

        lane_loop(x_lanes)

    scatter_o.first(into(near_o, term_o))
    totals_back(0)
    back_send(0, 0)
    scatter_o.second(onto(sum_o, term_o))
    back_take(0, 0)
    back_send(1, 0)
    totals_back(1)
    back_send(0, 1)
    for level in range(1, z.levels):
        back_take(level, 0)
        if level < z.levels - 1:
            back_send(level + 1, 0)
        back_take(level - 1, 1)
        back_send(level, 1)
        if level == 1:
            each(z.M, branch_to)
            scatter_1.first(into(near_i, term_1))
    scatter_o.send(0)
    back_take(z.levels - 1, 1)
    scatter_1.second(onto(sum_1, term_1))
    scatter_1.send(0)
    for copy in scatter_1.sent[: len(z.masks)]:
        copy.wait_send()
    scatter_1.sent = scatter_1.sent[len(z.masks) :]
    tree_o.drain()
    walk_back(0)
    step_back(0)
    project_back(0)
    for step in range(depth - 1):
        scatter_o.fold(step)
    walk_back(1)
    for level in range(z.levels):
        pl.semaphore_signal(
            r.ready.at[level], inc=1, device_id=(seq ^ (1 << level), mp), device_id_type=MESH
        )
    step_back(1)
    project_back(1)
    sums_back(0)
    conv_back(0)
    for step in range(depth - 1):
        scatter_1.fold(step)

    last = depth - 1
    scatter_o.fold(last)

    def write_to(ref):
        def write(rows, value):
            ref[rows, :] = value

        return write

    scatter_o.total(write_to(r.dout))
    swap_out.wait()
    for away in range(1, z.M):
        owner = lax.rem(mp + away, z.M)
        swap_out.one(partial_of(owner), away).wait_send()

    def block_lanes(index):
        here = cut(index * LANE, LANE)
        total = r.normed[: z.R, cut(mp * z.Df + index * LANE, LANE)].astype(F32)
        for slot in range(z.M - 1):
            total = total + r.orecv[slot, :, here].astype(F32)
        r.blk[:, here] = (r.tok[:, here].astype(F32) + total).astype(BF16)

    each(z.Df // LANE, block_lanes)
    sums_back(1)
    conv_back(1)

    def put_small(first, lanes, value):
        count, at = value.shape[0], 0
        while at < count:
            block, inside = divmod(first + at, sg_rows)
            take = min(count - at, sg_rows - inside)
            sgp.block(block, inside, take)[:, lanes] = value[at : at + take].astype(BF16)
            at += take

    low_t = r.low[...].astype(F32).T.astype(BF16)
    used = 2 * z.RK + 2 * z.N + SGVEC

    def small_chunk(index):
        lanes = cut(index * 256, 256)
        put_small(0, lanes, nn(low_t, r.ddr[:, lanes]))
        put_small(z.RK, lanes, nn(r.dlowt[...], r.u[:, lanes]))
        put_small(2 * z.RK, lanes, nn(r.dst[...], r.u[:, lanes]))
        put_small(2 * z.RK + 2 * z.N, lanes, r.vec[:, lanes])
        if used < z.S * sg_rows:
            put_small(used, lanes, jnp.zeros((z.S * sg_rows - used, 256), F32))

    each(z.C // 256, small_chunk)
    for level in range(z.levels):
        pl.semaphore_wait(r.ready.at[level], 1)
    scatter_s.first(lambda device, mask: sgp.block(device))
    x_back(0)
    x_back(1)

    scatter_0.first(into(near_i, term_0))

    def add_small(device, mask):
        block, term = sum_s.block(mask // 2), sgp.block(device)

        def one(rows):
            block[rows, :] = (block[rows, :].astype(F32) + term[rows, :].astype(F32)).astype(BF16)

        by_rows(sg_rows, one)

    scatter_s.second(add_small)
    scatter_s.send(0)

    swap_n = Swap(z, links, lambda slot: r.nrecv.at[slot])

    def normed_to(index, means):
        away = index + 1
        owner = lax.rem(mp + away, z.M)
        for b in range(z.B):
            j = owner * z.B + b
            features = cut(j * z.Ds, z.Ds)
            part = nt(r.dxr[...], r.wx[0, features, :]) + nt(r.dzr[...], r.wx[1, features, :])
            r.normed[: z.R, features] = part.astype(BF16)
            scaled = part * r.tokg[j].astype(F32)
            by_gain = jnp.sum(scaled * wide(r.inv[...], z.Ds // LANE), axis=0, keepdims=True)
            for part in range(z.Ds // LANE):
                r.gv[pl.ds(j * (z.Ds // LANE) + part, 1), :] = by_gain[:, part * LANE : (part + 1) * LANE]
            means = means + jnp.sum(scaled * r.gain[:, features], axis=1, keepdims=True)

        @pl.when(away < z.M)
        def _():
            swap_n.one(partial_of(owner), away).start()

        return means

    means = lax.fori_loop(0, z.M, normed_to, jnp.zeros((z.R, 1), F32))
    swap_m = Swap(z, links, lambda slot: r.mrow.at[slot])
    mean_mine = r.mrow.at[z.M - 1]
    mean_mine[...] = jnp.broadcast_to(means, (z.R, LANE)).T[0:8]
    swap_m.start(mean_mine)

    gain_seq = SwapSeq(z, links, lambda slot: r.gvr.at[slot])
    gain_seq.start(r.gv)
    for step in range(depth - 1):
        scatter_s.fold(step)
    scatter_0.second(onto(sum_0, term_0))
    scatter_0.send(0)
    gain_seq.wait()
    gains = r.gv[...]
    for slot in range(z.S - 1):
        gains = gains + r.gvr[slot]
    r.gvs[...] = gains
    swap_g = Swap(z, links, lambda slot: r.gvm.at[slot])
    swap_g.start(r.gvs)
    scatter_s.fold(last)

    def write_small(rows, value):
        small.block(seq)[rows, :] = value.astype(BF16)

    scatter_s.total(write_small)
    tree_s = TreeGather(
        z,
        links,
        lambda owner, h: small.block(owner, *halves(sg_rows)[h]),
        small.block,
    )
    tree_s.first()
    tree_s.second()
    scatter_1.fold(last)
    scatter_1.total(write_to(r.fac))
    store_1 = pltpu.make_async_copy(r.fac.at[pl.ds(0, z.Ds)], r.din.at[1], local.at[3])
    store_1.start()
    for step in range(depth - 1):
        scatter_0.fold(step)
    tree_s.forward()
    tree_s.settle()

    swap_m.wait()
    mean = r.mrow[0]
    for slot in range(1, z.M):
        mean = mean + r.mrow[slot]
    r.mean[...] = jnp.concatenate([mean] * (LANE // 8), axis=0).T * (1.0 / z.D)
    swap_n.wait()

    def token_lanes(index):
        here = cut(index * LANE, LANE)
        inside = cut(mp * z.Df + index * LANE, LANE)
        for q in range(z.Q):
            rows = rows_of(q)
            total = r.normed[rows, inside].astype(F32)
            for slot in range(z.M - 1):
                total = total + r.nrecv[slot, rows, here].astype(F32)
            inv, x = r.inv[rows, :], r.tok[rows, here].astype(F32)
            value = inv * (total * r.gain[:, inside]) - x * (inv * inv * inv) * r.mean[rows, :]
            r.dtok[rows, here] = value + r.cot[rows, here] * seq_weight[q]

    each(z.Df // LANE, token_lanes)

    scatter_0.fold(last)
    scatter_0.total(write_to(r.s))
    store_0 = pltpu.make_async_copy(r.s.at[pl.ds(0, z.Ds)], r.din.at[0], local.at[4])
    store_0.start()
    tree_s.finish()
    for block in range(z.S):
        count = min(sg_rows, r.sg.shape[0] - block * sg_rows)
        if count > 0:
            r.sg[block * sg_rows : block * sg_rows + count, :] = small.block(block, 0, count)[...].astype(F32)
    swap_g.wait()
    gains = r.gvs[...]
    for slot in range(z.M - 1):
        gains = gains + r.gvm[slot]
    r.dgain[...] = gains

    hal.wait_send()
    for tree in (tree_x, tree_z, tree_s):
        tree.drain()
    for line in (line_t, line_h, line_d):
        line.drain()
    for q in range(z.Q):
        swap_st[q].drain(st_mine[q])
        swap_low[q].drain(low_mine[q])
        swap_dlow[q].drain(dlow_mine[q])
        swap_dst[q].drain(dst_mine[q])
    swap_m.drain(mean_mine)
    swap_g.drain(r.gvs)
    gain_seq.drain()
    for away in range(1, z.M):
        owner = lax.rem(mp + away, z.M)
        swap_n.one(partial_of(owner), away).wait_send()
    for copy in carry_copies + rim:
        copy.wait_send()
    for scatter in (scatter_o, scatter_1, scatter_0, scatter_s):
        scatter.drain()
    store_1.wait()
    store_0.wait()


def finish_kernel(z, blk, dtok, dgain, din, dout, sg, *outs):
    a, b, c = z.RK, 2 * z.RK, 2 * z.RK + 2 * z.N
    o_blk, o_dtok, o_dgain, o_din, o_convw, o_convb, o_low, o_state, o_delta, o_dbias, o_skip, o_dout = outs
    o_blk[...] = blk[...]
    o_dtok[...] = dtok[...]
    o_dgain[...] = dgain[...]
    o_din[...] = din[...]
    o_dout[...] = dout[...]
    o_delta[...] = sg[0:a, :]
    o_state[...] = sg[b:c, :]
    o_convw[...] = sg[c : c + 4, :]
    o_convb[...] = sg[c + 4 : c + 5, :]
    o_dbias[...] = sg[c + 5 : c + 6, :]
    o_skip[...] = sg[c + 6 : c + 7, :]
    for at in range(0, z.C, LANE):
        o_low[at : at + LANE, :] = sg[a:b, at : at + LANE].T


def fused(z, tokens, norm_gain, in_weight, conv_weight, conv_bias, low_weight, state_weight, delta_weight,
          delta_bias, skip_gain, out_weight, cotangent, seq_group, group_weight):
    V = pl.BlockSpec(memory_space=pltpu.VMEM)
    A = pl.BlockSpec(memory_space=pl.ANY)
    SM = pl.BlockSpec(memory_space=pltpu.SMEM)
    row = lambda value: value.reshape(1, -1)
    operands = dict(
        tok=(V, tokens.reshape(z.R, z.Df)),
        cot=(V, cotangent.reshape(z.R, z.Df)),
        gain=(V, row(norm_gain)),
        win=(A, in_weight),
        wout=(A, out_weight),
        convw=(V, conv_weight),
        convb=(V, row(conv_bias)),
        dbias=(V, row(delta_bias)),
        skip=(V, row(skip_gain)),
        loww=(V, low_weight),
        statewt=(V, state_weight.T),
        deltaw=(V, delta_weight),
        seqg=(SM, seq_group),
        groupw=(SM, group_weight),
    )
    scratch = scratch_of(z)
    sg_used = 2 * z.RK + 2 * z.N + SGVEC
    outs = dict(
        blk=(V, (z.R, z.Df), BF16),
        dtok=(V, (z.R, z.Df), F32),
        dgain=(V, (z.D // LANE, LANE), F32),
        din=(A, (2, z.Ds, z.C), F32),
        dout=(V, (z.C, z.Ds), F32),
        sg=(V, (sg_used, z.C), F32),
    )
    result = pl.pallas_call(
        functools.partial(fused_kernel, z, [*operands, *outs, *scratch]),
        out_shape=[jax.ShapeDtypeStruct(shape, kind) for _, shape, kind in outs.values()],
        in_specs=[spec for spec, _ in operands.values()],
        out_specs=[spec for spec, _, _ in outs.values()],
        scratch_shapes=list(scratch.values()),
        compiler_params=pltpu.CompilerParams(
            collective_id=0, has_side_effects=True, vmem_limit_bytes=VMEM_BYTES
        ),
    )(*[value for _, value in operands.values()])
    whole = (V, (1, z.C), F32)
    last = dict(
        blk=(V, (z.R, z.Df), BF16),
        dtok=(V, (z.R, z.Df), F32),
        dgain=(V, (z.D // LANE, LANE), F32),
        din=(V, (2, z.Ds, z.C), F32),
        convw=(V, (4, z.C), F32),
        convb=whole,
        low=(V, (z.C, z.RK), F32),
        state=(V, (2 * z.N, z.C), F32),
        delta=(V, (z.RK, z.C), F32),
        dbias=whole,
        skip=whole,
        dout=(V, (z.C, z.Ds), F32),
    )
    done = pl.pallas_call(
        functools.partial(finish_kernel, z),
        out_shape=[jax.ShapeDtypeStruct(shape, kind) for _, shape, kind in last.values()],
        in_specs=[V] * 6,
        out_specs=[spec for spec, _, _ in last.values()],
        compiler_params=pltpu.CompilerParams(vmem_limit_bytes=VMEM_BYTES),
    )(*result)
    done = dict(zip(last, done))
    done.update(blk=done["blk"].reshape(tokens.shape), dtok=done["dtok"].reshape(tokens.shape))
    done.update(dgain=done["dgain"].reshape(z.D), state=done["state"].T)
    done.update({name: done[name][0] for name in ("convb", "dbias", "skip")})
    return tuple(done.values())


def local(mesh_shape, *arrays):
    tokens, norm_gain, in_weight, conv_weight = arrays[:4]
    state_weight, delta_weight = arrays[6], arrays[7]
    z = Sizes(
        mesh_shape,
        tokens.shape[0],
        tokens.shape[1],
        tokens.shape[2],
        norm_gain.shape[0],
        in_weight.shape[2],
        state_weight.shape[1] // 2,
        delta_weight.shape[0],
    )
    if z.fits(conv_weight.shape[0]):
        return fused(z, *arrays)
    return plain(*arrays)


def solution(mesh):
    placed = (
        P(None, "seq", "mp"),
        P(),
        P(None, "seq", "mp"),
        P(None, "mp"),
        P("mp"),
        P("mp", None),
        P("mp", None),
        P(None, "mp"),
        P("mp"),
        P("mp"),
        P("mp", "seq"),
        P(None, "seq", "mp"),
        P(),
        P(),
    )
    return jax.shard_map(
        functools.partial(local, dict(mesh.shape)),
        mesh=mesh,
        in_specs=placed,
        out_specs=(
            P(None, "seq", "mp"),
            P(None, "seq", "mp"),
            P(),
            P(None, "seq", "mp"),
            P(None, "mp"),
            P("mp"),
            P("mp", None),
            P("mp", None),
            P(None, "mp"),
            P("mp"),
            P("mp"),
            P("mp", "seq"),
        ),
        check_vma=False,
    )
```

```python
import functools
import math

import jax
import jax.numpy as jnp
from jax import lax
from jax.experimental import pallas as pl
from jax.experimental.pallas import tpu as pltpu
from jax.sharding import PartitionSpec as P

SEQ_MB = 1
NMB = 2
EPSILON = 1e-05
VMEM_BYTES = 64 * 1024 * 1024 - 64 * 1024


def from_behind(value, axis, steps):
    count = lax.axis_size(axis)
    leading, last = (max(0, -steps), min(count, count - steps))
    return lax.ppermute(value, axis, [(source, source + steps) for source in range(leading, last)])


def prefix(value, axis, join, neutral, backward):
    count, mine = (lax.axis_size(axis), lax.axis_index(axis))
    pieces = jax.tree.map(lambda part: lax.all_gather(part, axis), value)
    if backward:
        pieces = jax.tree.map(lambda part: part[::-1], pieces)
        mine = count - 1 - mine
    subtotal = jax.tree.map(
        lambda part, zero: jnp.full_like(part, 0) + jnp.asarray(zero, part.dtype), value, neutral
    )

    def lap(position, subtotal):
        longer = join(subtotal, jax.tree.map(lambda part: part[position], pieces))
        return jax.tree.map(lambda new, old: jnp.where(position < mine, new, old), longer, subtotal)

    return lax.fori_loop(0, count - 1, lap, subtotal)


def combine(earlier, later):
    return (earlier[0] * later[0], later[0] * earlier[1] + later[1])


def make_gates(delta_raw, b_state, inputs):
    beta_gate = jax.nn.sigmoid(delta_raw)
    key_sq = jnp.sum(b_state * b_state, axis=-1, keepdims=True)
    step_size = beta_gate / (1.0 + beta_gate * key_sq)
    decays = 1.0 - step_size[:, :, None, :] * (b_state * b_state)[:, :, :, None]
    source = (step_size * inputs)[:, :, None, :] * b_state[:, :, :, None]
    return (decays, source)


def to_blocks(value, span_rows):
    old_shape = value.shape
    reshaped = value.reshape((old_shape[0], old_shape[1] // span_rows, span_rows) + old_shape[2:])
    return jnp.swapaxes(reshaped, 0, 1)


def from_blocks(value):
    joined = jnp.swapaxes(value, 0, 1)
    old_shape = joined.shape
    return joined.reshape((old_shape[0], old_shape[1] * old_shape[2]) + old_shape[3:])


def forward_block(carry_pair, block_items):
    delta_raw, b_state, inputs = block_items
    decays, source = make_gates(delta_raw, b_state, inputs)
    run_prod, run_state = carry_pair
    prod_list = []
    state_list = []
    for row_idx in range(decays.shape[1]):
        run_prod = run_prod * decays[:, row_idx]
        run_state = decays[:, row_idx] * run_state + source[:, row_idx]
        prod_list.append(run_prod)
        state_list.append(run_state)
    return ((run_prod, run_state), (jnp.stack(prod_list, axis=1), jnp.stack(state_list, axis=1)))


def backward_block(carry_trio, block_items):
    delta_raw, b_state, inputs, read_grad, c_state = block_items
    decays, _ = make_gates(delta_raw, b_state, inputs)
    grad_next, dec_next, tail_prod = carry_trio
    span_rows = decays.shape[1]
    grad_list = [None] * span_rows
    tail_list = [None] * span_rows
    for row_idx in reversed(range(span_rows)):
        drive_term = read_grad[:, row_idx][:, None, :] * c_state[:, row_idx][:, :, None]
        grad_next = drive_term + dec_next * grad_next
        tail_prod = dec_next * tail_prod
        grad_list[row_idx] = grad_next
        tail_list[row_idx] = tail_prod
        dec_next = decays[:, row_idx]
    return (
        (grad_next, dec_next, tail_prod),
        (jnp.stack(grad_list, axis=1), jnp.stack(tail_list, axis=1)),
    )


def silu_slope(value):
    sig_value = jax.nn.sigmoid(value)
    return sig_value * (1.0 + value * (1.0 - sig_value))


def plain(
    tokens,
    norm_gain,
    in_weight,
    conv_weight,
    conv_bias,
    low_weight,
    state_weight,
    delta_weight,
    delta_bias,
    skip_gain,
    out_weight,
    cotangent,
    seq_group,
    group_weight,
):
    stretch = tokens.shape[1]
    feature_dev = tokens.shape[2]
    channels = in_weight.shape[2]
    model_width = norm_gain.shape[0]
    num_taps = conv_weight.shape[0]
    nstate = state_weight.shape[1] // 2
    span_rows = math.gcd(stretch, 8)
    picks = (
        seq_group[:, None] == jnp.arange(group_weight.shape[0], dtype=jnp.int32)[None, :]
    ).astype(jnp.float32)
    seq_weight = jnp.sum(picks * group_weight[None, :], axis=1)
    feature_start = lax.axis_index("mp") * feature_dev
    ones_state = jnp.ones((SEQ_MB, nstate, channels), jnp.float32)
    zero_state = jnp.zeros_like(ones_state)
    acc_in = jnp.zeros((2, model_width, channels), jnp.float32)
    acc_out = jnp.zeros((channels, model_width), jnp.float32)
    acc_gain = jnp.zeros_like(norm_gain)
    acc_conv = jnp.zeros_like(conv_weight)
    acc_cbias = jnp.zeros_like(conv_bias)
    acc_low = jnp.zeros(low_weight.shape, jnp.float32)
    acc_state = jnp.zeros(state_weight.shape, jnp.float32)
    acc_delta = jnp.zeros(delta_weight.shape, jnp.float32)
    acc_dbias = jnp.zeros_like(delta_bias)
    acc_skip = jnp.zeros_like(skip_gain)
    outputs = []
    input_grads = []
    for micro_idx in range(NMB):
        whole_in, whole_out = (
            lax.all_gather(in_weight, "seq", axis=1, tiled=True),
            lax.all_gather(out_weight, "seq", axis=1, tiled=True),
        )
        first_seq = micro_idx * SEQ_MB
        block_tokens = tokens[first_seq : first_seq + SEQ_MB]
        full_tokens = lax.all_gather(block_tokens, "mp", axis=2, tiled=True).astype(jnp.float32)
        inv_rms = lax.rsqrt(jnp.mean(full_tokens * full_tokens, axis=-1, keepdims=True) + EPSILON)
        normed = (full_tokens * inv_rms * norm_gain).astype(jnp.bfloat16)
        both_parts = jnp.einsum(
            "scd,kdi->ksci", normed, whole_in, preferred_element_type=jnp.float32
        )
        x_round = both_parts[0].astype(jnp.bfloat16)
        z_part = both_parts[1]
        rim_rows = from_behind(x_round[:, stretch - (num_taps - 1) :], "seq", 1)
        padded = jnp.concatenate([rim_rows, x_round], axis=1).astype(jnp.float32)
        conv_sum = conv_bias + jnp.zeros((SEQ_MB, stretch, channels), jnp.float32)
        for tap_index in range(num_taps):
            conv_sum = (
                conv_sum + conv_weight[tap_index] * padded[:, tap_index : tap_index + stretch]
            )
        inputs_round = jax.nn.silu(conv_sum).astype(jnp.bfloat16)
        inputs_f = inputs_round.astype(jnp.float32)
        low_part = jnp.einsum(
            "sci,ir->scr", inputs_round, low_weight, preferred_element_type=jnp.float32
        )
        state_part = jnp.einsum(
            "sci,ir->scr", inputs_round, state_weight, preferred_element_type=jnp.float32
        )
        delta_low, state_proj = lax.psum((low_part, state_part), "mp")
        delta_round = delta_low.astype(jnp.bfloat16)
        delta_raw = (
            jnp.einsum("scr,ri->sci", delta_round, delta_weight, preferred_element_type=jnp.float32)
            + delta_bias
        )
        b_state = state_proj[..., :nstate]
        c_state = state_proj[..., nstate:]
        delta_blocks = to_blocks(delta_raw, span_rows)
        b_blocks = to_blocks(b_state, span_rows)
        c_blocks = to_blocks(c_state, span_rows)
        in_blocks = to_blocks(inputs_f, span_rows)
        stretch_pair, (prod_blocks, local_blocks) = lax.scan(
            forward_block, (ones_state, zero_state), (delta_blocks, b_blocks, in_blocks)
        )
        carried = prefix(stretch_pair, "seq", combine, (ones_state, zero_state), False)
        states = from_blocks(local_blocks) + from_blocks(prod_blocks) * carried[1][:, None]
        before = jnp.concatenate([carried[1][:, None], states[:, :-1]], axis=1)
        read_rec = jnp.einsum("scni,scn->sci", states, c_state)
        read_out = read_rec + skip_gain * inputs_f
        z_gate = jax.nn.silu(z_part)
        gated_round = (read_out * z_gate).astype(jnp.bfloat16)
        out_part = jnp.einsum(
            "sci,id->scd", gated_round, whole_out, preferred_element_type=jnp.float32
        )
        branch = lax.psum_scatter(out_part, "mp", scatter_dimension=2, tiled=True)
        outputs.append((block_tokens.astype(jnp.float32) + branch).astype(jnp.bfloat16))
        d_out = (
            cotangent[first_seq : first_seq + SEQ_MB]
            * seq_weight[first_seq : first_seq + SEQ_MB][:, None, None]
        )
        d_branch = lax.all_gather(d_out.astype(jnp.bfloat16), "mp", axis=2, tiled=True)
        acc_out = acc_out + jnp.einsum(
            "sci,scd->id", gated_round, d_branch, preferred_element_type=jnp.float32
        )
        d_gated = jnp.einsum("scd,id->sci", d_branch, whole_out, preferred_element_type=jnp.float32)
        d_read = d_gated * z_gate
        d_zpart = d_gated * read_out * silu_slope(z_part)
        acc_skip = acc_skip + jnp.sum(d_read * inputs_f, axis=(0, 1))
        read_blocks_grad = to_blocks(d_read, span_rows)
        (last_grad, first_dec, _), (grad_blocks, tail_blocks) = lax.scan(
            backward_block,
            (zero_state, ones_state, ones_state),
            (delta_blocks, b_blocks, in_blocks, read_blocks_grad, c_blocks),
            reverse=True,
        )
        tail_grad = first_dec * last_grad
        crossing = prefix(
            (stretch_pair[0], tail_grad), "seq", combine, (ones_state, zero_state), True
        )
        state_grad = from_blocks(grad_blocks) + from_blocks(tail_blocks) * crossing[1][:, None]
        _, gate_pullback = jax.vjp(make_gates, delta_raw, b_state, inputs_f)
        d_delta, d_bstate, d_inputs_state = gate_pullback((state_grad * before, state_grad))
        d_cstate = jnp.einsum("scni,sci->scn", states, d_read)
        acc_dbias = acc_dbias + jnp.sum(d_delta, axis=(0, 1))
        d_delta_round = d_delta.astype(jnp.bfloat16)
        acc_delta = acc_delta + jnp.einsum(
            "scr,sci->ri", delta_round, d_delta_round, preferred_element_type=jnp.float32
        )
        low_grad_part = jnp.einsum(
            "sci,ri->scr", d_delta_round, delta_weight, preferred_element_type=jnp.float32
        )
        state_grad_part = jnp.concatenate([d_bstate, d_cstate], axis=-1)
        d_low, d_state = lax.psum((low_grad_part, state_grad_part), "mp")
        d_low_round = d_low.astype(jnp.bfloat16)
        d_state_round = d_state.astype(jnp.bfloat16)
        acc_low = acc_low + jnp.einsum(
            "sci,scr->ir", inputs_round, d_low_round, preferred_element_type=jnp.float32
        )
        acc_state = acc_state + jnp.einsum(
            "sci,scr->ir", inputs_round, d_state_round, preferred_element_type=jnp.float32
        )
        d_inputs = d_read * skip_gain + d_inputs_state
        d_inputs = d_inputs + jnp.einsum(
            "scr,ir->sci", d_low_round, low_weight, preferred_element_type=jnp.float32
        )
        d_inputs = d_inputs + jnp.einsum(
            "scr,ir->sci", d_state_round, state_weight, preferred_element_type=jnp.float32
        )
        d_conv = d_inputs * silu_slope(conv_sum)
        acc_cbias = acc_cbias + jnp.sum(d_conv, axis=(0, 1))
        tap_grads = []
        d_padded = jnp.zeros((SEQ_MB, stretch + num_taps - 1, channels), jnp.float32)
        for tap_index in range(num_taps):
            tap_grads.append(
                jnp.sum(d_conv * padded[:, tap_index : tap_index + stretch], axis=(0, 1))
            )
            d_padded = d_padded + jnp.pad(
                conv_weight[tap_index] * d_conv,
                ((0, 0), (tap_index, num_taps - 1 - tap_index), (0, 0)),
            )
        acc_conv = acc_conv + jnp.stack(tap_grads)
        back_rim = from_behind(d_padded[:, : num_taps - 1], "seq", -1)
        d_xpart = d_padded[:, num_taps - 1 :] + jnp.pad(
            back_rim, ((0, 0), (stretch - (num_taps - 1), 0), (0, 0))
        )
        d_parts_round = jnp.stack([d_xpart, d_zpart]).astype(jnp.bfloat16)
        acc_in = acc_in + jnp.einsum(
            "scd,ksci->kdi", normed, d_parts_round, preferred_element_type=jnp.float32
        )
        norm_part = jnp.einsum(
            "ksci,kdi->scd", d_parts_round, whole_in, preferred_element_type=jnp.float32
        )
        d_normed = lax.psum(norm_part, "mp")
        acc_gain = acc_gain + jnp.sum(d_normed * full_tokens * inv_rms, axis=(0, 1))
        scaled = d_normed * norm_gain
        d_full = inv_rms * scaled - full_tokens * (inv_rms * inv_rms * inv_rms) * jnp.mean(
            scaled * full_tokens, axis=-1, keepdims=True
        )
        d_mine = lax.dynamic_slice_in_dim(d_full, feature_start, feature_dev, 2)
        input_grads.append(d_out + d_mine)
    d_in_weight, d_out_weight = (
        lax.psum_scatter(acc_in, "seq", scatter_dimension=1, tiled=True),
        lax.psum_scatter(acc_out, "seq", scatter_dimension=1, tiled=True),
    )
    summed = lax.psum(
        (acc_gain, acc_conv, acc_cbias, acc_low, acc_state, acc_delta, acc_dbias, acc_skip), "seq"
    )
    return (
        jnp.concatenate(outputs, axis=0),
        jnp.concatenate(input_grads, axis=0),
        summed[0],
        d_in_weight,
        summed[1],
        summed[2],
        summed[3],
        summed[4],
        summed[5],
        summed[6],
        summed[7],
        d_out_weight,
    )


MESH = pl.DeviceIdType.MESH
F32 = jnp.float32
BF16 = jnp.bfloat16
LANE = 128
GRP = 16
PADV = 8
SGVEC = 16


def nn(a, b):
    return lax.dot_general(a, b, (((1,), (0,)), ((), ())), preferred_element_type=F32)


def nt(a, b):
    return lax.dot_general(a, b, (((1,), (1,)), ((), ())), preferred_element_type=F32)


def tn(a, b):
    return lax.dot_general(a, b, (((0,), (0,)), ((), ())), preferred_element_type=F32)


def cut(start, size):
    return pl.ds(pl.multiple_of(start, size), size)


def each(count, step):
    lax.fori_loop(0, count, lambda index, unused: (step(index), unused)[1], 0)


def by_rows(count, step):
    size = 32 if count % 32 == 0 else 16
    each(count // size, lambda index: step(cut(index * size, size)))


def wide(value, times):
    return jnp.concatenate([value] * times, axis=1) if times > 1 else value


def groups_fit(channels):
    return (LANE // GRP) % min(LANE // GRP, channels // (GRP * GRP)) == 0


class Sizes:
    def __init__(self, mesh_shape, nseq, stretch, feature_dev, model, channels, nstate, rank):
        self.S, self.M = mesh_shape["seq"], mesh_shape["mp"]
        self.Q, self.T, self.Df, self.D, self.C = nseq, stretch, feature_dev, model, channels
        self.N, self.RK = nstate, rank
        self.R = nseq * stretch
        self.Ds = model // self.S
        self.B = max(1, feature_dev // self.Ds)
        self.levels = self.S.bit_length() - 1
        self.dims = [1 << bit for bit in range(1, self.levels)]
        self.masks = [2 * value for value in range(self.S // 2)]
        self.rows_sg = -(-(2 * rank + 2 * nstate + SGVEC) // (self.S * 16)) * 16
        self.E = max(self.R, self.Ds)

    def order(self, half):
        turn = half * (len(self.dims) // 2)
        return self.dims[turn:] + self.dims[:turn]

    def fits(self, taps):
        return (
            self.S in (4, 8)
            and self.M > 1
            and self.Q == 2
            and self.T == LANE
            and self.Ds == 256
            and self.Df % self.Ds == 0
            and self.C % 512 == 0
            and self.N == GRP
            and self.RK == LANE
            and taps == 4
            and self.D >= 2 * self.C
            and groups_fit(self.C)
            and self.C * self.D <= (1 << 21)
        )


class Bunch:
    def __init__(self, names, values):
        self.__dict__.update(zip(names, values))


class Rows:
    def __init__(self, ref, base, rows, count):
        self.ref, self.base, self.rows, self.end = ref, base, rows, base + rows * count

    def block(self, index, start=0, size=None):
        first = pl.multiple_of(self.base + index * self.rows + start, 16)
        return self.ref.at[pl.ds(first, self.rows if size is None else size), :]


class Links:
    def __init__(self, sems, seq, mp):
        self.sems, self.used, self.seq, self.mp = sems, 0, seq, mp

    def sem(self, count=1):
        first = self.used
        self.used += count
        return first

    def copy(self, src, dst, send, recv, seq=None, mp=None):
        target = (self.seq if seq is None else seq, self.mp if mp is None else mp)
        return pltpu.make_async_remote_copy(
            src_ref=src,
            dst_ref=dst,
            send_sem=self.sems.at[send],
            recv_sem=self.sems.at[recv],
            device_id=target,
            device_id_type=MESH,
        )

    def arrived(self, dst, recv):
        self.copy(dst, dst, recv, recv).wait_recv()


class TreeGather:
    def __init__(self, z, links, half_view, whole_view):
        self.z, self.links, self.half, self.whole = z, links, half_view, whole_view
        self.recv = {(mask, h): links.sem() for mask in z.masks[1:] for h in range(2)}
        self.near = {mask: links.sem() for mask in z.masks}
        self.sent = []

    def push(self, mask, h, dim):
        view = self.half(self.links.seq ^ mask, h)
        copy = self.links.copy(
            view, view, self.links.sem(), self.recv[mask | dim, h], seq=self.links.seq ^ dim
        )
        copy.start()
        self.sent.append(copy)

    def take(self, mask, h):
        self.links.arrived(self.half(self.links.seq ^ mask, h), self.recv[mask, h])

    def hand(self, mask):
        view = self.whole(self.links.seq ^ mask)
        copy = self.links.copy(view, view, self.links.sem(), self.near[mask], seq=self.links.seq ^ 1)
        copy.start()
        self.sent.append(copy)

    def first(self):
        for h in range(2):
            self.push(0, h, self.z.order(h)[0])

    def second(self, h):
        for dim in self.z.order(h)[1:]:
            self.push(0, h, dim)
        if h == 0:
            self.hand(0)

    def forward(self, h):
        order = self.z.order(h)
        if len(order) > 1:
            self.take(order[0], h)
            self.push(order[0], h, order[1])

    def settle(self, far=None):
        for mask in sorted(self.z.masks[1:], key=lambda mask: bin(mask).count("1")):
            if far is not None and far != (bin(mask).count("1") > 1):
                continue
            for h in range(2):
                order = self.z.order(h)
                if len(order) == 1 or mask != order[0]:
                    self.take(mask, h)
            self.hand(mask)

    def finish(self):
        for mask in self.z.masks:
            self.links.arrived(self.whole(self.links.seq ^ 1 ^ mask), self.near[mask])

    def drain(self):
        for copy in self.sent:
            copy.wait_send()


class LineGather:
    def __init__(self, z, links, view):
        self.z, self.links, self.view = z, links, view
        self.recv = links.sem(z.M)
        self.send = links.sem(2 * z.M)

    def parts(self, depth):
        for side, way in enumerate((1, -1)):
            owner, target = self.links.mp - way * depth, self.links.mp + way
            held = (owner >= 0) & (owner < self.z.M)
            more = held & (target >= 0) & (target < self.z.M)
            yield side, owner, target, held, more

    def copy(self, side, depth, owner, target):
        view = self.view(owner)
        return self.links.copy(view, view, self.send + 2 * depth + side, self.recv + owner, mp=target)

    def step(self, depth):
        for side, owner, target, held, more in self.parts(depth):
            if depth:

                @pl.when(held)
                def _():
                    self.links.arrived(self.view(owner), self.recv + owner)

            @pl.when(more)
            def _():
                self.copy(side, depth, owner, target).start()

    def drain(self):
        for depth in range(self.z.M):
            for side, owner, target, held, more in self.parts(depth):

                @pl.when(more)
                def _():
                    self.copy(side, depth, owner, target).wait_send()


class Swap:
    def __init__(self, z, links, slot):
        self.z, self.links, self.slot = z, links, slot
        self.recv = links.sem(z.M)
        self.send = links.sem(z.M)

    def one(self, src, away):
        target = lax.rem(self.links.mp + away, self.z.M)
        return self.links.copy(src, self.slot(away - 1), self.send + away, self.recv + away, mp=target)

    def start(self, src):
        for away in range(1, self.z.M):
            self.one(src, away).start()

    def wait(self):
        for away in range(1, self.z.M):
            self.links.arrived(self.slot(away - 1), self.recv + away)

    def drain(self, src):
        for away in range(1, self.z.M):
            self.one(src, away).wait_send()


class SwapSeq:
    def __init__(self, z, links, slot):
        self.links, self.slot = links, slot
        self.pairs = [(other, links.sem(), links.sem()) for other in range(1, z.S)]
        self.sent = []

    def start(self, src):
        for other, send, recv in self.pairs:
            copy = self.links.copy(src, self.slot(other - 1), send, recv, seq=self.links.seq ^ other)
            copy.start()
            self.sent.append(copy)

    def wait(self):
        for other, send, recv in self.pairs:
            self.links.arrived(self.slot(other - 1), recv)

    def drain(self):
        for copy in self.sent:
            copy.wait_send()


def halves(rows):
    first = -(-rows // 32) * 16
    return (0, first), (first, rows - first)


class Scatter:
    def __init__(self, z, links, out, sums, far, rows):
        self.z, self.links, self.out, self.sums, self.far, self.rows = z, links, out, sums, far, rows
        self.near = {mask: links.sem() for mask in z.masks}
        self.near_send = {mask: links.sem() for mask in z.masks}
        self.sent = []
        self.hops = {}
        place = 0
        for h in range(2):
            order = z.order(h)
            for step, dim in enumerate(order):
                for mask in z.masks:
                    if mask & dim and not any(mask & other for other in order[:step]):
                        self.hops[h, step, mask] = (dim, links.sem(), links.sem(), place)
                        place += 1
        self.slots = place

    def half(self, mask, h):
        start, size = halves(self.rows)[h]
        return self.sums.block(mask // 2, start, size)

    def came(self, h, place):
        return self.far.block(place, 0, halves(self.rows)[h][1])

    def first(self, make):
        links = self.links
        for mask in self.by_need():
            src = make(links.seq ^ 1 ^ mask, mask)
            copy = links.copy(src, self.sums.block(mask // 2), self.near_send[mask], self.near[mask], seq=links.seq ^ 1)
            copy.start()
            self.sent.append(copy)

    def by_need(self):
        return sorted(self.z.masks, key=lambda mask: -bin(mask).count("1"))

    def second(self, add, send=False, masks=None):
        links = self.links
        for mask in self.by_need() if masks is None else masks:
            links.arrived(self.sums.block(mask // 2), self.near[mask])
            add(links.seq ^ mask, mask)
            if send:
                self.send(0, mask)

    def send(self, step, only=None):
        links = self.links
        for (h, at, mask), (dim, send, recv, place) in self.hops.items():
            if at == step and only in (None, mask):
                copy = links.copy(
                    self.half(mask, h), self.came(h, place), send, recv, seq=links.seq ^ dim
                )
                copy.start()
                self.sent.append(copy)

    def fold(self, step):
        links = self.links
        for (h, at, mask), (dim, send, recv, place) in self.hops.items():
            if at != step:
                continue
            links.arrived(self.came(h, place), recv)
            if step < len(self.z.dims) - 1:
                half, came = self.half(mask ^ dim, h), self.came(h, place)

                def add(rows):
                    half[rows, :] = (half[rows, :].astype(F32) + came[rows, :].astype(F32)).astype(BF16)

                by_rows(halves(self.rows)[h][1], add)
        if step < len(self.z.dims) - 1:
            self.send(step + 1)

    def total(self, write):
        last = len(self.z.dims) - 1
        for (h, at, mask), (dim, send, recv, place) in self.hops.items():
            if at == last:
                half, came = self.half(0, h), self.came(h, place)
                first, count = halves(self.rows)[h]

                def add(rows):
                    value = half[rows, :].astype(F32) + came[rows, :].astype(F32)
                    write(pl.ds(pl.multiple_of(first + rows.start, 16), rows.size), value)

                by_rows(count, add)

    def drain(self):
        for copy in self.sent:
            copy.wait_send()


def slots_of(z):
    return Scatter(z, Links(None, 0, 0), None, None, None, 0).slots


def scratch_of(z):
    V = pltpu.VMEM
    half = z.S // 2
    slots = slots_of(z)
    return dict(
        tokg=V((z.S, z.R, z.Ds), BF16),
        halg=V((z.S, 16, z.Ds), BF16),
        hals=V((z.B, 16, z.Ds), BF16),
        db=V((z.R, z.D), BF16),
        inv=V((z.R, LANE), F32),
        normed=V((z.R + 16, z.D), BF16),
        normt=V((z.D, z.R), BF16),
        wx=V((2, z.D, z.C), BF16),
        wo=V((z.C, z.D), BF16),
        xpad=V((z.Q, 8 + z.T, z.C), F32),
        dcp=V((z.Q, z.T + 8, z.C), F32),
        conv=V((z.E, z.C), F32),
        s=V((z.E, z.C), F32),
        su=V((z.R, z.C), F32),
        fac=V((z.E, z.C), F32),
        zp=V((z.R, z.C), F32),
        rd=V((z.R, z.C), F32),
        dr=V((z.R, z.C), F32),
        u=V((z.R, z.C), BF16),
        gat=V((z.R, z.C), BF16),
        gatt=V((z.C, z.R), BF16),
        ddr=V((z.R, z.C), BF16),
        dzr=V((z.R, z.C), BF16),
        dxr=V((z.R, z.C), BF16),
        lowp=V((z.Q, z.M, z.T, z.RK), BF16),
        stp=V((z.Q, z.M, 2 * z.N, z.T), F32),
        low=V((z.R, z.RK), BF16),
        dlow=V((z.R, z.RK), BF16),
        dlowt=V((z.RK, z.R), BF16),
        dst=V((2 * z.N, z.R), BF16),
        st=V((2 * z.N, z.R), F32),
        blkb=V((z.R, GRP * z.N), BF16),
        blkk=V((z.R, GRP * z.N), BF16),
        blkc=V((z.R, GRP * z.N), BF16),
        bc=V((z.Q, z.T, 2 * z.N, LANE), F32),
        hist=V((z.Q * (z.T + 1) * z.N, z.C), BF16),
        ptot=V((z.Q, z.N, z.C), F32),
        stot=V((z.Q, z.N, z.C), F32),
        ppre=V((z.Q, z.N, z.C), F32),
        spre=V((z.Q, z.N, z.C), F32),
        csend=V((z.levels, z.Q, 2, z.N, z.C), BF16),
        crecv=V((z.levels, z.Q, 2, z.N, z.C), BF16),
        bsend=V((z.levels, z.Q, z.N, z.C), BF16),
        brecv=V((z.levels, z.Q, z.N, z.C), BF16),
        est=V((3, z.N, z.R), F32),
        dlowp=V((z.Q, z.M, z.T, z.RK), BF16),
        dstp=V((z.Q, z.M, 2 * z.N, z.T), BF16),
        orecv=V((z.M - 1, z.R, z.Df), BF16),
        nrecv=V((z.M - 1, z.R, z.Df), BF16),
        near_o=V((half * z.C, z.Ds), BF16),
        sum_o=V((half * z.C, z.Ds), BF16),
        far_o=V((slots * (z.C // 2), z.Ds), BF16),
        near_i=V((half * z.Ds, z.C), BF16),
        sum_1=V((half * z.Ds, z.C), BF16),
        far_1=V((slots * (z.Ds // 2), z.C), BF16),
        vec=V((SGVEC, z.C), F32),
        gv=V((z.D // LANE, LANE), F32),
        gvs=V((z.D // LANE, LANE), F32),
        gvr=V((z.S - 1, z.D // LANE, LANE), F32),
        gvm=V((z.M - 1, z.D // LANE, LANE), F32),
        mean=V((z.R, LANE), F32),
        mrow=V((z.M, 8, z.R), F32),
        sems=pltpu.SemaphoreType.DMA((420,)),
        local=pltpu.SemaphoreType.DMA((8,)),
        ready=pltpu.SemaphoreType.REGULAR((z.levels,)),
    )


def silu_parts(value):
    gate = 1.0 / (1.0 + jnp.exp(-value))
    return gate, value * gate


def fused_kernel(z, names, *refs):
    r = Bunch(names, refs)
    seq, mp = lax.axis_index("seq"), lax.axis_index("mp")
    links = Links(r.sems, seq, mp)
    lanes_all = z.C // LANE
    first_block = mp * z.B

    def lane_loop(step):
        each(z.C // LANE, lambda index: step(cut(index * LANE, LANE)))

    local = r.local
    mine_in = lambda k: r.wx.at[k, cut(seq * z.Ds, z.Ds), :]
    loads = [
        pltpu.make_async_copy(r.win.at[0], mine_in(0), local.at[0]),
        pltpu.make_async_copy(r.win.at[1], mine_in(1), local.at[1]),
        pltpu.make_async_copy(r.wout, r.wo.at[:, cut(seq * z.Ds, z.Ds)], local.at[2]),
    ]
    for load in loads:
        load.start()
    for b in range(z.B):
        r.tokg[first_block + b] = r.tok[:, b * z.Ds : (b + 1) * z.Ds]
        tails = [
            r.tok[q * z.T + z.T - 16 : q * z.T + z.T, b * z.Ds : (b + 1) * z.Ds].astype(F32)[8:]
            for q in range(z.Q)
        ]
        r.hals[b] = jnp.concatenate(tails, axis=0).astype(BF16)

    barrier = pltpu.get_barrier_semaphore()
    ahead, behind = lax.rem(seq + 1, z.S), lax.rem(seq + z.S - 1, z.S)
    partners = [(seq ^ other, mp) for other in range(1, z.S)] + [(ahead, mp), (behind, mp)]
    partners += [(seq, lax.rem(mp + away, z.M)) for away in range(1, z.M)]
    for partner in partners:
        pl.semaphore_signal(barrier, inc=1, device_id=partner, device_id_type=MESH)
    pl.semaphore_wait(barrier, len(partners))

    def of_in(k):
        def half(owner, h):
            return r.wx.at[k, cut(owner * z.Ds + h * (z.Ds // 2), z.Ds // 2), :]

        return TreeGather(z, links, half, lambda owner: r.wx.at[k, cut(owner * z.Ds, z.Ds), :])

    tree_x, tree_z = of_in(0), of_in(1)
    tree_o = TreeGather(
        z,
        links,
        lambda owner, h: r.wo.at[pl.ds(h * (z.C // 2), z.C // 2), cut(owner * z.Ds, z.Ds)],
        lambda owner: r.wo.at[:, cut(owner * z.Ds, z.Ds)],
    )
    line_t = [
        LineGather(z, links, lambda owner, q=q: r.tokg.at[pl.ds(owner * z.B, z.B), pl.ds(q * z.T, z.T), :])
        for q in range(z.Q)
    ]
    line_h = LineGather(z, links, lambda owner: r.halg.at[pl.ds(owner * z.B, z.B)])
    line_d = LineGather(z, links, lambda owner: r.db.at[:, cut(owner * z.Df, z.Df)])
    depth = len(z.dims)

    hal_send, hal_recv = links.sem(), links.sem()
    hal_mine = r.halg.at[pl.ds(first_block, z.B)]
    hal = links.copy(r.hals, hal_mine, hal_send, hal_recv, seq=ahead)
    hal.start()
    for line in line_t:
        line.step(0)
    loads[0].wait()
    tree_x.first()
    tree_x.second(0)
    tree_x.second(1)

    def weight_of(q):
        total = jnp.float32(0.0)
        for group in range(r.groupw.shape[0]):
            total = total + jnp.where(r.seqg[q] == group, r.groupw[group], 0.0)
        return total

    seq_weight = [weight_of(q) for q in range(z.Q)]
    for q in range(z.Q):
        rows = pl.ds(q * z.T, z.T)
        for b in range(z.B):
            part = r.cot[rows, b * z.Ds : (b + 1) * z.Ds] * seq_weight[q]
            r.db[rows, cut((first_block + b) * z.Ds, z.Ds)] = part.astype(BF16)

    links.arrived(hal_mine, hal_recv)
    line_h.step(0)
    for line in line_t:
        line.step(1)
    tree_x.forward(0)
    tree_x.forward(1)
    loads[1].wait()
    tree_z.first()
    tree_z.second(0)
    tree_z.second(1)
    line_h.step(1)
    for far in range(2, z.M):
        for line in line_t:
            line.step(far)
        line_h.step(far)
        if far == 2:
            tree_x.settle(False)
    if z.M == 2:
        tree_x.settle(False)
    line_d.step(0)

    def add_squares(j, total):
        part = r.tokg[j].astype(F32)
        edge = r.halg[j].astype(F32)
        return (
            total[0] + jnp.sum(part * part, axis=1, keepdims=True),
            total[1] + jnp.sum(edge * edge, axis=1, keepdims=True),
        )

    squares = lax.fori_loop(
        0, z.S, add_squares, (jnp.zeros((z.R, 1), F32), jnp.zeros((16, 1), F32))
    )
    inv = lax.rsqrt(squares[0] * (1.0 / z.D) + EPSILON)
    inv_edge = lax.rsqrt(squares[1] * (1.0 / z.D) + EPSILON)
    r.inv[...] = jnp.broadcast_to(inv, (z.R, LANE))

    def norm_block(j):
        features = cut(j * z.Ds, z.Ds)
        gain = r.gain[:, features]
        normed = r.tokg[j].astype(F32) * wide(r.inv[...], z.Ds // LANE) * gain
        r.normed[: z.R, features] = normed.astype(BF16)
        edge = r.halg[j].astype(F32) * inv_edge * gain
        r.normed[z.R :, features] = edge.astype(BF16)
        r.normt[features, :] = normed.T.astype(BF16)

    each(z.S, norm_block)
    tree_x.settle(True)
    tree_x.finish()

    def x_chunk(index):
        lanes = cut(index * 256, 256)
        part = nn(r.normed[...], r.wx[0, :, lanes]).astype(BF16).astype(F32)
        for q in range(z.Q):
            edge = part[z.R + 8 * q : z.R + 8 * q + 8]
            r.xpad[q, 0:8, lanes] = jnp.where(seq > 0, edge, 0.0)
            r.xpad[q, 8 : 8 + z.T, lanes] = part[q * z.T : (q + 1) * z.T]

    each(z.C // 256, x_chunk)
    tree_z.forward(0)
    tree_z.forward(1)
    loads[2].wait()
    tree_o.first()
    tree_o.second(0)

    def rows_of(q):
        return pl.ds(q * z.T, z.T)

    def conv(q):
        def conv_lanes(lanes):
            total = jnp.broadcast_to(r.convb[:, lanes], (z.T, LANE))
            for tap in range(4):
                total = total + r.convw[tap : tap + 1, lanes] * r.xpad[q, 5 + tap : 5 + tap + z.T, lanes]
            r.conv[rows_of(q), lanes] = total
            r.u[rows_of(q), lanes] = silu_parts(total)[1].astype(BF16)

        lane_loop(conv_lanes)

    swap_low = [Swap(z, links, lambda slot, q=q: r.lowp.at[q, slot]) for q in range(z.Q)]
    swap_st = [Swap(z, links, lambda slot, q=q: r.stp.at[q, slot]) for q in range(z.Q)]
    low_mine = [r.lowp.at[q, z.M - 1] for q in range(z.Q)]
    st_mine = [r.stp.at[q, z.M - 1] for q in range(z.Q)]

    def project(q):
        u = r.u[rows_of(q), :]
        st_mine[q][...] = nt(r.statewt[...], u)
        swap_st[q].start(st_mine[q])
        low_mine[q][...] = nn(u, r.loww[...]).astype(BF16)
        swap_low[q].start(low_mine[q])

    rows_i = lax.broadcasted_iota(jnp.int32, (z.T, GRP * z.N), 0)
    cols_i = lax.broadcasted_iota(jnp.int32, (z.T, GRP * z.N), 1)
    diagonal = lax.rem(rows_i, GRP) == cols_i // z.N
    rep_n = lax.broadcasted_iota(jnp.int32, (2 * z.N, GRP * z.N), 0)
    rep_j = lax.rem(lax.broadcasted_iota(jnp.int32, (2 * z.N, GRP * z.N), 1), z.N)
    rep_b = (rep_n == rep_j).astype(BF16)
    rep_c = (rep_n == rep_j + z.N).astype(BF16)
    only_b = lax.broadcasted_iota(jnp.int32, (z.T, LANE), 1) < z.N

    def columns_of(value):
        return jnp.concatenate([value, jnp.zeros((LANE - 2 * z.N, z.T), F32)], axis=0).T

    def keys(q):
        swap_st[q].wait()
        st = r.stp[q, 0]
        for slot in range(1, z.M):
            st = st + r.stp[q, slot]
        r.st[:, rows_of(q)] = st

        def spread(index):
            turned = pltpu.roll(st, lax.rem(z.T - index * 32, z.T), 1)
            for j in range(32):
                r.bc[q, index * 32 + j] = jnp.broadcast_to(turned[:, j : j + 1], (2 * z.N, LANE))

        each(z.T // 32, spread)
        nat = columns_of(st)
        key_sq = jnp.sum(jnp.where(only_b, nat * nat, 0.0), axis=1, keepdims=True)
        swap_low[q].wait()
        low = r.lowp[q, 0].astype(F32)
        for slot in range(1, z.M):
            low = low + r.lowp[q, slot].astype(F32)
        low = low.astype(BF16)
        r.low[rows_of(q), :] = low

        def step_chunk(index):
            lanes = cut(index * 256, 256)
            raw = nn(low, r.deltaw[:, lanes]) + r.dbias[:, lanes]
            beta = 1.0 / (1.0 + jnp.exp(-raw))
            scale = 1.0 / (1.0 + beta * key_sq)
            step = beta * scale
            r.s[rows_of(q), lanes] = step
            r.su[rows_of(q), lanes] = step * r.u[rows_of(q), lanes].astype(F32)
            r.fac[rows_of(q), lanes] = scale * step * (1.0 - beta)

        each(z.C // 256, step_chunk)

    def key_blocks(q):
        nat16 = columns_of(r.st[:, rows_of(q)])[:, : 2 * z.N].astype(BF16)
        spread_b = jnp.where(diagonal, nn(nat16, rep_b), 0.0)
        r.blkb[rows_of(q), :] = spread_b.astype(BF16)
        r.blkk[rows_of(q), :] = (spread_b * spread_b).astype(BF16)
        r.blkc[rows_of(q), :] = jnp.where(diagonal, nn(nat16, rep_c), 0.0).astype(BF16)

    span = 512 if z.C % 512 == 0 else 256

    def token(q, t):
        return pl.ds(q * z.T + t, 1)

    def totals(q):
        def lane_part(index):
            lanes = cut(index * span, span)

            def tokens8(i, carry):
                product, state = carry
                for j in range(8):
                    row = token(q, i * 8 + j)
                    step, drive = r.s[row, lanes], r.su[row, lanes]
                    key = r.bc[q, i * 8 + j, : z.N, :]
                    decay = 1.0 - step * wide(key * key, span // LANE)
                    product = product * decay
                    state = decay * state + drive * wide(key, span // LANE)
                return product, state

            start = (jnp.ones((z.N, span), F32), jnp.zeros((z.N, span), F32))
            product, state = lax.fori_loop(0, z.T // 8, tokens8, start)
            r.ptot[q, :, lanes] = product
            r.stot[q, :, lanes] = state

        each(z.C // span, lane_part)

    carry_sems = [[(links.sem(), links.sem()) for q in range(z.Q)] for level in range(z.levels)]
    back_sems = [[(links.sem(), links.sem()) for q in range(z.Q)] for level in range(z.levels)]
    carry_copies = []

    def upper_at(level):
        return lax.rem(seq // (1 << level), 2) == 1

    def carry_send(level, q):
        r.csend[level, q, 0] = r.ptot[q].astype(BF16)
        r.csend[level, q, 1] = r.stot[q].astype(BF16)
        copy = links.copy(
            r.csend.at[level, q], r.crecv.at[level, q], *carry_sems[level][q], seq=seq ^ (1 << level)
        )
        copy.start()
        carry_copies.append(copy)

    def carry_take(level, q):
        links.arrived(r.crecv.at[level, q], carry_sems[level][q][1])
        upper = upper_at(level)
        other_p, other_s = r.crecv[level, q, 0].astype(F32), r.crecv[level, q, 1].astype(F32)
        mine_p, mine_s = r.ptot[q], r.stot[q]
        if level == 0:
            r.spre[q] = jnp.where(upper, other_s, 0.0)
            r.ppre[q] = jnp.where(upper, other_p, 1.0)
        else:
            pre_p, pre_s = r.ppre[q], r.spre[q]
            r.spre[q] = jnp.where(upper, pre_p * other_s + pre_s, pre_s)
            r.ppre[q] = jnp.where(upper, pre_p * other_p, pre_p)
        if level < z.levels - 1:
            r.stot[q] = jnp.where(upper, mine_p * other_s + mine_s, other_p * mine_s + other_s)
            r.ptot[q] = mine_p * other_p

    def back_send(level, q):
        r.bsend[level, q] = r.stot[q].astype(BF16)
        copy = links.copy(
            r.bsend.at[level, q], r.brecv.at[level, q], *back_sems[level][q], seq=seq ^ (1 << level)
        )
        copy.start()
        carry_copies.append(copy)

    def back_take(level, q):
        links.arrived(r.brecv.at[level, q], back_sems[level][q][1])
        upper = upper_at(level)
        other = r.brecv[level, q].astype(F32)
        other_p, mine_p = r.crecv[level, q, 0].astype(F32), r.csend[level, q, 0].astype(F32)
        mine = r.stot[q]
        if level == 0:
            r.spre[q] = jnp.where(upper, 0.0, other)
            r.ppre[q] = jnp.where(upper, 1.0, other_p)
        else:
            pre_p, pre = r.ppre[q], r.spre[q]
            r.spre[q] = jnp.where(upper, pre, pre + pre_p * other)
            r.ppre[q] = jnp.where(upper, pre_p, pre_p * other_p)
        if level < z.levels - 1:
            r.stot[q] = jnp.where(upper, other + other_p * mine, mine + mine_p * other)

    def past_rows(q, slot, count=1):
        return pl.ds(pl.multiple_of((q * (z.T + 1) + slot) * z.N, z.N), count * z.N)

    groups = z.T // GRP

    def walk(q):
        r.hist[past_rows(q, 0), :] = r.spre[q].astype(BF16)

        def lane_part(index):
            lanes = cut(index * span, span)

            def tokens8(i, state):
                for j in range(8):
                    row = token(q, i * 8 + j)
                    step, drive = r.s[row, lanes], r.su[row, lanes]
                    key = r.bc[q, i * 8 + j, : z.N, :]
                    decay = 1.0 - step * wide(key * key, span // LANE)
                    state = decay * state + drive * wide(key, span // LANE)
                    r.hist[past_rows(q, i * 8 + j + 1), lanes] = state.astype(BF16)
                return state

            lax.fori_loop(0, z.T // 8, tokens8, r.spre[q, :, lanes])

        each(z.C // span, lane_part)
        reads = []
        for i in range(groups):
            rows = pl.ds(q * z.T + i * GRP, GRP)
            reads.append((rows, nn(r.blkc[rows, :], r.hist[past_rows(q, i * GRP + 1, GRP), :])))
        for rows, value in reads:
            r.rd[rows, :] = value

    def z_chunk(index):
        lanes = cut(index * 256, 256)
        r.zp[:, lanes] = nn(r.normed[: z.R, :], r.wx[1, :, lanes])

    conv(0)
    project(0)
    conv(1)
    project(1)
    line_d.step(1)
    keys(0)
    totals(0)
    carry_send(0, 0)
    keys(1)
    carry_take(0, 0)
    carry_send(1, 0)
    totals(1)
    carry_send(0, 1)
    carry_take(0, 1)
    carry_send(1, 1)
    tree_o.second(1)
    tree_o.forward(1)
    line_d.step(2)
    tree_z.settle()
    key_blocks(0)
    key_blocks(1)
    for level in range(1, z.levels - 1):
        for q in range(z.Q):
            carry_take(level, q)
            carry_send(level + 1, q)
    tree_o.forward(0)
    tree_z.finish()
    each(z.C // 256, z_chunk)
    carry_take(z.levels - 1, 0)
    walk(0)
    for far in range(3, z.M):
        line_d.step(far)
    tree_o.settle(False)
    carry_take(z.levels - 1, 1)
    walk(1)
    tree_o.settle(True)
    tree_o.finish()

    def gated_grad(index):
        lanes = cut(index * 256, 256)
        r.dr[:, lanes] = nt(r.db[...], r.wo[lanes, :])

    each(z.C // 256, gated_grad)
    r.vec[...] = jnp.zeros_like(r.vec)

    def gate_lanes(lanes):
        for q in range(z.Q):
            rows = rows_of(q)
            u = r.u[rows, lanes].astype(F32)
            out = r.rd[rows, lanes] + r.skip[:, lanes] * u
            part, grad = r.zp[rows, lanes], r.dr[rows, lanes]
            gate, silu = silu_parts(part)
            gated = out * silu
            r.gat[rows, lanes] = gated.astype(BF16)
            r.gatt[lanes, rows] = gated.T.astype(BF16)
            d_read = grad * silu
            r.dr[rows, lanes] = d_read
            r.dzr[rows, lanes] = (grad * out * gate * (1.0 + part * (1.0 - gate))).astype(BF16)
            r.vec[6:7, lanes] += jnp.sum(d_read * u, axis=0, keepdims=True)

    lane_loop(gate_lanes)

    swap_out = Swap(z, links, lambda slot: r.orecv.at[slot])

    def partial_of(owner):
        return r.normed.at[pl.ds(0, z.R), cut(owner * z.Df, z.Df)]

    def branch_to(index):
        away = index + 1
        owner = lax.rem(mp + away, z.M)
        for b in range(z.B):
            j = owner * z.B + b
            r.normed[: z.R, cut(j * z.Ds, z.Ds)] = nn(r.gat[...], r.wo[:, cut(j * z.Ds, z.Ds)]).astype(BF16)

        @pl.when(away < z.M)
        def _():
            swap_out.one(partial_of(owner), away).start()

    def into(near, term):
        def make(device, mask):
            block = near.block(mask // 2)
            block[...] = term(device).astype(BF16)
            return block

        return make

    def onto(sums, term):
        def add(device, mask):
            block = sums.block(mask // 2)
            block[...] = (term(device) + block[...].astype(F32)).astype(BF16)

        return add

    half_s, slots = z.S // 2, slots_of(z)
    sg_rows = z.rows_sg
    near_o, near_i = Rows(r.near_o, 0, z.C, half_s), Rows(r.near_i, 0, z.Ds, half_s)
    sum_o, far_o = Rows(r.sum_o, 0, z.C, half_s), Rows(r.far_o, 0, z.C // 2, slots)
    sum_1, far_1 = Rows(r.sum_1, 0, z.Ds, half_s), Rows(r.far_1, 0, z.Ds // 2, slots)
    sum_0 = Rows(r.hist, 0, z.Ds, half_s)
    far_0 = Rows(r.hist, sum_0.end, z.Ds // 2, slots)
    sum_s = Rows(r.hist, far_0.end, sg_rows, half_s)
    far_s = Rows(r.hist, sum_s.end, halves(sg_rows)[0][1], slots)
    sgp = Rows(r.hist, far_s.end, sg_rows, z.S)
    small = Rows(r.hist, sgp.end, sg_rows, z.S)
    scatter_o = Scatter(z, links, None, sum_o, far_o, z.C)
    scatter_1 = Scatter(z, links, None, sum_1, far_1, z.Ds)
    scatter_0 = Scatter(z, links, None, sum_0, far_0, z.Ds)
    scatter_s = Scatter(z, links, None, sum_s, far_s, sg_rows)
    term_o = lambda device: nn(r.gatt[...], r.db[:, cut(device * z.Ds, z.Ds)])
    term_1 = lambda device: nn(r.normt[cut(device * z.Ds, z.Ds), :], r.dzr[...])
    term_0 = lambda device: nn(r.normt[cut(device * z.Ds, z.Ds), :], r.dxr[...])

    def totals_back(q):
        def lane_part(index):
            lanes = cut(index * span, span)

            def tokens8(i, tail):
                for j in reversed(range(8)):
                    t = z.T - 8 - i * 8 + j
                    row = token(q, t)
                    step, grad = r.s[row, lanes], r.dr[row, lanes]
                    key, query = r.bc[q, t, : z.N, :], r.bc[q, t, z.N :, :]
                    decay = 1.0 - step * wide(key * key, span // LANE)
                    tail = decay * (grad * wide(query, span // LANE) + tail)
                return tail

            r.stot[q, :, lanes] = lax.fori_loop(0, z.T // 8, tokens8, jnp.zeros((z.N, span), F32))

        each(z.C // span, lane_part)

    lane_index = lax.broadcasted_iota(jnp.int32, (z.N, LANE), 1)

    def lane_sum(value):
        total = value[:, :LANE]
        for part in range(1, lanes_all):
            total = total + value[:, part * LANE : (part + 1) * LANE]
        return jnp.sum(total, axis=1, keepdims=True)

    batch = min(groups, z.C // (GRP * z.N))

    def walk_back(q):
        def group(index, carry):
            tail, sum_gh, sum_g, sum_h = carry
            i = groups - 1 - index
            for j in reversed(range(GRP)):
                t = i * GRP + j
                row = token(q, t)
                step, drive, grad = r.s[row, :], r.su[row, :], r.dr[row, :]
                key, query = r.bc[q, t, : z.N, :], r.bc[q, t, z.N :, :]
                before = r.hist[past_rows(q, t), :].astype(F32)
                now = r.hist[past_rows(q, t + 1), :].astype(F32)
                state_grad = grad * wide(query, lanes_all) + tail
                crossed = state_grad * before
                place = pl.ds(pl.multiple_of(lax.rem(i, batch) * GRP * z.N + j * z.N, z.N), z.N)
                r.wo[place, : z.C] = state_grad.astype(BF16)
                r.wo[place, z.C : 2 * z.C] = crossed.astype(BF16)
                here = lane_index == t
                sum_gh = jnp.where(here, lane_sum(step * crossed), sum_gh)
                sum_g = jnp.where(here, lane_sum(drive * state_grad), sum_g)
                sum_h = jnp.where(here, lane_sum(grad * now), sum_h)
                tail = (1.0 - step * wide(key * key, lanes_all)) * state_grad
            return tail, sum_gh, sum_g, sum_h

        zero = jnp.zeros((z.N, LANE), F32)
        carry = (r.spre[q], zero, zero, zero)
        for start in range(0, groups, batch):
            carry = lax.fori_loop(start, start + batch, group, carry)
            sums = []
            for slot in range(batch):
                rows = pl.ds(q * z.T + (groups - start - batch + slot) * GRP, GRP)
                place = pl.ds(slot * GRP * z.N, GRP * z.N)
                sums.append(
                    (
                        rows,
                        nn(r.blkb[rows, :], r.wo[place, : z.C]),
                        nn(r.blkk[rows, :], r.wo[place, z.C : 2 * z.C]),
                    )
                )
            for rows, by_key, by_square in sums:
                r.rd[rows, :] = by_key
                r.zp[rows, :] = by_square
        columns = rows_of(q)
        for part in range(3):
            r.est[part, :, columns] = carry[1 + part]

    def step_back(q):
        rows = rows_of(q)

        def step_lanes(lanes):
            sum_b, step = r.rd[rows, lanes], r.s[rows, lanes]
            d_step = r.u[rows, lanes].astype(F32) * sum_b - r.zp[rows, lanes]
            r.rd[rows, lanes] = step * sum_b
            d_raw = d_step * r.fac[rows, lanes]
            r.ddr[rows, lanes] = d_raw.astype(BF16)
            r.gat[rows, lanes] = (d_step * step * step).astype(BF16)
            r.vec[5:6, lanes] += jnp.sum(d_raw, axis=0, keepdims=True)

        lane_loop(step_lanes)

    swap_dlow = [Swap(z, links, lambda slot, q=q: r.dlowp.at[q, slot]) for q in range(z.Q)]
    swap_dst = [Swap(z, links, lambda slot, q=q: r.dstp.at[q, slot]) for q in range(z.Q)]
    dlow_mine = [r.dlowp.at[q, z.M - 1] for q in range(z.Q)]
    dst_mine = [r.dstp.at[q, z.M - 1] for q in range(z.Q)]

    def project_back(q):
        rows = rows_of(q)
        key_grad = nt(jnp.ones((16, z.C), BF16), r.gat[rows, :])[0:1]
        now = r.st[: z.N, rows]
        d_key = r.est[1, :, rows] - 2.0 * now * r.est[0, :, rows] - 2.0 * now * key_grad
        dst_mine[q][...] = jnp.concatenate([d_key, r.est[2, :, rows]], axis=0).astype(BF16)
        swap_dst[q].start(dst_mine[q])
        dlow_mine[q][...] = nt(r.ddr[rows, :], r.deltaw[...]).astype(BF16)
        swap_dlow[q].start(dlow_mine[q])

    def sums_back(q):
        rows = rows_of(q)
        swap_dlow[q].wait()
        swap_dst[q].wait()
        dlow = r.dlowp[q, 0].astype(F32)
        dst = r.dstp[q, 0].astype(F32)
        for slot in range(1, z.M):
            dlow = dlow + r.dlowp[q, slot].astype(F32)
            dst = dst + r.dstp[q, slot].astype(F32)
        r.dlow[rows, :] = dlow.astype(BF16)
        r.dlowt[:, rows] = dlow.T.astype(BF16)
        r.dst[:, rows] = dst.astype(BF16)
        dlow16, dst16 = dlow.astype(BF16), columns_of(dst)[:, : 2 * z.N].astype(BF16)

        def inputs_chunk(index):
            lanes = cut(index * 256, 256)
            r.su[rows, lanes] = nt(dlow16, r.loww[lanes, :]) + nn(dst16, r.statewt[:, lanes])

        each(z.C // 256, inputs_chunk)

    rim = [
        links.copy(
            r.dcp.at[q, pl.ds(0, 8), :],
            r.dcp.at[q, pl.ds(z.T, 8), :],
            links.sem(),
            links.sem(),
            seq=behind,
        )
        for q in range(z.Q)
    ]

    def conv_back(q):
        rows = rows_of(q)

        def conv_lanes(lanes):
            total = r.su[rows, lanes] + r.rd[rows, lanes] + r.skip[:, lanes] * r.dr[rows, lanes]
            value = r.conv[rows, lanes]
            gate = silu_parts(value)[0]
            d_conv = total * gate * (1.0 + value * (1.0 - gate))
            r.dcp[q, 0 : z.T, lanes] = d_conv
            r.vec[4:5, lanes] += jnp.sum(d_conv, axis=0, keepdims=True)
            for tap in range(4):
                r.vec[tap : tap + 1, lanes] += jnp.sum(
                    d_conv * r.xpad[q, 5 + tap : 5 + tap + z.T, lanes], axis=0, keepdims=True
                )

        lane_loop(conv_lanes)
        rim[q].start()

    def x_back(q):
        rim[q].wait_recv()

        def x_lanes(lanes):
            edge = r.dcp[q, z.T : z.T + 8, lanes]
            r.dcp[q, z.T : z.T + 8, lanes] = jnp.where(seq < z.S - 1, edge, 0.0)
            total = jnp.zeros((z.T, LANE), F32)
            for tap in range(4):
                total = total + r.convw[tap : tap + 1, lanes] * r.dcp[q, 3 - tap : 3 - tap + z.T, lanes]
            r.dxr[rows_of(q), lanes] = total.astype(BF16)

        lane_loop(x_lanes)

    swap_n = [Swap(z, links, lambda slot, q=q: r.nrecv.at[slot, rows_of(q), :]) for q in range(z.Q)]

    def normed_of(q, owner):
        return r.normed.at[rows_of(q), cut(owner * z.Df, z.Df)]

    def normed_part(q):
        rows = rows_of(q)

        def normed_to(index, means):
            away = index + 1
            owner = lax.rem(mp + away, z.M)
            for b in range(z.B):
                j = owner * z.B + b
                features = cut(j * z.Ds, z.Ds)
                part = nt(r.dxr[rows, :], r.wx[0, features, :]) + nt(r.dzr[rows, :], r.wx[1, features, :])
                r.normed[rows, features] = part.astype(BF16)
                scaled = part * r.tokg[j, rows, :].astype(F32)
                by_gain = jnp.sum(scaled * wide(r.inv[rows, :], z.Ds // LANE), axis=0, keepdims=True)
                for piece in range(z.Ds // LANE):
                    place = pl.ds(j * (z.Ds // LANE) + piece, 1)
                    value = by_gain[:, piece * LANE : (piece + 1) * LANE]
                    r.gv[place, :] = value if q == 0 else r.gv[place, :] + value
                means = means + jnp.sum(scaled * r.gain[:, features], axis=1, keepdims=True)

            @pl.when(away < z.M)
            def _():
                swap_n[q].one(normed_of(q, owner), away).start()

            return means

        means = lax.fori_loop(0, z.M, normed_to, jnp.zeros((z.T, 1), F32))
        mean_mine[:, rows] = jnp.broadcast_to(means, (z.T, LANE)).T[0:8]

    swap_m = Swap(z, links, lambda slot: r.mrow.at[slot])
    mean_mine = r.mrow.at[z.M - 1]

    def settle_back(level, q):
        back_take(level, q)
        if level < z.levels - 1:
            back_send(level + 1, q)

    most = scatter_o.by_need()
    scatter_o.first(into(near_o, term_o))
    scatter_o.second(onto(sum_o, term_o), send=True, masks=most[:1])
    totals_back(0)
    back_send(0, 0)
    each(z.M, branch_to)
    scatter_o.second(onto(sum_o, term_o), masks=most[1:])
    settle_back(0, 0)
    totals_back(1)
    back_send(0, 1)
    settle_back(0, 1)
    for mask in most[1:]:
        if mask & z.dims[0]:
            scatter_o.send(0, mask)
    scatter_1.first(into(near_i, term_1))
    for level in range(1, z.levels - 1):
        for q in range(z.Q):
            settle_back(level, q)
    for mask in most[1:]:
        if not mask & z.dims[0]:
            scatter_o.send(0, mask)
    scatter_1.second(onto(sum_1, term_1), send=True)
    for q in range(z.Q):
        back_take(z.levels - 1, q)
    for copy in scatter_1.sent[: len(z.masks)]:
        copy.wait_send()
    scatter_1.sent = scatter_1.sent[len(z.masks) :]
    tree_o.drain()
    walk_back(0)
    step_back(0)
    project_back(0)
    for step in range(depth - 1):
        scatter_o.fold(step)
    walk_back(1)
    for level in range(z.levels):
        pl.semaphore_signal(
            r.ready.at[level], inc=1, device_id=(seq ^ (1 << level), mp), device_id_type=MESH
        )
    step_back(1)
    project_back(1)
    for step in range(depth - 1):
        scatter_1.fold(step)
    sums_back(0)
    conv_back(0)

    last = depth - 1
    scatter_o.fold(last)

    def write_to(ref):
        def write(rows, value):
            ref[rows, :] = value

        return write

    scatter_o.total(write_to(r.dout))
    swap_out.wait()
    for away in range(1, z.M):
        owner = lax.rem(mp + away, z.M)
        swap_out.one(partial_of(owner), away).wait_send()

    def block_lanes(index):
        here = cut(index * LANE, LANE)
        total = r.normed[: z.R, cut(mp * z.Df + index * LANE, LANE)].astype(F32)
        for slot in range(z.M - 1):
            total = total + r.orecv[slot, :, here].astype(F32)
        r.blk[:, here] = (r.tok[:, here].astype(F32) + total).astype(BF16)

    each(z.Df // LANE, block_lanes)
    x_back(0)
    normed_part(0)
    sums_back(1)
    conv_back(1)

    def put_small(first, lanes, value):
        count, at = value.shape[0], 0
        while at < count:
            block, inside = divmod(first + at, sg_rows)
            take = min(count - at, sg_rows - inside)
            sgp.block(block, inside, take)[:, lanes] = value[at : at + take].astype(BF16)
            at += take

    low_t = r.low[...].astype(F32).T.astype(BF16)
    used = 2 * z.RK + 2 * z.N + SGVEC

    def small_chunk(index):
        lanes = cut(index * 256, 256)
        put_small(0, lanes, nn(low_t, r.ddr[:, lanes]))
        put_small(z.RK, lanes, nn(r.dlowt[...], r.u[:, lanes]))
        put_small(2 * z.RK, lanes, nn(r.dst[...], r.u[:, lanes]))
        put_small(2 * z.RK + 2 * z.N, lanes, r.vec[:, lanes])
        if used < z.S * sg_rows:
            put_small(used, lanes, jnp.zeros((z.S * sg_rows - used, 256), F32))

    each(z.C // 256, small_chunk)
    for level in range(z.levels):
        pl.semaphore_wait(r.ready.at[level], 1)
    scatter_s.first(lambda device, mask: sgp.block(device))
    x_back(1)

    def add_small(device, mask):
        block, term = sum_s.block(mask // 2), sgp.block(device)

        def one(rows):
            block[rows, :] = (block[rows, :].astype(F32) + term[rows, :].astype(F32)).astype(BF16)

        by_rows(sg_rows, one)

    scatter_s.second(add_small, send=True)
    scatter_0.first(into(near_i, term_0))
    scatter_0.second(onto(sum_0, term_0), send=True, masks=most[:1])
    for step in range(depth - 1):
        scatter_s.fold(step)
    scatter_0.second(onto(sum_0, term_0), send=True, masks=most[1:])

    normed_part(1)
    swap_m.start(mean_mine)

    gain_seq = SwapSeq(z, links, lambda slot: r.gvr.at[slot])
    gain_seq.start(r.gv)
    scatter_s.fold(last)

    def write_small(rows, value):
        small.block(seq)[rows, :] = value.astype(BF16)

    scatter_s.total(write_small)
    tree_s = TreeGather(
        z,
        links,
        lambda owner, h: small.block(owner, *halves(sg_rows)[h]),
        small.block,
    )
    tree_s.first()
    tree_s.second(0)
    tree_s.second(1)
    for step in range(depth - 1):
        scatter_0.fold(step)
    gain_seq.wait()
    gains = r.gv[...]
    for slot in range(z.S - 1):
        gains = gains + r.gvr[slot]
    r.gvs[...] = gains
    swap_g = Swap(z, links, lambda slot: r.gvm.at[slot])
    swap_g.start(r.gvs)
    tree_s.forward(0)
    tree_s.forward(1)
    scatter_1.fold(last)
    scatter_1.total(write_to(r.fac))
    store_1 = pltpu.make_async_copy(r.fac.at[pl.ds(0, z.Ds)], r.din.at[1], local.at[3])
    store_1.start()
    tree_s.settle()

    swap_m.wait()
    mean = r.mrow[0]
    for slot in range(1, z.M):
        mean = mean + r.mrow[slot]
    r.mean[...] = jnp.concatenate([mean] * (LANE // 8), axis=0).T * (1.0 / z.D)
    for swap in swap_n:
        swap.wait()

    def token_lanes(index):
        here = cut(index * LANE, LANE)
        inside = cut(mp * z.Df + index * LANE, LANE)
        for q in range(z.Q):
            rows = rows_of(q)
            total = r.normed[rows, inside].astype(F32)
            for slot in range(z.M - 1):
                total = total + r.nrecv[slot, rows, here].astype(F32)
            inv, x = r.inv[rows, :], r.tok[rows, here].astype(F32)
            value = inv * (total * r.gain[:, inside]) - x * (inv * inv * inv) * r.mean[rows, :]
            r.dtok[rows, here] = value + r.cot[rows, here] * seq_weight[q]

    each(z.Df // LANE, token_lanes)

    scatter_0.fold(last)
    scatter_0.total(write_to(r.s))
    store_0 = pltpu.make_async_copy(r.s.at[pl.ds(0, z.Ds)], r.din.at[0], local.at[4])
    store_0.start()
    tree_s.finish()
    for block in range(z.S):
        count = min(sg_rows, r.sg.shape[0] - block * sg_rows)
        if count > 0:
            r.sg[block * sg_rows : block * sg_rows + count, :] = small.block(block, 0, count)[...].astype(F32)
    swap_g.wait()
    gains = r.gvs[...]
    for slot in range(z.M - 1):
        gains = gains + r.gvm[slot]
    r.dgain[...] = gains

    hal.wait_send()
    for tree in (tree_x, tree_z, tree_s):
        tree.drain()
    for line in (*line_t, line_h, line_d):
        line.drain()
    for q in range(z.Q):
        swap_st[q].drain(st_mine[q])
        swap_low[q].drain(low_mine[q])
        swap_dlow[q].drain(dlow_mine[q])
        swap_dst[q].drain(dst_mine[q])
    swap_m.drain(mean_mine)
    swap_g.drain(r.gvs)
    gain_seq.drain()
    for away in range(1, z.M):
        owner = lax.rem(mp + away, z.M)
        for q in range(z.Q):
            swap_n[q].one(normed_of(q, owner), away).wait_send()
    for copy in carry_copies + rim:
        copy.wait_send()
    for scatter in (scatter_o, scatter_1, scatter_0, scatter_s):
        scatter.drain()
    store_1.wait()
    store_0.wait()


def finish_kernel(z, blk, dtok, dgain, din, dout, sg, *outs):
    a, b, c = z.RK, 2 * z.RK, 2 * z.RK + 2 * z.N
    o_blk, o_dtok, o_dgain, o_din, o_convw, o_convb, o_low, o_state, o_delta, o_dbias, o_skip, o_dout = outs
    o_blk[...] = blk[...]
    o_dtok[...] = dtok[...]
    o_dgain[...] = dgain[...]
    o_din[...] = din[...]
    o_dout[...] = dout[...]
    o_delta[...] = sg[0:a, :]
    o_state[...] = sg[b:c, :]
    o_convw[...] = sg[c : c + 4, :]
    o_convb[...] = sg[c + 4 : c + 5, :]
    o_dbias[...] = sg[c + 5 : c + 6, :]
    o_skip[...] = sg[c + 6 : c + 7, :]
    for at in range(0, z.C, LANE):
        o_low[at : at + LANE, :] = sg[a:b, at : at + LANE].T


def fused(z, tokens, norm_gain, in_weight, conv_weight, conv_bias, low_weight, state_weight, delta_weight,
          delta_bias, skip_gain, out_weight, cotangent, seq_group, group_weight):
    V = pl.BlockSpec(memory_space=pltpu.VMEM)
    A = pl.BlockSpec(memory_space=pl.ANY)
    SM = pl.BlockSpec(memory_space=pltpu.SMEM)
    row = lambda value: value.reshape(1, -1)
    operands = dict(
        tok=(V, tokens.reshape(z.R, z.Df)),
        cot=(V, cotangent.reshape(z.R, z.Df)),
        gain=(V, row(norm_gain)),
        win=(A, in_weight),
        wout=(A, out_weight),
        convw=(V, conv_weight),
        convb=(V, row(conv_bias)),
        dbias=(V, row(delta_bias)),
        skip=(V, row(skip_gain)),
        loww=(V, low_weight),
        statewt=(V, state_weight.T),
        deltaw=(V, delta_weight),
        seqg=(SM, seq_group),
        groupw=(SM, group_weight),
    )
    scratch = scratch_of(z)
    sg_used = 2 * z.RK + 2 * z.N + SGVEC
    outs = dict(
        blk=(V, (z.R, z.Df), BF16),
        dtok=(V, (z.R, z.Df), F32),
        dgain=(V, (z.D // LANE, LANE), F32),
        din=(A, (2, z.Ds, z.C), F32),
        dout=(V, (z.C, z.Ds), F32),
        sg=(V, (sg_used, z.C), F32),
    )
    result = pl.pallas_call(
        functools.partial(fused_kernel, z, [*operands, *outs, *scratch]),
        out_shape=[jax.ShapeDtypeStruct(shape, kind) for _, shape, kind in outs.values()],
        in_specs=[spec for spec, _ in operands.values()],
        out_specs=[spec for spec, _, _ in outs.values()],
        scratch_shapes=list(scratch.values()),
        compiler_params=pltpu.CompilerParams(
            collective_id=0, has_side_effects=True, vmem_limit_bytes=VMEM_BYTES
        ),
    )(*[value for _, value in operands.values()])
    whole = (V, (1, z.C), F32)
    last = dict(
        blk=(V, (z.R, z.Df), BF16),
        dtok=(V, (z.R, z.Df), F32),
        dgain=(V, (z.D // LANE, LANE), F32),
        din=(V, (2, z.Ds, z.C), F32),
        convw=(V, (4, z.C), F32),
        convb=whole,
        low=(V, (z.C, z.RK), F32),
        state=(V, (2 * z.N, z.C), F32),
        delta=(V, (z.RK, z.C), F32),
        dbias=whole,
        skip=whole,
        dout=(V, (z.C, z.Ds), F32),
    )
    done = pl.pallas_call(
        functools.partial(finish_kernel, z),
        out_shape=[jax.ShapeDtypeStruct(shape, kind) for _, shape, kind in last.values()],
        in_specs=[V] * 6,
        out_specs=[spec for spec, _, _ in last.values()],
        compiler_params=pltpu.CompilerParams(vmem_limit_bytes=VMEM_BYTES),
    )(*result)
    done = dict(zip(last, done))
    done.update(blk=done["blk"].reshape(tokens.shape), dtok=done["dtok"].reshape(tokens.shape))
    done.update(dgain=done["dgain"].reshape(z.D), state=done["state"].T)
    done.update({name: done[name][0] for name in ("convb", "dbias", "skip")})
    return tuple(done.values())


def local(mesh_shape, *arrays):
    tokens, norm_gain, in_weight, conv_weight = arrays[:4]
    state_weight, delta_weight = arrays[6], arrays[7]
    z = Sizes(
        mesh_shape,
        tokens.shape[0],
        tokens.shape[1],
        tokens.shape[2],
        norm_gain.shape[0],
        in_weight.shape[2],
        state_weight.shape[1] // 2,
        delta_weight.shape[0],
    )
    if z.fits(conv_weight.shape[0]):
        return fused(z, *arrays)
    return plain(*arrays)


def solution(mesh):
    placed = (
        P(None, "seq", "mp"),
        P(),
        P(None, "seq", "mp"),
        P(None, "mp"),
        P("mp"),
        P("mp", None),
        P("mp", None),
        P(None, "mp"),
        P("mp"),
        P("mp"),
        P("mp", "seq"),
        P(None, "seq", "mp"),
        P(),
        P(),
    )
    return jax.shard_map(
        functools.partial(local, dict(mesh.shape)),
        mesh=mesh,
        in_specs=placed,
        out_specs=(
            P(None, "seq", "mp"),
            P(None, "seq", "mp"),
            P(),
            P(None, "seq", "mp"),
            P(None, "mp"),
            P("mp"),
            P("mp", None),
            P("mp", None),
            P(None, "mp"),
            P("mp"),
            P("mp"),
            P("mp", "seq"),
        ),
        check_vma=False,
    )
```

```python
import functools
import math

import jax
import jax.numpy as jnp
from jax import lax
from jax.experimental import pallas as pl
from jax.experimental.pallas import tpu as pltpu
from jax.sharding import PartitionSpec as P

SEQ_MB = 1
NMB = 2
EPSILON = 1e-05
VMEM_BYTES = 64 * 1024 * 1024 - 64 * 1024


def from_behind(value, axis, steps):
    count = lax.axis_size(axis)
    leading, last = (max(0, -steps), min(count, count - steps))
    return lax.ppermute(value, axis, [(source, source + steps) for source in range(leading, last)])


def prefix(value, axis, join, neutral, backward):
    count, mine = (lax.axis_size(axis), lax.axis_index(axis))
    pieces = jax.tree.map(lambda part: lax.all_gather(part, axis), value)
    if backward:
        pieces = jax.tree.map(lambda part: part[::-1], pieces)
        mine = count - 1 - mine
    subtotal = jax.tree.map(
        lambda part, zero: jnp.full_like(part, 0) + jnp.asarray(zero, part.dtype), value, neutral
    )

    def lap(position, subtotal):
        longer = join(subtotal, jax.tree.map(lambda part: part[position], pieces))
        return jax.tree.map(lambda new, old: jnp.where(position < mine, new, old), longer, subtotal)

    return lax.fori_loop(0, count - 1, lap, subtotal)


def combine(earlier, later):
    return (earlier[0] * later[0], later[0] * earlier[1] + later[1])


def make_gates(delta_raw, b_state, inputs):
    beta_gate = jax.nn.sigmoid(delta_raw)
    key_sq = jnp.sum(b_state * b_state, axis=-1, keepdims=True)
    step_size = beta_gate / (1.0 + beta_gate * key_sq)
    decays = 1.0 - step_size[:, :, None, :] * (b_state * b_state)[:, :, :, None]
    source = (step_size * inputs)[:, :, None, :] * b_state[:, :, :, None]
    return (decays, source)


def to_blocks(value, span_rows):
    old_shape = value.shape
    reshaped = value.reshape((old_shape[0], old_shape[1] // span_rows, span_rows) + old_shape[2:])
    return jnp.swapaxes(reshaped, 0, 1)


def from_blocks(value):
    joined = jnp.swapaxes(value, 0, 1)
    old_shape = joined.shape
    return joined.reshape((old_shape[0], old_shape[1] * old_shape[2]) + old_shape[3:])


def forward_block(carry_pair, block_items):
    delta_raw, b_state, inputs = block_items
    decays, source = make_gates(delta_raw, b_state, inputs)
    run_prod, run_state = carry_pair
    prod_list = []
    state_list = []
    for row_idx in range(decays.shape[1]):
        run_prod = run_prod * decays[:, row_idx]
        run_state = decays[:, row_idx] * run_state + source[:, row_idx]
        prod_list.append(run_prod)
        state_list.append(run_state)
    return ((run_prod, run_state), (jnp.stack(prod_list, axis=1), jnp.stack(state_list, axis=1)))


def backward_block(carry_trio, block_items):
    delta_raw, b_state, inputs, read_grad, c_state = block_items
    decays, _ = make_gates(delta_raw, b_state, inputs)
    grad_next, dec_next, tail_prod = carry_trio
    span_rows = decays.shape[1]
    grad_list = [None] * span_rows
    tail_list = [None] * span_rows
    for row_idx in reversed(range(span_rows)):
        drive_term = read_grad[:, row_idx][:, None, :] * c_state[:, row_idx][:, :, None]
        grad_next = drive_term + dec_next * grad_next
        tail_prod = dec_next * tail_prod
        grad_list[row_idx] = grad_next
        tail_list[row_idx] = tail_prod
        dec_next = decays[:, row_idx]
    return (
        (grad_next, dec_next, tail_prod),
        (jnp.stack(grad_list, axis=1), jnp.stack(tail_list, axis=1)),
    )


def silu_slope(value):
    sig_value = jax.nn.sigmoid(value)
    return sig_value * (1.0 + value * (1.0 - sig_value))


def plain(
    tokens,
    norm_gain,
    in_weight,
    conv_weight,
    conv_bias,
    low_weight,
    state_weight,
    delta_weight,
    delta_bias,
    skip_gain,
    out_weight,
    cotangent,
    seq_group,
    group_weight,
):
    stretch = tokens.shape[1]
    feature_dev = tokens.shape[2]
    channels = in_weight.shape[2]
    model_width = norm_gain.shape[0]
    num_taps = conv_weight.shape[0]
    nstate = state_weight.shape[1] // 2
    span_rows = math.gcd(stretch, 8)
    picks = (
        seq_group[:, None] == jnp.arange(group_weight.shape[0], dtype=jnp.int32)[None, :]
    ).astype(jnp.float32)
    seq_weight = jnp.sum(picks * group_weight[None, :], axis=1)
    feature_start = lax.axis_index("mp") * feature_dev
    ones_state = jnp.ones((SEQ_MB, nstate, channels), jnp.float32)
    zero_state = jnp.zeros_like(ones_state)
    acc_in = jnp.zeros((2, model_width, channels), jnp.float32)
    acc_out = jnp.zeros((channels, model_width), jnp.float32)
    acc_gain = jnp.zeros_like(norm_gain)
    acc_conv = jnp.zeros_like(conv_weight)
    acc_cbias = jnp.zeros_like(conv_bias)
    acc_low = jnp.zeros(low_weight.shape, jnp.float32)
    acc_state = jnp.zeros(state_weight.shape, jnp.float32)
    acc_delta = jnp.zeros(delta_weight.shape, jnp.float32)
    acc_dbias = jnp.zeros_like(delta_bias)
    acc_skip = jnp.zeros_like(skip_gain)
    outputs = []
    input_grads = []
    for micro_idx in range(NMB):
        whole_in, whole_out = (
            lax.all_gather(in_weight, "seq", axis=1, tiled=True),
            lax.all_gather(out_weight, "seq", axis=1, tiled=True),
        )
        first_seq = micro_idx * SEQ_MB
        block_tokens = tokens[first_seq : first_seq + SEQ_MB]
        full_tokens = lax.all_gather(block_tokens, "mp", axis=2, tiled=True).astype(jnp.float32)
        inv_rms = lax.rsqrt(jnp.mean(full_tokens * full_tokens, axis=-1, keepdims=True) + EPSILON)
        normed = (full_tokens * inv_rms * norm_gain).astype(jnp.bfloat16)
        both_parts = jnp.einsum(
            "scd,kdi->ksci", normed, whole_in, preferred_element_type=jnp.float32
        )
        x_round = both_parts[0].astype(jnp.bfloat16)
        z_part = both_parts[1]
        rim_rows = from_behind(x_round[:, stretch - (num_taps - 1) :], "seq", 1)
        padded = jnp.concatenate([rim_rows, x_round], axis=1).astype(jnp.float32)
        conv_sum = conv_bias + jnp.zeros((SEQ_MB, stretch, channels), jnp.float32)
        for tap_index in range(num_taps):
            conv_sum = (
                conv_sum + conv_weight[tap_index] * padded[:, tap_index : tap_index + stretch]
            )
        inputs_round = jax.nn.silu(conv_sum).astype(jnp.bfloat16)
        inputs_f = inputs_round.astype(jnp.float32)
        low_part = jnp.einsum(
            "sci,ir->scr", inputs_round, low_weight, preferred_element_type=jnp.float32
        )
        state_part = jnp.einsum(
            "sci,ir->scr", inputs_round, state_weight, preferred_element_type=jnp.float32
        )
        delta_low, state_proj = lax.psum((low_part, state_part), "mp")
        delta_round = delta_low.astype(jnp.bfloat16)
        delta_raw = (
            jnp.einsum("scr,ri->sci", delta_round, delta_weight, preferred_element_type=jnp.float32)
            + delta_bias
        )
        b_state = state_proj[..., :nstate]
        c_state = state_proj[..., nstate:]
        delta_blocks = to_blocks(delta_raw, span_rows)
        b_blocks = to_blocks(b_state, span_rows)
        c_blocks = to_blocks(c_state, span_rows)
        in_blocks = to_blocks(inputs_f, span_rows)
        stretch_pair, (prod_blocks, local_blocks) = lax.scan(
            forward_block, (ones_state, zero_state), (delta_blocks, b_blocks, in_blocks)
        )
        carried = prefix(stretch_pair, "seq", combine, (ones_state, zero_state), False)
        states = from_blocks(local_blocks) + from_blocks(prod_blocks) * carried[1][:, None]
        before = jnp.concatenate([carried[1][:, None], states[:, :-1]], axis=1)
        read_rec = jnp.einsum("scni,scn->sci", states, c_state)
        read_out = read_rec + skip_gain * inputs_f
        z_gate = jax.nn.silu(z_part)
        gated_round = (read_out * z_gate).astype(jnp.bfloat16)
        out_part = jnp.einsum(
            "sci,id->scd", gated_round, whole_out, preferred_element_type=jnp.float32
        )
        branch = lax.psum_scatter(out_part, "mp", scatter_dimension=2, tiled=True)
        outputs.append((block_tokens.astype(jnp.float32) + branch).astype(jnp.bfloat16))
        d_out = (
            cotangent[first_seq : first_seq + SEQ_MB]
            * seq_weight[first_seq : first_seq + SEQ_MB][:, None, None]
        )
        d_branch = lax.all_gather(d_out.astype(jnp.bfloat16), "mp", axis=2, tiled=True)
        acc_out = acc_out + jnp.einsum(
            "sci,scd->id", gated_round, d_branch, preferred_element_type=jnp.float32
        )
        d_gated = jnp.einsum("scd,id->sci", d_branch, whole_out, preferred_element_type=jnp.float32)
        d_read = d_gated * z_gate
        d_zpart = d_gated * read_out * silu_slope(z_part)
        acc_skip = acc_skip + jnp.sum(d_read * inputs_f, axis=(0, 1))
        read_blocks_grad = to_blocks(d_read, span_rows)
        (last_grad, first_dec, _), (grad_blocks, tail_blocks) = lax.scan(
            backward_block,
            (zero_state, ones_state, ones_state),
            (delta_blocks, b_blocks, in_blocks, read_blocks_grad, c_blocks),
            reverse=True,
        )
        tail_grad = first_dec * last_grad
        crossing = prefix(
            (stretch_pair[0], tail_grad), "seq", combine, (ones_state, zero_state), True
        )
        state_grad = from_blocks(grad_blocks) + from_blocks(tail_blocks) * crossing[1][:, None]
        _, gate_pullback = jax.vjp(make_gates, delta_raw, b_state, inputs_f)
        d_delta, d_bstate, d_inputs_state = gate_pullback((state_grad * before, state_grad))
        d_cstate = jnp.einsum("scni,sci->scn", states, d_read)
        acc_dbias = acc_dbias + jnp.sum(d_delta, axis=(0, 1))
        d_delta_round = d_delta.astype(jnp.bfloat16)
        acc_delta = acc_delta + jnp.einsum(
            "scr,sci->ri", delta_round, d_delta_round, preferred_element_type=jnp.float32
        )
        low_grad_part = jnp.einsum(
            "sci,ri->scr", d_delta_round, delta_weight, preferred_element_type=jnp.float32
        )
        state_grad_part = jnp.concatenate([d_bstate, d_cstate], axis=-1)
        d_low, d_state = lax.psum((low_grad_part, state_grad_part), "mp")
        d_low_round = d_low.astype(jnp.bfloat16)
        d_state_round = d_state.astype(jnp.bfloat16)
        acc_low = acc_low + jnp.einsum(
            "sci,scr->ir", inputs_round, d_low_round, preferred_element_type=jnp.float32
        )
        acc_state = acc_state + jnp.einsum(
            "sci,scr->ir", inputs_round, d_state_round, preferred_element_type=jnp.float32
        )
        d_inputs = d_read * skip_gain + d_inputs_state
        d_inputs = d_inputs + jnp.einsum(
            "scr,ir->sci", d_low_round, low_weight, preferred_element_type=jnp.float32
        )
        d_inputs = d_inputs + jnp.einsum(
            "scr,ir->sci", d_state_round, state_weight, preferred_element_type=jnp.float32
        )
        d_conv = d_inputs * silu_slope(conv_sum)
        acc_cbias = acc_cbias + jnp.sum(d_conv, axis=(0, 1))
        tap_grads = []
        d_padded = jnp.zeros((SEQ_MB, stretch + num_taps - 1, channels), jnp.float32)
        for tap_index in range(num_taps):
            tap_grads.append(
                jnp.sum(d_conv * padded[:, tap_index : tap_index + stretch], axis=(0, 1))
            )
            d_padded = d_padded + jnp.pad(
                conv_weight[tap_index] * d_conv,
                ((0, 0), (tap_index, num_taps - 1 - tap_index), (0, 0)),
            )
        acc_conv = acc_conv + jnp.stack(tap_grads)
        back_rim = from_behind(d_padded[:, : num_taps - 1], "seq", -1)
        d_xpart = d_padded[:, num_taps - 1 :] + jnp.pad(
            back_rim, ((0, 0), (stretch - (num_taps - 1), 0), (0, 0))
        )
        d_parts_round = jnp.stack([d_xpart, d_zpart]).astype(jnp.bfloat16)
        acc_in = acc_in + jnp.einsum(
            "scd,ksci->kdi", normed, d_parts_round, preferred_element_type=jnp.float32
        )
        norm_part = jnp.einsum(
            "ksci,kdi->scd", d_parts_round, whole_in, preferred_element_type=jnp.float32
        )
        d_normed = lax.psum(norm_part, "mp")
        acc_gain = acc_gain + jnp.sum(d_normed * full_tokens * inv_rms, axis=(0, 1))
        scaled = d_normed * norm_gain
        d_full = inv_rms * scaled - full_tokens * (inv_rms * inv_rms * inv_rms) * jnp.mean(
            scaled * full_tokens, axis=-1, keepdims=True
        )
        d_mine = lax.dynamic_slice_in_dim(d_full, feature_start, feature_dev, 2)
        input_grads.append(d_out + d_mine)
    d_in_weight, d_out_weight = (
        lax.psum_scatter(acc_in, "seq", scatter_dimension=1, tiled=True),
        lax.psum_scatter(acc_out, "seq", scatter_dimension=1, tiled=True),
    )
    summed = lax.psum(
        (acc_gain, acc_conv, acc_cbias, acc_low, acc_state, acc_delta, acc_dbias, acc_skip), "seq"
    )
    return (
        jnp.concatenate(outputs, axis=0),
        jnp.concatenate(input_grads, axis=0),
        summed[0],
        d_in_weight,
        summed[1],
        summed[2],
        summed[3],
        summed[4],
        summed[5],
        summed[6],
        summed[7],
        d_out_weight,
    )


MESH = pl.DeviceIdType.MESH
F32 = jnp.float32
BF16 = jnp.bfloat16
LANE = 128
GRP = 16
PADV = 8
SGVEC = 16


def nn(a, b):
    return lax.dot_general(a, b, (((1,), (0,)), ((), ())), preferred_element_type=F32)


def nt(a, b):
    return lax.dot_general(a, b, (((1,), (1,)), ((), ())), preferred_element_type=F32)


def tn(a, b):
    return lax.dot_general(a, b, (((0,), (0,)), ((), ())), preferred_element_type=F32)


def cut(start, size):
    return pl.ds(pl.multiple_of(start, size), size)


def each(count, step):
    lax.fori_loop(0, count, lambda index, unused: (step(index), unused)[1], 0)


def by_rows(count, step):
    size = 32 if count % 32 == 0 else 16
    each(count // size, lambda index: step(cut(index * size, size)))


def wide(value, times):
    return jnp.concatenate([value] * times, axis=1) if times > 1 else value


def groups_fit(channels):
    return (LANE // GRP) % min(LANE // GRP, channels // (GRP * GRP)) == 0


class Sizes:
    def __init__(self, mesh_shape, nseq, stretch, feature_dev, model, channels, nstate, rank):
        self.S, self.M = mesh_shape["seq"], mesh_shape["mp"]
        self.Q, self.T, self.Df, self.D, self.C = nseq, stretch, feature_dev, model, channels
        self.N, self.RK = nstate, rank
        self.R = nseq * stretch
        self.Ds = model // self.S
        self.B = max(1, feature_dev // self.Ds)
        self.levels = self.S.bit_length() - 1
        self.dims = [1 << bit for bit in range(1, self.levels)]
        self.masks = [2 * value for value in range(self.S // 2)]
        self.rows_sg = -(-(2 * rank + 2 * nstate + SGVEC) // (self.S * 16)) * 16
        self.E = max(self.R, self.Ds)

    def order(self, half):
        turn = half * (len(self.dims) // 2)
        return self.dims[turn:] + self.dims[:turn]

    def fits(self, taps):
        return (
            self.S in (4, 8)
            and self.M > 1
            and self.Q == 2
            and self.T == LANE
            and self.Ds == 256
            and self.Df % self.Ds == 0
            and self.C % 512 == 0
            and self.N == GRP
            and self.RK == LANE
            and taps == 4
            and self.D >= 2 * self.C
            and groups_fit(self.C)
            and self.C * self.D <= (1 << 21)
        )


class Bunch:
    def __init__(self, names, values):
        self.__dict__.update(zip(names, values))


class Rows:
    def __init__(self, ref, base, rows, count):
        self.ref, self.base, self.rows, self.end = ref, base, rows, base + rows * count

    def block(self, index, start=0, size=None):
        first = pl.multiple_of(self.base + index * self.rows + start, 16)
        return self.ref.at[pl.ds(first, self.rows if size is None else size), :]


class Links:
    def __init__(self, sems, seq, mp):
        self.sems, self.used, self.seq, self.mp = sems, 0, seq, mp

    def sem(self, count=1):
        first = self.used
        self.used += count
        return first

    def copy(self, src, dst, send, recv, seq=None, mp=None):
        target = (self.seq if seq is None else seq, self.mp if mp is None else mp)
        return pltpu.make_async_remote_copy(
            src_ref=src,
            dst_ref=dst,
            send_sem=self.sems.at[send],
            recv_sem=self.sems.at[recv],
            device_id=target,
            device_id_type=MESH,
        )

    def arrived(self, dst, recv):
        self.copy(dst, dst, recv, recv).wait_recv()


class TreeGather:
    def __init__(self, z, links, half_view, whole_view):
        self.z, self.links, self.half, self.whole = z, links, half_view, whole_view
        self.recv = {(mask, h): links.sem() for mask in z.masks[1:] for h in range(2)}
        self.near = {mask: links.sem() for mask in z.masks}
        self.sent = []

    def push(self, mask, h, dim):
        view = self.half(self.links.seq ^ mask, h)
        copy = self.links.copy(
            view, view, self.links.sem(), self.recv[mask | dim, h], seq=self.links.seq ^ dim
        )
        copy.start()
        self.sent.append(copy)

    def take(self, mask, h):
        self.links.arrived(self.half(self.links.seq ^ mask, h), self.recv[mask, h])

    def hand(self, mask):
        view = self.whole(self.links.seq ^ mask)
        copy = self.links.copy(view, view, self.links.sem(), self.near[mask], seq=self.links.seq ^ 1)
        copy.start()
        self.sent.append(copy)

    def first(self):
        for h in range(2):
            self.push(0, h, self.z.order(h)[0])

    def second(self, h):
        for dim in self.z.order(h)[1:]:
            self.push(0, h, dim)
        if h == 0:
            self.hand(0)

    def forward(self, h):
        order = self.z.order(h)
        if len(order) > 1:
            self.take(order[0], h)
            self.push(order[0], h, order[1])

    def settle(self, far=None):
        for mask in sorted(self.z.masks[1:], key=lambda mask: bin(mask).count("1")):
            if far is not None and far != (bin(mask).count("1") > 1):
                continue
            for h in range(2):
                order = self.z.order(h)
                if len(order) == 1 or mask != order[0]:
                    self.take(mask, h)
            self.hand(mask)

    def finish(self):
        for mask in self.z.masks:
            self.links.arrived(self.whole(self.links.seq ^ 1 ^ mask), self.near[mask])

    def drain(self):
        for copy in self.sent:
            copy.wait_send()


class LineGather:
    def __init__(self, z, links, view):
        self.z, self.links, self.view = z, links, view
        self.recv = links.sem(z.M)
        self.send = links.sem(2 * z.M)

    def parts(self, depth):
        for side, way in enumerate((1, -1)):
            owner, target = self.links.mp - way * depth, self.links.mp + way
            held = (owner >= 0) & (owner < self.z.M)
            more = held & (target >= 0) & (target < self.z.M)
            yield side, owner, target, held, more

    def copy(self, side, depth, owner, target):
        view = self.view(owner)
        return self.links.copy(view, view, self.send + 2 * depth + side, self.recv + owner, mp=target)

    def step(self, depth):
        for side, owner, target, held, more in self.parts(depth):
            if depth:

                @pl.when(held)
                def _():
                    self.links.arrived(self.view(owner), self.recv + owner)

            @pl.when(more)
            def _():
                self.copy(side, depth, owner, target).start()

    def drain(self):
        for depth in range(self.z.M):
            for side, owner, target, held, more in self.parts(depth):

                @pl.when(more)
                def _():
                    self.copy(side, depth, owner, target).wait_send()


class Swap:
    def __init__(self, z, links, slot):
        self.z, self.links, self.slot = z, links, slot
        self.recv = links.sem(z.M)
        self.send = links.sem(z.M)

    def one(self, src, away):
        target = lax.rem(self.links.mp + away, self.z.M)
        return self.links.copy(src, self.slot(away - 1), self.send + away, self.recv + away, mp=target)

    def start(self, src):
        for away in range(1, self.z.M):
            self.one(src, away).start()

    def wait(self):
        for away in range(1, self.z.M):
            self.links.arrived(self.slot(away - 1), self.recv + away)

    def drain(self, src):
        for away in range(1, self.z.M):
            self.one(src, away).wait_send()


class SwapSeq:
    def __init__(self, z, links, slot):
        self.links, self.slot = links, slot
        self.pairs = [(other, links.sem(), links.sem()) for other in range(1, z.S)]
        self.sent = []

    def start(self, src):
        for other, send, recv in self.pairs:
            copy = self.links.copy(src, self.slot(other - 1), send, recv, seq=self.links.seq ^ other)
            copy.start()
            self.sent.append(copy)

    def wait(self):
        for other, send, recv in self.pairs:
            self.links.arrived(self.slot(other - 1), recv)

    def drain(self):
        for copy in self.sent:
            copy.wait_send()


def halves(rows):
    first = -(-rows // 32) * 16
    return (0, first), (first, rows - first)


class Scatter:
    def __init__(self, z, links, out, sums, far, rows):
        self.z, self.links, self.out, self.sums, self.far, self.rows = z, links, out, sums, far, rows
        self.near = {mask: links.sem() for mask in z.masks}
        self.near_send = {mask: links.sem() for mask in z.masks}
        self.sent = []
        self.hops = {}
        place = 0
        for h in range(2):
            order = z.order(h)
            for step, dim in enumerate(order):
                for mask in z.masks:
                    if mask & dim and not any(mask & other for other in order[:step]):
                        self.hops[h, step, mask] = (dim, links.sem(), links.sem(), place)
                        place += 1
        self.slots = place

    def half(self, mask, h):
        start, size = halves(self.rows)[h]
        return self.sums.block(mask // 2, start, size)

    def came(self, h, place):
        return self.far.block(place, 0, halves(self.rows)[h][1])

    def first(self, make):
        links = self.links
        for mask in self.by_need():
            src = make(links.seq ^ 1 ^ mask, mask)
            copy = links.copy(src, self.sums.block(mask // 2), self.near_send[mask], self.near[mask], seq=links.seq ^ 1)
            copy.start()
            self.sent.append(copy)

    def by_need(self):
        return sorted(self.z.masks, key=lambda mask: -bin(mask).count("1"))

    def second(self, add, send=False, masks=None):
        links = self.links
        for mask in self.by_need() if masks is None else masks:
            links.arrived(self.sums.block(mask // 2), self.near[mask])
            add(links.seq ^ mask, mask)
            if send:
                self.send(0, mask)

    def send(self, step, only=None):
        links = self.links
        for (h, at, mask), (dim, send, recv, place) in self.hops.items():
            if at == step and only in (None, mask):
                copy = links.copy(
                    self.half(mask, h), self.came(h, place), send, recv, seq=links.seq ^ dim
                )
                copy.start()
                self.sent.append(copy)

    def fold(self, step):
        links = self.links
        for (h, at, mask), (dim, send, recv, place) in self.hops.items():
            if at != step:
                continue
            links.arrived(self.came(h, place), recv)
            if step < len(self.z.dims) - 1:
                half, came = self.half(mask ^ dim, h), self.came(h, place)

                def add(rows):
                    half[rows, :] = (half[rows, :].astype(F32) + came[rows, :].astype(F32)).astype(BF16)

                by_rows(halves(self.rows)[h][1], add)
        if step < len(self.z.dims) - 1:
            self.send(step + 1)

    def total(self, write):
        last = len(self.z.dims) - 1
        for (h, at, mask), (dim, send, recv, place) in self.hops.items():
            if at == last:
                half, came = self.half(0, h), self.came(h, place)
                first, count = halves(self.rows)[h]

                def add(rows):
                    value = half[rows, :].astype(F32) + came[rows, :].astype(F32)
                    write(pl.ds(pl.multiple_of(first + rows.start, 16), rows.size), value)

                by_rows(count, add)

    def drain(self):
        for copy in self.sent:
            copy.wait_send()


def slots_of(z):
    return Scatter(z, Links(None, 0, 0), None, None, None, 0).slots


def scratch_of(z):
    V = pltpu.VMEM
    half = z.S // 2
    slots = slots_of(z)
    return dict(
        tok=V((z.R, z.Df), BF16),
        cot=V((z.R, z.Df), F32),
        gain=V((1, z.D), F32),
        convw=V((4, z.C), F32),
        convb=V((1, z.C), F32),
        dbias=V((1, z.C), F32),
        skip=V((1, z.C), F32),
        loww=V((z.C, z.RK), BF16),
        statewt=V((2 * z.N, z.C), BF16),
        deltaw=V((z.RK, z.C), BF16),
        tokg=V((z.S, z.R, z.Ds), BF16),
        halg=V((z.S, 16, z.Ds), BF16),
        hals=V((z.B, 16, z.Ds), BF16),
        db=V((z.R, z.D), BF16),
        inv=V((z.R, LANE), F32),
        normed=V((z.R + 16, z.D), BF16),
        normt=V((z.D, z.R), BF16),
        wx=V((2, z.D, z.C), BF16),
        wo=V((z.C, z.D), BF16),
        xpad=V((z.Q, 8 + z.T, z.C), F32),
        dcp=V((z.Q, z.T + 8, z.C), F32),
        conv=V((z.E, z.C), F32),
        s=V((z.E, z.C), F32),
        su=V((z.R, z.C), F32),
        fac=V((z.E, z.C), F32),
        zp=V((z.R, z.C), F32),
        rd=V((z.R, z.C), F32),
        dr=V((z.R, z.C), F32),
        u=V((z.R, z.C), BF16),
        gat=V((z.R, z.C), BF16),
        gatt=V((z.C, z.R), BF16),
        ddr=V((z.R, z.C), BF16),
        dzr=V((z.R, z.C), BF16),
        dxr=V((z.R, z.C), BF16),
        lowp=V((z.Q, z.M, z.T, z.RK), BF16),
        stp=V((z.Q, z.M, 2 * z.N, z.T), F32),
        low=V((z.R, z.RK), BF16),
        dlow=V((z.R, z.RK), BF16),
        dlowt=V((z.RK, z.R), BF16),
        dst=V((2 * z.N, z.R), BF16),
        st=V((2 * z.N, z.R), F32),
        blkb=V((z.R, GRP * z.N), BF16),
        blkk=V((z.R, GRP * z.N), BF16),
        blkc=V((z.R, GRP * z.N), BF16),
        bc=V((z.Q, z.T, 2 * z.N, LANE), F32),
        hist=V((z.Q * (z.T + 1) * z.N, z.C), BF16),
        ptot=V((z.Q, z.N, z.C), F32),
        stot=V((z.Q, z.N, z.C), F32),
        ppre=V((z.Q, z.N, z.C), F32),
        spre=V((z.Q, z.N, z.C), F32),
        csend=V((z.levels, z.Q, 2, z.N, z.C), BF16),
        crecv=V((z.levels, z.Q, 2, z.N, z.C), BF16),
        bsend=V((z.levels, z.Q, z.N, z.C), BF16),
        brecv=V((z.levels, z.Q, z.N, z.C), BF16),
        est=V((3, z.N, z.R), F32),
        dlowp=V((z.Q, z.M, z.T, z.RK), BF16),
        dstp=V((z.Q, z.M, 2 * z.N, z.T), BF16),
        orecv=V((z.M - 1, z.R, z.Df), BF16),
        nrecv=V((z.M - 1, z.R, z.Df), BF16),
        near_o=V((half * z.C, z.Ds), BF16),
        sum_o=V((half * z.C, z.Ds), BF16),
        far_o=V((slots * (z.C // 2), z.Ds), BF16),
        near_i=V((half * z.Ds, z.C), BF16),
        sum_1=V((half * z.Ds, z.C), BF16),
        far_1=V((slots * (z.Ds // 2), z.C), BF16),
        vec=V((SGVEC, z.C), F32),
        gv=V((z.D // LANE, LANE), F32),
        gvs=V((z.D // LANE, LANE), F32),
        gvr=V((z.S - 1, z.D // LANE, LANE), F32),
        gvm=V((z.M - 1, z.D // LANE, LANE), F32),
        mean=V((z.R, LANE), F32),
        mrow=V((z.M, 8, z.R), F32),
        sems=pltpu.SemaphoreType.DMA((420,)),
        local=pltpu.SemaphoreType.DMA((16,)),
        ready=pltpu.SemaphoreType.REGULAR((z.levels,)),
    )


def silu_parts(value):
    gate = 1.0 / (1.0 + jnp.exp(-value))
    return gate, value * gate


def fused_kernel(z, names, *refs):
    r = Bunch(names, refs)
    seq, mp = lax.axis_index("seq"), lax.axis_index("mp")
    links = Links(r.sems, seq, mp)
    lanes_all = z.C // LANE
    first_block = mp * z.B

    def lane_loop(step):
        each(z.C // LANE, lambda index: step(cut(index * LANE, LANE)))

    local = r.local
    mine_in = lambda k: r.wx.at[k, cut(seq * z.Ds, z.Ds), :]
    loads = [
        pltpu.make_async_copy(r.win.at[0], mine_in(0), local.at[0]),
        pltpu.make_async_copy(r.win.at[1], mine_in(1), local.at[1]),
        pltpu.make_async_copy(r.wout, r.wo.at[:, cut(seq * z.Ds, z.Ds)], local.at[2]),
    ]
    pairs = [
        (r.tok_in, r.tok),
        (r.cot_in, r.cot),
        (r.gain_in, r.gain),
        (r.convw_in, r.convw),
        (r.convb_in, r.convb),
        (r.dbias_in, r.dbias),
        (r.skip_in, r.skip),
        (r.loww_in, r.loww),
        (r.statewt_in, r.statewt),
        (r.deltaw_in, r.deltaw),
    ]
    own = [pltpu.make_async_copy(src, dst, local.at[5 + index]) for index, (src, dst) in enumerate(pairs)]
    own[0].start()
    for load in loads:
        load.start()
    for copy in own[1:]:
        copy.start()
    own[0].wait()
    for b in range(z.B):
        r.tokg[first_block + b] = r.tok[:, b * z.Ds : (b + 1) * z.Ds]
        tails = [
            r.tok[q * z.T + z.T - 16 : q * z.T + z.T, b * z.Ds : (b + 1) * z.Ds].astype(F32)[8:]
            for q in range(z.Q)
        ]
        r.hals[b] = jnp.concatenate(tails, axis=0).astype(BF16)

    barrier = pltpu.get_barrier_semaphore()
    ahead, behind = lax.rem(seq + 1, z.S), lax.rem(seq + z.S - 1, z.S)
    partners = [(seq ^ other, mp) for other in range(1, z.S)] + [(ahead, mp), (behind, mp)]
    partners += [(seq, lax.rem(mp + away, z.M)) for away in range(1, z.M)]
    for partner in partners:
        pl.semaphore_signal(barrier, inc=1, device_id=partner, device_id_type=MESH)
    pl.semaphore_wait(barrier, len(partners))

    def of_in(k):
        def half(owner, h):
            return r.wx.at[k, cut(owner * z.Ds + h * (z.Ds // 2), z.Ds // 2), :]

        return TreeGather(z, links, half, lambda owner: r.wx.at[k, cut(owner * z.Ds, z.Ds), :])

    tree_x, tree_z = of_in(0), of_in(1)
    tree_o = TreeGather(
        z,
        links,
        lambda owner, h: r.wo.at[pl.ds(h * (z.C // 2), z.C // 2), cut(owner * z.Ds, z.Ds)],
        lambda owner: r.wo.at[:, cut(owner * z.Ds, z.Ds)],
    )
    line_t = [
        LineGather(z, links, lambda owner, q=q: r.tokg.at[pl.ds(owner * z.B, z.B), pl.ds(q * z.T, z.T), :])
        for q in range(z.Q)
    ]
    line_h = LineGather(z, links, lambda owner: r.halg.at[pl.ds(owner * z.B, z.B)])
    line_d = LineGather(z, links, lambda owner: r.db.at[:, cut(owner * z.Df, z.Df)])
    depth = len(z.dims)

    hal_send, hal_recv = links.sem(), links.sem()
    hal_mine = r.halg.at[pl.ds(first_block, z.B)]
    hal = links.copy(r.hals, hal_mine, hal_send, hal_recv, seq=ahead)
    hal.start()
    for line in line_t:
        line.step(0)
    loads[0].wait()
    tree_x.first()
    tree_x.second(0)
    tree_x.second(1)

    for copy in own[1:]:
        copy.wait()

    def weight_of(q):
        total = jnp.float32(0.0)
        for group in range(r.groupw.shape[0]):
            total = total + jnp.where(r.seqg[q] == group, r.groupw[group], 0.0)
        return total

    seq_weight = [weight_of(q) for q in range(z.Q)]
    for q in range(z.Q):
        rows = pl.ds(q * z.T, z.T)
        for b in range(z.B):
            part = r.cot[rows, b * z.Ds : (b + 1) * z.Ds] * seq_weight[q]
            r.db[rows, cut((first_block + b) * z.Ds, z.Ds)] = part.astype(BF16)

    links.arrived(hal_mine, hal_recv)
    line_h.step(0)
    for line in line_t:
        line.step(1)
    tree_x.forward(0)
    tree_x.forward(1)
    loads[1].wait()
    tree_z.first()
    tree_z.second(0)
    tree_z.second(1)
    line_h.step(1)
    for far in range(2, z.M):
        for line in line_t:
            line.step(far)
        line_h.step(far)
        if far == 2:
            tree_x.settle(False)
    if z.M == 2:
        tree_x.settle(False)
    line_d.step(0)

    def add_squares(j, total):
        part = r.tokg[j].astype(F32)
        edge = r.halg[j].astype(F32)
        return (
            total[0] + jnp.sum(part * part, axis=1, keepdims=True),
            total[1] + jnp.sum(edge * edge, axis=1, keepdims=True),
        )

    squares = lax.fori_loop(
        0, z.S, add_squares, (jnp.zeros((z.R, 1), F32), jnp.zeros((16, 1), F32))
    )
    inv = lax.rsqrt(squares[0] * (1.0 / z.D) + EPSILON)
    inv_edge = lax.rsqrt(squares[1] * (1.0 / z.D) + EPSILON)
    r.inv[...] = jnp.broadcast_to(inv, (z.R, LANE))

    def norm_block(j):
        features = cut(j * z.Ds, z.Ds)
        gain = r.gain[:, features]
        normed = r.tokg[j].astype(F32) * wide(r.inv[...], z.Ds // LANE) * gain
        r.normed[: z.R, features] = normed.astype(BF16)
        edge = r.halg[j].astype(F32) * inv_edge * gain
        r.normed[z.R :, features] = edge.astype(BF16)
        r.normt[features, :] = normed.T.astype(BF16)

    each(z.S, norm_block)
    tree_x.settle(True)
    tree_x.finish()

    def x_chunk(index):
        lanes = cut(index * 256, 256)
        part = nn(r.normed[...], r.wx[0, :, lanes]).astype(BF16).astype(F32)
        for q in range(z.Q):
            edge = part[z.R + 8 * q : z.R + 8 * q + 8]
            r.xpad[q, 0:8, lanes] = jnp.where(seq > 0, edge, 0.0)
            r.xpad[q, 8 : 8 + z.T, lanes] = part[q * z.T : (q + 1) * z.T]

    each(z.C // 256, x_chunk)
    tree_z.forward(0)
    tree_z.forward(1)
    loads[2].wait()
    tree_o.first()
    tree_o.second(0)

    def rows_of(q):
        return pl.ds(q * z.T, z.T)

    def conv(q):
        def conv_lanes(lanes):
            total = jnp.broadcast_to(r.convb[:, lanes], (z.T, LANE))
            for tap in range(4):
                total = total + r.convw[tap : tap + 1, lanes] * r.xpad[q, 5 + tap : 5 + tap + z.T, lanes]
            r.conv[rows_of(q), lanes] = total
            r.u[rows_of(q), lanes] = silu_parts(total)[1].astype(BF16)

        lane_loop(conv_lanes)

    swap_low = [Swap(z, links, lambda slot, q=q: r.lowp.at[q, slot]) for q in range(z.Q)]
    swap_st = [Swap(z, links, lambda slot, q=q: r.stp.at[q, slot]) for q in range(z.Q)]
    low_mine = [r.lowp.at[q, z.M - 1] for q in range(z.Q)]
    st_mine = [r.stp.at[q, z.M - 1] for q in range(z.Q)]

    def project(q):
        u = r.u[rows_of(q), :]
        st_mine[q][...] = nt(r.statewt[...], u)
        swap_st[q].start(st_mine[q])
        low_mine[q][...] = nn(u, r.loww[...]).astype(BF16)
        swap_low[q].start(low_mine[q])

    rows_i = lax.broadcasted_iota(jnp.int32, (z.T, GRP * z.N), 0)
    cols_i = lax.broadcasted_iota(jnp.int32, (z.T, GRP * z.N), 1)
    diagonal = lax.rem(rows_i, GRP) == cols_i // z.N
    rep_n = lax.broadcasted_iota(jnp.int32, (2 * z.N, GRP * z.N), 0)
    rep_j = lax.rem(lax.broadcasted_iota(jnp.int32, (2 * z.N, GRP * z.N), 1), z.N)
    rep_b = (rep_n == rep_j).astype(BF16)
    rep_c = (rep_n == rep_j + z.N).astype(BF16)
    only_b = lax.broadcasted_iota(jnp.int32, (z.T, LANE), 1) < z.N

    def columns_of(value):
        return jnp.concatenate([value, jnp.zeros((LANE - 2 * z.N, z.T), F32)], axis=0).T

    def keys(q):
        swap_st[q].wait()
        st = r.stp[q, 0]
        for slot in range(1, z.M):
            st = st + r.stp[q, slot]
        r.st[:, rows_of(q)] = st

        def spread(index):
            turned = pltpu.roll(st, lax.rem(z.T - index * 32, z.T), 1)
            for j in range(32):
                r.bc[q, index * 32 + j] = jnp.broadcast_to(turned[:, j : j + 1], (2 * z.N, LANE))

        each(z.T // 32, spread)
        nat = columns_of(st)
        key_sq = jnp.sum(jnp.where(only_b, nat * nat, 0.0), axis=1, keepdims=True)
        swap_low[q].wait()
        low = r.lowp[q, 0].astype(F32)
        for slot in range(1, z.M):
            low = low + r.lowp[q, slot].astype(F32)
        low = low.astype(BF16)
        r.low[rows_of(q), :] = low

        def step_chunk(index):
            lanes = cut(index * 256, 256)
            raw = nn(low, r.deltaw[:, lanes]) + r.dbias[:, lanes]
            beta = 1.0 / (1.0 + jnp.exp(-raw))
            scale = 1.0 / (1.0 + beta * key_sq)
            step = beta * scale
            r.s[rows_of(q), lanes] = step
            r.su[rows_of(q), lanes] = step * r.u[rows_of(q), lanes].astype(F32)
            r.fac[rows_of(q), lanes] = scale * step * (1.0 - beta)

        each(z.C // 256, step_chunk)

    def key_blocks(q):
        nat16 = columns_of(r.st[:, rows_of(q)])[:, : 2 * z.N].astype(BF16)
        spread_b = jnp.where(diagonal, nn(nat16, rep_b), 0.0)
        r.blkb[rows_of(q), :] = spread_b.astype(BF16)
        r.blkk[rows_of(q), :] = (spread_b * spread_b).astype(BF16)
        r.blkc[rows_of(q), :] = jnp.where(diagonal, nn(nat16, rep_c), 0.0).astype(BF16)

    span = 512 if z.C % 512 == 0 else 256

    def token(q, t):
        return pl.ds(q * z.T + t, 1)

    def totals(q):
        def lane_part(index):
            lanes = cut(index * span, span)

            def tokens8(i, carry):
                product, state = carry
                for j in range(8):
                    row = token(q, i * 8 + j)
                    step, drive = r.s[row, lanes], r.su[row, lanes]
                    key = r.bc[q, i * 8 + j, : z.N, :]
                    decay = 1.0 - step * wide(key * key, span // LANE)
                    product = product * decay
                    state = decay * state + drive * wide(key, span // LANE)
                return product, state

            start = (jnp.ones((z.N, span), F32), jnp.zeros((z.N, span), F32))
            product, state = lax.fori_loop(0, z.T // 8, tokens8, start)
            r.ptot[q, :, lanes] = product
            r.stot[q, :, lanes] = state

        each(z.C // span, lane_part)

    carry_sems = [[(links.sem(), links.sem()) for q in range(z.Q)] for level in range(z.levels)]
    back_sems = [[(links.sem(), links.sem()) for q in range(z.Q)] for level in range(z.levels)]
    carry_copies = []

    def upper_at(level):
        return lax.rem(seq // (1 << level), 2) == 1

    def carry_send(level, q):
        r.csend[level, q, 0] = r.ptot[q].astype(BF16)
        r.csend[level, q, 1] = r.stot[q].astype(BF16)
        copy = links.copy(
            r.csend.at[level, q], r.crecv.at[level, q], *carry_sems[level][q], seq=seq ^ (1 << level)
        )
        copy.start()
        carry_copies.append(copy)

    def carry_take(level, q):
        links.arrived(r.crecv.at[level, q], carry_sems[level][q][1])
        upper = upper_at(level)
        other_p, other_s = r.crecv[level, q, 0].astype(F32), r.crecv[level, q, 1].astype(F32)
        mine_p, mine_s = r.ptot[q], r.stot[q]
        if level == 0:
            r.spre[q] = jnp.where(upper, other_s, 0.0)
            r.ppre[q] = jnp.where(upper, other_p, 1.0)
        else:
            pre_p, pre_s = r.ppre[q], r.spre[q]
            r.spre[q] = jnp.where(upper, pre_p * other_s + pre_s, pre_s)
            r.ppre[q] = jnp.where(upper, pre_p * other_p, pre_p)
        if level < z.levels - 1:
            r.stot[q] = jnp.where(upper, mine_p * other_s + mine_s, other_p * mine_s + other_s)
            r.ptot[q] = mine_p * other_p

    def back_send(level, q):
        r.bsend[level, q] = r.stot[q].astype(BF16)
        copy = links.copy(
            r.bsend.at[level, q], r.brecv.at[level, q], *back_sems[level][q], seq=seq ^ (1 << level)
        )
        copy.start()
        carry_copies.append(copy)

    def back_take(level, q):
        links.arrived(r.brecv.at[level, q], back_sems[level][q][1])
        upper = upper_at(level)
        other = r.brecv[level, q].astype(F32)
        other_p, mine_p = r.crecv[level, q, 0].astype(F32), r.csend[level, q, 0].astype(F32)
        mine = r.stot[q]
        if level == 0:
            r.spre[q] = jnp.where(upper, 0.0, other)
            r.ppre[q] = jnp.where(upper, 1.0, other_p)
        else:
            pre_p, pre = r.ppre[q], r.spre[q]
            r.spre[q] = jnp.where(upper, pre, pre + pre_p * other)
            r.ppre[q] = jnp.where(upper, pre_p, pre_p * other_p)
        if level < z.levels - 1:
            r.stot[q] = jnp.where(upper, other + other_p * mine, mine + mine_p * other)

    def past_rows(q, slot, count=1):
        return pl.ds(pl.multiple_of((q * (z.T + 1) + slot) * z.N, z.N), count * z.N)

    groups = z.T // GRP

    def walk(q):
        r.hist[past_rows(q, 0), :] = r.spre[q].astype(BF16)

        def lane_part(index):
            lanes = cut(index * span, span)

            def tokens8(i, state):
                for j in range(8):
                    row = token(q, i * 8 + j)
                    step, drive = r.s[row, lanes], r.su[row, lanes]
                    key = r.bc[q, i * 8 + j, : z.N, :]
                    decay = 1.0 - step * wide(key * key, span // LANE)
                    state = decay * state + drive * wide(key, span // LANE)
                    r.hist[past_rows(q, i * 8 + j + 1), lanes] = state.astype(BF16)
                return state

            lax.fori_loop(0, z.T // 8, tokens8, r.spre[q, :, lanes])

        each(z.C // span, lane_part)
        reads = []
        for i in range(groups):
            rows = pl.ds(q * z.T + i * GRP, GRP)
            reads.append((rows, nn(r.blkc[rows, :], r.hist[past_rows(q, i * GRP + 1, GRP), :])))
        for rows, value in reads:
            r.rd[rows, :] = value

    def z_chunk(index):
        lanes = cut(index * 256, 256)
        r.zp[:, lanes] = nn(r.normed[: z.R, :], r.wx[1, :, lanes])

    conv(0)
    project(0)
    conv(1)
    project(1)
    line_d.step(1)
    keys(0)
    totals(0)
    carry_send(0, 0)
    keys(1)
    carry_take(0, 0)
    carry_send(1, 0)
    totals(1)
    carry_send(0, 1)
    carry_take(0, 1)
    carry_send(1, 1)
    tree_o.second(1)
    tree_o.forward(1)
    line_d.step(2)
    tree_z.settle()
    key_blocks(0)
    key_blocks(1)
    for level in range(1, z.levels - 1):
        for q in range(z.Q):
            carry_take(level, q)
            carry_send(level + 1, q)
    tree_o.forward(0)
    tree_z.finish()
    each(z.C // 256, z_chunk)
    carry_take(z.levels - 1, 0)
    walk(0)
    for far in range(3, z.M):
        line_d.step(far)
    tree_o.settle(False)
    carry_take(z.levels - 1, 1)
    walk(1)
    r.vec[...] = jnp.zeros_like(r.vec)

    def gate_lanes(lanes):
        for q in range(z.Q):
            rows = rows_of(q)
            out = r.rd[rows, lanes] + r.skip[:, lanes] * r.u[rows, lanes].astype(F32)
            r.rd[rows, lanes] = out
            gated = out * silu_parts(r.zp[rows, lanes])[1]
            r.gat[rows, lanes] = gated.astype(BF16)
            r.gatt[lanes, rows] = gated.T.astype(BF16)

    lane_loop(gate_lanes)

    def into(near, term):
        def make(device, mask):
            block = near.block(mask // 2)
            block[...] = term(device).astype(BF16)
            return block

        return make

    def onto(sums, term):
        def add(device, mask):
            block = sums.block(mask // 2)
            block[...] = (term(device) + block[...].astype(F32)).astype(BF16)

        return add

    half_s, slots = z.S // 2, slots_of(z)
    sg_rows = z.rows_sg
    near_o, near_i = Rows(r.near_o, 0, z.C, half_s), Rows(r.near_i, 0, z.Ds, half_s)
    sum_o, far_o = Rows(r.sum_o, 0, z.C, half_s), Rows(r.far_o, 0, z.C // 2, slots)
    sum_1, far_1 = Rows(r.sum_1, 0, z.Ds, half_s), Rows(r.far_1, 0, z.Ds // 2, slots)
    sum_0 = Rows(r.hist, 0, z.Ds, half_s)
    far_0 = Rows(r.hist, sum_0.end, z.Ds // 2, slots)
    sum_s = Rows(r.hist, far_0.end, sg_rows, half_s)
    far_s = Rows(r.hist, sum_s.end, halves(sg_rows)[0][1], slots)
    sgp = Rows(r.hist, far_s.end, sg_rows, z.S)
    small = Rows(r.hist, sgp.end, sg_rows, z.S)
    scatter_o = Scatter(z, links, None, sum_o, far_o, z.C)
    scatter_1 = Scatter(z, links, None, sum_1, far_1, z.Ds)
    scatter_0 = Scatter(z, links, None, sum_0, far_0, z.Ds)
    scatter_s = Scatter(z, links, None, sum_s, far_s, sg_rows)
    term_o = lambda device: nn(r.gatt[...], r.db[:, cut(device * z.Ds, z.Ds)])
    term_1 = lambda device: nn(r.normt[cut(device * z.Ds, z.Ds), :], r.dzr[...])
    term_0 = lambda device: nn(r.normt[cut(device * z.Ds, z.Ds), :], r.dxr[...])

    tree_o.settle(True)
    most = scatter_o.by_need()
    scatter_o.first(into(near_o, term_o))
    scatter_o.second(onto(sum_o, term_o), send=True, masks=most[:1])
    tree_o.finish()

    def gated_grad(index):
        lanes = cut(index * 256, 256)
        r.dr[:, lanes] = nt(r.db[...], r.wo[lanes, :])

    each(z.C // 256, gated_grad)

    def gate_back(lanes):
        for q in range(z.Q):
            rows = rows_of(q)
            part, grad = r.zp[rows, lanes], r.dr[rows, lanes]
            gate, silu = silu_parts(part)
            d_read = grad * silu
            r.dr[rows, lanes] = d_read
            r.dzr[rows, lanes] = (grad * r.rd[rows, lanes] * gate * (1.0 + part * (1.0 - gate))).astype(BF16)
            r.vec[6:7, lanes] += jnp.sum(d_read * r.u[rows, lanes].astype(F32), axis=0, keepdims=True)

    lane_loop(gate_back)

    swap_out = Swap(z, links, lambda slot: r.orecv.at[slot])

    def partial_of(owner):
        return r.normed.at[pl.ds(0, z.R), cut(owner * z.Df, z.Df)]

    def branch_to(index):
        away = index + 1
        owner = lax.rem(mp + away, z.M)
        for b in range(z.B):
            j = owner * z.B + b
            r.normed[: z.R, cut(j * z.Ds, z.Ds)] = nn(r.gat[...], r.wo[:, cut(j * z.Ds, z.Ds)]).astype(BF16)

        @pl.when(away < z.M)
        def _():
            swap_out.one(partial_of(owner), away).start()

    def totals_back(q):
        def lane_part(index):
            lanes = cut(index * span, span)

            def tokens8(i, tail):
                for j in reversed(range(8)):
                    t = z.T - 8 - i * 8 + j
                    row = token(q, t)
                    step, grad = r.s[row, lanes], r.dr[row, lanes]
                    key, query = r.bc[q, t, : z.N, :], r.bc[q, t, z.N :, :]
                    decay = 1.0 - step * wide(key * key, span // LANE)
                    tail = decay * (grad * wide(query, span // LANE) + tail)
                return tail

            r.stot[q, :, lanes] = lax.fori_loop(0, z.T // 8, tokens8, jnp.zeros((z.N, span), F32))

        each(z.C // span, lane_part)

    lane_index = lax.broadcasted_iota(jnp.int32, (z.N, LANE), 1)

    def lane_sum(value):
        total = value[:, :LANE]
        for part in range(1, lanes_all):
            total = total + value[:, part * LANE : (part + 1) * LANE]
        return jnp.sum(total, axis=1, keepdims=True)

    batch = min(groups, z.C // (GRP * z.N))

    def walk_back(q):
        def group(index, carry):
            tail, sum_gh, sum_g = carry
            i = groups - 1 - index
            for j in reversed(range(GRP)):
                t = i * GRP + j
                row = token(q, t)
                step, drive, grad = r.s[row, :], r.su[row, :], r.dr[row, :]
                key, query = r.bc[q, t, : z.N, :], r.bc[q, t, z.N :, :]
                before = r.hist[past_rows(q, t), :].astype(F32)
                state_grad = grad * wide(query, lanes_all) + tail
                crossed = state_grad * before
                place = pl.ds(pl.multiple_of(lax.rem(i, batch) * GRP * z.N + j * z.N, z.N), z.N)
                r.wo[place, : z.C] = state_grad.astype(BF16)
                r.wo[place, z.C : 2 * z.C] = crossed.astype(BF16)
                here = lane_index == t
                sum_gh = jnp.where(here, lane_sum(step * crossed), sum_gh)
                sum_g = jnp.where(here, lane_sum(drive * state_grad), sum_g)
                tail = (1.0 - step * wide(key * key, lanes_all)) * state_grad
            return tail, sum_gh, sum_g

        zero = jnp.zeros((z.N, LANE), F32)
        carry = (r.spre[q], zero, zero)
        for start in range(0, groups, batch):
            carry = lax.fori_loop(start, start + batch, group, carry)
            sums = []
            for slot in range(batch):
                rows = pl.ds(q * z.T + (groups - start - batch + slot) * GRP, GRP)
                place = pl.ds(slot * GRP * z.N, GRP * z.N)
                sums.append(
                    (
                        rows,
                        nn(r.blkb[rows, :], r.wo[place, : z.C]),
                        nn(r.blkk[rows, :], r.wo[place, z.C : 2 * z.C]),
                    )
                )
            for rows, by_key, by_square in sums:
                r.rd[rows, :] = by_key
                r.zp[rows, :] = by_square
        columns = rows_of(q)
        for part in range(2):
            r.est[part, :, columns] = carry[1 + part]

    def query_sums(q):
        parts = []
        for i in range(groups):
            rows = pl.ds(q * z.T + i * GRP, GRP)
            parts.append(nt(r.dr[rows, :].astype(BF16), r.hist[past_rows(q, i * GRP + 1, GRP), :]))
        blocks = jnp.where(diagonal, jnp.concatenate(parts, axis=0), 0.0).astype(BF16)
        r.est[2, :, rows_of(q)] = nt(rep_b[: z.N], blocks)

    def step_back(q):
        rows = rows_of(q)

        def step_lanes(lanes):
            sum_b, step = r.rd[rows, lanes], r.s[rows, lanes]
            d_step = r.u[rows, lanes].astype(F32) * sum_b - r.zp[rows, lanes]
            r.rd[rows, lanes] = step * sum_b
            d_raw = d_step * r.fac[rows, lanes]
            r.ddr[rows, lanes] = d_raw.astype(BF16)
            r.gat[rows, lanes] = (d_step * step * step).astype(BF16)
            r.vec[5:6, lanes] += jnp.sum(d_raw, axis=0, keepdims=True)

        lane_loop(step_lanes)

    swap_dlow = [Swap(z, links, lambda slot, q=q: r.dlowp.at[q, slot]) for q in range(z.Q)]
    swap_dst = [Swap(z, links, lambda slot, q=q: r.dstp.at[q, slot]) for q in range(z.Q)]
    dlow_mine = [r.dlowp.at[q, z.M - 1] for q in range(z.Q)]
    dst_mine = [r.dstp.at[q, z.M - 1] for q in range(z.Q)]

    def project_back(q):
        rows = rows_of(q)
        key_grad = nt(jnp.ones((16, z.C), BF16), r.gat[rows, :])[0:1]
        now = r.st[: z.N, rows]
        d_key = r.est[1, :, rows] - 2.0 * now * r.est[0, :, rows] - 2.0 * now * key_grad
        dst_mine[q][...] = jnp.concatenate([d_key, r.est[2, :, rows]], axis=0).astype(BF16)
        swap_dst[q].start(dst_mine[q])
        dlow_mine[q][...] = nt(r.ddr[rows, :], r.deltaw[...]).astype(BF16)
        swap_dlow[q].start(dlow_mine[q])

    def sums_back(q):
        rows = rows_of(q)
        swap_dlow[q].wait()
        swap_dst[q].wait()
        dlow = r.dlowp[q, 0].astype(F32)
        dst = r.dstp[q, 0].astype(F32)
        for slot in range(1, z.M):
            dlow = dlow + r.dlowp[q, slot].astype(F32)
            dst = dst + r.dstp[q, slot].astype(F32)
        r.dlow[rows, :] = dlow.astype(BF16)
        r.dlowt[:, rows] = dlow.T.astype(BF16)
        r.dst[:, rows] = dst.astype(BF16)
        dlow16, dst16 = dlow.astype(BF16), columns_of(dst)[:, : 2 * z.N].astype(BF16)

        def inputs_chunk(index):
            lanes = cut(index * 256, 256)
            r.su[rows, lanes] = nt(dlow16, r.loww[lanes, :]) + nn(dst16, r.statewt[:, lanes])

        each(z.C // 256, inputs_chunk)

    rim = [
        links.copy(
            r.dcp.at[q, pl.ds(0, 8), :],
            r.dcp.at[q, pl.ds(z.T, 8), :],
            links.sem(),
            links.sem(),
            seq=behind,
        )
        for q in range(z.Q)
    ]

    def conv_back(q):
        rows = rows_of(q)

        def conv_lanes(lanes):
            total = r.su[rows, lanes] + r.rd[rows, lanes] + r.skip[:, lanes] * r.dr[rows, lanes]
            value = r.conv[rows, lanes]
            gate = silu_parts(value)[0]
            d_conv = total * gate * (1.0 + value * (1.0 - gate))
            r.dcp[q, 0 : z.T, lanes] = d_conv
            r.vec[4:5, lanes] += jnp.sum(d_conv, axis=0, keepdims=True)
            for tap in range(4):
                r.vec[tap : tap + 1, lanes] += jnp.sum(
                    d_conv * r.xpad[q, 5 + tap : 5 + tap + z.T, lanes], axis=0, keepdims=True
                )

        lane_loop(conv_lanes)
        rim[q].start()

    def x_back(q):
        rim[q].wait_recv()

        def x_lanes(lanes):
            edge = r.dcp[q, z.T : z.T + 8, lanes]
            r.dcp[q, z.T : z.T + 8, lanes] = jnp.where(seq < z.S - 1, edge, 0.0)
            total = jnp.zeros((z.T, LANE), F32)
            for tap in range(4):
                total = total + r.convw[tap : tap + 1, lanes] * r.dcp[q, 3 - tap : 3 - tap + z.T, lanes]
            r.dxr[rows_of(q), lanes] = total.astype(BF16)

        lane_loop(x_lanes)

    swap_n = [Swap(z, links, lambda slot, q=q: r.nrecv.at[slot, rows_of(q), :]) for q in range(z.Q)]

    def normed_of(q, owner):
        return r.normed.at[rows_of(q), cut(owner * z.Df, z.Df)]

    def normed_part(q):
        rows = rows_of(q)

        def normed_to(index, means):
            away = index + 1
            owner = lax.rem(mp + away, z.M)
            for b in range(z.B):
                j = owner * z.B + b
                features = cut(j * z.Ds, z.Ds)
                part = nt(r.dxr[rows, :], r.wx[0, features, :]) + nt(r.dzr[rows, :], r.wx[1, features, :])
                r.normed[rows, features] = part.astype(BF16)
                scaled = part * r.tokg[j, rows, :].astype(F32)
                by_gain = jnp.sum(scaled * wide(r.inv[rows, :], z.Ds // LANE), axis=0, keepdims=True)
                for piece in range(z.Ds // LANE):
                    place = pl.ds(j * (z.Ds // LANE) + piece, 1)
                    value = by_gain[:, piece * LANE : (piece + 1) * LANE]
                    r.gv[place, :] = value if q == 0 else r.gv[place, :] + value
                means = means + jnp.sum(scaled * r.gain[:, features], axis=1, keepdims=True)

            @pl.when(away < z.M)
            def _():
                swap_n[q].one(normed_of(q, owner), away).start()

            return means

        means = lax.fori_loop(0, z.M, normed_to, jnp.zeros((z.T, 1), F32))
        mean_mine[:, rows] = jnp.broadcast_to(means, (z.T, LANE)).T[0:8]

    swap_m = Swap(z, links, lambda slot: r.mrow.at[slot])
    mean_mine = r.mrow.at[z.M - 1]

    def settle_back(level, q):
        back_take(level, q)
        if level < z.levels - 1:
            back_send(level + 1, q)

    totals_back(0)
    back_send(0, 0)
    each(z.M, branch_to)
    scatter_o.second(onto(sum_o, term_o), masks=most[1:])
    settle_back(0, 0)
    totals_back(1)
    back_send(0, 1)
    settle_back(0, 1)
    for mask in most[1:]:
        if mask & z.dims[0]:
            scatter_o.send(0, mask)
    scatter_1.first(into(near_i, term_1))
    for level in range(1, z.levels - 1):
        for q in range(z.Q):
            settle_back(level, q)
    for mask in most[1:]:
        if not mask & z.dims[0]:
            scatter_o.send(0, mask)
    scatter_1.second(onto(sum_1, term_1), send=True)
    query_sums(0)
    query_sums(1)
    for q in range(z.Q):
        back_take(z.levels - 1, q)
    for copy in scatter_1.sent[: len(z.masks)]:
        copy.wait_send()
    scatter_1.sent = scatter_1.sent[len(z.masks) :]
    tree_o.drain()
    walk_back(0)
    step_back(0)
    project_back(0)
    for step in range(depth - 1):
        scatter_o.fold(step)
    walk_back(1)
    for level in range(z.levels):
        pl.semaphore_signal(
            r.ready.at[level], inc=1, device_id=(seq ^ (1 << level), mp), device_id_type=MESH
        )
    step_back(1)
    project_back(1)
    sums_back(0)
    conv_back(0)

    last = depth - 1

    def write_to(ref):
        def write(rows, value):
            ref[rows, :] = value

        return write

    swap_out.wait()
    for away in range(1, z.M):
        owner = lax.rem(mp + away, z.M)
        swap_out.one(partial_of(owner), away).wait_send()

    def block_lanes(index):
        here = cut(index * LANE, LANE)
        total = r.normed[: z.R, cut(mp * z.Df + index * LANE, LANE)].astype(F32)
        for slot in range(z.M - 1):
            total = total + r.orecv[slot, :, here].astype(F32)
        r.blk[:, here] = (r.tok[:, here].astype(F32) + total).astype(BF16)

    each(z.Df // LANE, block_lanes)
    sums_back(1)
    conv_back(1)
    for step in range(depth - 1):
        scatter_1.fold(step)
    x_back(0)
    normed_part(0)

    def put_small(first, lanes, value):
        count, at = value.shape[0], 0
        while at < count:
            block, inside = divmod(first + at, sg_rows)
            take = min(count - at, sg_rows - inside)
            sgp.block(block, inside, take)[:, lanes] = value[at : at + take].astype(BF16)
            at += take

    low_t = r.low[...].astype(F32).T.astype(BF16)
    used = 2 * z.RK + 2 * z.N + SGVEC

    def small_chunk(index):
        lanes = cut(index * 256, 256)
        put_small(0, lanes, nn(low_t, r.ddr[:, lanes]))
        put_small(z.RK, lanes, nn(r.dlowt[...], r.u[:, lanes]))
        put_small(2 * z.RK, lanes, nn(r.dst[...], r.u[:, lanes]))
        put_small(2 * z.RK + 2 * z.N, lanes, r.vec[:, lanes])
        if used < z.S * sg_rows:
            put_small(used, lanes, jnp.zeros((z.S * sg_rows - used, 256), F32))

    each(z.C // 256, small_chunk)
    for level in range(z.levels):
        pl.semaphore_wait(r.ready.at[level], 1)
    scatter_s.first(lambda device, mask: sgp.block(device))
    x_back(1)

    def add_small(device, mask):
        block, term = sum_s.block(mask // 2), sgp.block(device)

        def one(rows):
            block[rows, :] = (block[rows, :].astype(F32) + term[rows, :].astype(F32)).astype(BF16)

        by_rows(sg_rows, one)

    scatter_s.second(add_small, send=True)
    scatter_0.first(into(near_i, term_0))
    scatter_0.second(onto(sum_0, term_0), send=True, masks=most[:1])
    for step in range(depth - 1):
        scatter_s.fold(step)
    scatter_0.second(onto(sum_0, term_0), send=True, masks=most[1:])

    normed_part(1)
    swap_m.start(mean_mine)

    gain_seq = SwapSeq(z, links, lambda slot: r.gvr.at[slot])
    gain_seq.start(r.gv)
    scatter_s.fold(last)

    def write_small(rows, value):
        small.block(seq)[rows, :] = value.astype(BF16)

    scatter_s.total(write_small)
    tree_s = TreeGather(
        z,
        links,
        lambda owner, h: small.block(owner, *halves(sg_rows)[h]),
        small.block,
    )
    tree_s.first()
    tree_s.second(0)
    tree_s.second(1)
    for step in range(depth - 1):
        scatter_0.fold(step)
    gain_seq.wait()
    gains = r.gv[...]
    for slot in range(z.S - 1):
        gains = gains + r.gvr[slot]
    r.gvs[...] = gains
    swap_g = Swap(z, links, lambda slot: r.gvm.at[slot])
    swap_g.start(r.gvs)
    tree_s.forward(0)
    tree_s.forward(1)
    scatter_o.fold(last)
    scatter_o.total(write_to(r.dout))
    scatter_1.fold(last)
    scatter_1.total(write_to(r.fac))
    store_1 = pltpu.make_async_copy(r.fac.at[pl.ds(0, z.Ds)], r.din.at[1], local.at[3])
    store_1.start()
    tree_s.settle()

    swap_m.wait()
    mean = r.mrow[0]
    for slot in range(1, z.M):
        mean = mean + r.mrow[slot]
    r.mean[...] = jnp.concatenate([mean] * (LANE // 8), axis=0).T * (1.0 / z.D)
    for swap in swap_n:
        swap.wait()

    def token_lanes(index):
        here = cut(index * LANE, LANE)
        inside = cut(mp * z.Df + index * LANE, LANE)
        for q in range(z.Q):
            rows = rows_of(q)
            total = r.normed[rows, inside].astype(F32)
            for slot in range(z.M - 1):
                total = total + r.nrecv[slot, rows, here].astype(F32)
            inv, x = r.inv[rows, :], r.tok[rows, here].astype(F32)
            value = inv * (total * r.gain[:, inside]) - x * (inv * inv * inv) * r.mean[rows, :]
            r.dtok[rows, here] = value + r.cot[rows, here] * seq_weight[q]

    each(z.Df // LANE, token_lanes)

    scatter_0.fold(last)
    scatter_0.total(write_to(r.s))
    store_0 = pltpu.make_async_copy(r.s.at[pl.ds(0, z.Ds)], r.din.at[0], local.at[4])
    store_0.start()
    tree_s.finish()
    for block in range(z.S):
        count = min(sg_rows, r.sg.shape[0] - block * sg_rows)
        if count > 0:
            r.sg[block * sg_rows : block * sg_rows + count, :] = small.block(block, 0, count)[...].astype(F32)
    swap_g.wait()
    gains = r.gvs[...]
    for slot in range(z.M - 1):
        gains = gains + r.gvm[slot]
    r.dgain[...] = gains

    hal.wait_send()
    for tree in (tree_x, tree_z, tree_s):
        tree.drain()
    for line in (*line_t, line_h, line_d):
        line.drain()
    for q in range(z.Q):
        swap_st[q].drain(st_mine[q])
        swap_low[q].drain(low_mine[q])
        swap_dlow[q].drain(dlow_mine[q])
        swap_dst[q].drain(dst_mine[q])
    swap_m.drain(mean_mine)
    swap_g.drain(r.gvs)
    gain_seq.drain()
    for away in range(1, z.M):
        owner = lax.rem(mp + away, z.M)
        for q in range(z.Q):
            swap_n[q].one(normed_of(q, owner), away).wait_send()
    for copy in carry_copies + rim:
        copy.wait_send()
    for scatter in (scatter_o, scatter_1, scatter_0, scatter_s):
        scatter.drain()
    store_1.wait()
    store_0.wait()


def finish_kernel(z, blk, dtok, dgain, din, dout, sg, *outs):
    a, b, c = z.RK, 2 * z.RK, 2 * z.RK + 2 * z.N
    o_blk, o_dtok, o_dgain, o_din, o_convw, o_convb, o_low, o_state, o_delta, o_dbias, o_skip, o_dout = outs
    o_blk[...] = blk[...]
    o_dtok[...] = dtok[...]
    o_dgain[...] = dgain[...]
    o_din[...] = din[...]
    o_dout[...] = dout[...]
    o_delta[...] = sg[0:a, :]
    o_state[...] = sg[b:c, :]
    o_convw[...] = sg[c : c + 4, :]
    o_convb[...] = sg[c + 4 : c + 5, :]
    o_dbias[...] = sg[c + 5 : c + 6, :]
    o_skip[...] = sg[c + 6 : c + 7, :]
    for at in range(0, sg.shape[1], LANE):
        o_low[at : at + LANE, :] = sg[a:b, at : at + LANE].T


def fused(z, tokens, norm_gain, in_weight, conv_weight, conv_bias, low_weight, state_weight, delta_weight,
          delta_bias, skip_gain, out_weight, cotangent, seq_group, group_weight):
    V = pl.BlockSpec(memory_space=pltpu.VMEM)
    A = pl.BlockSpec(memory_space=pl.ANY)
    SM = pl.BlockSpec(memory_space=pltpu.SMEM)
    row = lambda value: value.reshape(1, -1)
    operands = dict(
        tok_in=(A, tokens.reshape(z.R, z.Df)),
        cot_in=(A, cotangent.reshape(z.R, z.Df)),
        gain_in=(A, row(norm_gain)),
        win=(A, in_weight),
        wout=(A, out_weight),
        convw_in=(A, conv_weight),
        convb_in=(A, row(conv_bias)),
        dbias_in=(A, row(delta_bias)),
        skip_in=(A, row(skip_gain)),
        loww_in=(A, low_weight),
        statewt_in=(A, state_weight.T),
        deltaw_in=(A, delta_weight),
        seqg=(SM, seq_group),
        groupw=(SM, group_weight),
    )
    scratch = scratch_of(z)
    sg_used = 2 * z.RK + 2 * z.N + SGVEC
    outs = dict(
        blk=(V, (z.R, z.Df), BF16),
        dtok=(V, (z.R, z.Df), F32),
        dgain=(V, (z.D // LANE, LANE), F32),
        din=(A, (2, z.Ds, z.C), F32),
        dout=(V, (z.C, z.Ds), F32),
        sg=(V, (sg_used, z.C), F32),
    )
    result = pl.pallas_call(
        functools.partial(fused_kernel, z, [*operands, *outs, *scratch]),
        out_shape=[jax.ShapeDtypeStruct(shape, kind) for _, shape, kind in outs.values()],
        in_specs=[spec for spec, _ in operands.values()],
        out_specs=[spec for spec, _, _ in outs.values()],
        scratch_shapes=list(scratch.values()),
        compiler_params=pltpu.CompilerParams(
            collective_id=0, has_side_effects=True, vmem_limit_bytes=VMEM_BYTES
        ),
    )(*[value for _, value in operands.values()])
    whole = (V, (1, z.C), F32)
    last = dict(
        blk=(V, (z.R, z.Df), BF16),
        dtok=(V, (z.R, z.Df), F32),
        dgain=(V, (z.D // LANE, LANE), F32),
        din=(V, (2, z.Ds, z.C), F32),
        convw=(V, (4, z.C), F32),
        convb=whole,
        low=(V, (z.C, z.RK), F32),
        state=(V, (2 * z.N, z.C), F32),
        delta=(V, (z.RK, z.C), F32),
        dbias=whole,
        skip=whole,
        dout=(V, (z.C, z.Ds), F32),
    )
    done = pl.pallas_call(
        functools.partial(finish_kernel, z),
        out_shape=[jax.ShapeDtypeStruct(shape, kind) for _, shape, kind in last.values()],
        in_specs=[V] * 6,
        out_specs=[spec for spec, _, _ in last.values()],
        compiler_params=pltpu.CompilerParams(vmem_limit_bytes=VMEM_BYTES),
    )(*result)
    done = dict(zip(last, done))
    done.update(blk=done["blk"].reshape(tokens.shape), dtok=done["dtok"].reshape(tokens.shape))
    done.update(dgain=done["dgain"].reshape(z.D), state=done["state"].T)
    done.update({name: done[name][0] for name in ("convb", "dbias", "skip")})
    return tuple(done.values())


def local(mesh_shape, *arrays):
    tokens, norm_gain, in_weight, conv_weight = arrays[:4]
    state_weight, delta_weight = arrays[6], arrays[7]
    z = Sizes(
        mesh_shape,
        tokens.shape[0],
        tokens.shape[1],
        tokens.shape[2],
        norm_gain.shape[0],
        in_weight.shape[2],
        state_weight.shape[1] // 2,
        delta_weight.shape[0],
    )
    if z.fits(conv_weight.shape[0]):
        return fused(z, *arrays)
    return plain(*arrays)


def solution(mesh):
    placed = (
        P(None, "seq", "mp"),
        P(),
        P(None, "seq", "mp"),
        P(None, "mp"),
        P("mp"),
        P("mp", None),
        P("mp", None),
        P(None, "mp"),
        P("mp"),
        P("mp"),
        P("mp", "seq"),
        P(None, "seq", "mp"),
        P(),
        P(),
    )
    return jax.shard_map(
        functools.partial(local, dict(mesh.shape)),
        mesh=mesh,
        in_specs=placed,
        out_specs=(
            P(None, "seq", "mp"),
            P(None, "seq", "mp"),
            P(),
            P(None, "seq", "mp"),
            P(None, "mp"),
            P("mp"),
            P("mp", None),
            P("mp", None),
            P(None, "mp"),
            P("mp"),
            P("mp"),
            P("mp", "seq"),
        ),
        check_vma=False,
    )
```

```python
import functools
import math

import jax
import jax.numpy as jnp
from jax import lax
from jax.experimental import pallas as pl
from jax.experimental.pallas import tpu as pltpu
from jax.sharding import PartitionSpec as P

SEQ_MB = 1
NMB = 2
EPSILON = 1e-05
VMEM_BYTES = 64 * 1024 * 1024 - 64 * 1024


def from_behind(value, axis, steps):
    count = lax.axis_size(axis)
    leading, last = (max(0, -steps), min(count, count - steps))
    return lax.ppermute(value, axis, [(source, source + steps) for source in range(leading, last)])


def prefix(value, axis, join, neutral, backward):
    count, mine = (lax.axis_size(axis), lax.axis_index(axis))
    pieces = jax.tree.map(lambda part: lax.all_gather(part, axis), value)
    if backward:
        pieces = jax.tree.map(lambda part: part[::-1], pieces)
        mine = count - 1 - mine
    subtotal = jax.tree.map(
        lambda part, zero: jnp.full_like(part, 0) + jnp.asarray(zero, part.dtype), value, neutral
    )

    def lap(position, subtotal):
        longer = join(subtotal, jax.tree.map(lambda part: part[position], pieces))
        return jax.tree.map(lambda new, old: jnp.where(position < mine, new, old), longer, subtotal)

    return lax.fori_loop(0, count - 1, lap, subtotal)


def combine(earlier, later):
    return (earlier[0] * later[0], later[0] * earlier[1] + later[1])


def make_gates(delta_raw, b_state, inputs):
    beta_gate = jax.nn.sigmoid(delta_raw)
    key_sq = jnp.sum(b_state * b_state, axis=-1, keepdims=True)
    step_size = beta_gate / (1.0 + beta_gate * key_sq)
    decays = 1.0 - step_size[:, :, None, :] * (b_state * b_state)[:, :, :, None]
    source = (step_size * inputs)[:, :, None, :] * b_state[:, :, :, None]
    return (decays, source)


def to_blocks(value, span_rows):
    old_shape = value.shape
    reshaped = value.reshape((old_shape[0], old_shape[1] // span_rows, span_rows) + old_shape[2:])
    return jnp.swapaxes(reshaped, 0, 1)


def from_blocks(value):
    joined = jnp.swapaxes(value, 0, 1)
    old_shape = joined.shape
    return joined.reshape((old_shape[0], old_shape[1] * old_shape[2]) + old_shape[3:])


def forward_block(carry_pair, block_items):
    delta_raw, b_state, inputs = block_items
    decays, source = make_gates(delta_raw, b_state, inputs)
    run_prod, run_state = carry_pair
    prod_list = []
    state_list = []
    for row_idx in range(decays.shape[1]):
        run_prod = run_prod * decays[:, row_idx]
        run_state = decays[:, row_idx] * run_state + source[:, row_idx]
        prod_list.append(run_prod)
        state_list.append(run_state)
    return ((run_prod, run_state), (jnp.stack(prod_list, axis=1), jnp.stack(state_list, axis=1)))


def backward_block(carry_trio, block_items):
    delta_raw, b_state, inputs, read_grad, c_state = block_items
    decays, _ = make_gates(delta_raw, b_state, inputs)
    grad_next, dec_next, tail_prod = carry_trio
    span_rows = decays.shape[1]
    grad_list = [None] * span_rows
    tail_list = [None] * span_rows
    for row_idx in reversed(range(span_rows)):
        drive_term = read_grad[:, row_idx][:, None, :] * c_state[:, row_idx][:, :, None]
        grad_next = drive_term + dec_next * grad_next
        tail_prod = dec_next * tail_prod
        grad_list[row_idx] = grad_next
        tail_list[row_idx] = tail_prod
        dec_next = decays[:, row_idx]
    return (
        (grad_next, dec_next, tail_prod),
        (jnp.stack(grad_list, axis=1), jnp.stack(tail_list, axis=1)),
    )


def silu_slope(value):
    sig_value = jax.nn.sigmoid(value)
    return sig_value * (1.0 + value * (1.0 - sig_value))


def plain(
    tokens,
    norm_gain,
    in_weight,
    conv_weight,
    conv_bias,
    low_weight,
    state_weight,
    delta_weight,
    delta_bias,
    skip_gain,
    out_weight,
    cotangent,
    seq_group,
    group_weight,
):
    stretch = tokens.shape[1]
    feature_dev = tokens.shape[2]
    channels = in_weight.shape[2]
    model_width = norm_gain.shape[0]
    num_taps = conv_weight.shape[0]
    nstate = state_weight.shape[1] // 2
    span_rows = math.gcd(stretch, 8)
    picks = (
        seq_group[:, None] == jnp.arange(group_weight.shape[0], dtype=jnp.int32)[None, :]
    ).astype(jnp.float32)
    seq_weight = jnp.sum(picks * group_weight[None, :], axis=1)
    feature_start = lax.axis_index("mp") * feature_dev
    ones_state = jnp.ones((SEQ_MB, nstate, channels), jnp.float32)
    zero_state = jnp.zeros_like(ones_state)
    acc_in = jnp.zeros((2, model_width, channels), jnp.float32)
    acc_out = jnp.zeros((channels, model_width), jnp.float32)
    acc_gain = jnp.zeros_like(norm_gain)
    acc_conv = jnp.zeros_like(conv_weight)
    acc_cbias = jnp.zeros_like(conv_bias)
    acc_low = jnp.zeros(low_weight.shape, jnp.float32)
    acc_state = jnp.zeros(state_weight.shape, jnp.float32)
    acc_delta = jnp.zeros(delta_weight.shape, jnp.float32)
    acc_dbias = jnp.zeros_like(delta_bias)
    acc_skip = jnp.zeros_like(skip_gain)
    outputs = []
    input_grads = []
    for micro_idx in range(NMB):
        whole_in, whole_out = (
            lax.all_gather(in_weight, "seq", axis=1, tiled=True),
            lax.all_gather(out_weight, "seq", axis=1, tiled=True),
        )
        first_seq = micro_idx * SEQ_MB
        block_tokens = tokens[first_seq : first_seq + SEQ_MB]
        full_tokens = lax.all_gather(block_tokens, "mp", axis=2, tiled=True).astype(jnp.float32)
        inv_rms = lax.rsqrt(jnp.mean(full_tokens * full_tokens, axis=-1, keepdims=True) + EPSILON)
        normed = (full_tokens * inv_rms * norm_gain).astype(jnp.bfloat16)
        both_parts = jnp.einsum(
            "scd,kdi->ksci", normed, whole_in, preferred_element_type=jnp.float32
        )
        x_round = both_parts[0].astype(jnp.bfloat16)
        z_part = both_parts[1]
        rim_rows = from_behind(x_round[:, stretch - (num_taps - 1) :], "seq", 1)
        padded = jnp.concatenate([rim_rows, x_round], axis=1).astype(jnp.float32)
        conv_sum = conv_bias + jnp.zeros((SEQ_MB, stretch, channels), jnp.float32)
        for tap_index in range(num_taps):
            conv_sum = (
                conv_sum + conv_weight[tap_index] * padded[:, tap_index : tap_index + stretch]
            )
        inputs_round = jax.nn.silu(conv_sum).astype(jnp.bfloat16)
        inputs_f = inputs_round.astype(jnp.float32)
        low_part = jnp.einsum(
            "sci,ir->scr", inputs_round, low_weight, preferred_element_type=jnp.float32
        )
        state_part = jnp.einsum(
            "sci,ir->scr", inputs_round, state_weight, preferred_element_type=jnp.float32
        )
        delta_low, state_proj = lax.psum((low_part, state_part), "mp")
        delta_round = delta_low.astype(jnp.bfloat16)
        delta_raw = (
            jnp.einsum("scr,ri->sci", delta_round, delta_weight, preferred_element_type=jnp.float32)
            + delta_bias
        )
        b_state = state_proj[..., :nstate]
        c_state = state_proj[..., nstate:]
        delta_blocks = to_blocks(delta_raw, span_rows)
        b_blocks = to_blocks(b_state, span_rows)
        c_blocks = to_blocks(c_state, span_rows)
        in_blocks = to_blocks(inputs_f, span_rows)
        stretch_pair, (prod_blocks, local_blocks) = lax.scan(
            forward_block, (ones_state, zero_state), (delta_blocks, b_blocks, in_blocks)
        )
        carried = prefix(stretch_pair, "seq", combine, (ones_state, zero_state), False)
        states = from_blocks(local_blocks) + from_blocks(prod_blocks) * carried[1][:, None]
        before = jnp.concatenate([carried[1][:, None], states[:, :-1]], axis=1)
        read_rec = jnp.einsum("scni,scn->sci", states, c_state)
        read_out = read_rec + skip_gain * inputs_f
        z_gate = jax.nn.silu(z_part)
        gated_round = (read_out * z_gate).astype(jnp.bfloat16)
        out_part = jnp.einsum(
            "sci,id->scd", gated_round, whole_out, preferred_element_type=jnp.float32
        )
        branch = lax.psum_scatter(out_part, "mp", scatter_dimension=2, tiled=True)
        outputs.append((block_tokens.astype(jnp.float32) + branch).astype(jnp.bfloat16))
        d_out = (
            cotangent[first_seq : first_seq + SEQ_MB]
            * seq_weight[first_seq : first_seq + SEQ_MB][:, None, None]
        )
        d_branch = lax.all_gather(d_out.astype(jnp.bfloat16), "mp", axis=2, tiled=True)
        acc_out = acc_out + jnp.einsum(
            "sci,scd->id", gated_round, d_branch, preferred_element_type=jnp.float32
        )
        d_gated = jnp.einsum("scd,id->sci", d_branch, whole_out, preferred_element_type=jnp.float32)
        d_read = d_gated * z_gate
        d_zpart = d_gated * read_out * silu_slope(z_part)
        acc_skip = acc_skip + jnp.sum(d_read * inputs_f, axis=(0, 1))
        read_blocks_grad = to_blocks(d_read, span_rows)
        (last_grad, first_dec, _), (grad_blocks, tail_blocks) = lax.scan(
            backward_block,
            (zero_state, ones_state, ones_state),
            (delta_blocks, b_blocks, in_blocks, read_blocks_grad, c_blocks),
            reverse=True,
        )
        tail_grad = first_dec * last_grad
        crossing = prefix(
            (stretch_pair[0], tail_grad), "seq", combine, (ones_state, zero_state), True
        )
        state_grad = from_blocks(grad_blocks) + from_blocks(tail_blocks) * crossing[1][:, None]
        _, gate_pullback = jax.vjp(make_gates, delta_raw, b_state, inputs_f)
        d_delta, d_bstate, d_inputs_state = gate_pullback((state_grad * before, state_grad))
        d_cstate = jnp.einsum("scni,sci->scn", states, d_read)
        acc_dbias = acc_dbias + jnp.sum(d_delta, axis=(0, 1))
        d_delta_round = d_delta.astype(jnp.bfloat16)
        acc_delta = acc_delta + jnp.einsum(
            "scr,sci->ri", delta_round, d_delta_round, preferred_element_type=jnp.float32
        )
        low_grad_part = jnp.einsum(
            "sci,ri->scr", d_delta_round, delta_weight, preferred_element_type=jnp.float32
        )
        state_grad_part = jnp.concatenate([d_bstate, d_cstate], axis=-1)
        d_low, d_state = lax.psum((low_grad_part, state_grad_part), "mp")
        d_low_round = d_low.astype(jnp.bfloat16)
        d_state_round = d_state.astype(jnp.bfloat16)
        acc_low = acc_low + jnp.einsum(
            "sci,scr->ir", inputs_round, d_low_round, preferred_element_type=jnp.float32
        )
        acc_state = acc_state + jnp.einsum(
            "sci,scr->ir", inputs_round, d_state_round, preferred_element_type=jnp.float32
        )
        d_inputs = d_read * skip_gain + d_inputs_state
        d_inputs = d_inputs + jnp.einsum(
            "scr,ir->sci", d_low_round, low_weight, preferred_element_type=jnp.float32
        )
        d_inputs = d_inputs + jnp.einsum(
            "scr,ir->sci", d_state_round, state_weight, preferred_element_type=jnp.float32
        )
        d_conv = d_inputs * silu_slope(conv_sum)
        acc_cbias = acc_cbias + jnp.sum(d_conv, axis=(0, 1))
        tap_grads = []
        d_padded = jnp.zeros((SEQ_MB, stretch + num_taps - 1, channels), jnp.float32)
        for tap_index in range(num_taps):
            tap_grads.append(
                jnp.sum(d_conv * padded[:, tap_index : tap_index + stretch], axis=(0, 1))
            )
            d_padded = d_padded + jnp.pad(
                conv_weight[tap_index] * d_conv,
                ((0, 0), (tap_index, num_taps - 1 - tap_index), (0, 0)),
            )
        acc_conv = acc_conv + jnp.stack(tap_grads)
        back_rim = from_behind(d_padded[:, : num_taps - 1], "seq", -1)
        d_xpart = d_padded[:, num_taps - 1 :] + jnp.pad(
            back_rim, ((0, 0), (stretch - (num_taps - 1), 0), (0, 0))
        )
        d_parts_round = jnp.stack([d_xpart, d_zpart]).astype(jnp.bfloat16)
        acc_in = acc_in + jnp.einsum(
            "scd,ksci->kdi", normed, d_parts_round, preferred_element_type=jnp.float32
        )
        norm_part = jnp.einsum(
            "ksci,kdi->scd", d_parts_round, whole_in, preferred_element_type=jnp.float32
        )
        d_normed = lax.psum(norm_part, "mp")
        acc_gain = acc_gain + jnp.sum(d_normed * full_tokens * inv_rms, axis=(0, 1))
        scaled = d_normed * norm_gain
        d_full = inv_rms * scaled - full_tokens * (inv_rms * inv_rms * inv_rms) * jnp.mean(
            scaled * full_tokens, axis=-1, keepdims=True
        )
        d_mine = lax.dynamic_slice_in_dim(d_full, feature_start, feature_dev, 2)
        input_grads.append(d_out + d_mine)
    d_in_weight, d_out_weight = (
        lax.psum_scatter(acc_in, "seq", scatter_dimension=1, tiled=True),
        lax.psum_scatter(acc_out, "seq", scatter_dimension=1, tiled=True),
    )
    summed = lax.psum(
        (acc_gain, acc_conv, acc_cbias, acc_low, acc_state, acc_delta, acc_dbias, acc_skip), "seq"
    )
    return (
        jnp.concatenate(outputs, axis=0),
        jnp.concatenate(input_grads, axis=0),
        summed[0],
        d_in_weight,
        summed[1],
        summed[2],
        summed[3],
        summed[4],
        summed[5],
        summed[6],
        summed[7],
        d_out_weight,
    )


MESH = pl.DeviceIdType.MESH
F32 = jnp.float32
BF16 = jnp.bfloat16
LANE = 128
GRP = 16
PADV = 8
SGVEC = 16


def nn(a, b):
    return lax.dot_general(a, b, (((1,), (0,)), ((), ())), preferred_element_type=F32)


def nt(a, b):
    return lax.dot_general(a, b, (((1,), (1,)), ((), ())), preferred_element_type=F32)


def tn(a, b):
    return lax.dot_general(a, b, (((0,), (0,)), ((), ())), preferred_element_type=F32)


def cut(start, size):
    return pl.ds(pl.multiple_of(start, size), size)


def each(count, step):
    lax.fori_loop(0, count, lambda index, unused: (step(index), unused)[1], 0)


def by_rows(count, step):
    size = 32 if count % 32 == 0 else 16
    each(count // size, lambda index: step(cut(index * size, size)))


def wide(value, times):
    return jnp.concatenate([value] * times, axis=1) if times > 1 else value


def groups_fit(channels):
    return (LANE // GRP) % min(LANE // GRP, channels // (GRP * GRP)) == 0


class Sizes:
    def __init__(self, mesh_shape, nseq, stretch, feature_dev, model, channels, nstate, rank):
        self.S, self.M = mesh_shape["seq"], mesh_shape["mp"]
        self.Q, self.T, self.Df, self.D, self.C = nseq, stretch, feature_dev, model, channels
        self.N, self.RK = nstate, rank
        self.R = nseq * stretch
        self.Ds = model // self.S
        self.B = max(1, feature_dev // self.Ds)
        self.levels = self.S.bit_length() - 1
        self.dims = [1 << bit for bit in range(1, self.levels)]
        self.masks = [2 * value for value in range(self.S // 2)]
        self.rows_sg = -(-(2 * rank + 2 * nstate + SGVEC) // (self.S * 16)) * 16
        self.E = max(self.R, self.Ds)

    def order(self, half):
        turn = half * (len(self.dims) // 2)
        return self.dims[turn:] + self.dims[:turn]

    def fits(self, taps):
        return (
            self.S in (4, 8)
            and self.M > 1
            and self.Q == 2
            and self.T == LANE
            and self.Ds == 256
            and self.Df % self.Ds == 0
            and self.C % 512 == 0
            and self.N == GRP
            and self.RK == LANE
            and taps == 4
            and self.D >= 2 * self.C
            and groups_fit(self.C)
            and self.C * self.D <= (1 << 21)
        )


class Bunch:
    def __init__(self, names, values):
        self.__dict__.update(zip(names, values))


class Rows:
    def __init__(self, ref, base, rows, count):
        self.ref, self.base, self.rows, self.end = ref, base, rows, base + rows * count

    def block(self, index, start=0, size=None):
        first = pl.multiple_of(self.base + index * self.rows + start, 16)
        return self.ref.at[pl.ds(first, self.rows if size is None else size), :]


class Links:
    def __init__(self, sems, seq, mp):
        self.sems, self.used, self.seq, self.mp = sems, 0, seq, mp

    def sem(self, count=1):
        first = self.used
        self.used += count
        return first

    def copy(self, src, dst, send, recv, seq=None, mp=None):
        target = (self.seq if seq is None else seq, self.mp if mp is None else mp)
        return pltpu.make_async_remote_copy(
            src_ref=src,
            dst_ref=dst,
            send_sem=self.sems.at[send],
            recv_sem=self.sems.at[recv],
            device_id=target,
            device_id_type=MESH,
        )

    def arrived(self, dst, recv):
        self.copy(dst, dst, recv, recv).wait_recv()


class TreeGather:
    def __init__(self, z, links, half_view, whole_view):
        self.z, self.links, self.half, self.whole = z, links, half_view, whole_view
        self.recv = {(mask, h): links.sem() for mask in z.masks[1:] for h in range(2)}
        self.near = {mask: links.sem() for mask in z.masks}
        self.sent = []

    def push(self, mask, h, dim):
        view = self.half(self.links.seq ^ mask, h)
        copy = self.links.copy(
            view, view, self.links.sem(), self.recv[mask | dim, h], seq=self.links.seq ^ dim
        )
        copy.start()
        self.sent.append(copy)

    def take(self, mask, h):
        self.links.arrived(self.half(self.links.seq ^ mask, h), self.recv[mask, h])

    def hand(self, mask):
        view = self.whole(self.links.seq ^ mask)
        copy = self.links.copy(view, view, self.links.sem(), self.near[mask], seq=self.links.seq ^ 1)
        copy.start()
        self.sent.append(copy)

    def first(self):
        for h in range(2):
            self.push(0, h, self.z.order(h)[0])

    def second(self, h):
        for dim in self.z.order(h)[1:]:
            self.push(0, h, dim)
        if h == 0:
            self.hand(0)

    def forward(self, h):
        order = self.z.order(h)
        if len(order) > 1:
            self.take(order[0], h)
            self.push(order[0], h, order[1])

    def settle(self, far=None):
        for mask in sorted(self.z.masks[1:], key=lambda mask: bin(mask).count("1")):
            if far is not None and far != (bin(mask).count("1") > 1):
                continue
            for h in range(2):
                order = self.z.order(h)
                if len(order) == 1 or mask != order[0]:
                    self.take(mask, h)
            self.hand(mask)

    def finish(self):
        for mask in self.z.masks:
            self.links.arrived(self.whole(self.links.seq ^ 1 ^ mask), self.near[mask])

    def drain(self):
        for copy in self.sent:
            copy.wait_send()


class LineGather:
    def __init__(self, z, links, view):
        self.z, self.links, self.view = z, links, view
        self.recv = links.sem(z.M)
        self.send = links.sem(2 * z.M)

    def parts(self, depth):
        for side, way in enumerate((1, -1)):
            owner, target = self.links.mp - way * depth, self.links.mp + way
            held = (owner >= 0) & (owner < self.z.M)
            more = held & (target >= 0) & (target < self.z.M)
            yield side, owner, target, held, more

    def copy(self, side, depth, owner, target):
        view = self.view(owner)
        return self.links.copy(view, view, self.send + 2 * depth + side, self.recv + owner, mp=target)

    def step(self, depth):
        for side, owner, target, held, more in self.parts(depth):
            if depth:

                @pl.when(held)
                def _():
                    self.links.arrived(self.view(owner), self.recv + owner)

            @pl.when(more)
            def _():
                self.copy(side, depth, owner, target).start()

    def drain(self):
        for depth in range(self.z.M):
            for side, owner, target, held, more in self.parts(depth):

                @pl.when(more)
                def _():
                    self.copy(side, depth, owner, target).wait_send()


class Swap:
    def __init__(self, z, links, slot):
        self.z, self.links, self.slot = z, links, slot
        self.recv = links.sem(z.M)
        self.send = links.sem(z.M)

    def one(self, src, away):
        target = lax.rem(self.links.mp + away, self.z.M)
        return self.links.copy(src, self.slot(away - 1), self.send + away, self.recv + away, mp=target)

    def start(self, src):
        for away in range(1, self.z.M):
            self.one(src, away).start()

    def wait(self):
        for away in range(1, self.z.M):
            self.links.arrived(self.slot(away - 1), self.recv + away)

    def drain(self, src):
        for away in range(1, self.z.M):
            self.one(src, away).wait_send()


class SwapSeq:
    def __init__(self, z, links, slot):
        self.links, self.slot = links, slot
        self.pairs = [(other, links.sem(), links.sem()) for other in range(1, z.S)]
        self.sent = []

    def start(self, src):
        for other, send, recv in self.pairs:
            copy = self.links.copy(src, self.slot(other - 1), send, recv, seq=self.links.seq ^ other)
            copy.start()
            self.sent.append(copy)

    def wait(self):
        for other, send, recv in self.pairs:
            self.links.arrived(self.slot(other - 1), recv)

    def drain(self):
        for copy in self.sent:
            copy.wait_send()


def halves(rows):
    first = -(-rows // 32) * 16
    return (0, first), (first, rows - first)


class Scatter:
    def __init__(self, z, links, out, sums, far, rows):
        self.z, self.links, self.out, self.sums, self.far, self.rows = z, links, out, sums, far, rows
        self.near = {mask: links.sem() for mask in z.masks}
        self.near_send = {mask: links.sem() for mask in z.masks}
        self.sent = []
        self.late = []
        self.hops = {}
        place = 0
        for h in range(2):
            order = z.order(h)
            for step, dim in enumerate(order):
                for mask in z.masks:
                    if mask & dim and not any(mask & other for other in order[:step]):
                        self.hops[h, step, mask] = (dim, links.sem(), links.sem(), place)
                        place += 1
        self.slots = place

    def half(self, mask, h):
        start, size = halves(self.rows)[h]
        return self.sums.block(mask // 2, start, size)

    def came(self, h, place):
        return self.far.block(place, 0, halves(self.rows)[h][1])

    def first(self, make):
        links = self.links
        for mask in self.by_need():
            src = make(links.seq ^ 1 ^ mask, mask)
            copy = links.copy(src, self.sums.block(mask // 2), self.near_send[mask], self.near[mask], seq=links.seq ^ 1)
            copy.start()
            self.sent.append(copy)

    def by_need(self):
        return sorted(self.z.masks, key=lambda mask: -bin(mask).count("1"))

    def second(self, add, send=False, masks=None):
        links = self.links
        for mask in self.by_need() if masks is None else masks:
            links.arrived(self.sums.block(mask // 2), self.near[mask])
            add(links.seq ^ mask, mask)
            if send:
                self.send(0, mask)

    def send(self, step, only=None):
        links = self.links
        for (h, at, mask), (dim, send, recv, place) in self.hops.items():
            if at == step and only in (None, mask):
                copy = links.copy(
                    self.half(mask, h), self.came(h, place), send, recv, seq=links.seq ^ dim
                )
                copy.start()
                self.sent.append(copy)

    def fold(self, step):
        self.late.append(step)
        if step < len(self.z.dims) - 1:
            going = {(h, mask) for h, at, mask in self.hops if at == step + 1}
            self.take(step, lambda h, into: (h, into) in going)
            self.send(step + 1)

    def rest(self):
        for step in self.late:
            going = {(h, mask) for h, at, mask in self.hops if at == step + 1}
            self.take(step, lambda h, into: (h, into) not in going)

    def take(self, step, wanted):
        for (h, at, mask), (dim, send, recv, place) in self.hops.items():
            if at != step or not wanted(h, mask ^ dim):
                continue
            self.links.arrived(self.came(h, place), recv)
            if step < len(self.z.dims) - 1:
                half, came = self.half(mask ^ dim, h), self.came(h, place)

                def add(rows):
                    half[rows, :] = (half[rows, :].astype(F32) + came[rows, :].astype(F32)).astype(BF16)

                by_rows(halves(self.rows)[h][1], add)

    def total(self, write):
        self.rest()
        last = len(self.z.dims) - 1
        for (h, at, mask), (dim, send, recv, place) in self.hops.items():
            if at == last:
                half, came = self.half(0, h), self.came(h, place)
                first, count = halves(self.rows)[h]

                def add(rows):
                    value = half[rows, :].astype(F32) + came[rows, :].astype(F32)
                    write(pl.ds(pl.multiple_of(first + rows.start, 16), rows.size), value)

                by_rows(count, add)

    def drain(self):
        for copy in self.sent:
            copy.wait_send()


def slots_of(z):
    return Scatter(z, Links(None, 0, 0), None, None, None, 0).slots


def scratch_of(z):
    V = pltpu.VMEM
    half = z.S // 2
    slots = slots_of(z)
    return dict(
        tok=V((z.R, z.Df), BF16),
        cot=V((z.R, z.Df), F32),
        gain=V((1, z.D), F32),
        convw=V((4, z.C), F32),
        convb=V((1, z.C), F32),
        dbias=V((1, z.C), F32),
        skip=V((1, z.C), F32),
        loww=V((z.C, z.RK), BF16),
        statewt=V((2 * z.N, z.C), BF16),
        deltaw=V((z.RK, z.C), BF16),
        tokg=V((z.S, z.R, z.Ds), BF16),
        halg=V((z.S, 16, z.Ds), BF16),
        hals=V((z.B, 16, z.Ds), BF16),
        db=V((z.R, z.D), BF16),
        inv=V((z.R, LANE), F32),
        normed=V((z.R + 16, z.D), BF16),
        normt=V((z.D, z.R), BF16),
        wx=V((2, z.D, z.C), BF16),
        wo=V((z.C, z.D), BF16),
        xpad=V((z.Q, 8 + z.T, z.C), F32),
        dcp=V((z.Q, z.T + 8, z.C), F32),
        conv=V((z.E, z.C), F32),
        s=V((z.E, z.C), F32),
        su=V((z.R, z.C), F32),
        fac=V((z.E, z.C), F32),
        zp=V((z.R, z.C), F32),
        rd=V((z.R, z.C), F32),
        dr=V((z.R, z.C), F32),
        u=V((z.R, z.C), BF16),
        gat=V((z.R, z.C), BF16),
        gatt=V((z.C, z.R), BF16),
        ddr=V((z.R, z.C), BF16),
        dzr=V((z.R, z.C), BF16),
        dxr=V((z.R, z.C), BF16),
        lowp=V((z.Q, z.M, z.T, z.RK), BF16),
        stp=V((z.Q, z.M, 2 * z.N, z.T), F32),
        low=V((z.R, z.RK), BF16),
        dlow=V((z.R, z.RK), BF16),
        dlowt=V((z.RK, z.R), BF16),
        dst=V((2 * z.N, z.R), BF16),
        st=V((2 * z.N, z.R), F32),
        blkb=V((z.R, GRP * z.N), BF16),
        blkk=V((z.R, GRP * z.N), BF16),
        blkc=V((z.R, GRP * z.N), BF16),
        bc=V((z.Q, z.T, 2 * z.N, LANE), F32),
        hist=V((z.Q * (z.T + 1) * z.N, z.C), BF16),
        ptot=V((z.Q, z.N, z.C), F32),
        stot=V((z.Q, z.N, z.C), F32),
        ppre=V((z.Q, z.N, z.C), F32),
        spre=V((z.Q, z.N, z.C), F32),
        csend=V((z.levels, z.Q, 2, z.N, z.C), BF16),
        crecv=V((z.levels, z.Q, 2, z.N, z.C), BF16),
        bsend=V((z.levels, z.Q, z.N, z.C), BF16),
        brecv=V((z.levels, z.Q, z.N, z.C), BF16),
        est=V((3, z.N, z.R), F32),
        dlowp=V((z.Q, z.M, z.T, z.RK), BF16),
        dstp=V((z.Q, z.M, 2 * z.N, z.T), BF16),
        orecv=V((z.M - 1, z.R, z.Df), BF16),
        nrecv=V((z.M - 1, z.R, z.Df), BF16),
        near_o=V((half * z.C, z.Ds), BF16),
        sum_o=V((half * z.C, z.Ds), BF16),
        far_o=V((slots * (z.C // 2), z.Ds), BF16),
        near_i=V((half * z.Ds, z.C), BF16),
        sum_1=V((half * z.Ds, z.C), BF16),
        far_1=V((slots * (z.Ds // 2), z.C), BF16),
        vec=V((SGVEC, z.C), F32),
        gv=V((z.D // LANE, LANE), F32),
        gvs=V((z.D // LANE, LANE), F32),
        gvr=V((z.S - 1, z.D // LANE, LANE), F32),
        gvm=V((z.M - 1, z.D // LANE, LANE), F32),
        mean=V((z.R, LANE), F32),
        mrow=V((z.M, 8, z.R), F32),
        sems=pltpu.SemaphoreType.DMA((420,)),
        local=pltpu.SemaphoreType.DMA((16,)),
        ready=pltpu.SemaphoreType.REGULAR((z.levels,)),
    )


def silu_parts(value):
    gate = 1.0 / (1.0 + jnp.exp(-value))
    return gate, value * gate


def fused_kernel(z, names, *refs):
    r = Bunch(names, refs)
    seq, mp = lax.axis_index("seq"), lax.axis_index("mp")
    links = Links(r.sems, seq, mp)
    lanes_all = z.C // LANE
    first_block = mp * z.B

    def lane_loop(step):
        each(z.C // LANE, lambda index: step(cut(index * LANE, LANE)))

    barrier = pltpu.get_barrier_semaphore()
    ahead, behind = lax.rem(seq + 1, z.S), lax.rem(seq + z.S - 1, z.S)
    partners = [(seq ^ other, mp) for other in range(1, z.S)] + [(ahead, mp), (behind, mp)]
    partners += [(seq, lax.rem(mp + away, z.M)) for away in range(1, z.M)]
    for partner in partners:
        pl.semaphore_signal(barrier, inc=1, device_id=partner, device_id_type=MESH)
    local = r.local
    mine_in = lambda k: r.wx.at[k, cut(seq * z.Ds, z.Ds), :]
    loads = [
        pltpu.make_async_copy(r.win.at[0], mine_in(0), local.at[0]),
        pltpu.make_async_copy(r.win.at[1], mine_in(1), local.at[1]),
        pltpu.make_async_copy(r.wout, r.wo.at[:, cut(seq * z.Ds, z.Ds)], local.at[2]),
    ]
    pairs = [
        (r.tok_in, r.tok),
        (r.cot_in, r.cot),
        (r.gain_in, r.gain),
        (r.convw_in, r.convw),
        (r.convb_in, r.convb),
        (r.dbias_in, r.dbias),
        (r.skip_in, r.skip),
        (r.loww_in, r.loww),
        (r.statewt_in, r.statewt),
        (r.deltaw_in, r.deltaw),
    ]
    own = [pltpu.make_async_copy(src, dst, local.at[5 + index]) for index, (src, dst) in enumerate(pairs)]
    own[0].start()
    for load in loads:
        load.start()
    for copy in own[1:]:
        copy.start()
    own[0].wait()
    for b in range(z.B):
        r.tokg[first_block + b] = r.tok[:, b * z.Ds : (b + 1) * z.Ds]
        tails = [
            r.tok[q * z.T + z.T - 16 : q * z.T + z.T, b * z.Ds : (b + 1) * z.Ds].astype(F32)[8:]
            for q in range(z.Q)
        ]
        r.hals[b] = jnp.concatenate(tails, axis=0).astype(BF16)

    pl.semaphore_wait(barrier, len(partners))

    def of_in(k):
        def half(owner, h):
            return r.wx.at[k, cut(owner * z.Ds + h * (z.Ds // 2), z.Ds // 2), :]

        return TreeGather(z, links, half, lambda owner: r.wx.at[k, cut(owner * z.Ds, z.Ds), :])

    tree_x, tree_z = of_in(0), of_in(1)
    tree_o = TreeGather(
        z,
        links,
        lambda owner, h: r.wo.at[pl.ds(h * (z.C // 2), z.C // 2), cut(owner * z.Ds, z.Ds)],
        lambda owner: r.wo.at[:, cut(owner * z.Ds, z.Ds)],
    )
    line_t = [
        LineGather(z, links, lambda owner, q=q: r.tokg.at[pl.ds(owner * z.B, z.B), pl.ds(q * z.T, z.T), :])
        for q in range(z.Q)
    ]
    line_h = LineGather(z, links, lambda owner: r.halg.at[pl.ds(owner * z.B, z.B)])
    line_d = LineGather(z, links, lambda owner: r.db.at[:, cut(owner * z.Df, z.Df)])
    depth = len(z.dims)

    hal_send, hal_recv = links.sem(), links.sem()
    hal_mine = r.halg.at[pl.ds(first_block, z.B)]
    hal = links.copy(r.hals, hal_mine, hal_send, hal_recv, seq=ahead)
    hal.start()
    for line in line_t:
        line.step(0)
    loads[0].wait()
    tree_x.first()
    tree_x.second(0)
    tree_x.second(1)

    for copy in own[1:]:
        copy.wait()

    def weight_of(q):
        total = jnp.float32(0.0)
        for group in range(r.groupw.shape[0]):
            total = total + jnp.where(r.seqg[q] == group, r.groupw[group], 0.0)
        return total

    seq_weight = [weight_of(q) for q in range(z.Q)]
    for q in range(z.Q):
        rows = pl.ds(q * z.T, z.T)
        for b in range(z.B):
            part = r.cot[rows, b * z.Ds : (b + 1) * z.Ds] * seq_weight[q]
            r.db[rows, cut((first_block + b) * z.Ds, z.Ds)] = part.astype(BF16)

    links.arrived(hal_mine, hal_recv)
    line_h.step(0)
    for line in line_t:
        line.step(1)
    tree_x.forward(0)
    tree_x.forward(1)
    loads[1].wait()
    tree_z.first()
    tree_z.second(0)
    tree_z.second(1)
    line_h.step(1)
    for far in range(2, z.M):
        for line in line_t:
            line.step(far)
        line_h.step(far)
        if far == 2:
            tree_x.settle(False)
    if z.M == 2:
        tree_x.settle(False)
    line_d.step(0)

    def add_squares(j, total):
        part = r.tokg[j].astype(F32)
        edge = r.halg[j].astype(F32)
        return (
            total[0] + jnp.sum(part * part, axis=1, keepdims=True),
            total[1] + jnp.sum(edge * edge, axis=1, keepdims=True),
        )

    squares = lax.fori_loop(
        0, z.S, add_squares, (jnp.zeros((z.R, 1), F32), jnp.zeros((16, 1), F32))
    )
    inv = lax.rsqrt(squares[0] * (1.0 / z.D) + EPSILON)
    inv_edge = lax.rsqrt(squares[1] * (1.0 / z.D) + EPSILON)
    r.inv[...] = jnp.broadcast_to(inv, (z.R, LANE))

    def norm_block(j):
        features = cut(j * z.Ds, z.Ds)
        gain = r.gain[:, features]
        normed = r.tokg[j].astype(F32) * wide(r.inv[...], z.Ds // LANE) * gain
        r.normed[: z.R, features] = normed.astype(BF16)
        edge = r.halg[j].astype(F32) * inv_edge * gain
        r.normed[z.R :, features] = edge.astype(BF16)
        r.normt[features, :] = normed.T.astype(BF16)

    each(z.S, norm_block)
    tree_x.settle(True)
    tree_x.finish()

    def x_chunk(index):
        lanes = cut(index * 256, 256)
        part = nn(r.normed[...], r.wx[0, :, lanes]).astype(BF16).astype(F32)
        for q in range(z.Q):
            edge = part[z.R + 8 * q : z.R + 8 * q + 8]
            r.xpad[q, 0:8, lanes] = jnp.where(seq > 0, edge, 0.0)
            r.xpad[q, 8 : 8 + z.T, lanes] = part[q * z.T : (q + 1) * z.T]

    each(z.C // 256, x_chunk)
    tree_z.forward(0)
    tree_z.forward(1)
    loads[2].wait()
    tree_o.first()
    tree_o.second(0)

    def rows_of(q):
        return pl.ds(q * z.T, z.T)

    def conv(q):
        def conv_lanes(lanes):
            total = jnp.broadcast_to(r.convb[:, lanes], (z.T, LANE))
            for tap in range(4):
                total = total + r.convw[tap : tap + 1, lanes] * r.xpad[q, 5 + tap : 5 + tap + z.T, lanes]
            r.conv[rows_of(q), lanes] = total
            r.u[rows_of(q), lanes] = silu_parts(total)[1].astype(BF16)

        lane_loop(conv_lanes)

    swap_low = [Swap(z, links, lambda slot, q=q: r.lowp.at[q, slot]) for q in range(z.Q)]
    swap_st = [Swap(z, links, lambda slot, q=q: r.stp.at[q, slot]) for q in range(z.Q)]
    low_mine = [r.lowp.at[q, z.M - 1] for q in range(z.Q)]
    st_mine = [r.stp.at[q, z.M - 1] for q in range(z.Q)]

    def project(q):
        u = r.u[rows_of(q), :]
        st_mine[q][...] = nt(r.statewt[...], u)
        swap_st[q].start(st_mine[q])
        low_mine[q][...] = nn(u, r.loww[...]).astype(BF16)
        swap_low[q].start(low_mine[q])

    rows_i = lax.broadcasted_iota(jnp.int32, (z.T, GRP * z.N), 0)
    cols_i = lax.broadcasted_iota(jnp.int32, (z.T, GRP * z.N), 1)
    diagonal = lax.rem(rows_i, GRP) == cols_i // z.N
    rep_n = lax.broadcasted_iota(jnp.int32, (2 * z.N, GRP * z.N), 0)
    rep_j = lax.rem(lax.broadcasted_iota(jnp.int32, (2 * z.N, GRP * z.N), 1), z.N)
    rep_b = (rep_n == rep_j).astype(BF16)
    rep_c = (rep_n == rep_j + z.N).astype(BF16)
    only_b = lax.broadcasted_iota(jnp.int32, (z.T, LANE), 1) < z.N

    def columns_of(value):
        return jnp.concatenate([value, jnp.zeros((LANE - 2 * z.N, z.T), F32)], axis=0).T

    def keys(q):
        swap_st[q].wait()
        st = r.stp[q, 0]
        for slot in range(1, z.M):
            st = st + r.stp[q, slot]
        r.st[:, rows_of(q)] = st

        def spread(index):
            turned = pltpu.roll(st, lax.rem(z.T - index * 32, z.T), 1)
            for j in range(32):
                r.bc[q, index * 32 + j] = jnp.broadcast_to(turned[:, j : j + 1], (2 * z.N, LANE))

        each(z.T // 32, spread)
        nat = columns_of(st)
        key_sq = jnp.sum(jnp.where(only_b, nat * nat, 0.0), axis=1, keepdims=True)
        swap_low[q].wait()
        low = r.lowp[q, 0].astype(F32)
        for slot in range(1, z.M):
            low = low + r.lowp[q, slot].astype(F32)
        low = low.astype(BF16)
        r.low[rows_of(q), :] = low

        def step_chunk(index):
            lanes = cut(index * 256, 256)
            raw = nn(low, r.deltaw[:, lanes]) + r.dbias[:, lanes]
            beta = 1.0 / (1.0 + jnp.exp(-raw))
            scale = 1.0 / (1.0 + beta * key_sq)
            step = beta * scale
            r.s[rows_of(q), lanes] = step
            r.su[rows_of(q), lanes] = step * r.u[rows_of(q), lanes].astype(F32)
            r.fac[rows_of(q), lanes] = scale * step * (1.0 - beta)

        each(z.C // 256, step_chunk)

    def key_blocks(q):
        nat16 = columns_of(r.st[:, rows_of(q)])[:, : 2 * z.N].astype(BF16)
        spread_b = jnp.where(diagonal, nn(nat16, rep_b), 0.0)
        r.blkb[rows_of(q), :] = spread_b.astype(BF16)
        r.blkk[rows_of(q), :] = (spread_b * spread_b).astype(BF16)
        r.blkc[rows_of(q), :] = jnp.where(diagonal, nn(nat16, rep_c), 0.0).astype(BF16)

    span = 512 if z.C % 512 == 0 else 256

    def token(q, t):
        return pl.ds(q * z.T + t, 1)

    def totals(q):
        def lane_part(index):
            lanes = cut(index * span, span)

            def tokens8(i, carry):
                product, state = carry
                for j in range(8):
                    row = token(q, i * 8 + j)
                    step, drive = r.s[row, lanes], r.su[row, lanes]
                    key = r.bc[q, i * 8 + j, : z.N, :]
                    decay = 1.0 - step * wide(key * key, span // LANE)
                    product = product * decay
                    state = decay * state + drive * wide(key, span // LANE)
                return product, state

            start = (jnp.ones((z.N, span), F32), jnp.zeros((z.N, span), F32))
            product, state = lax.fori_loop(0, z.T // 8, tokens8, start)
            r.ptot[q, :, lanes] = product
            r.stot[q, :, lanes] = state

        each(z.C // span, lane_part)

    carry_sems = [[(links.sem(), links.sem()) for q in range(z.Q)] for level in range(z.levels)]
    back_sems = [[(links.sem(), links.sem()) for q in range(z.Q)] for level in range(z.levels)]
    carry_copies = []

    def upper_at(level):
        return lax.rem(seq // (1 << level), 2) == 1

    def carry_send(level, q):
        r.csend[level, q, 0] = r.ptot[q].astype(BF16)
        r.csend[level, q, 1] = r.stot[q].astype(BF16)
        copy = links.copy(
            r.csend.at[level, q], r.crecv.at[level, q], *carry_sems[level][q], seq=seq ^ (1 << level)
        )
        copy.start()
        carry_copies.append(copy)

    def carry_take(level, q):
        links.arrived(r.crecv.at[level, q], carry_sems[level][q][1])
        upper = upper_at(level)
        other_p, other_s = r.crecv[level, q, 0].astype(F32), r.crecv[level, q, 1].astype(F32)
        mine_p, mine_s = r.ptot[q], r.stot[q]
        if level == 0:
            r.spre[q] = jnp.where(upper, other_s, 0.0)
            r.ppre[q] = jnp.where(upper, other_p, 1.0)
        else:
            pre_p, pre_s = r.ppre[q], r.spre[q]
            r.spre[q] = jnp.where(upper, pre_p * other_s + pre_s, pre_s)
            r.ppre[q] = jnp.where(upper, pre_p * other_p, pre_p)
        if level < z.levels - 1:
            r.stot[q] = jnp.where(upper, mine_p * other_s + mine_s, other_p * mine_s + other_s)
            r.ptot[q] = mine_p * other_p

    def back_send(level, q):
        r.bsend[level, q] = r.stot[q].astype(BF16)
        copy = links.copy(
            r.bsend.at[level, q], r.brecv.at[level, q], *back_sems[level][q], seq=seq ^ (1 << level)
        )
        copy.start()
        carry_copies.append(copy)

    def back_take(level, q):
        links.arrived(r.brecv.at[level, q], back_sems[level][q][1])
        upper = upper_at(level)
        other = r.brecv[level, q].astype(F32)
        other_p, mine_p = r.crecv[level, q, 0].astype(F32), r.csend[level, q, 0].astype(F32)
        mine = r.stot[q]
        if level == 0:
            r.spre[q] = jnp.where(upper, 0.0, other)
            r.ppre[q] = jnp.where(upper, 1.0, other_p)
        else:
            pre_p, pre = r.ppre[q], r.spre[q]
            r.spre[q] = jnp.where(upper, pre, pre + pre_p * other)
            r.ppre[q] = jnp.where(upper, pre_p, pre_p * other_p)
        if level < z.levels - 1:
            r.stot[q] = jnp.where(upper, other + other_p * mine, mine + mine_p * other)

    def past_rows(q, slot, count=1):
        return pl.ds(pl.multiple_of((q * (z.T + 1) + slot) * z.N, z.N), count * z.N)

    groups = z.T // GRP

    def walk(q):
        r.hist[past_rows(q, 0), :] = r.spre[q].astype(BF16)

        def lane_part(index):
            lanes = cut(index * span, span)

            def tokens8(i, state):
                for j in range(8):
                    row = token(q, i * 8 + j)
                    step, drive = r.s[row, lanes], r.su[row, lanes]
                    key = r.bc[q, i * 8 + j, : z.N, :]
                    decay = 1.0 - step * wide(key * key, span // LANE)
                    state = decay * state + drive * wide(key, span // LANE)
                    r.hist[past_rows(q, i * 8 + j + 1), lanes] = state.astype(BF16)
                return state

            lax.fori_loop(0, z.T // 8, tokens8, r.spre[q, :, lanes])

        each(z.C // span, lane_part)
        reads = []
        for i in range(groups):
            rows = pl.ds(q * z.T + i * GRP, GRP)
            reads.append((rows, nn(r.blkc[rows, :], r.hist[past_rows(q, i * GRP + 1, GRP), :])))
        for rows, value in reads:
            r.rd[rows, :] = value

    def z_chunk(index):
        lanes = cut(index * 256, 256)
        r.zp[:, lanes] = nn(r.normed[: z.R, :], r.wx[1, :, lanes])

    conv(0)
    project(0)
    conv(1)
    project(1)
    line_d.step(1)
    keys(0)
    totals(0)
    carry_send(0, 0)
    keys(1)
    carry_take(0, 0)
    carry_send(1, 0)
    totals(1)
    carry_send(0, 1)
    carry_take(0, 1)
    carry_send(1, 1)
    tree_o.second(1)
    tree_o.forward(1)
    line_d.step(2)
    tree_z.settle()
    key_blocks(0)
    key_blocks(1)
    for level in range(1, z.levels - 1):
        for q in range(z.Q):
            carry_take(level, q)
            carry_send(level + 1, q)
    tree_o.forward(0)
    tree_z.finish()
    each(z.C // 256, z_chunk)
    carry_take(z.levels - 1, 0)
    walk(0)
    for far in range(3, z.M):
        line_d.step(far)
    tree_o.settle(False)
    carry_take(z.levels - 1, 1)
    walk(1)
    r.vec[...] = jnp.zeros_like(r.vec)

    def gate_lanes(lanes):
        for q in range(z.Q):
            rows = rows_of(q)
            out = r.rd[rows, lanes] + r.skip[:, lanes] * r.u[rows, lanes].astype(F32)
            r.rd[rows, lanes] = out
            gated = out * silu_parts(r.zp[rows, lanes])[1]
            r.gat[rows, lanes] = gated.astype(BF16)
            r.gatt[lanes, rows] = gated.T.astype(BF16)

    lane_loop(gate_lanes)

    def into(near, term):
        def make(device, mask):
            block = near.block(mask // 2)
            block[...] = term(device).astype(BF16)
            return block

        return make

    def onto(sums, term):
        def add(device, mask):
            block = sums.block(mask // 2)
            block[...] = (term(device) + block[...].astype(F32)).astype(BF16)

        return add

    half_s, slots = z.S // 2, slots_of(z)
    sg_rows = z.rows_sg
    near_o, near_i = Rows(r.near_o, 0, z.C, half_s), Rows(r.near_i, 0, z.Ds, half_s)
    sum_o, far_o = Rows(r.sum_o, 0, z.C, half_s), Rows(r.far_o, 0, z.C // 2, slots)
    sum_1, far_1 = Rows(r.sum_1, 0, z.Ds, half_s), Rows(r.far_1, 0, z.Ds // 2, slots)
    sum_0 = Rows(r.hist, 0, z.Ds, half_s)
    far_0 = Rows(r.hist, sum_0.end, z.Ds // 2, slots)
    sum_s = Rows(r.hist, far_0.end, sg_rows, half_s)
    far_s = Rows(r.hist, sum_s.end, halves(sg_rows)[0][1], slots)
    sgp = Rows(r.hist, far_s.end, sg_rows, z.S)
    small = Rows(r.hist, sgp.end, sg_rows, z.S)
    scatter_o = Scatter(z, links, None, sum_o, far_o, z.C)
    scatter_1 = Scatter(z, links, None, sum_1, far_1, z.Ds)
    scatter_0 = Scatter(z, links, None, sum_0, far_0, z.Ds)
    scatter_s = Scatter(z, links, None, sum_s, far_s, sg_rows)
    term_o = lambda device: nn(r.gatt[...], r.db[:, cut(device * z.Ds, z.Ds)])
    term_1 = lambda device: nn(r.normt[cut(device * z.Ds, z.Ds), :], r.dzr[...])
    term_0 = lambda device: nn(r.normt[cut(device * z.Ds, z.Ds), :], r.dxr[...])

    tree_o.settle(True)
    most = scatter_o.by_need()
    scatter_o.first(into(near_o, term_o))
    tree_o.finish()

    def gated_grad(index):
        lanes = cut(index * 256, 256)
        r.dr[:, lanes] = nt(r.db[...], r.wo[lanes, :])

    each(z.C // 256, gated_grad)

    def gate_back(lanes):
        for q in range(z.Q):
            rows = rows_of(q)
            part, grad = r.zp[rows, lanes], r.dr[rows, lanes]
            gate, silu = silu_parts(part)
            d_read = grad * silu
            r.dr[rows, lanes] = d_read
            r.dzr[rows, lanes] = (grad * r.rd[rows, lanes] * gate * (1.0 + part * (1.0 - gate))).astype(BF16)
            r.vec[6:7, lanes] += jnp.sum(d_read * r.u[rows, lanes].astype(F32), axis=0, keepdims=True)

    lane_loop(gate_back)
    scatter_o.second(onto(sum_o, term_o), send=True, masks=most[:1])

    swap_out = Swap(z, links, lambda slot: r.orecv.at[slot])

    def partial_of(owner):
        return r.normed.at[pl.ds(0, z.R), cut(owner * z.Df, z.Df)]

    def branch_to(index):
        away = index + 1
        owner = lax.rem(mp + away, z.M)
        for b in range(z.B):
            j = owner * z.B + b
            r.normed[: z.R, cut(j * z.Ds, z.Ds)] = nn(r.gat[...], r.wo[:, cut(j * z.Ds, z.Ds)]).astype(BF16)

        @pl.when(away < z.M)
        def _():
            swap_out.one(partial_of(owner), away).start()

    def totals_back(q):
        def lane_part(index):
            lanes = cut(index * span, span)

            def tokens8(i, tail):
                for j in reversed(range(8)):
                    t = z.T - 8 - i * 8 + j
                    row = token(q, t)
                    step, grad = r.s[row, lanes], r.dr[row, lanes]
                    key, query = r.bc[q, t, : z.N, :], r.bc[q, t, z.N :, :]
                    decay = 1.0 - step * wide(key * key, span // LANE)
                    tail = decay * (grad * wide(query, span // LANE) + tail)
                return tail

            r.stot[q, :, lanes] = lax.fori_loop(0, z.T // 8, tokens8, jnp.zeros((z.N, span), F32))

        each(z.C // span, lane_part)

    lane_index = lax.broadcasted_iota(jnp.int32, (z.N, LANE), 1)

    def lane_sum(value):
        total = value[:, :LANE]
        for part in range(1, lanes_all):
            total = total + value[:, part * LANE : (part + 1) * LANE]
        return jnp.sum(total, axis=1, keepdims=True)

    batch = min(groups, z.C // (GRP * z.N))

    def walk_back(q):
        def group(index, carry):
            tail, sum_gh, sum_g = carry
            i = groups - 1 - index
            for j in reversed(range(GRP)):
                t = i * GRP + j
                row = token(q, t)
                step, drive, grad = r.s[row, :], r.su[row, :], r.dr[row, :]
                key, query = r.bc[q, t, : z.N, :], r.bc[q, t, z.N :, :]
                before = r.hist[past_rows(q, t), :].astype(F32)
                state_grad = grad * wide(query, lanes_all) + tail
                crossed = state_grad * before
                place = pl.ds(pl.multiple_of(lax.rem(i, batch) * GRP * z.N + j * z.N, z.N), z.N)
                r.wo[place, : z.C] = state_grad.astype(BF16)
                r.wo[place, z.C : 2 * z.C] = crossed.astype(BF16)
                here = lane_index == t
                sum_gh = jnp.where(here, lane_sum(step * crossed), sum_gh)
                sum_g = jnp.where(here, lane_sum(drive * state_grad), sum_g)
                tail = (1.0 - step * wide(key * key, lanes_all)) * state_grad
            return tail, sum_gh, sum_g

        zero = jnp.zeros((z.N, LANE), F32)
        carry = (r.spre[q], zero, zero)
        for start in range(0, groups, batch):
            carry = lax.fori_loop(start, start + batch, group, carry)
            sums = []
            for slot in range(batch):
                rows = pl.ds(q * z.T + (groups - start - batch + slot) * GRP, GRP)
                place = pl.ds(slot * GRP * z.N, GRP * z.N)
                sums.append(
                    (
                        rows,
                        nn(r.blkb[rows, :], r.wo[place, : z.C]),
                        nn(r.blkk[rows, :], r.wo[place, z.C : 2 * z.C]),
                    )
                )
            for rows, by_key, by_square in sums:
                r.rd[rows, :] = by_key
                r.zp[rows, :] = by_square
        columns = rows_of(q)
        for part in range(2):
            r.est[part, :, columns] = carry[1 + part]

    def query_sums(q):
        parts = []
        for i in range(groups):
            rows = pl.ds(q * z.T + i * GRP, GRP)
            parts.append(nt(r.dr[rows, :].astype(BF16), r.hist[past_rows(q, i * GRP + 1, GRP), :]))
        blocks = jnp.where(diagonal, jnp.concatenate(parts, axis=0), 0.0).astype(BF16)
        r.est[2, :, rows_of(q)] = nt(rep_b[: z.N], blocks)

    def step_back(q):
        rows = rows_of(q)

        def step_lanes(lanes):
            sum_b, step = r.rd[rows, lanes], r.s[rows, lanes]
            d_step = r.u[rows, lanes].astype(F32) * sum_b - r.zp[rows, lanes]
            r.rd[rows, lanes] = step * sum_b
            d_raw = d_step * r.fac[rows, lanes]
            r.ddr[rows, lanes] = d_raw.astype(BF16)
            r.gat[rows, lanes] = (d_step * step * step).astype(BF16)
            r.vec[5:6, lanes] += jnp.sum(d_raw, axis=0, keepdims=True)

        lane_loop(step_lanes)

    swap_dlow = [Swap(z, links, lambda slot, q=q: r.dlowp.at[q, slot]) for q in range(z.Q)]
    swap_dst = [Swap(z, links, lambda slot, q=q: r.dstp.at[q, slot]) for q in range(z.Q)]
    dlow_mine = [r.dlowp.at[q, z.M - 1] for q in range(z.Q)]
    dst_mine = [r.dstp.at[q, z.M - 1] for q in range(z.Q)]

    def project_back(q):
        rows = rows_of(q)
        key_grad = nt(jnp.ones((16, z.C), BF16), r.gat[rows, :])[0:1]
        now = r.st[: z.N, rows]
        d_key = r.est[1, :, rows] - 2.0 * now * r.est[0, :, rows] - 2.0 * now * key_grad
        dst_mine[q][...] = jnp.concatenate([d_key, r.est[2, :, rows]], axis=0).astype(BF16)
        swap_dst[q].start(dst_mine[q])
        dlow_mine[q][...] = nt(r.ddr[rows, :], r.deltaw[...]).astype(BF16)
        swap_dlow[q].start(dlow_mine[q])

    def sums_back(q):
        rows = rows_of(q)
        swap_dlow[q].wait()
        swap_dst[q].wait()
        dlow = r.dlowp[q, 0].astype(F32)
        dst = r.dstp[q, 0].astype(F32)
        for slot in range(1, z.M):
            dlow = dlow + r.dlowp[q, slot].astype(F32)
            dst = dst + r.dstp[q, slot].astype(F32)
        r.dlow[rows, :] = dlow.astype(BF16)
        r.dlowt[:, rows] = dlow.T.astype(BF16)
        r.dst[:, rows] = dst.astype(BF16)
        dlow16, dst16 = dlow.astype(BF16), columns_of(dst)[:, : 2 * z.N].astype(BF16)

        def inputs_chunk(index):
            lanes = cut(index * 256, 256)
            r.su[rows, lanes] = nt(dlow16, r.loww[lanes, :]) + nn(dst16, r.statewt[:, lanes])

        each(z.C // 256, inputs_chunk)

    rim = [
        links.copy(
            r.dcp.at[q, pl.ds(0, 8), :],
            r.dcp.at[q, pl.ds(z.T, 8), :],
            links.sem(),
            links.sem(),
            seq=behind,
        )
        for q in range(z.Q)
    ]

    def conv_back(q):
        rows = rows_of(q)

        def conv_lanes(lanes):
            total = r.su[rows, lanes] + r.rd[rows, lanes] + r.skip[:, lanes] * r.dr[rows, lanes]
            value = r.conv[rows, lanes]
            gate = silu_parts(value)[0]
            d_conv = total * gate * (1.0 + value * (1.0 - gate))
            r.dcp[q, 0 : z.T, lanes] = d_conv
            r.vec[4:5, lanes] += jnp.sum(d_conv, axis=0, keepdims=True)
            for tap in range(4):
                r.vec[tap : tap + 1, lanes] += jnp.sum(
                    d_conv * r.xpad[q, 5 + tap : 5 + tap + z.T, lanes], axis=0, keepdims=True
                )

        lane_loop(conv_lanes)
        rim[q].start()

    def x_back(q):
        rim[q].wait_recv()

        def x_lanes(lanes):
            edge = r.dcp[q, z.T : z.T + 8, lanes]
            r.dcp[q, z.T : z.T + 8, lanes] = jnp.where(seq < z.S - 1, edge, 0.0)
            total = jnp.zeros((z.T, LANE), F32)
            for tap in range(4):
                total = total + r.convw[tap : tap + 1, lanes] * r.dcp[q, 3 - tap : 3 - tap + z.T, lanes]
            r.dxr[rows_of(q), lanes] = total.astype(BF16)

        lane_loop(x_lanes)

    swap_n = [Swap(z, links, lambda slot, q=q: r.nrecv.at[slot, rows_of(q), :]) for q in range(z.Q)]

    def normed_of(q, owner):
        return r.normed.at[rows_of(q), cut(owner * z.Df, z.Df)]

    def normed_part(q):
        rows = rows_of(q)

        def normed_to(index, means):
            away = index + 1
            owner = lax.rem(mp + away, z.M)
            for b in range(z.B):
                j = owner * z.B + b
                features = cut(j * z.Ds, z.Ds)
                part = nt(r.dxr[rows, :], r.wx[0, features, :]) + nt(r.dzr[rows, :], r.wx[1, features, :])
                r.normed[rows, features] = part.astype(BF16)
                scaled = part * r.tokg[j, rows, :].astype(F32)
                by_gain = jnp.sum(scaled * wide(r.inv[rows, :], z.Ds // LANE), axis=0, keepdims=True)
                for piece in range(z.Ds // LANE):
                    place = pl.ds(j * (z.Ds // LANE) + piece, 1)
                    value = by_gain[:, piece * LANE : (piece + 1) * LANE]
                    r.gv[place, :] = value if q == 0 else r.gv[place, :] + value
                means = means + jnp.sum(scaled * r.gain[:, features], axis=1, keepdims=True)

            @pl.when(away < z.M)
            def _():
                swap_n[q].one(normed_of(q, owner), away).start()

            return means

        means = lax.fori_loop(0, z.M, normed_to, jnp.zeros((z.T, 1), F32))
        mean_mine[:, rows] = jnp.broadcast_to(means, (z.T, LANE)).T[0:8]

    swap_m = Swap(z, links, lambda slot: r.mrow.at[slot])
    mean_mine = r.mrow.at[z.M - 1]

    def settle_back(level, q):
        back_take(level, q)
        if level < z.levels - 1:
            back_send(level + 1, q)

    totals_back(0)
    back_send(0, 0)
    each(z.M, branch_to)
    scatter_o.second(onto(sum_o, term_o), masks=most[1:])
    settle_back(0, 0)
    totals_back(1)
    back_send(0, 1)
    settle_back(0, 1)
    for mask in most[1:]:
        if mask & z.dims[0]:
            scatter_o.send(0, mask)
    scatter_1.first(into(near_i, term_1))
    for level in range(1, z.levels - 1):
        for q in range(z.Q):
            settle_back(level, q)
    for mask in most[1:]:
        if not mask & z.dims[0]:
            scatter_o.send(0, mask)
    scatter_1.second(onto(sum_1, term_1), send=True)
    query_sums(0)
    query_sums(1)
    for q in range(z.Q):
        back_take(z.levels - 1, q)
    for copy in scatter_1.sent[: len(z.masks)]:
        copy.wait_send()
    scatter_1.sent = scatter_1.sent[len(z.masks) :]
    tree_o.drain()
    walk_back(0)
    step_back(0)
    project_back(0)
    for step in range(depth - 1):
        scatter_o.fold(step)
    walk_back(1)
    for level in range(z.levels):
        pl.semaphore_signal(
            r.ready.at[level], inc=1, device_id=(seq ^ (1 << level), mp), device_id_type=MESH
        )
    step_back(1)
    project_back(1)
    for step in range(depth - 1):
        scatter_1.fold(step)
    sums_back(0)
    conv_back(0)

    last = depth - 1

    def write_to(ref):
        def write(rows, value):
            ref[rows, :] = value

        return write

    swap_out.wait()
    for away in range(1, z.M):
        owner = lax.rem(mp + away, z.M)
        swap_out.one(partial_of(owner), away).wait_send()

    def block_lanes(index):
        here = cut(index * LANE, LANE)
        total = r.normed[: z.R, cut(mp * z.Df + index * LANE, LANE)].astype(F32)
        for slot in range(z.M - 1):
            total = total + r.orecv[slot, :, here].astype(F32)
        r.blk[:, here] = (r.tok[:, here].astype(F32) + total).astype(BF16)

    each(z.Df // LANE, block_lanes)
    sums_back(1)
    conv_back(1)

    def put_small(first, lanes, value):
        count, at = value.shape[0], 0
        while at < count:
            block, inside = divmod(first + at, sg_rows)
            take = min(count - at, sg_rows - inside)
            sgp.block(block, inside, take)[:, lanes] = value[at : at + take].astype(BF16)
            at += take

    low_t = r.low[...].astype(F32).T.astype(BF16)
    used = 2 * z.RK + 2 * z.N + SGVEC

    def small_chunk(index):
        lanes = cut(index * 256, 256)
        put_small(0, lanes, nn(low_t, r.ddr[:, lanes]))
        put_small(z.RK, lanes, nn(r.dlowt[...], r.u[:, lanes]))
        put_small(2 * z.RK, lanes, nn(r.dst[...], r.u[:, lanes]))
        put_small(2 * z.RK + 2 * z.N, lanes, r.vec[:, lanes])
        if used < z.S * sg_rows:
            put_small(used, lanes, jnp.zeros((z.S * sg_rows - used, 256), F32))

    each(z.C // 256, small_chunk)
    for level in range(z.levels):
        pl.semaphore_wait(r.ready.at[level], 1)
    scatter_s.first(lambda device, mask: sgp.block(device))
    x_back(0)

    def add_small(device, mask):
        block, term = sum_s.block(mask // 2), sgp.block(device)

        def one(rows):
            block[rows, :] = (block[rows, :].astype(F32) + term[rows, :].astype(F32)).astype(BF16)

        by_rows(sg_rows, one)

    scatter_s.second(add_small, send=True)
    normed_part(0)
    for step in range(depth - 1):
        scatter_s.fold(step)

    x_back(1)

    scatter_0.first(into(near_i, term_0))
    scatter_0.second(onto(sum_0, term_0), send=True, masks=most[:1])
    scatter_0.second(onto(sum_0, term_0), send=True, masks=most[1:])

    normed_part(1)
    swap_m.start(mean_mine)

    gain_seq = SwapSeq(z, links, lambda slot: r.gvr.at[slot])
    gain_seq.start(r.gv)
    scatter_s.fold(last)

    def write_small(rows, value):
        small.block(seq)[rows, :] = value.astype(BF16)

    scatter_s.total(write_small)
    tree_s = TreeGather(
        z,
        links,
        lambda owner, h: small.block(owner, *halves(sg_rows)[h]),
        small.block,
    )
    tree_s.first()
    tree_s.second(0)
    tree_s.second(1)
    for step in range(depth - 1):
        scatter_0.fold(step)
    gain_seq.wait()
    gains = r.gv[...]
    for slot in range(z.S - 1):
        gains = gains + r.gvr[slot]
    r.gvs[...] = gains
    swap_g = Swap(z, links, lambda slot: r.gvm.at[slot])
    swap_g.start(r.gvs)
    tree_s.forward(0)
    tree_s.forward(1)
    scatter_o.fold(last)
    scatter_o.total(write_to(r.dout))
    scatter_1.fold(last)
    scatter_1.total(write_to(r.fac))
    store_1 = pltpu.make_async_copy(r.fac.at[pl.ds(0, z.Ds)], r.din.at[1], local.at[3])
    store_1.start()
    tree_s.settle()

    swap_m.wait()
    mean = r.mrow[0]
    for slot in range(1, z.M):
        mean = mean + r.mrow[slot]
    r.mean[...] = jnp.concatenate([mean] * (LANE // 8), axis=0).T * (1.0 / z.D)
    for swap in swap_n:
        swap.wait()

    def token_lanes(index):
        here = cut(index * LANE, LANE)
        inside = cut(mp * z.Df + index * LANE, LANE)
        for q in range(z.Q):
            rows = rows_of(q)
            total = r.normed[rows, inside].astype(F32)
            for slot in range(z.M - 1):
                total = total + r.nrecv[slot, rows, here].astype(F32)
            inv, x = r.inv[rows, :], r.tok[rows, here].astype(F32)
            value = inv * (total * r.gain[:, inside]) - x * (inv * inv * inv) * r.mean[rows, :]
            r.dtok[rows, here] = value + r.cot[rows, here] * seq_weight[q]

    each(z.Df // LANE, token_lanes)

    tree_s.finish()
    for block in range(z.S):
        count = min(sg_rows, r.sg.shape[0] - block * sg_rows)
        if count > 0:
            r.sg[block * sg_rows : block * sg_rows + count, :] = small.block(block, 0, count)[...].astype(F32)
    swap_g.wait()
    gains = r.gvs[...]
    for slot in range(z.M - 1):
        gains = gains + r.gvm[slot]
    r.dgain[...] = gains
    scatter_0.fold(last)
    scatter_0.total(write_to(r.s))
    store_0 = pltpu.make_async_copy(r.s.at[pl.ds(0, z.Ds)], r.din.at[0], local.at[4])
    store_0.start()

    hal.wait_send()
    for tree in (tree_x, tree_z, tree_s):
        tree.drain()
    for line in (*line_t, line_h, line_d):
        line.drain()
    for q in range(z.Q):
        swap_st[q].drain(st_mine[q])
        swap_low[q].drain(low_mine[q])
        swap_dlow[q].drain(dlow_mine[q])
        swap_dst[q].drain(dst_mine[q])
    swap_m.drain(mean_mine)
    swap_g.drain(r.gvs)
    gain_seq.drain()
    for away in range(1, z.M):
        owner = lax.rem(mp + away, z.M)
        for q in range(z.Q):
            swap_n[q].one(normed_of(q, owner), away).wait_send()
    for copy in carry_copies + rim:
        copy.wait_send()
    for scatter in (scatter_o, scatter_1, scatter_0, scatter_s):
        scatter.drain()
    store_1.wait()
    store_0.wait()


def finish_kernel(z, blk, dtok, dgain, din, dout, sg, *outs):
    a, b, c = z.RK, 2 * z.RK, 2 * z.RK + 2 * z.N
    o_blk, o_dtok, o_dgain, o_din, o_convw, o_convb, o_low, o_state, o_delta, o_dbias, o_skip, o_dout = outs
    o_blk[...] = blk[...]
    o_dtok[...] = dtok[...]
    o_dgain[...] = dgain[...]
    o_din[...] = din[...]
    o_dout[...] = dout[...]
    o_delta[...] = sg[0:a, :]
    o_state[...] = sg[b:c, :]
    o_convw[...] = sg[c : c + 4, :]
    o_convb[...] = sg[c + 4 : c + 5, :]
    o_dbias[...] = sg[c + 5 : c + 6, :]
    o_skip[...] = sg[c + 6 : c + 7, :]
    for at in range(0, sg.shape[1], LANE):
        o_low[at : at + LANE, :] = sg[a:b, at : at + LANE].T


def fused(z, tokens, norm_gain, in_weight, conv_weight, conv_bias, low_weight, state_weight, delta_weight,
          delta_bias, skip_gain, out_weight, cotangent, seq_group, group_weight):
    V = pl.BlockSpec(memory_space=pltpu.VMEM)
    A = pl.BlockSpec(memory_space=pl.ANY)
    SM = pl.BlockSpec(memory_space=pltpu.SMEM)
    row = lambda value: value.reshape(1, -1)
    operands = dict(
        tok_in=(A, tokens.reshape(z.R, z.Df)),
        cot_in=(A, cotangent.reshape(z.R, z.Df)),
        gain_in=(A, row(norm_gain)),
        win=(A, in_weight),
        wout=(A, out_weight),
        convw_in=(A, conv_weight),
        convb_in=(A, row(conv_bias)),
        dbias_in=(A, row(delta_bias)),
        skip_in=(A, row(skip_gain)),
        loww_in=(A, low_weight),
        statewt_in=(A, state_weight.T),
        deltaw_in=(A, delta_weight),
        seqg=(SM, seq_group),
        groupw=(SM, group_weight),
    )
    scratch = scratch_of(z)
    sg_used = 2 * z.RK + 2 * z.N + SGVEC
    outs = dict(
        blk=(V, (z.R, z.Df), BF16),
        dtok=(V, (z.R, z.Df), F32),
        dgain=(V, (z.D // LANE, LANE), F32),
        din=(A, (2, z.Ds, z.C), F32),
        dout=(V, (z.C, z.Ds), F32),
        sg=(V, (sg_used, z.C), F32),
    )
    result = pl.pallas_call(
        functools.partial(fused_kernel, z, [*operands, *outs, *scratch]),
        out_shape=[jax.ShapeDtypeStruct(shape, kind) for _, shape, kind in outs.values()],
        in_specs=[spec for spec, _ in operands.values()],
        out_specs=[spec for spec, _, _ in outs.values()],
        scratch_shapes=list(scratch.values()),
        compiler_params=pltpu.CompilerParams(
            collective_id=0, has_side_effects=True, vmem_limit_bytes=VMEM_BYTES
        ),
    )(*[value for _, value in operands.values()])
    whole = (V, (1, z.C), F32)
    last = dict(
        blk=(V, (z.R, z.Df), BF16),
        dtok=(V, (z.R, z.Df), F32),
        dgain=(V, (z.D // LANE, LANE), F32),
        din=(V, (2, z.Ds, z.C), F32),
        convw=(V, (4, z.C), F32),
        convb=whole,
        low=(V, (z.C, z.RK), F32),
        state=(V, (2 * z.N, z.C), F32),
        delta=(V, (z.RK, z.C), F32),
        dbias=whole,
        skip=whole,
        dout=(V, (z.C, z.Ds), F32),
    )
    done = pl.pallas_call(
        functools.partial(finish_kernel, z),
        out_shape=[jax.ShapeDtypeStruct(shape, kind) for _, shape, kind in last.values()],
        in_specs=[V] * 6,
        out_specs=[spec for spec, _, _ in last.values()],
        compiler_params=pltpu.CompilerParams(vmem_limit_bytes=VMEM_BYTES),
    )(*result)
    done = dict(zip(last, done))
    done.update(blk=done["blk"].reshape(tokens.shape), dtok=done["dtok"].reshape(tokens.shape))
    done.update(dgain=done["dgain"].reshape(z.D), state=done["state"].T)
    done.update({name: done[name][0] for name in ("convb", "dbias", "skip")})
    return tuple(done.values())


def local(mesh_shape, *arrays):
    tokens, norm_gain, in_weight, conv_weight = arrays[:4]
    state_weight, delta_weight = arrays[6], arrays[7]
    z = Sizes(
        mesh_shape,
        tokens.shape[0],
        tokens.shape[1],
        tokens.shape[2],
        norm_gain.shape[0],
        in_weight.shape[2],
        state_weight.shape[1] // 2,
        delta_weight.shape[0],
    )
    if z.fits(conv_weight.shape[0]):
        return fused(z, *arrays)
    return plain(*arrays)


def solution(mesh):
    placed = (
        P(None, "seq", "mp"),
        P(),
        P(None, "seq", "mp"),
        P(None, "mp"),
        P("mp"),
        P("mp", None),
        P("mp", None),
        P(None, "mp"),
        P("mp"),
        P("mp"),
        P("mp", "seq"),
        P(None, "seq", "mp"),
        P(),
        P(),
    )
    return jax.shard_map(
        functools.partial(local, dict(mesh.shape)),
        mesh=mesh,
        in_specs=placed,
        out_specs=(
            P(None, "seq", "mp"),
            P(None, "seq", "mp"),
            P(),
            P(None, "seq", "mp"),
            P(None, "mp"),
            P("mp"),
            P("mp", None),
            P("mp", None),
            P(None, "mp"),
            P("mp"),
            P("mp"),
            P("mp", "seq"),
        ),
        check_vma=False,
    )
```

```python
import functools
import math

import jax
import jax.numpy as jnp
from jax import lax
from jax.experimental import pallas as pl
from jax.experimental.pallas import tpu as pltpu
from jax.sharding import PartitionSpec as P

SEQ_MB = 1
NMB = 2
EPSILON = 1e-05
VMEM_BYTES = 64 * 1024 * 1024 - 64 * 1024


def from_behind(value, axis, steps):
    count = lax.axis_size(axis)
    leading, last = (max(0, -steps), min(count, count - steps))
    return lax.ppermute(value, axis, [(source, source + steps) for source in range(leading, last)])


def prefix(value, axis, join, neutral, backward):
    count, mine = (lax.axis_size(axis), lax.axis_index(axis))
    pieces = jax.tree.map(lambda part: lax.all_gather(part, axis), value)
    if backward:
        pieces = jax.tree.map(lambda part: part[::-1], pieces)
        mine = count - 1 - mine
    subtotal = jax.tree.map(
        lambda part, zero: jnp.full_like(part, 0) + jnp.asarray(zero, part.dtype), value, neutral
    )

    def lap(position, subtotal):
        longer = join(subtotal, jax.tree.map(lambda part: part[position], pieces))
        return jax.tree.map(lambda new, old: jnp.where(position < mine, new, old), longer, subtotal)

    return lax.fori_loop(0, count - 1, lap, subtotal)


def combine(earlier, later):
    return (earlier[0] * later[0], later[0] * earlier[1] + later[1])


def make_gates(delta_raw, b_state, inputs):
    beta_gate = jax.nn.sigmoid(delta_raw)
    key_sq = jnp.sum(b_state * b_state, axis=-1, keepdims=True)
    step_size = beta_gate / (1.0 + beta_gate * key_sq)
    decays = 1.0 - step_size[:, :, None, :] * (b_state * b_state)[:, :, :, None]
    source = (step_size * inputs)[:, :, None, :] * b_state[:, :, :, None]
    return (decays, source)


def to_blocks(value, span_rows):
    old_shape = value.shape
    reshaped = value.reshape((old_shape[0], old_shape[1] // span_rows, span_rows) + old_shape[2:])
    return jnp.swapaxes(reshaped, 0, 1)


def from_blocks(value):
    joined = jnp.swapaxes(value, 0, 1)
    old_shape = joined.shape
    return joined.reshape((old_shape[0], old_shape[1] * old_shape[2]) + old_shape[3:])


def forward_block(carry_pair, block_items):
    delta_raw, b_state, inputs = block_items
    decays, source = make_gates(delta_raw, b_state, inputs)
    run_prod, run_state = carry_pair
    prod_list = []
    state_list = []
    for row_idx in range(decays.shape[1]):
        run_prod = run_prod * decays[:, row_idx]
        run_state = decays[:, row_idx] * run_state + source[:, row_idx]
        prod_list.append(run_prod)
        state_list.append(run_state)
    return ((run_prod, run_state), (jnp.stack(prod_list, axis=1), jnp.stack(state_list, axis=1)))


def backward_block(carry_trio, block_items):
    delta_raw, b_state, inputs, read_grad, c_state = block_items
    decays, _ = make_gates(delta_raw, b_state, inputs)
    grad_next, dec_next, tail_prod = carry_trio
    span_rows = decays.shape[1]
    grad_list = [None] * span_rows
    tail_list = [None] * span_rows
    for row_idx in reversed(range(span_rows)):
        drive_term = read_grad[:, row_idx][:, None, :] * c_state[:, row_idx][:, :, None]
        grad_next = drive_term + dec_next * grad_next
        tail_prod = dec_next * tail_prod
        grad_list[row_idx] = grad_next
        tail_list[row_idx] = tail_prod
        dec_next = decays[:, row_idx]
    return (
        (grad_next, dec_next, tail_prod),
        (jnp.stack(grad_list, axis=1), jnp.stack(tail_list, axis=1)),
    )


def silu_slope(value):
    sig_value = jax.nn.sigmoid(value)
    return sig_value * (1.0 + value * (1.0 - sig_value))


def plain(
    tokens,
    norm_gain,
    in_weight,
    conv_weight,
    conv_bias,
    low_weight,
    state_weight,
    delta_weight,
    delta_bias,
    skip_gain,
    out_weight,
    cotangent,
    seq_group,
    group_weight,
):
    stretch = tokens.shape[1]
    feature_dev = tokens.shape[2]
    channels = in_weight.shape[2]
    model_width = norm_gain.shape[0]
    num_taps = conv_weight.shape[0]
    nstate = state_weight.shape[1] // 2
    span_rows = math.gcd(stretch, 8)
    picks = (
        seq_group[:, None] == jnp.arange(group_weight.shape[0], dtype=jnp.int32)[None, :]
    ).astype(jnp.float32)
    seq_weight = jnp.sum(picks * group_weight[None, :], axis=1)
    feature_start = lax.axis_index("mp") * feature_dev
    ones_state = jnp.ones((SEQ_MB, nstate, channels), jnp.float32)
    zero_state = jnp.zeros_like(ones_state)
    acc_in = jnp.zeros((2, model_width, channels), jnp.float32)
    acc_out = jnp.zeros((channels, model_width), jnp.float32)
    acc_gain = jnp.zeros_like(norm_gain)
    acc_conv = jnp.zeros_like(conv_weight)
    acc_cbias = jnp.zeros_like(conv_bias)
    acc_low = jnp.zeros(low_weight.shape, jnp.float32)
    acc_state = jnp.zeros(state_weight.shape, jnp.float32)
    acc_delta = jnp.zeros(delta_weight.shape, jnp.float32)
    acc_dbias = jnp.zeros_like(delta_bias)
    acc_skip = jnp.zeros_like(skip_gain)
    outputs = []
    input_grads = []
    for micro_idx in range(NMB):
        whole_in, whole_out = (
            lax.all_gather(in_weight, "seq", axis=1, tiled=True),
            lax.all_gather(out_weight, "seq", axis=1, tiled=True),
        )
        first_seq = micro_idx * SEQ_MB
        block_tokens = tokens[first_seq : first_seq + SEQ_MB]
        full_tokens = lax.all_gather(block_tokens, "mp", axis=2, tiled=True).astype(jnp.float32)
        inv_rms = lax.rsqrt(jnp.mean(full_tokens * full_tokens, axis=-1, keepdims=True) + EPSILON)
        normed = (full_tokens * inv_rms * norm_gain).astype(jnp.bfloat16)
        both_parts = jnp.einsum(
            "scd,kdi->ksci", normed, whole_in, preferred_element_type=jnp.float32
        )
        x_round = both_parts[0].astype(jnp.bfloat16)
        z_part = both_parts[1]
        rim_rows = from_behind(x_round[:, stretch - (num_taps - 1) :], "seq", 1)
        padded = jnp.concatenate([rim_rows, x_round], axis=1).astype(jnp.float32)
        conv_sum = conv_bias + jnp.zeros((SEQ_MB, stretch, channels), jnp.float32)
        for tap_index in range(num_taps):
            conv_sum = (
                conv_sum + conv_weight[tap_index] * padded[:, tap_index : tap_index + stretch]
            )
        inputs_round = jax.nn.silu(conv_sum).astype(jnp.bfloat16)
        inputs_f = inputs_round.astype(jnp.float32)
        low_part = jnp.einsum(
            "sci,ir->scr", inputs_round, low_weight, preferred_element_type=jnp.float32
        )
        state_part = jnp.einsum(
            "sci,ir->scr", inputs_round, state_weight, preferred_element_type=jnp.float32
        )
        delta_low, state_proj = lax.psum((low_part, state_part), "mp")
        delta_round = delta_low.astype(jnp.bfloat16)
        delta_raw = (
            jnp.einsum("scr,ri->sci", delta_round, delta_weight, preferred_element_type=jnp.float32)
            + delta_bias
        )
        b_state = state_proj[..., :nstate]
        c_state = state_proj[..., nstate:]
        delta_blocks = to_blocks(delta_raw, span_rows)
        b_blocks = to_blocks(b_state, span_rows)
        c_blocks = to_blocks(c_state, span_rows)
        in_blocks = to_blocks(inputs_f, span_rows)
        stretch_pair, (prod_blocks, local_blocks) = lax.scan(
            forward_block, (ones_state, zero_state), (delta_blocks, b_blocks, in_blocks)
        )
        carried = prefix(stretch_pair, "seq", combine, (ones_state, zero_state), False)
        states = from_blocks(local_blocks) + from_blocks(prod_blocks) * carried[1][:, None]
        before = jnp.concatenate([carried[1][:, None], states[:, :-1]], axis=1)
        read_rec = jnp.einsum("scni,scn->sci", states, c_state)
        read_out = read_rec + skip_gain * inputs_f
        z_gate = jax.nn.silu(z_part)
        gated_round = (read_out * z_gate).astype(jnp.bfloat16)
        out_part = jnp.einsum(
            "sci,id->scd", gated_round, whole_out, preferred_element_type=jnp.float32
        )
        branch = lax.psum_scatter(out_part, "mp", scatter_dimension=2, tiled=True)
        outputs.append((block_tokens.astype(jnp.float32) + branch).astype(jnp.bfloat16))
        d_out = (
            cotangent[first_seq : first_seq + SEQ_MB]
            * seq_weight[first_seq : first_seq + SEQ_MB][:, None, None]
        )
        d_branch = lax.all_gather(d_out.astype(jnp.bfloat16), "mp", axis=2, tiled=True)
        acc_out = acc_out + jnp.einsum(
            "sci,scd->id", gated_round, d_branch, preferred_element_type=jnp.float32
        )
        d_gated = jnp.einsum("scd,id->sci", d_branch, whole_out, preferred_element_type=jnp.float32)
        d_read = d_gated * z_gate
        d_zpart = d_gated * read_out * silu_slope(z_part)
        acc_skip = acc_skip + jnp.sum(d_read * inputs_f, axis=(0, 1))
        read_blocks_grad = to_blocks(d_read, span_rows)
        (last_grad, first_dec, _), (grad_blocks, tail_blocks) = lax.scan(
            backward_block,
            (zero_state, ones_state, ones_state),
            (delta_blocks, b_blocks, in_blocks, read_blocks_grad, c_blocks),
            reverse=True,
        )
        tail_grad = first_dec * last_grad
        crossing = prefix(
            (stretch_pair[0], tail_grad), "seq", combine, (ones_state, zero_state), True
        )
        state_grad = from_blocks(grad_blocks) + from_blocks(tail_blocks) * crossing[1][:, None]
        _, gate_pullback = jax.vjp(make_gates, delta_raw, b_state, inputs_f)
        d_delta, d_bstate, d_inputs_state = gate_pullback((state_grad * before, state_grad))
        d_cstate = jnp.einsum("scni,sci->scn", states, d_read)
        acc_dbias = acc_dbias + jnp.sum(d_delta, axis=(0, 1))
        d_delta_round = d_delta.astype(jnp.bfloat16)
        acc_delta = acc_delta + jnp.einsum(
            "scr,sci->ri", delta_round, d_delta_round, preferred_element_type=jnp.float32
        )
        low_grad_part = jnp.einsum(
            "sci,ri->scr", d_delta_round, delta_weight, preferred_element_type=jnp.float32
        )
        state_grad_part = jnp.concatenate([d_bstate, d_cstate], axis=-1)
        d_low, d_state = lax.psum((low_grad_part, state_grad_part), "mp")
        d_low_round = d_low.astype(jnp.bfloat16)
        d_state_round = d_state.astype(jnp.bfloat16)
        acc_low = acc_low + jnp.einsum(
            "sci,scr->ir", inputs_round, d_low_round, preferred_element_type=jnp.float32
        )
        acc_state = acc_state + jnp.einsum(
            "sci,scr->ir", inputs_round, d_state_round, preferred_element_type=jnp.float32
        )
        d_inputs = d_read * skip_gain + d_inputs_state
        d_inputs = d_inputs + jnp.einsum(
            "scr,ir->sci", d_low_round, low_weight, preferred_element_type=jnp.float32
        )
        d_inputs = d_inputs + jnp.einsum(
            "scr,ir->sci", d_state_round, state_weight, preferred_element_type=jnp.float32
        )
        d_conv = d_inputs * silu_slope(conv_sum)
        acc_cbias = acc_cbias + jnp.sum(d_conv, axis=(0, 1))
        tap_grads = []
        d_padded = jnp.zeros((SEQ_MB, stretch + num_taps - 1, channels), jnp.float32)
        for tap_index in range(num_taps):
            tap_grads.append(
                jnp.sum(d_conv * padded[:, tap_index : tap_index + stretch], axis=(0, 1))
            )
            d_padded = d_padded + jnp.pad(
                conv_weight[tap_index] * d_conv,
                ((0, 0), (tap_index, num_taps - 1 - tap_index), (0, 0)),
            )
        acc_conv = acc_conv + jnp.stack(tap_grads)
        back_rim = from_behind(d_padded[:, : num_taps - 1], "seq", -1)
        d_xpart = d_padded[:, num_taps - 1 :] + jnp.pad(
            back_rim, ((0, 0), (stretch - (num_taps - 1), 0), (0, 0))
        )
        d_parts_round = jnp.stack([d_xpart, d_zpart]).astype(jnp.bfloat16)
        acc_in = acc_in + jnp.einsum(
            "scd,ksci->kdi", normed, d_parts_round, preferred_element_type=jnp.float32
        )
        norm_part = jnp.einsum(
            "ksci,kdi->scd", d_parts_round, whole_in, preferred_element_type=jnp.float32
        )
        d_normed = lax.psum(norm_part, "mp")
        acc_gain = acc_gain + jnp.sum(d_normed * full_tokens * inv_rms, axis=(0, 1))
        scaled = d_normed * norm_gain
        d_full = inv_rms * scaled - full_tokens * (inv_rms * inv_rms * inv_rms) * jnp.mean(
            scaled * full_tokens, axis=-1, keepdims=True
        )
        d_mine = lax.dynamic_slice_in_dim(d_full, feature_start, feature_dev, 2)
        input_grads.append(d_out + d_mine)
    d_in_weight, d_out_weight = (
        lax.psum_scatter(acc_in, "seq", scatter_dimension=1, tiled=True),
        lax.psum_scatter(acc_out, "seq", scatter_dimension=1, tiled=True),
    )
    summed = lax.psum(
        (acc_gain, acc_conv, acc_cbias, acc_low, acc_state, acc_delta, acc_dbias, acc_skip), "seq"
    )
    return (
        jnp.concatenate(outputs, axis=0),
        jnp.concatenate(input_grads, axis=0),
        summed[0],
        d_in_weight,
        summed[1],
        summed[2],
        summed[3],
        summed[4],
        summed[5],
        summed[6],
        summed[7],
        d_out_weight,
    )


MESH = pl.DeviceIdType.MESH
F32 = jnp.float32
BF16 = jnp.bfloat16
LANE = 128
GRP = 16
PADV = 8
SGVEC = 16


def nn(a, b):
    return lax.dot_general(a, b, (((1,), (0,)), ((), ())), preferred_element_type=F32)


def nt(a, b):
    return lax.dot_general(a, b, (((1,), (1,)), ((), ())), preferred_element_type=F32)


def tn(a, b):
    return lax.dot_general(a, b, (((0,), (0,)), ((), ())), preferred_element_type=F32)


def cut(start, size):
    return pl.ds(pl.multiple_of(start, size), size)


def each(count, step):
    lax.fori_loop(0, count, lambda index, unused: (step(index), unused)[1], 0)


def by_rows(count, step):
    size = 32 if count % 32 == 0 else 16
    each(count // size, lambda index: step(cut(index * size, size)))


def wide(value, times):
    return jnp.concatenate([value] * times, axis=1) if times > 1 else value


def groups_fit(channels):
    return (LANE // GRP) % min(LANE // GRP, channels // (GRP * GRP)) == 0


class Sizes:
    def __init__(self, mesh_shape, nseq, stretch, feature_dev, model, channels, nstate, rank):
        self.S, self.M = mesh_shape["seq"], mesh_shape["mp"]
        self.Q, self.T, self.Df, self.D, self.C = nseq, stretch, feature_dev, model, channels
        self.N, self.RK = nstate, rank
        self.R = nseq * stretch
        self.Ds = model // self.S
        self.B = max(1, feature_dev // self.Ds)
        self.levels = self.S.bit_length() - 1
        self.dims = [1 << bit for bit in range(1, self.levels)]
        self.masks = [2 * value for value in range(self.S // 2)]
        self.rows_sg = -(-(2 * rank + 2 * nstate + SGVEC) // (self.S * 16)) * 16
        self.E = max(self.R, self.Ds)

    def order(self, half):
        turn = half * (len(self.dims) // 2)
        return self.dims[turn:] + self.dims[:turn]

    def fits(self, taps):
        return (
            self.S in (4, 8)
            and self.M > 1
            and self.Q == 2
            and self.T == LANE
            and self.Ds == 256
            and self.Df % self.Ds == 0
            and self.C % 512 == 0
            and self.N == GRP
            and self.RK == LANE
            and taps == 4
            and self.D >= 2 * self.C
            and groups_fit(self.C)
            and self.C * self.D <= (1 << 21)
        )


class Bunch:
    def __init__(self, names, values):
        self.__dict__.update(zip(names, values))


class Rows:
    def __init__(self, ref, base, rows, count):
        self.ref, self.base, self.rows, self.end = ref, base, rows, base + rows * count

    def block(self, index, start=0, size=None):
        first = pl.multiple_of(self.base + index * self.rows + start, 16)
        return self.ref.at[pl.ds(first, self.rows if size is None else size), :]


class Links:
    def __init__(self, sems, seq, mp):
        self.sems, self.used, self.seq, self.mp = sems, 0, seq, mp

    def sem(self, count=1):
        first = self.used
        self.used += count
        return first

    def copy(self, src, dst, send, recv, seq=None, mp=None):
        target = (self.seq if seq is None else seq, self.mp if mp is None else mp)
        return pltpu.make_async_remote_copy(
            src_ref=src,
            dst_ref=dst,
            send_sem=self.sems.at[send],
            recv_sem=self.sems.at[recv],
            device_id=target,
            device_id_type=MESH,
        )

    def arrived(self, dst, recv):
        self.copy(dst, dst, recv, recv).wait_recv()


class TreeGather:
    def __init__(self, z, links, half_view, whole_view):
        self.z, self.links, self.half, self.whole = z, links, half_view, whole_view
        self.recv = {(mask, h): links.sem() for mask in z.masks[1:] for h in range(2)}
        self.near = {(mask, h): links.sem() for mask in z.masks for h in range(2)}
        self.sent = []

    def push(self, mask, h, dim):
        view = self.half(self.links.seq ^ mask, h)
        copy = self.links.copy(
            view, view, self.links.sem(), self.recv[mask | dim, h], seq=self.links.seq ^ dim
        )
        copy.start()
        self.sent.append(copy)

    def take(self, mask, h):
        self.links.arrived(self.half(self.links.seq ^ mask, h), self.recv[mask, h])

    def hand(self, mask, h):
        view = self.half(self.links.seq ^ mask, h)
        copy = self.links.copy(view, view, self.links.sem(), self.near[mask, h], seq=self.links.seq ^ 1)
        copy.start()
        self.sent.append(copy)

    def first(self):
        for h in range(2):
            self.push(0, h, self.z.order(h)[0])

    def second(self, h):
        for dim in self.z.order(h)[1:]:
            self.push(0, h, dim)
        self.hand(0, h)

    def forward(self, h):
        order = self.z.order(h)
        if len(order) > 1:
            self.take(order[0], h)
            self.push(order[0], h, order[1])
            self.hand(order[0], h)

    def settle(self, far=None):
        for mask in sorted(self.z.masks[1:], key=lambda mask: bin(mask).count("1")):
            if far is not None and far != (bin(mask).count("1") > 1):
                continue
            for h in range(2):
                order = self.z.order(h)
                if len(order) == 1 or mask != order[0]:
                    self.take(mask, h)
                    self.hand(mask, h)

    def finish(self):
        for mask, h in self.near:
            self.links.arrived(self.half(self.links.seq ^ 1 ^ mask, h), self.near[mask, h])

    def drain(self):
        for copy in self.sent:
            copy.wait_send()


class LineGather:
    def __init__(self, z, links, view):
        self.z, self.links, self.view = z, links, view
        self.recv = links.sem(z.M)
        self.send = links.sem(2 * z.M)

    def parts(self, depth):
        for side, way in enumerate((1, -1)):
            owner, target = self.links.mp - way * depth, self.links.mp + way
            held = (owner >= 0) & (owner < self.z.M)
            more = held & (target >= 0) & (target < self.z.M)
            yield side, owner, target, held, more

    def copy(self, side, depth, owner, target):
        view = self.view(owner)
        return self.links.copy(view, view, self.send + 2 * depth + side, self.recv + owner, mp=target)

    def step(self, depth):
        for side, owner, target, held, more in self.parts(depth):
            if depth:

                @pl.when(held)
                def _():
                    self.links.arrived(self.view(owner), self.recv + owner)

            @pl.when(more)
            def _():
                self.copy(side, depth, owner, target).start()

    def drain(self):
        for depth in range(self.z.M):
            for side, owner, target, held, more in self.parts(depth):

                @pl.when(more)
                def _():
                    self.copy(side, depth, owner, target).wait_send()


class Swap:
    def __init__(self, z, links, slot):
        self.z, self.links, self.slot = z, links, slot
        self.recv = links.sem(z.M)
        self.send = links.sem(z.M)

    def one(self, src, away):
        target = lax.rem(self.links.mp + away, self.z.M)
        return self.links.copy(src, self.slot(away - 1), self.send + away, self.recv + away, mp=target)

    def start(self, src):
        for away in range(1, self.z.M):
            self.one(src, away).start()

    def wait(self):
        for away in range(1, self.z.M):
            self.links.arrived(self.slot(away - 1), self.recv + away)

    def drain(self, src):
        for away in range(1, self.z.M):
            self.one(src, away).wait_send()


class SwapSeq:
    def __init__(self, z, links, slot):
        self.links, self.slot = links, slot
        self.pairs = [(other, links.sem(), links.sem()) for other in range(1, z.S)]
        self.sent = []

    def start(self, src):
        for other, send, recv in self.pairs:
            copy = self.links.copy(src, self.slot(other - 1), send, recv, seq=self.links.seq ^ other)
            copy.start()
            self.sent.append(copy)

    def wait(self):
        for other, send, recv in self.pairs:
            self.links.arrived(self.slot(other - 1), recv)

    def drain(self):
        for copy in self.sent:
            copy.wait_send()


def halves(rows):
    first = -(-rows // 32) * 16
    return (0, first), (first, rows - first)


class Scatter:
    def __init__(self, z, links, out, sums, far, rows):
        self.z, self.links, self.out, self.sums, self.far, self.rows = z, links, out, sums, far, rows
        self.near = {mask: links.sem() for mask in z.masks}
        self.near_send = {mask: links.sem() for mask in z.masks}
        self.sent = []
        self.late = []
        self.hops = {}
        place = 0
        for h in range(2):
            order = z.order(h)
            for step, dim in enumerate(order):
                for mask in z.masks:
                    if mask & dim and not any(mask & other for other in order[:step]):
                        self.hops[h, step, mask] = (dim, links.sem(), links.sem(), place)
                        place += 1
        self.slots = place

    def half(self, mask, h):
        start, size = halves(self.rows)[h]
        return self.sums.block(mask // 2, start, size)

    def came(self, h, place):
        return self.far.block(place, 0, halves(self.rows)[h][1])

    def first(self, make):
        links = self.links
        for mask in self.by_need():
            src = make(links.seq ^ 1 ^ mask, mask)
            copy = links.copy(src, self.sums.block(mask // 2), self.near_send[mask], self.near[mask], seq=links.seq ^ 1)
            copy.start()
            self.sent.append(copy)

    def by_need(self):
        return sorted(self.z.masks, key=lambda mask: -bin(mask).count("1"))

    def second(self, add, send=False, masks=None):
        links = self.links
        for mask in self.by_need() if masks is None else masks:
            links.arrived(self.sums.block(mask // 2), self.near[mask])
            add(links.seq ^ mask, mask)
            if send:
                self.send(0, mask)

    def send(self, step, only=None):
        links = self.links
        for (h, at, mask), (dim, send, recv, place) in self.hops.items():
            if at == step and only in (None, mask):
                copy = links.copy(
                    self.half(mask, h), self.came(h, place), send, recv, seq=links.seq ^ dim
                )
                copy.start()
                self.sent.append(copy)

    def fold(self, step):
        self.late.append(step)
        if step < len(self.z.dims) - 1:
            going = {(h, mask) for h, at, mask in self.hops if at == step + 1}
            self.take(step, lambda h, into: (h, into) in going)
            self.send(step + 1)

    def rest(self):
        for step in self.late:
            going = {(h, mask) for h, at, mask in self.hops if at == step + 1}
            self.take(step, lambda h, into: (h, into) not in going)

    def take(self, step, wanted):
        for (h, at, mask), (dim, send, recv, place) in self.hops.items():
            if at != step or not wanted(h, mask ^ dim):
                continue
            self.links.arrived(self.came(h, place), recv)
            if step < len(self.z.dims) - 1:
                half, came = self.half(mask ^ dim, h), self.came(h, place)

                def add(rows):
                    half[rows, :] = (half[rows, :].astype(F32) + came[rows, :].astype(F32)).astype(BF16)

                by_rows(halves(self.rows)[h][1], add)

    def total(self, write):
        self.rest()
        last = len(self.z.dims) - 1
        for (h, at, mask), (dim, send, recv, place) in self.hops.items():
            if at == last:
                half, came = self.half(0, h), self.came(h, place)
                first, count = halves(self.rows)[h]

                def add(rows):
                    value = half[rows, :].astype(F32) + came[rows, :].astype(F32)
                    write(pl.ds(pl.multiple_of(first + rows.start, 16), rows.size), value)

                by_rows(count, add)

    def drain(self):
        for copy in self.sent:
            copy.wait_send()


def slots_of(z):
    return Scatter(z, Links(None, 0, 0), None, None, None, 0).slots


def scratch_of(z):
    V = pltpu.VMEM
    half = z.S // 2
    slots = slots_of(z)
    return dict(
        tok=V((z.R, z.Df), BF16),
        cot=V((z.R, z.Df), F32),
        gain=V((1, z.D), F32),
        convw=V((4, z.C), F32),
        convb=V((1, z.C), F32),
        dbias=V((1, z.C), F32),
        skip=V((1, z.C), F32),
        loww=V((z.C, z.RK), BF16),
        statewt=V((2 * z.N, z.C), BF16),
        deltaw=V((z.RK, z.C), BF16),
        tokg=V((z.S, z.R, z.Ds), BF16),
        halg=V((z.S, 16, z.Ds), BF16),
        hals=V((z.B, 16, z.Ds), BF16),
        db=V((z.R, z.D), BF16),
        inv=V((z.R, LANE), F32),
        normed=V((z.R + 16, z.D), BF16),
        normt=V((z.D, z.R), BF16),
        wx=V((2, z.D, z.C), BF16),
        wo=V((z.C, z.D), BF16),
        xpad=V((z.Q, 8 + z.T, z.C), F32),
        dcp=V((z.Q, z.T + 8, z.C), F32),
        conv=V((z.E, z.C), F32),
        s=V((z.E, z.C), F32),
        su=V((z.R, z.C), F32),
        fac=V((z.E, z.C), F32),
        zp=V((z.R, z.C), F32),
        rd=V((z.R, z.C), F32),
        dr=V((z.R, z.C), F32),
        u=V((z.R, z.C), BF16),
        gat=V((z.R, z.C), BF16),
        gatt=V((z.C, z.R), BF16),
        ddr=V((z.R, z.C), BF16),
        dzr=V((z.R, z.C), BF16),
        dxr=V((z.R, z.C), BF16),
        lowp=V((z.Q, z.M, z.T, z.RK), BF16),
        stp=V((z.Q, z.M, 2 * z.N, z.T), F32),
        low=V((z.R, z.RK), BF16),
        dlow=V((z.R, z.RK), BF16),
        dlowt=V((z.RK, z.R), BF16),
        dst=V((2 * z.N, z.R), BF16),
        st=V((2 * z.N, z.R), F32),
        blkb=V((z.R, GRP * z.N), BF16),
        blkk=V((z.R, GRP * z.N), BF16),
        blkc=V((z.R, GRP * z.N), BF16),
        bc=V((z.Q, z.T, 2 * z.N, LANE), F32),
        hist=V((z.Q * (z.T + 1) * z.N, z.C), BF16),
        ptot=V((z.Q, z.N, z.C), F32),
        stot=V((z.Q, z.N, z.C), F32),
        ppre=V((z.Q, z.N, z.C), F32),
        spre=V((z.Q, z.N, z.C), F32),
        csend=V((z.levels, z.Q, 2, z.N, z.C), BF16),
        crecv=V((z.levels, z.Q, 2, z.N, z.C), BF16),
        bsend=V((z.levels, z.Q, z.N, z.C), BF16),
        brecv=V((z.levels, z.Q, z.N, z.C), BF16),
        est=V((3, z.N, z.R), F32),
        dlowp=V((z.Q, z.M, z.T, z.RK), BF16),
        dstp=V((z.Q, z.M, 2 * z.N, z.T), BF16),
        orecv=V((z.M - 1, z.R, z.Df), BF16),
        nrecv=V((z.M - 1, z.R, z.Df), BF16),
        near_o=V((half * z.C, z.Ds), BF16),
        sum_o=V((half * z.C, z.Ds), BF16),
        far_o=V((slots * (z.C // 2), z.Ds), BF16),
        near_i=V((half * z.Ds, z.C), BF16),
        sum_1=V((half * z.Ds, z.C), BF16),
        far_1=V((slots * (z.Ds // 2), z.C), BF16),
        vec=V((SGVEC, z.C), F32),
        gv=V((z.D // LANE, LANE), F32),
        gvs=V((z.D // LANE, LANE), F32),
        gvr=V((z.S - 1, z.D // LANE, LANE), F32),
        gvm=V((z.M - 1, z.D // LANE, LANE), F32),
        mean=V((z.R, LANE), F32),
        mrow=V((z.M, 8, z.R), F32),
        sems=pltpu.SemaphoreType.DMA((420,)),
        local=pltpu.SemaphoreType.DMA((16,)),
        ready=pltpu.SemaphoreType.REGULAR((z.levels,)),
    )


def silu_parts(value):
    gate = 1.0 / (1.0 + jnp.exp(-value))
    return gate, value * gate


def fused_kernel(z, names, *refs):
    r = Bunch(names, refs)
    seq, mp = lax.axis_index("seq"), lax.axis_index("mp")
    links = Links(r.sems, seq, mp)
    lanes_all = z.C // LANE
    first_block = mp * z.B

    def lane_loop(step):
        each(z.C // LANE, lambda index: step(cut(index * LANE, LANE)))

    barrier = pltpu.get_barrier_semaphore()
    ahead, behind = lax.rem(seq + 1, z.S), lax.rem(seq + z.S - 1, z.S)
    partners = [(seq ^ other, mp) for other in range(1, z.S)] + [(ahead, mp), (behind, mp)]
    partners += [(seq, lax.rem(mp + away, z.M)) for away in range(1, z.M)]
    for partner in partners:
        pl.semaphore_signal(barrier, inc=1, device_id=partner, device_id_type=MESH)
    local = r.local
    mine_in = lambda k: r.wx.at[k, cut(seq * z.Ds, z.Ds), :]
    loads = [
        pltpu.make_async_copy(r.win.at[0], mine_in(0), local.at[0]),
        pltpu.make_async_copy(r.win.at[1], mine_in(1), local.at[1]),
        pltpu.make_async_copy(r.wout, r.wo.at[:, cut(seq * z.Ds, z.Ds)], local.at[2]),
    ]
    pairs = [
        (r.tok_in, r.tok),
        (r.cot_in, r.cot),
        (r.gain_in, r.gain),
        (r.convw_in, r.convw),
        (r.convb_in, r.convb),
        (r.dbias_in, r.dbias),
        (r.skip_in, r.skip),
        (r.loww_in, r.loww),
        (r.statewt_in, r.statewt),
        (r.deltaw_in, r.deltaw),
    ]
    own = [pltpu.make_async_copy(src, dst, local.at[5 + index]) for index, (src, dst) in enumerate(pairs)]
    own[0].start()
    for load in loads:
        load.start()
    for copy in own[1:]:
        copy.start()
    own[0].wait()
    for b in range(z.B):
        r.tokg[first_block + b] = r.tok[:, b * z.Ds : (b + 1) * z.Ds]
        tails = [
            r.tok[q * z.T + z.T - 16 : q * z.T + z.T, b * z.Ds : (b + 1) * z.Ds].astype(F32)[8:]
            for q in range(z.Q)
        ]
        r.hals[b] = jnp.concatenate(tails, axis=0).astype(BF16)

    pl.semaphore_wait(barrier, len(partners))

    def of_in(k):
        def half(owner, h):
            return r.wx.at[k, cut(owner * z.Ds + h * (z.Ds // 2), z.Ds // 2), :]

        return TreeGather(z, links, half, lambda owner: r.wx.at[k, cut(owner * z.Ds, z.Ds), :])

    tree_x, tree_z = of_in(0), of_in(1)
    tree_o = TreeGather(
        z,
        links,
        lambda owner, h: r.wo.at[pl.ds(h * (z.C // 2), z.C // 2), cut(owner * z.Ds, z.Ds)],
        lambda owner: r.wo.at[:, cut(owner * z.Ds, z.Ds)],
    )
    line_t = [
        LineGather(z, links, lambda owner, q=q: r.tokg.at[pl.ds(owner * z.B, z.B), pl.ds(q * z.T, z.T), :])
        for q in range(z.Q)
    ]
    line_h = LineGather(z, links, lambda owner: r.halg.at[pl.ds(owner * z.B, z.B)])
    line_d = LineGather(z, links, lambda owner: r.db.at[:, cut(owner * z.Df, z.Df)])
    depth = len(z.dims)

    hal_send, hal_recv = links.sem(), links.sem()
    hal_mine = r.halg.at[pl.ds(first_block, z.B)]
    hal = links.copy(r.hals, hal_mine, hal_send, hal_recv, seq=ahead)
    hal.start()
    for line in line_t:
        line.step(0)
    loads[0].wait()
    tree_x.first()
    tree_x.second(0)
    tree_x.second(1)

    for copy in own[1:]:
        copy.wait()

    def weight_of(q):
        total = jnp.float32(0.0)
        for group in range(r.groupw.shape[0]):
            total = total + jnp.where(r.seqg[q] == group, r.groupw[group], 0.0)
        return total

    seq_weight = [weight_of(q) for q in range(z.Q)]
    for q in range(z.Q):
        rows = pl.ds(q * z.T, z.T)
        for b in range(z.B):
            part = r.cot[rows, b * z.Ds : (b + 1) * z.Ds] * seq_weight[q]
            r.db[rows, cut((first_block + b) * z.Ds, z.Ds)] = part.astype(BF16)

    links.arrived(hal_mine, hal_recv)
    line_h.step(0)
    for line in line_t:
        line.step(1)
    tree_x.forward(0)
    tree_x.forward(1)
    loads[1].wait()
    tree_z.first()
    tree_z.second(0)
    tree_z.second(1)
    line_h.step(1)
    for far in range(2, z.M):
        for line in line_t:
            line.step(far)
        line_h.step(far)
        if far == 2:
            tree_x.settle(False)
    if z.M == 2:
        tree_x.settle(False)
    line_d.step(0)

    def add_squares(j, total):
        part = r.tokg[j].astype(F32)
        edge = r.halg[j].astype(F32)
        return (
            total[0] + jnp.sum(part * part, axis=1, keepdims=True),
            total[1] + jnp.sum(edge * edge, axis=1, keepdims=True),
        )

    squares = lax.fori_loop(
        0, z.S, add_squares, (jnp.zeros((z.R, 1), F32), jnp.zeros((16, 1), F32))
    )
    inv = lax.rsqrt(squares[0] * (1.0 / z.D) + EPSILON)
    inv_edge = lax.rsqrt(squares[1] * (1.0 / z.D) + EPSILON)
    r.inv[...] = jnp.broadcast_to(inv, (z.R, LANE))

    def norm_block(j):
        features = cut(j * z.Ds, z.Ds)
        gain = r.gain[:, features]
        normed = r.tokg[j].astype(F32) * wide(r.inv[...], z.Ds // LANE) * gain
        r.normed[: z.R, features] = normed.astype(BF16)
        edge = r.halg[j].astype(F32) * inv_edge * gain
        r.normed[z.R :, features] = edge.astype(BF16)
        r.normt[features, :] = normed.T.astype(BF16)

    each(z.S, norm_block)
    tree_x.settle(True)
    tree_x.finish()

    def x_chunk(index):
        lanes = cut(index * 256, 256)
        part = nn(r.normed[...], r.wx[0, :, lanes]).astype(BF16).astype(F32)
        for q in range(z.Q):
            edge = part[z.R + 8 * q : z.R + 8 * q + 8]
            r.xpad[q, 0:8, lanes] = jnp.where(seq > 0, edge, 0.0)
            r.xpad[q, 8 : 8 + z.T, lanes] = part[q * z.T : (q + 1) * z.T]

    each(z.C // 256, x_chunk)
    tree_z.forward(0)
    tree_z.forward(1)
    loads[2].wait()
    tree_o.first()
    tree_o.second(0)

    def rows_of(q):
        return pl.ds(q * z.T, z.T)

    def conv(q):
        def conv_lanes(lanes):
            total = jnp.broadcast_to(r.convb[:, lanes], (z.T, LANE))
            for tap in range(4):
                total = total + r.convw[tap : tap + 1, lanes] * r.xpad[q, 5 + tap : 5 + tap + z.T, lanes]
            r.conv[rows_of(q), lanes] = total
            r.u[rows_of(q), lanes] = silu_parts(total)[1].astype(BF16)

        lane_loop(conv_lanes)

    swap_low = [Swap(z, links, lambda slot, q=q: r.lowp.at[q, slot]) for q in range(z.Q)]
    swap_st = [Swap(z, links, lambda slot, q=q: r.stp.at[q, slot]) for q in range(z.Q)]
    low_mine = [r.lowp.at[q, z.M - 1] for q in range(z.Q)]
    st_mine = [r.stp.at[q, z.M - 1] for q in range(z.Q)]

    def project(q):
        u = r.u[rows_of(q), :]
        st_mine[q][...] = nt(r.statewt[...], u)
        swap_st[q].start(st_mine[q])
        low_mine[q][...] = nn(u, r.loww[...]).astype(BF16)
        swap_low[q].start(low_mine[q])

    rows_i = lax.broadcasted_iota(jnp.int32, (z.T, GRP * z.N), 0)
    cols_i = lax.broadcasted_iota(jnp.int32, (z.T, GRP * z.N), 1)
    diagonal = lax.rem(rows_i, GRP) == cols_i // z.N
    rep_n = lax.broadcasted_iota(jnp.int32, (2 * z.N, GRP * z.N), 0)
    rep_j = lax.rem(lax.broadcasted_iota(jnp.int32, (2 * z.N, GRP * z.N), 1), z.N)
    rep_b = (rep_n == rep_j).astype(BF16)
    rep_c = (rep_n == rep_j + z.N).astype(BF16)
    only_b = lax.broadcasted_iota(jnp.int32, (z.T, LANE), 1) < z.N

    def columns_of(value):
        return jnp.concatenate([value, jnp.zeros((LANE - 2 * z.N, z.T), F32)], axis=0).T

    def keys(q):
        swap_st[q].wait()
        st = r.stp[q, 0]
        for slot in range(1, z.M):
            st = st + r.stp[q, slot]
        r.st[:, rows_of(q)] = st

        def spread(index):
            turned = pltpu.roll(st, lax.rem(z.T - index * 32, z.T), 1)
            for j in range(32):
                r.bc[q, index * 32 + j] = jnp.broadcast_to(turned[:, j : j + 1], (2 * z.N, LANE))

        each(z.T // 32, spread)
        nat = columns_of(st)
        key_sq = jnp.sum(jnp.where(only_b, nat * nat, 0.0), axis=1, keepdims=True)
        swap_low[q].wait()
        low = r.lowp[q, 0].astype(F32)
        for slot in range(1, z.M):
            low = low + r.lowp[q, slot].astype(F32)
        low = low.astype(BF16)
        r.low[rows_of(q), :] = low

        def step_chunk(index):
            lanes = cut(index * 256, 256)
            raw = nn(low, r.deltaw[:, lanes]) + r.dbias[:, lanes]
            beta = 1.0 / (1.0 + jnp.exp(-raw))
            scale = 1.0 / (1.0 + beta * key_sq)
            step = beta * scale
            r.s[rows_of(q), lanes] = step
            r.su[rows_of(q), lanes] = step * r.u[rows_of(q), lanes].astype(F32)
            r.fac[rows_of(q), lanes] = scale * step * (1.0 - beta)

        each(z.C // 256, step_chunk)

    def key_blocks(q):
        nat16 = columns_of(r.st[:, rows_of(q)])[:, : 2 * z.N].astype(BF16)
        spread_b = jnp.where(diagonal, nn(nat16, rep_b), 0.0)
        r.blkb[rows_of(q), :] = spread_b.astype(BF16)
        r.blkk[rows_of(q), :] = (spread_b * spread_b).astype(BF16)
        r.blkc[rows_of(q), :] = jnp.where(diagonal, nn(nat16, rep_c), 0.0).astype(BF16)

    span = 512 if z.C % 512 == 0 else 256

    def token(q, t):
        return pl.ds(q * z.T + t, 1)

    def totals(q):
        def lane_part(index):
            lanes = cut(index * span, span)

            def tokens8(i, carry):
                product, state = carry
                for j in range(8):
                    row = token(q, i * 8 + j)
                    step, drive = r.s[row, lanes], r.su[row, lanes]
                    key = r.bc[q, i * 8 + j, : z.N, :]
                    decay = 1.0 - step * wide(key * key, span // LANE)
                    product = product * decay
                    state = decay * state + drive * wide(key, span // LANE)
                return product, state

            start = (jnp.ones((z.N, span), F32), jnp.zeros((z.N, span), F32))
            product, state = lax.fori_loop(0, z.T // 8, tokens8, start)
            r.ptot[q, :, lanes] = product
            r.stot[q, :, lanes] = state

        each(z.C // span, lane_part)

    carry_sems = [[(links.sem(), links.sem()) for q in range(z.Q)] for level in range(z.levels)]
    back_sems = [[(links.sem(), links.sem()) for q in range(z.Q)] for level in range(z.levels)]
    carry_copies = []

    def upper_at(level):
        return lax.rem(seq // (1 << level), 2) == 1

    def carry_send(level, q):
        r.csend[level, q, 0] = r.ptot[q].astype(BF16)
        r.csend[level, q, 1] = r.stot[q].astype(BF16)
        copy = links.copy(
            r.csend.at[level, q], r.crecv.at[level, q], *carry_sems[level][q], seq=seq ^ (1 << level)
        )
        copy.start()
        carry_copies.append(copy)

    def carry_take(level, q):
        links.arrived(r.crecv.at[level, q], carry_sems[level][q][1])
        upper = upper_at(level)
        other_p, other_s = r.crecv[level, q, 0].astype(F32), r.crecv[level, q, 1].astype(F32)
        mine_p, mine_s = r.ptot[q], r.stot[q]
        if level == 0:
            r.spre[q] = jnp.where(upper, other_s, 0.0)
            r.ppre[q] = jnp.where(upper, other_p, 1.0)
        else:
            pre_p, pre_s = r.ppre[q], r.spre[q]
            r.spre[q] = jnp.where(upper, pre_p * other_s + pre_s, pre_s)
            r.ppre[q] = jnp.where(upper, pre_p * other_p, pre_p)
        if level < z.levels - 1:
            r.stot[q] = jnp.where(upper, mine_p * other_s + mine_s, other_p * mine_s + other_s)
            r.ptot[q] = mine_p * other_p

    def back_send(level, q):
        r.bsend[level, q] = r.stot[q].astype(BF16)
        copy = links.copy(
            r.bsend.at[level, q], r.brecv.at[level, q], *back_sems[level][q], seq=seq ^ (1 << level)
        )
        copy.start()
        carry_copies.append(copy)

    def back_take(level, q):
        links.arrived(r.brecv.at[level, q], back_sems[level][q][1])
        upper = upper_at(level)
        other = r.brecv[level, q].astype(F32)
        other_p, mine_p = r.crecv[level, q, 0].astype(F32), r.csend[level, q, 0].astype(F32)
        mine = r.stot[q]
        if level == 0:
            r.spre[q] = jnp.where(upper, 0.0, other)
            r.ppre[q] = jnp.where(upper, 1.0, other_p)
        else:
            pre_p, pre = r.ppre[q], r.spre[q]
            r.spre[q] = jnp.where(upper, pre, pre + pre_p * other)
            r.ppre[q] = jnp.where(upper, pre_p, pre_p * other_p)
        if level < z.levels - 1:
            r.stot[q] = jnp.where(upper, other + other_p * mine, mine + mine_p * other)

    def past_rows(q, slot, count=1):
        return pl.ds(pl.multiple_of((q * (z.T + 1) + slot) * z.N, z.N), count * z.N)

    groups = z.T // GRP

    def walk(q):
        r.hist[past_rows(q, 0), :] = r.spre[q].astype(BF16)

        def lane_part(index):
            lanes = cut(index * span, span)

            def tokens8(i, state):
                for j in range(8):
                    row = token(q, i * 8 + j)
                    step, drive = r.s[row, lanes], r.su[row, lanes]
                    key = r.bc[q, i * 8 + j, : z.N, :]
                    decay = 1.0 - step * wide(key * key, span // LANE)
                    state = decay * state + drive * wide(key, span // LANE)
                    r.hist[past_rows(q, i * 8 + j + 1), lanes] = state.astype(BF16)
                return state

            lax.fori_loop(0, z.T // 8, tokens8, r.spre[q, :, lanes])

        each(z.C // span, lane_part)
        reads = []
        for i in range(groups):
            rows = pl.ds(q * z.T + i * GRP, GRP)
            reads.append((rows, nn(r.blkc[rows, :], r.hist[past_rows(q, i * GRP + 1, GRP), :])))
        for rows, value in reads:
            r.rd[rows, :] = value

    def z_chunk(index):
        lanes = cut(index * 256, 256)
        r.zp[:, lanes] = nn(r.normed[: z.R, :], r.wx[1, :, lanes])

    conv(0)
    project(0)
    conv(1)
    project(1)
    line_d.step(1)
    keys(0)
    totals(0)
    carry_send(0, 0)
    keys(1)
    carry_take(0, 0)
    carry_send(1, 0)
    totals(1)
    carry_send(0, 1)
    carry_take(0, 1)
    carry_send(1, 1)
    tree_o.second(1)
    tree_o.forward(1)
    line_d.step(2)
    tree_z.settle()
    key_blocks(0)
    key_blocks(1)
    for level in range(1, z.levels - 1):
        for q in range(z.Q):
            carry_take(level, q)
            carry_send(level + 1, q)
    tree_o.forward(0)
    tree_z.finish()
    each(z.C // 256, z_chunk)
    carry_take(z.levels - 1, 0)
    walk(0)
    for far in range(3, z.M):
        line_d.step(far)
    tree_o.settle(False)
    carry_take(z.levels - 1, 1)
    walk(1)
    r.vec[...] = jnp.zeros_like(r.vec)

    def gate_lanes(lanes):
        for q in range(z.Q):
            rows = rows_of(q)
            out = r.rd[rows, lanes] + r.skip[:, lanes] * r.u[rows, lanes].astype(F32)
            r.rd[rows, lanes] = out
            gated = out * silu_parts(r.zp[rows, lanes])[1]
            r.gat[rows, lanes] = gated.astype(BF16)
            r.gatt[lanes, rows] = gated.T.astype(BF16)

    lane_loop(gate_lanes)

    def into(near, term):
        def make(device, mask):
            block = near.block(mask // 2)
            block[...] = term(device).astype(BF16)
            return block

        return make

    def onto(sums, term):
        def add(device, mask):
            block = sums.block(mask // 2)
            block[...] = (term(device) + block[...].astype(F32)).astype(BF16)

        return add

    half_s, slots = z.S // 2, slots_of(z)
    sg_rows = z.rows_sg
    near_o, near_i = Rows(r.near_o, 0, z.C, half_s), Rows(r.near_i, 0, z.Ds, half_s)
    sum_o, far_o = Rows(r.sum_o, 0, z.C, half_s), Rows(r.far_o, 0, z.C // 2, slots)
    sum_1, far_1 = Rows(r.sum_1, 0, z.Ds, half_s), Rows(r.far_1, 0, z.Ds // 2, slots)
    sum_0 = Rows(r.hist, 0, z.Ds, half_s)
    far_0 = Rows(r.hist, sum_0.end, z.Ds // 2, slots)
    sum_s = Rows(r.hist, far_0.end, sg_rows, half_s)
    far_s = Rows(r.hist, sum_s.end, halves(sg_rows)[0][1], slots)
    sgp = Rows(r.hist, far_s.end, sg_rows, z.S)
    small = Rows(r.hist, sgp.end, sg_rows, z.S)
    scatter_o = Scatter(z, links, None, sum_o, far_o, z.C)
    scatter_1 = Scatter(z, links, None, sum_1, far_1, z.Ds)
    scatter_0 = Scatter(z, links, None, sum_0, far_0, z.Ds)
    scatter_s = Scatter(z, links, None, sum_s, far_s, sg_rows)
    term_o = lambda device: nn(r.gatt[...], r.db[:, cut(device * z.Ds, z.Ds)])
    term_1 = lambda device: nn(r.normt[cut(device * z.Ds, z.Ds), :], r.dzr[...])
    term_0 = lambda device: nn(r.normt[cut(device * z.Ds, z.Ds), :], r.dxr[...])

    tree_o.settle(True)
    most = scatter_o.by_need()
    scatter_o.first(into(near_o, term_o))
    tree_o.finish()

    def gated_grad(index):
        lanes = cut(index * 256, 256)
        r.dr[:, lanes] = nt(r.db[...], r.wo[lanes, :])

    each(z.C // 256, gated_grad)

    def gate_back(lanes):
        for q in range(z.Q):
            rows = rows_of(q)
            part, grad = r.zp[rows, lanes], r.dr[rows, lanes]
            gate, silu = silu_parts(part)
            d_read = grad * silu
            r.dr[rows, lanes] = d_read
            r.dzr[rows, lanes] = (grad * r.rd[rows, lanes] * gate * (1.0 + part * (1.0 - gate))).astype(BF16)
            r.vec[6:7, lanes] += jnp.sum(d_read * r.u[rows, lanes].astype(F32), axis=0, keepdims=True)

    lane_loop(gate_back)
    scatter_o.second(onto(sum_o, term_o), send=True, masks=most[:1])

    swap_out = Swap(z, links, lambda slot: r.orecv.at[slot])

    def partial_of(owner):
        return r.normed.at[pl.ds(0, z.R), cut(owner * z.Df, z.Df)]

    def branch_to(index):
        away = index + 1
        owner = lax.rem(mp + away, z.M)
        for b in range(z.B):
            j = owner * z.B + b
            r.normed[: z.R, cut(j * z.Ds, z.Ds)] = nn(r.gat[...], r.wo[:, cut(j * z.Ds, z.Ds)]).astype(BF16)

        @pl.when(away < z.M)
        def _():
            swap_out.one(partial_of(owner), away).start()

    def totals_back(q):
        def lane_part(index):
            lanes = cut(index * span, span)

            def tokens8(i, tail):
                for j in reversed(range(8)):
                    t = z.T - 8 - i * 8 + j
                    row = token(q, t)
                    step, grad = r.s[row, lanes], r.dr[row, lanes]
                    key, query = r.bc[q, t, : z.N, :], r.bc[q, t, z.N :, :]
                    decay = 1.0 - step * wide(key * key, span // LANE)
                    tail = decay * (grad * wide(query, span // LANE) + tail)
                return tail

            r.stot[q, :, lanes] = lax.fori_loop(0, z.T // 8, tokens8, jnp.zeros((z.N, span), F32))

        each(z.C // span, lane_part)

    lane_index = lax.broadcasted_iota(jnp.int32, (z.N, LANE), 1)

    def lane_sum(value):
        total = value[:, :LANE]
        for part in range(1, lanes_all):
            total = total + value[:, part * LANE : (part + 1) * LANE]
        return jnp.sum(total, axis=1, keepdims=True)

    batch = min(groups, z.C // (GRP * z.N))

    def walk_back(q):
        def group(index, carry):
            tail, sum_gh, sum_g = carry
            i = groups - 1 - index
            for j in reversed(range(GRP)):
                t = i * GRP + j
                row = token(q, t)
                step, drive, grad = r.s[row, :], r.su[row, :], r.dr[row, :]
                key, query = r.bc[q, t, : z.N, :], r.bc[q, t, z.N :, :]
                before = r.hist[past_rows(q, t), :].astype(F32)
                state_grad = grad * wide(query, lanes_all) + tail
                crossed = state_grad * before
                place = pl.ds(pl.multiple_of(lax.rem(i, batch) * GRP * z.N + j * z.N, z.N), z.N)
                r.wo[place, : z.C] = state_grad.astype(BF16)
                r.wo[place, z.C : 2 * z.C] = crossed.astype(BF16)
                here = lane_index == t
                sum_gh = jnp.where(here, lane_sum(step * crossed), sum_gh)
                sum_g = jnp.where(here, lane_sum(drive * state_grad), sum_g)
                tail = (1.0 - step * wide(key * key, lanes_all)) * state_grad
            return tail, sum_gh, sum_g

        zero = jnp.zeros((z.N, LANE), F32)
        carry = (r.spre[q], zero, zero)
        for start in range(0, groups, batch):
            carry = lax.fori_loop(start, start + batch, group, carry)
            sums = []
            for slot in range(batch):
                rows = pl.ds(q * z.T + (groups - start - batch + slot) * GRP, GRP)
                place = pl.ds(slot * GRP * z.N, GRP * z.N)
                sums.append(
                    (
                        rows,
                        nn(r.blkb[rows, :], r.wo[place, : z.C]),
                        nn(r.blkk[rows, :], r.wo[place, z.C : 2 * z.C]),
                    )
                )
            for rows, by_key, by_square in sums:
                r.rd[rows, :] = by_key
                r.zp[rows, :] = by_square
        columns = rows_of(q)
        for part in range(2):
            r.est[part, :, columns] = carry[1 + part]

    def query_sums(q):
        parts = []
        for i in range(groups):
            rows = pl.ds(q * z.T + i * GRP, GRP)
            parts.append(nt(r.dr[rows, :].astype(BF16), r.hist[past_rows(q, i * GRP + 1, GRP), :]))
        blocks = jnp.where(diagonal, jnp.concatenate(parts, axis=0), 0.0).astype(BF16)
        r.est[2, :, rows_of(q)] = nt(rep_b[: z.N], blocks)

    def step_back(q):
        rows = rows_of(q)

        def step_lanes(lanes):
            sum_b, step = r.rd[rows, lanes], r.s[rows, lanes]
            d_step = r.u[rows, lanes].astype(F32) * sum_b - r.zp[rows, lanes]
            r.rd[rows, lanes] = step * sum_b
            d_raw = d_step * r.fac[rows, lanes]
            r.ddr[rows, lanes] = d_raw.astype(BF16)
            r.gat[rows, lanes] = (d_step * step * step).astype(BF16)
            r.vec[5:6, lanes] += jnp.sum(d_raw, axis=0, keepdims=True)

        lane_loop(step_lanes)

    swap_dlow = [Swap(z, links, lambda slot, q=q: r.dlowp.at[q, slot]) for q in range(z.Q)]
    swap_dst = [Swap(z, links, lambda slot, q=q: r.dstp.at[q, slot]) for q in range(z.Q)]
    dlow_mine = [r.dlowp.at[q, z.M - 1] for q in range(z.Q)]
    dst_mine = [r.dstp.at[q, z.M - 1] for q in range(z.Q)]

    def project_back(q):
        rows = rows_of(q)
        key_grad = nt(jnp.ones((16, z.C), BF16), r.gat[rows, :])[0:1]
        now = r.st[: z.N, rows]
        d_key = r.est[1, :, rows] - 2.0 * now * r.est[0, :, rows] - 2.0 * now * key_grad
        dst_mine[q][...] = jnp.concatenate([d_key, r.est[2, :, rows]], axis=0).astype(BF16)
        swap_dst[q].start(dst_mine[q])
        dlow_mine[q][...] = nt(r.ddr[rows, :], r.deltaw[...]).astype(BF16)
        swap_dlow[q].start(dlow_mine[q])

    def sums_back(q):
        rows = rows_of(q)
        swap_dlow[q].wait()
        swap_dst[q].wait()
        dlow = r.dlowp[q, 0].astype(F32)
        dst = r.dstp[q, 0].astype(F32)
        for slot in range(1, z.M):
            dlow = dlow + r.dlowp[q, slot].astype(F32)
            dst = dst + r.dstp[q, slot].astype(F32)
        r.dlow[rows, :] = dlow.astype(BF16)
        r.dlowt[:, rows] = dlow.T.astype(BF16)
        r.dst[:, rows] = dst.astype(BF16)
        dlow16, dst16 = dlow.astype(BF16), columns_of(dst)[:, : 2 * z.N].astype(BF16)

        def inputs_chunk(index):
            lanes = cut(index * 256, 256)
            r.su[rows, lanes] = nt(dlow16, r.loww[lanes, :]) + nn(dst16, r.statewt[:, lanes])

        each(z.C // 256, inputs_chunk)

    rim = [
        links.copy(
            r.dcp.at[q, pl.ds(0, 8), :],
            r.dcp.at[q, pl.ds(z.T, 8), :],
            links.sem(),
            links.sem(),
            seq=behind,
        )
        for q in range(z.Q)
    ]

    def conv_back(q):
        rows = rows_of(q)

        def conv_lanes(lanes):
            total = r.su[rows, lanes] + r.rd[rows, lanes] + r.skip[:, lanes] * r.dr[rows, lanes]
            value = r.conv[rows, lanes]
            gate = silu_parts(value)[0]
            d_conv = total * gate * (1.0 + value * (1.0 - gate))
            r.dcp[q, 0 : z.T, lanes] = d_conv
            r.vec[4:5, lanes] += jnp.sum(d_conv, axis=0, keepdims=True)
            for tap in range(4):
                r.vec[tap : tap + 1, lanes] += jnp.sum(
                    d_conv * r.xpad[q, 5 + tap : 5 + tap + z.T, lanes], axis=0, keepdims=True
                )

        lane_loop(conv_lanes)
        rim[q].start()

    def x_back(q):
        rim[q].wait_recv()

        def x_lanes(lanes):
            edge = r.dcp[q, z.T : z.T + 8, lanes]
            r.dcp[q, z.T : z.T + 8, lanes] = jnp.where(seq < z.S - 1, edge, 0.0)
            total = jnp.zeros((z.T, LANE), F32)
            for tap in range(4):
                total = total + r.convw[tap : tap + 1, lanes] * r.dcp[q, 3 - tap : 3 - tap + z.T, lanes]
            r.dxr[rows_of(q), lanes] = total.astype(BF16)

        lane_loop(x_lanes)

    swap_n = [Swap(z, links, lambda slot, q=q: r.nrecv.at[slot, rows_of(q), :]) for q in range(z.Q)]

    def normed_of(q, owner):
        return r.normed.at[rows_of(q), cut(owner * z.Df, z.Df)]

    def normed_part(q):
        rows = rows_of(q)

        def normed_to(index, means):
            away = index + 1
            owner = lax.rem(mp + away, z.M)
            for b in range(z.B):
                j = owner * z.B + b
                features = cut(j * z.Ds, z.Ds)
                part = nt(r.dxr[rows, :], r.wx[0, features, :]) + nt(r.dzr[rows, :], r.wx[1, features, :])
                r.normed[rows, features] = part.astype(BF16)
                scaled = part * r.tokg[j, rows, :].astype(F32)
                by_gain = jnp.sum(scaled * wide(r.inv[rows, :], z.Ds // LANE), axis=0, keepdims=True)
                for piece in range(z.Ds // LANE):
                    place = pl.ds(j * (z.Ds // LANE) + piece, 1)
                    value = by_gain[:, piece * LANE : (piece + 1) * LANE]
                    r.gv[place, :] = value if q == 0 else r.gv[place, :] + value
                means = means + jnp.sum(scaled * r.gain[:, features], axis=1, keepdims=True)

            @pl.when(away < z.M)
            def _():
                swap_n[q].one(normed_of(q, owner), away).start()

            return means

        means = lax.fori_loop(0, z.M, normed_to, jnp.zeros((z.T, 1), F32))
        mean_mine[:, rows] = jnp.broadcast_to(means, (z.T, LANE)).T[0:8]

    swap_m = Swap(z, links, lambda slot: r.mrow.at[slot])
    mean_mine = r.mrow.at[z.M - 1]

    def settle_back(level, q):
        back_take(level, q)
        if level < z.levels - 1:
            back_send(level + 1, q)

    totals_back(0)
    back_send(0, 0)
    each(z.M, branch_to)
    scatter_o.second(onto(sum_o, term_o), masks=most[1:])
    settle_back(0, 0)
    totals_back(1)
    back_send(0, 1)
    settle_back(0, 1)
    for mask in most[1:]:
        if mask & z.dims[0]:
            scatter_o.send(0, mask)
    scatter_1.first(into(near_i, term_1))
    for level in range(1, z.levels - 1):
        for q in range(z.Q):
            settle_back(level, q)
    for mask in most[1:]:
        if not mask & z.dims[0]:
            scatter_o.send(0, mask)
    scatter_1.second(onto(sum_1, term_1), send=True)
    query_sums(0)
    query_sums(1)
    for q in range(z.Q):
        back_take(z.levels - 1, q)
    for copy in scatter_1.sent[: len(z.masks)]:
        copy.wait_send()
    scatter_1.sent = scatter_1.sent[len(z.masks) :]
    tree_o.drain()
    walk_back(0)
    step_back(0)
    project_back(0)
    for step in range(depth - 1):
        scatter_o.fold(step)
    walk_back(1)
    for level in range(z.levels):
        pl.semaphore_signal(
            r.ready.at[level], inc=1, device_id=(seq ^ (1 << level), mp), device_id_type=MESH
        )
    step_back(1)
    project_back(1)
    for step in range(depth - 1):
        scatter_1.fold(step)
    sums_back(0)
    conv_back(0)

    last = depth - 1

    def write_to(ref):
        def write(rows, value):
            ref[rows, :] = value

        return write

    swap_out.wait()
    for away in range(1, z.M):
        owner = lax.rem(mp + away, z.M)
        swap_out.one(partial_of(owner), away).wait_send()

    def block_lanes(index):
        here = cut(index * LANE, LANE)
        total = r.normed[: z.R, cut(mp * z.Df + index * LANE, LANE)].astype(F32)
        for slot in range(z.M - 1):
            total = total + r.orecv[slot, :, here].astype(F32)
        r.blk[:, here] = (r.tok[:, here].astype(F32) + total).astype(BF16)

    each(z.Df // LANE, block_lanes)
    sums_back(1)
    conv_back(1)

    def put_small(first, lanes, value):
        count, at = value.shape[0], 0
        while at < count:
            block, inside = divmod(first + at, sg_rows)
            take = min(count - at, sg_rows - inside)
            sgp.block(block, inside, take)[:, lanes] = value[at : at + take].astype(BF16)
            at += take

    low_t = r.low[...].astype(F32).T.astype(BF16)
    used = 2 * z.RK + 2 * z.N + SGVEC

    def small_chunk(index):
        lanes = cut(index * 256, 256)
        put_small(0, lanes, nn(low_t, r.ddr[:, lanes]))
        put_small(z.RK, lanes, nn(r.dlowt[...], r.u[:, lanes]))
        put_small(2 * z.RK, lanes, nn(r.dst[...], r.u[:, lanes]))
        put_small(2 * z.RK + 2 * z.N, lanes, r.vec[:, lanes])
        if used < z.S * sg_rows:
            put_small(used, lanes, jnp.zeros((z.S * sg_rows - used, 256), F32))

    each(z.C // 256, small_chunk)
    for level in range(z.levels):
        pl.semaphore_wait(r.ready.at[level], 1)
    scatter_s.first(lambda device, mask: sgp.block(device))
    x_back(0)

    def add_small(device, mask):
        block, term = sum_s.block(mask // 2), sgp.block(device)

        def one(rows):
            block[rows, :] = (block[rows, :].astype(F32) + term[rows, :].astype(F32)).astype(BF16)

        by_rows(sg_rows, one)

    scatter_s.second(add_small, send=True)
    normed_part(0)
    for step in range(depth - 1):
        scatter_s.fold(step)

    x_back(1)

    scatter_0.first(into(near_i, term_0))
    scatter_0.second(onto(sum_0, term_0), send=True, masks=most[:1])
    scatter_0.second(onto(sum_0, term_0), send=True, masks=most[1:])

    normed_part(1)
    swap_m.start(mean_mine)

    gain_seq = SwapSeq(z, links, lambda slot: r.gvr.at[slot])
    gain_seq.start(r.gv)
    scatter_s.fold(last)

    def write_small(rows, value):
        small.block(seq)[rows, :] = value.astype(BF16)

    scatter_s.total(write_small)
    tree_s = TreeGather(
        z,
        links,
        lambda owner, h: small.block(owner, *halves(sg_rows)[h]),
        small.block,
    )
    tree_s.first()
    tree_s.second(0)
    tree_s.second(1)
    for step in range(depth - 1):
        scatter_0.fold(step)
    gain_seq.wait()
    gains = r.gv[...]
    for slot in range(z.S - 1):
        gains = gains + r.gvr[slot]
    r.gvs[...] = gains
    swap_g = Swap(z, links, lambda slot: r.gvm.at[slot])
    swap_g.start(r.gvs)
    tree_s.forward(0)
    tree_s.forward(1)
    scatter_o.fold(last)
    scatter_o.total(write_to(r.dout))
    scatter_1.fold(last)
    scatter_1.total(write_to(r.fac))
    store_1 = pltpu.make_async_copy(r.fac.at[pl.ds(0, z.Ds)], r.din.at[1], local.at[3])
    store_1.start()
    tree_s.settle()

    swap_m.wait()
    mean = r.mrow[0]
    for slot in range(1, z.M):
        mean = mean + r.mrow[slot]
    r.mean[...] = jnp.concatenate([mean] * (LANE // 8), axis=0).T * (1.0 / z.D)
    for swap in swap_n:
        swap.wait()

    def token_lanes(index):
        here = cut(index * LANE, LANE)
        inside = cut(mp * z.Df + index * LANE, LANE)
        for q in range(z.Q):
            rows = rows_of(q)
            total = r.normed[rows, inside].astype(F32)
            for slot in range(z.M - 1):
                total = total + r.nrecv[slot, rows, here].astype(F32)
            inv, x = r.inv[rows, :], r.tok[rows, here].astype(F32)
            value = inv * (total * r.gain[:, inside]) - x * (inv * inv * inv) * r.mean[rows, :]
            r.dtok[rows, here] = value + r.cot[rows, here] * seq_weight[q]

    each(z.Df // LANE, token_lanes)

    tree_s.finish()
    for block in range(z.S):
        count = min(sg_rows, r.sg.shape[0] - block * sg_rows)
        if count > 0:
            r.sg[block * sg_rows : block * sg_rows + count, :] = small.block(block, 0, count)[...].astype(F32)
    swap_g.wait()
    gains = r.gvs[...]
    for slot in range(z.M - 1):
        gains = gains + r.gvm[slot]
    r.dgain[...] = gains
    scatter_0.fold(last)
    scatter_0.total(write_to(r.s))
    store_0 = pltpu.make_async_copy(r.s.at[pl.ds(0, z.Ds)], r.din.at[0], local.at[4])
    store_0.start()

    hal.wait_send()
    for tree in (tree_x, tree_z, tree_s):
        tree.drain()
    for line in (*line_t, line_h, line_d):
        line.drain()
    for q in range(z.Q):
        swap_st[q].drain(st_mine[q])
        swap_low[q].drain(low_mine[q])
        swap_dlow[q].drain(dlow_mine[q])
        swap_dst[q].drain(dst_mine[q])
    swap_m.drain(mean_mine)
    swap_g.drain(r.gvs)
    gain_seq.drain()
    for away in range(1, z.M):
        owner = lax.rem(mp + away, z.M)
        for q in range(z.Q):
            swap_n[q].one(normed_of(q, owner), away).wait_send()
    for copy in carry_copies + rim:
        copy.wait_send()
    for scatter in (scatter_o, scatter_1, scatter_0, scatter_s):
        scatter.drain()
    store_1.wait()
    store_0.wait()


def finish_kernel(z, blk, dtok, dgain, din, dout, sg, *outs):
    a, b, c = z.RK, 2 * z.RK, 2 * z.RK + 2 * z.N
    o_blk, o_dtok, o_dgain, o_din, o_convw, o_convb, o_low, o_state, o_delta, o_dbias, o_skip, o_dout = outs
    o_blk[...] = blk[...]
    o_dtok[...] = dtok[...]
    o_dgain[...] = dgain[...]
    o_din[...] = din[...]
    o_dout[...] = dout[...]
    o_delta[...] = sg[0:a, :]
    o_state[...] = sg[b:c, :]
    o_convw[...] = sg[c : c + 4, :]
    o_convb[...] = sg[c + 4 : c + 5, :]
    o_dbias[...] = sg[c + 5 : c + 6, :]
    o_skip[...] = sg[c + 6 : c + 7, :]
    for at in range(0, sg.shape[1], LANE):
        o_low[at : at + LANE, :] = sg[a:b, at : at + LANE].T


def fused(z, tokens, norm_gain, in_weight, conv_weight, conv_bias, low_weight, state_weight, delta_weight,
          delta_bias, skip_gain, out_weight, cotangent, seq_group, group_weight):
    V = pl.BlockSpec(memory_space=pltpu.VMEM)
    A = pl.BlockSpec(memory_space=pl.ANY)
    SM = pl.BlockSpec(memory_space=pltpu.SMEM)
    row = lambda value: value.reshape(1, -1)
    operands = dict(
        tok_in=(A, tokens.reshape(z.R, z.Df)),
        cot_in=(A, cotangent.reshape(z.R, z.Df)),
        gain_in=(A, row(norm_gain)),
        win=(A, in_weight),
        wout=(A, out_weight),
        convw_in=(A, conv_weight),
        convb_in=(A, row(conv_bias)),
        dbias_in=(A, row(delta_bias)),
        skip_in=(A, row(skip_gain)),
        loww_in=(A, low_weight),
        statewt_in=(A, state_weight.T),
        deltaw_in=(A, delta_weight),
        seqg=(SM, seq_group),
        groupw=(SM, group_weight),
    )
    scratch = scratch_of(z)
    sg_used = 2 * z.RK + 2 * z.N + SGVEC
    outs = dict(
        blk=(V, (z.R, z.Df), BF16),
        dtok=(V, (z.R, z.Df), F32),
        dgain=(V, (z.D // LANE, LANE), F32),
        din=(A, (2, z.Ds, z.C), F32),
        dout=(V, (z.C, z.Ds), F32),
        sg=(V, (sg_used, z.C), F32),
    )
    result = pl.pallas_call(
        functools.partial(fused_kernel, z, [*operands, *outs, *scratch]),
        out_shape=[jax.ShapeDtypeStruct(shape, kind) for _, shape, kind in outs.values()],
        in_specs=[spec for spec, _ in operands.values()],
        out_specs=[spec for spec, _, _ in outs.values()],
        scratch_shapes=list(scratch.values()),
        compiler_params=pltpu.CompilerParams(
            collective_id=0, has_side_effects=True, vmem_limit_bytes=VMEM_BYTES
        ),
    )(*[value for _, value in operands.values()])
    whole = (V, (1, z.C), F32)
    last = dict(
        blk=(V, (z.R, z.Df), BF16),
        dtok=(V, (z.R, z.Df), F32),
        dgain=(V, (z.D // LANE, LANE), F32),
        din=(V, (2, z.Ds, z.C), F32),
        convw=(V, (4, z.C), F32),
        convb=whole,
        low=(V, (z.C, z.RK), F32),
        state=(V, (2 * z.N, z.C), F32),
        delta=(V, (z.RK, z.C), F32),
        dbias=whole,
        skip=whole,
        dout=(V, (z.C, z.Ds), F32),
    )
    done = pl.pallas_call(
        functools.partial(finish_kernel, z),
        out_shape=[jax.ShapeDtypeStruct(shape, kind) for _, shape, kind in last.values()],
        in_specs=[V] * 6,
        out_specs=[spec for spec, _, _ in last.values()],
        compiler_params=pltpu.CompilerParams(vmem_limit_bytes=VMEM_BYTES),
    )(*result)
    done = dict(zip(last, done))
    done.update(blk=done["blk"].reshape(tokens.shape), dtok=done["dtok"].reshape(tokens.shape))
    done.update(dgain=done["dgain"].reshape(z.D), state=done["state"].T)
    done.update({name: done[name][0] for name in ("convb", "dbias", "skip")})
    return tuple(done.values())


def local(mesh_shape, *arrays):
    tokens, norm_gain, in_weight, conv_weight = arrays[:4]
    state_weight, delta_weight = arrays[6], arrays[7]
    z = Sizes(
        mesh_shape,
        tokens.shape[0],
        tokens.shape[1],
        tokens.shape[2],
        norm_gain.shape[0],
        in_weight.shape[2],
        state_weight.shape[1] // 2,
        delta_weight.shape[0],
    )
    if z.fits(conv_weight.shape[0]):
        return fused(z, *arrays)
    return plain(*arrays)


def solution(mesh):
    placed = (
        P(None, "seq", "mp"),
        P(),
        P(None, "seq", "mp"),
        P(None, "mp"),
        P("mp"),
        P("mp", None),
        P("mp", None),
        P(None, "mp"),
        P("mp"),
        P("mp"),
        P("mp", "seq"),
        P(None, "seq", "mp"),
        P(),
        P(),
    )
    return jax.shard_map(
        functools.partial(local, dict(mesh.shape)),
        mesh=mesh,
        in_specs=placed,
        out_specs=(
            P(None, "seq", "mp"),
            P(None, "seq", "mp"),
            P(),
            P(None, "seq", "mp"),
            P(None, "mp"),
            P("mp"),
            P("mp", None),
            P("mp", None),
            P(None, "mp"),
            P("mp"),
            P("mp"),
            P("mp", "seq"),
        ),
        check_vma=False,
    )
```
